32 devices in a mesh: dp: 4 (over z), expert: 8 (over y, x, core).
Axes of the slice: x: 2, y: 2, z: 4, core: 2. Of those that a mesh axis runs over, the one named last changes fastest.
Arguments:
- route_ids: int32 [4096, 8], P(('dp', 'expert')), may hold values from 0 to 127, all different within a row; in each aligned block of 128 rows (0 to 127, 128 to 255, ...) at most 16 rows name the same one
- route_probs: float32 [4096, 8], P(('dp', 'expert')), may hold values from 0.05 to 0.6
- capacity: int32 [8], replicated, may hold values from 4 to 16, as said below
- hot_lists: int32 [4, 4], P('dp'), may hold values from 0 to 7, as said below
- gate_up: bfloat16 [4, 8, 128, 1536], P('dp', 'expert'), may hold values from -6 to 6
- w_quant: bfloat16 [8, 768, 4096], P('expert'), may hold values from -0.21875 to 0.21875
- w_scale: float32 [8, 6, 32], P('expert'), may hold values from 0.5 to 2
- d_out: bfloat16 [4096, 4096], P(('dp', 'expert')), may hold values from -6 to 6
Outputs:
- combined: bfloat16 [4096, 4096], P(('dp', 'expert'))
- d_probs: float32 [4096, 8], P(('dp', 'expert'))
- d_gate_up: bfloat16 [4, 8, 128, 1536], P('dp', 'expert')
- d_w_down: bfloat16 [8, 4096, 768], P('expert', 'dp')
The draws below stay inside these ranges and needn't reach their ends.
Inputs may be any that keep to these rules, and one draw needn't show every extreme that they name: `route_ids`: each row names 8 different experts; among the rows of one device no expert is named more than 16 times, a bound that some block reaches. `capacity`: each entry is a multiple of 4; some expert has exactly 16. `hot_lists`: each row names 4 different experts among the 8 computed ones.
All inputs are finite; a program needn't handle non-finite values.
Results may differ from the reference program's by a relative error of at most 0.017.
Values may be sent and summed in bfloat16 or wider, within the bound.
No kernel may reach another device: no remote copies, remote signals or barrier semaphores. Data moves between devices by JAX's collectives and lax.ppermute only.
A program may use at most 128 MiB of HBM per device.

```python
import math
import jax
import jax.numpy as jnp
import numpy as np
from jax import lax

D = 4096
NE = 128
TOPK = 8
HID = 768
QB = 128
HOT = 4
TOK_DEV = 128
CAP = 16
FLIGHT = 8
GROUPS = 4
SLOTS = 128
TOKENS = 4096
N_DP = 4
N_EXPERT = 8


def draw_capacity(key, part):
    step_size = CAP // 4
    levels = jax.random.randint(key, (FLIGHT,), 1, 5)
    chosen = jax.random.randint(jax.random.fold_in(key, 7), (), 0, FLIGHT)
    values = jnp.where(jnp.arange(FLIGHT) == chosen, 4, levels) * step_size
    return values.astype(jnp.int32)


def draw_hot_lists(key, part):
    group_keys = jax.random.split(key, GROUPS)

    def one_group(group_key):
        return jax.random.permutation(group_key, FLIGHT)[:HOT]
    return jax.vmap(one_group)(group_keys).astype(jnp.int32)


def level_of(own_key, dims, cuts, low, high):
    gain, own = 1.0, jax.random.fold_in(own_key, 6)
    for dim, blocks in cuts:
        draws = jnp.exp(jax.random.uniform(jax.random.fold_in(own, dim), (blocks,), jnp.float32, low / len(cuts), high / len(cuts)))
        gain = gain * jnp.repeat(draws, dims[dim] // blocks).reshape([-1 if axis == dim else 1 for axis in range(len(dims))])
    return gain


def routed_block(key, own, number, rows, number_of, top, most, lean):
    order = jax.random.permutation(key, number_of)
    heavy_load, common = load_shares(number_of, rows * top, most, lean, True), load_shares(number_of, rows * top, most, lean, False)
    places = jnp.arange(number_of)

    def named(lengths, rotation):
        used = int((lengths > 0).sum())
        fixed = max(1, used // 4)
        passed = fixed + (places - fixed + rotation * (used - fixed)) % max(1, number_of - fixed)
        return jnp.zeros((number_of,), jnp.int32).at[order[jnp.where(places < fixed, places, passed)]].set(jnp.asarray(lengths, jnp.int32))

    lengths = jnp.where(number % 4 == 0, named(heavy_load, number // 4), named(common, number - number // 4 - 1))
    mixed = jax.random.permutation(jax.random.fold_in(own, 3), number_of)
    giver, sink = mixed[0:number_of // 2 * 2:2], mixed[1:number_of // 2 * 2:2]
    slack = jnp.minimum(lengths[giver] - 1, most - lengths[sink]) // 2
    slack = jnp.where((giver == order[0]) | (sink == order[0]) | (lengths[sink] == 0), 0, jnp.maximum(slack, 0))
    passed = jax.random.randint(jax.random.fold_in(own, 4), (number_of // 2,), 0, 1 << 20) % (slack + 1)
    lengths = lengths.at[giver].add(-passed).at[sink].add(passed)
    members = jnp.searchsorted(jnp.cumsum(lengths), jnp.arange(rows * top), side="right").astype(jnp.int32)
    table = members.reshape(top, rows).T
    table = table[jax.random.permutation(jax.random.fold_in(own, 1), rows)]
    rotation = jax.random.randint(jax.random.fold_in(own, 2), (rows, 1), 0, top)
    return jnp.take_along_axis(table, (jnp.arange(top)[None, :] + rotation) % top, axis=1)


def load_shares(number_of, total, most, skew, full):
    portions = [(1 << 20) // math.isqrt(standing ** skew) + 1 for standing in range(1, number_of + 1)]
    largest = most if full else min(most, max(-(-total // number_of), total * portions[0] // sum(portions)))
    least = 1 if total - largest >= number_of - 1 else 0
    given, rest = [largest] + [least] * (number_of - 1), total - largest - least * (number_of - 1)
    while rest > 0:
        free = [i for i in range(1, number_of) if given[i] < largest] or [i for i in range(1, number_of) if given[i] < most]
        whole, remaining = sum([portions[i] for i in free]), rest
        for i in free:
            extra = min(most - given[i], max(1, remaining * portions[i] // whole), rest)
            given[i] = given[i] + extra
            rest = rest - extra
    return np.array(given)


def normal_values(key, extent, deviation, most, cuts=(), kind=jnp.bfloat16):
    factor_of = level_of(key, extent, cuts, -0.22, 0.18) if cuts else 1.0
    values = jax.random.normal(key, extent, jnp.float32) * deviation * factor_of
    return jnp.minimum(jnp.maximum(values, -most), most).astype(kind)


def setup_inputs(seed: int = 0) -> dict:
    keys = jax.random.split(jax.random.key(seed), 9)
    route_ids_keys = jax.random.split(jax.random.fold_in(keys[0], 1), TOKENS // TOK_DEV)
    route_ids_turns = jax.random.permutation(jax.random.fold_in(keys[0], 3), TOKENS // TOK_DEV)
    route_ids = jax.vmap(lambda own, number: routed_block(jax.random.fold_in(keys[0], 2), own, number, TOK_DEV, NE, TOPK, CAP, 2))(route_ids_keys, route_ids_turns).reshape((TOKENS, TOPK))
    route_probs = jnp.clip(jnp.exp(math.log(0.6) - 2.4849067 * jax.random.uniform(keys[1], (TOKENS, TOPK), jnp.float32) ** level_of(keys[1], (TOKENS, TOPK), ((0, 32),), -0.2, 0.2)), 0.05, 0.6)
    capacity = draw_capacity(jax.random.fold_in(keys[8], 71), 0)
    hot_lists = draw_hot_lists(jax.random.fold_in(keys[8], 71), 0)
    gate_up = normal_values(keys[4], (GROUPS, FLIGHT, SLOTS, 2 * HID), 1.0, 6.0, ((0, 4), (1, 8)))
    w_quant = normal_values(keys[5], (FLIGHT, HID, D), HID ** -0.5, 0.21875, ((0, 8),))
    w_scale = jnp.clip(jnp.exp(math.log(2.0) - 1.3862944 * jax.random.uniform(keys[6], (FLIGHT, HID // QB, D // QB), jnp.float32) ** level_of(keys[6], (FLIGHT, HID // QB, D // QB), ((0, 8),), -0.2, 0.2)), 0.5, 2.0)
    d_out = normal_values(keys[7], (TOKENS, D), 1.0, 6.0, ((0, 32),))
    return {"route_ids": route_ids, "route_probs": route_probs, "capacity": capacity, "hot_lists": hot_lists, "gate_up": gate_up, "w_quant": w_quant, "w_scale": w_scale, "d_out": d_out}


def routing(expert_ids, capacity, hot_row, flight):
    experts_iota = jnp.arange(flight, dtype=jnp.int32)
    onehot = (expert_ids[:, None] == experts_iota[None, :]).astype(jnp.int32)
    earlier = jnp.cumsum(onehot, axis=0) - onehot
    slot_rank = jnp.sum(earlier * onehot, axis=1)
    hot_count = jnp.sum((hot_row[:, None] == experts_iota[None, :]).astype(jnp.int32), axis=0)
    limits = jnp.where(hot_count > 0, CAP, capacity)
    row_limit = jnp.sum(onehot * limits[None, :], axis=1)
    kept_mask = (expert_ids < flight) & (slot_rank < row_limit)
    return kept_mask, slot_rank


def dequant(quantized, block_scale):
    expanded = jnp.repeat(jnp.repeat(block_scale, QB, axis=0), QB, axis=1)
    return (quantized.astype(jnp.float32) * expanded).astype(jnp.bfloat16)


def swiglu_parts(arrived):
    gate_in = arrived[..., :HID].astype(jnp.float32)
    up_in = arrived[..., HID:].astype(jnp.float32)
    return gate_in, up_in, jax.nn.sigmoid(gate_in)


def reference(route_ids, route_probs, capacity, hot_lists, gate_up, w_quant, w_scale, d_out):
    flight = N_EXPERT
    slot_count = N_EXPERT * CAP
    per_device = TOK_DEV * TOPK
    group_ids = route_ids.reshape(N_DP, N_EXPERT, per_device)

    def route_group(device_ids, hot_row):
        def route_device(one_device):
            return routing(one_device, capacity, hot_row, flight)
        return jax.vmap(route_device)(device_ids)

    kept_mask, slot_rank = jax.vmap(route_group)(group_ids, hot_lists)
    source_iota = jnp.arange(N_EXPERT, dtype=jnp.int32)[None, :, None]
    slot_index = jnp.where(kept_mask, group_ids * slot_count + source_iota * CAP + slot_rank, flight * slot_count).astype(jnp.int32)
    route_weight = jnp.where(kept_mask, route_probs.reshape(N_DP, N_EXPERT, per_device), 0.0)
    cotangent = d_out.reshape(N_DP, N_EXPERT, TOK_DEV, D)

    def expert_forward(inputs):
        quantized, block_scale, arrived = inputs
        weight = dequant(quantized, block_scale)
        gate_in, up_in, sig_gate = swiglu_parts(arrived)
        hidden = (gate_in * sig_gate * up_in).astype(jnp.bfloat16)
        expert_out = jnp.dot(hidden.reshape(N_DP * slot_count, HID), weight, preferred_element_type=jnp.float32)
        return expert_out.astype(jnp.bfloat16).reshape(N_DP, slot_count, D)

    by_expert = jnp.moveaxis(gate_up, 1, 0)
    outputs = jnp.moveaxis(lax.map(expert_forward, (w_quant, w_scale, by_expert)), 1, 0)

    def source_group(inputs):
        group_out, group_index, group_weight, group_cot = inputs
        padded = jnp.concatenate([group_out.reshape(flight * slot_count, D), jnp.zeros((1, D), jnp.bfloat16)], axis=0)
        picked = padded[group_index.reshape(-1)].reshape(N_EXPERT, TOK_DEV, TOPK, D).astype(jnp.float32)
        weights_here = group_weight.reshape(N_EXPERT, TOK_DEV, TOPK)
        combined = jnp.sum(picked * weights_here[..., None], axis=2).astype(jnp.bfloat16)
        cot_float = group_cot.astype(jnp.float32)
        d_probs = jnp.sum(picked * cot_float[:, :, None, :], axis=3)
        sent_rows = (weights_here[..., None] * cot_float[:, :, None, :]).astype(jnp.bfloat16).reshape(N_EXPERT * per_device, D)
        grad_slots = jnp.zeros((flight * slot_count + 1, D), jnp.bfloat16).at[group_index.reshape(-1)].set(sent_rows)
        return combined, d_probs, grad_slots[:flight * slot_count].reshape(flight, slot_count, D)

    combined, d_probs, grad_slots = lax.map(source_group, (outputs, slot_index, route_weight, cotangent))
    grad_by_expert = jnp.moveaxis(grad_slots, 1, 0)

    def expert_backward(inputs):
        quantized, block_scale, arrived, arrived_grads = inputs
        weight = dequant(quantized, block_scale)
        gate_in, up_in, sig_gate = swiglu_parts(arrived)
        silu_gate = gate_in * sig_gate
        hidden = (silu_gate * up_in).astype(jnp.bfloat16)
        d_hidden = jnp.dot(arrived_grads.reshape(N_DP * slot_count, D), weight.T, preferred_element_type=jnp.float32).reshape(N_DP, slot_count, HID)
        d_gate = d_hidden * up_in * sig_gate * (1.0 + gate_in * (1.0 - sig_gate))
        d_up = d_hidden * silu_gate
        d_arrived = jnp.concatenate([d_gate, d_up], axis=-1).astype(jnp.bfloat16)
        group_terms = jnp.einsum("gsh,gsd->gdh", hidden.astype(jnp.float32), arrived_grads.astype(jnp.float32))
        rounded = lax.optimization_barrier(group_terms.astype(jnp.bfloat16))
        d_weight = jnp.sum(rounded.astype(jnp.float32), axis=0).astype(jnp.bfloat16)
        return d_arrived, d_weight

    d_arrived, d_weight = lax.map(expert_backward, (w_quant, w_scale, by_expert, grad_by_expert))
    return (combined.reshape(N_DP * N_EXPERT * TOK_DEV, D), d_probs.reshape(N_DP * N_EXPERT * TOK_DEV, TOPK), jnp.moveaxis(d_arrived, 0, 1), d_weight)
```

```python
import functools

import jax
import jax.numpy as jnp
from jax import lax
from jax.experimental import pallas as pl
from jax.experimental.pallas import tpu as pltpu
from jax.sharding import PartitionSpec as P

QB = 128
CAP = 16
VMEM_LIMIT = 48 * 1024 * 1024

bf16 = jnp.bfloat16
f32 = jnp.float32


def params():
    return pltpu.CompilerParams(vmem_limit_bytes=VMEM_LIMIT)


def vmem_spec():
    return pl.BlockSpec(memory_space=pltpu.VMEM)


def smem_spec():
    return pl.BlockSpec(memory_space=pltpu.SMEM)


def dispatch_kernel(flight, groups, cap_ref, hot_ref, ids_ref, probs_ref, dout_ref, full_ref, parts_ref, own_ref):
    tokens, topk = ids_ref.shape
    slots = flight * CAP
    lane = lax.broadcasted_iota(jnp.int32, (1, slots), 1)
    lane_expert = lane // CAP
    lane_rank = (lane % CAP).astype(f32)
    limit = jnp.zeros((1, slots), jnp.int32)
    for e in range(flight):
        hot = hot_ref[0, 0] == e
        for h in range(1, hot_ref.shape[1]):
            hot = jnp.logical_or(hot, hot_ref[0, h] == e)
        limit = jnp.where(lane_expert == e, jnp.where(hot, CAP, cap_ref[e]), limit)
    limit = limit.astype(f32)
    ids = ids_ref[...]
    probs = probs_ref[...]
    named = jnp.zeros((tokens, slots), f32)
    weight = jnp.zeros((tokens, slots), f32)
    for k in range(topk):
        hit = ids[:, k : k + 1] == lane_expert
        named = jnp.where(hit, 1.0, named)
        weight = jnp.where(hit, probs[:, k : k + 1], weight)
    row = lax.broadcasted_iota(jnp.int32, (tokens, tokens), 0)
    col = lax.broadcasted_iota(jnp.int32, (tokens, tokens), 1)
    before = (col < row).astype(f32).astype(bf16)
    rank = jnp.dot(before, named.astype(bf16), preferred_element_type=f32)
    owns = (named > 0.0) & (rank == lane_rank) & (rank < limit)
    own_weight = jnp.where(owns, weight, 0.0)
    own_ref[...] = own_weight
    owner = jnp.where(owns, 1.0, 0.0).T.astype(bf16)
    slot_weight = jnp.sum(own_weight.T, axis=1, keepdims=True)
    share = dout_ref.shape[1] // groups
    for g in range(groups):
        cols = pl.ds(g * share, share)
        rows = jnp.dot(owner, dout_ref[:, cols], preferred_element_type=f32)
        rows = (rows * slot_weight).astype(bf16)
        full_ref[:, cols] = rows
        parts_ref[g] = rows


def dispatch(capacity, hot_row, route_ids, route_probs, d_out, flight, groups):
    tokens, width = d_out.shape
    slots = flight * CAP
    return pl.pallas_call(
        functools.partial(dispatch_kernel, flight, groups),
        out_shape=(
            jax.ShapeDtypeStruct((slots, width), bf16),
            jax.ShapeDtypeStruct((groups, slots, width // groups), bf16),
            jax.ShapeDtypeStruct((tokens, slots), f32),
        ),
        in_specs=[smem_spec(), smem_spec(), vmem_spec(), vmem_spec(), vmem_spec()],
        out_specs=(vmem_spec(), vmem_spec(), vmem_spec()),
        compiler_params=params(),
        name="dispatch",
    )(capacity, hot_row, route_ids, route_probs, d_out)


def forward_kernel(block, scale_ref, gate_up_ref, quant_ref, hidden_ref, weight_ref, out_ref):
    step = pl.program_id(0)
    hid = hidden_ref.shape[1]

    @pl.when(step == 0)
    def _():
        gate = gate_up_ref[:, :hid].astype(f32)
        up = gate_up_ref[:, hid:].astype(f32)
        hidden_ref[...] = (gate * jax.nn.sigmoid(gate) * up).astype(bf16)

    for i in range(hid // QB):
        for j in range(block // QB):
            at = (pl.ds(i * QB, QB), pl.ds(j * QB, QB))
            scale = scale_ref[i, step * (block // QB) + j]
            weight_ref[at] = (quant_ref[at].astype(f32) * scale).astype(bf16)
    out_ref[...] = jnp.dot(hidden_ref[...], weight_ref[...], preferred_element_type=f32).astype(bf16)


def forward(w_scale, gate_up, w_quant, block=512):
    slots, double = gate_up.shape
    hid, width = w_quant.shape
    return pl.pallas_call(
        functools.partial(forward_kernel, block),
        grid=(width // block,),
        out_shape=(
            jax.ShapeDtypeStruct((slots, hid), bf16),
            jax.ShapeDtypeStruct((hid, width), bf16),
            jax.ShapeDtypeStruct((slots, width), bf16),
        ),
        in_specs=[
            smem_spec(),
            pl.BlockSpec((slots, double), lambda i: (0, 0)),
            pl.BlockSpec((hid, block), lambda i: (0, i)),
        ],
        out_specs=(
            pl.BlockSpec((slots, hid), lambda i: (0, 0)),
            pl.BlockSpec((hid, block), lambda i: (0, i)),
            pl.BlockSpec((slots, block), lambda i: (0, i)),
        ),
        compiler_params=params(),
        name="expert_forward",
    )(w_scale, gate_up, w_quant)


def backward_kernel(gate_up_ref, grads_ref, weight_ref, out_ref, acc_ref):
    step = pl.program_id(0)
    hid = acc_ref.shape[1]
    part = lax.dot_general(
        grads_ref[...], weight_ref[...], (((1,), (1,)), ((), ())), preferred_element_type=f32
    )

    @pl.when(step == 0)
    def _():
        acc_ref[...] = part

    @pl.when(step > 0)
    def _():
        acc_ref[...] += part

    @pl.when(step == pl.num_programs(0) - 1)
    def _():
        gate = gate_up_ref[:, :hid].astype(f32)
        up = gate_up_ref[:, hid:].astype(f32)
        sig = jax.nn.sigmoid(gate)
        d_hidden = acc_ref[...]
        out_ref[:, :hid] = (d_hidden * up * sig * (1.0 + gate * (1.0 - sig))).astype(bf16)
        out_ref[:, hid:] = (d_hidden * (gate * sig)).astype(bf16)


def backward(gate_up, grads, weight, block=1024):
    slots, double = gate_up.shape
    hid, width = weight.shape
    return pl.pallas_call(
        backward_kernel,
        grid=(width // block,),
        out_shape=jax.ShapeDtypeStruct((slots, double), bf16),
        in_specs=[
            pl.BlockSpec((slots, double), lambda i: (0, 0)),
            pl.BlockSpec((slots, block), lambda i: (0, i)),
            pl.BlockSpec((hid, block), lambda i: (0, i)),
        ],
        out_specs=pl.BlockSpec((slots, double), lambda i: (0, 0)),
        scratch_shapes=[pltpu.VMEM((slots, hid), f32)],
        compiler_params=params(),
        name="expert_backward",
    )(gate_up, grads, weight)


def combine_kernel(ids_ref, own_ref, dout_ref, ret_ref, out_ref, dprobs_ref, acc_ref):
    step = pl.program_id(0)
    tokens, topk = ids_ref.shape
    slots = own_ref.shape[1]
    own = own_ref[...]
    high = own.astype(bf16)
    low = (own - high.astype(f32)).astype(bf16)
    ret = ret_ref[...]
    out = jnp.dot(high, ret, preferred_element_type=f32)
    out = out + jnp.dot(low, ret, preferred_element_type=f32)
    out_ref[...] = out.astype(bf16)
    part = lax.dot_general(
        dout_ref[...], ret, (((1,), (1,)), ((), ())), preferred_element_type=f32
    )

    @pl.when(step == 0)
    def _():
        acc_ref[...] = part

    @pl.when(step > 0)
    def _():
        acc_ref[...] += part

    @pl.when(step == pl.num_programs(0) - 1)
    def _():
        inner = jnp.where(own > 0.0, acc_ref[...], 0.0)
        lane_expert = lax.broadcasted_iota(jnp.int32, (1, slots), 1) // CAP
        place = lax.broadcasted_iota(jnp.int32, (tokens, topk), 1)
        ids = ids_ref[...]
        result = jnp.zeros((tokens, topk), f32)
        for k in range(topk):
            mine = jnp.where(ids[:, k : k + 1] == lane_expert, inner, 0.0)
            result = jnp.where(place == k, jnp.sum(mine, axis=1, keepdims=True), result)
        dprobs_ref[...] = result


def combine(route_ids, own, d_out, returned, block=1024):
    tokens, width = d_out.shape
    topk = route_ids.shape[1]
    slots = own.shape[1]
    return pl.pallas_call(
        combine_kernel,
        grid=(width // block,),
        out_shape=(
            jax.ShapeDtypeStruct((tokens, width), bf16),
            jax.ShapeDtypeStruct((tokens, topk), f32),
        ),
        in_specs=[
            pl.BlockSpec((tokens, topk), lambda i: (0, 0)),
            pl.BlockSpec((tokens, slots), lambda i: (0, 0)),
            pl.BlockSpec((tokens, block), lambda i: (0, i)),
            pl.BlockSpec((slots, block), lambda i: (0, i)),
        ],
        out_specs=(
            pl.BlockSpec((tokens, block), lambda i: (0, i)),
            pl.BlockSpec((tokens, topk), lambda i: (0, 0)),
        ),
        scratch_shapes=[pltpu.VMEM((tokens, slots), f32)],
        compiler_params=params(),
        name="combine",
    )(route_ids, own, d_out, returned)


def weight_grad_kernel(grads_ref, hidden_ref, out_ref):
    out_ref[...] = lax.dot_general(
        grads_ref[...], hidden_ref[...], (((0,), (0,)), ((), ())), preferred_element_type=f32
    ).astype(bf16)


def weight_grad(grads, hidden, block=256):
    rows, share = grads.shape
    hid = hidden.shape[1]
    return pl.pallas_call(
        weight_grad_kernel,
        grid=(share // block,),
        out_shape=jax.ShapeDtypeStruct((share, hid), bf16),
        in_specs=[
            pl.BlockSpec((rows, block), lambda i: (0, i)),
            pl.BlockSpec((rows, hid), lambda i: (0, 0)),
        ],
        out_specs=pl.BlockSpec((block, hid), lambda i: (i, 0)),
        compiler_params=params(),
        name="weight_grad",
    )(grads, hidden)


def shards(route_ids, route_probs, capacity, hot_lists, gate_up, w_quant, w_scale, d_out):
    flight = lax.axis_size("expert")
    groups = lax.axis_size("dp")
    slots = flight * CAP
    width = d_out.shape[1]
    gate_up = gate_up[0, 0]
    full, parts, own = dispatch(
        capacity, hot_lists, route_ids, route_probs, d_out, flight, groups
    )
    crossed = lax.all_to_all(
        parts.reshape(groups * flight, CAP, width // groups),
        ("dp", "expert"),
        split_axis=0,
        concat_axis=0,
        tiled=True,
    )
    arrived = lax.all_to_all(
        full.reshape(flight, CAP, width), "expert", split_axis=0, concat_axis=0, tiled=True
    )
    hidden, weight, expert_out = forward(w_scale[0], gate_up, w_quant[0])
    hidden_all = lax.all_gather(hidden, "dp", axis=0, tiled=True)
    returned = lax.all_to_all(
        expert_out.reshape(flight, CAP, width), "expert", split_axis=0, concat_axis=0, tiled=True
    )
    d_gate_up = backward(gate_up, arrived.reshape(slots, width), weight)
    combined, d_probs = combine(route_ids, own, d_out, returned.reshape(slots, width))
    d_weight = weight_grad(crossed.reshape(groups * slots, width // groups), hidden_all)
    return (combined, d_probs, d_gate_up[None, None], d_weight[None])


def solution(mesh):
    placed = (
        P(("dp", "expert"), None),
        P(("dp", "expert"), None),
        P(),
        P("dp", None),
        P("dp", "expert", None, None),
        P("expert", None, None),
        P("expert", None, None),
        P(("dp", "expert"), None),
    )
    return jax.shard_map(
        shards,
        mesh=mesh,
        in_specs=placed,
        out_specs=(
            P(("dp", "expert"), None),
            P(("dp", "expert"), None),
            P("dp", "expert", None, None),
            P("expert", "dp", None),
        ),
        check_vma=False,
    )
```

```python
import functools

import jax
import jax.numpy as jnp
from jax import lax
from jax.experimental import pallas as pl
from jax.experimental.pallas import tpu as pltpu
from jax.sharding import PartitionSpec as P

QB = 128
CAP = 16
VMEM_LIMIT = 40 * 1024 * 1024

bf16 = jnp.bfloat16
f32 = jnp.float32

VMEM = pl.BlockSpec(memory_space=pltpu.VMEM)
SMEM = pl.BlockSpec(memory_space=pltpu.SMEM)
ANY = pl.BlockSpec(memory_space=pl.ANY)


def params():
    return pltpu.CompilerParams(vmem_limit_bytes=VMEM_LIMIT)


def cost(flops, moved):
    return pl.CostEstimate(flops=flops, bytes_accessed=moved, transcendentals=0)


def chunks(total, size):
    return [pl.ds(start, size) for start in range(0, total, size)]


def hidden_kernel(gate_up_ref, out_ref):
    hid = out_ref.shape[1]
    gate = gate_up_ref[:, :hid].astype(f32)
    up = gate_up_ref[:, hid:].astype(f32)
    out_ref[...] = (gate * jax.nn.sigmoid(gate) * up).astype(bf16)


def make_hidden(gate_up):
    slots, double = gate_up.shape
    return pl.pallas_call(
        hidden_kernel,
        out_shape=pltpu.HBM((slots, double // 2), bf16),
        in_specs=[VMEM],
        out_specs=VMEM,
        compiler_params=params(),
        name="hidden",
    )(gate_up)


def dispatch_kernel(flight, groups, cap_ref, hot_ref, ids_ref, probs_ref, dout_ref, own_ref, parts_ref, *full_refs):
    topk, tokens = ids_ref.shape
    slots = flight * CAP
    me = lax.axis_index("expert")
    row = lax.broadcasted_iota(jnp.int32, (slots, 1), 0)
    row_expert = (row // CAP) ^ me
    row_rank = (row % CAP).astype(f32)
    limit = jnp.zeros((slots, 1), jnp.int32)
    for e in range(flight):
        hot = hot_ref[0, 0] == e
        for h in range(1, hot_ref.shape[1]):
            hot = jnp.logical_or(hot, hot_ref[0, h] == e)
        limit = jnp.where(row_expert == e, jnp.where(hot, CAP, cap_ref[e]), limit)
    limit = limit.astype(f32)
    named = jnp.zeros((slots, tokens), f32)
    weight = jnp.zeros((slots, tokens), f32)
    for k in range(topk):
        hit = ids_ref[k : k + 1, :] == row_expert
        named = jnp.where(hit, 1.0, named)
        weight = jnp.where(hit, probs_ref[k : k + 1, :], weight)
    first = lax.broadcasted_iota(jnp.int32, (tokens, tokens), 0)
    second = lax.broadcasted_iota(jnp.int32, (tokens, tokens), 1)
    before = (first < second).astype(f32).astype(bf16)
    rank = jnp.dot(named.astype(bf16), before, preferred_element_type=f32)
    owns = (named > 0.0) & (rank == row_rank) & (rank < limit)
    own_weight = jnp.where(owns, weight, 0.0)
    own_ref[...] = own_weight
    owner = jnp.where(owns, 1.0, 0.0).astype(bf16)
    slot_weight = jnp.sum(own_weight, axis=1, keepdims=True)
    share = dout_ref.shape[1] // groups
    for g in range(groups):
        cols = pl.ds(g * share, share)
        rows = jnp.dot(owner, dout_ref[:, cols], preferred_element_type=f32)
        rows = (rows * slot_weight).astype(bf16)
        for j in range(flight):
            block = rows[j * CAP : (j + 1) * CAP, :]
            full_refs[j][:, cols] = block
            parts_ref[g, pl.ds(pl.multiple_of((me ^ j) * CAP, CAP), CAP), :] = block


def dispatch(capacity, hot_row, ids, probs, d_out, flight, groups):
    tokens, width = d_out.shape
    slots = flight * CAP
    return pl.pallas_call(
        functools.partial(dispatch_kernel, flight, groups),
        out_shape=(
            jax.ShapeDtypeStruct((slots, tokens), f32),
            pltpu.HBM((groups, slots, width // groups), bf16),
        )
        + (pltpu.HBM((CAP, width), bf16),) * flight,
        in_specs=[SMEM, SMEM, VMEM, VMEM, VMEM],
        out_specs=(VMEM,) * (2 + flight),
        compiler_params=params(),
        name="dispatch",
    )(capacity, hot_row, ids, probs, d_out)


def forward_kernel(flight, block, scale_ref, hidden_ref, quant_ref, tie_ref, weight_ref, *refs):
    out_refs, (quant, rows, sems) = refs[:flight], refs[flight:]
    hid, width = quant.shape
    me = lax.axis_index("expert")
    copies = [
        pltpu.make_async_copy(quant_ref.at[:, cols], quant.at[:, cols], sems.at[c])
        for c, cols in enumerate(chunks(width, block))
    ]
    for copy in copies:
        copy.start()
    for j in range(flight):
        rows[pl.ds(j * CAP, CAP), :] = hidden_ref[pl.ds(pl.multiple_of((me ^ j) * CAP, CAP), CAP), :]
    for c, cols in enumerate(chunks(width, block)):
        copies[c].wait()
        for i in range(hid // QB):
            for j in range(block // QB):
                at = (pl.ds(i * QB, QB), pl.ds(c * block + j * QB, QB))
                scale = scale_ref[i, 0, c * (block // QB) + j]
                weight_ref[at] = (quant[at].astype(f32) * scale).astype(bf16)
        out = jnp.dot(rows[...], weight_ref[:, cols], preferred_element_type=f32).astype(bf16)
        for j in range(flight):
            out_refs[j][:, cols] = out[j * CAP : (j + 1) * CAP, :]


def forward(scale, hidden, quant, tie, flight, block=512):
    hid, width = quant.shape
    return pl.pallas_call(
        functools.partial(forward_kernel, flight, block),
        out_shape=(jax.ShapeDtypeStruct((hid, width), bf16),)
        + (pltpu.HBM((CAP, width), bf16),) * flight,
        in_specs=[SMEM, VMEM, ANY, ANY],
        out_specs=(VMEM,) * (1 + flight),
        scratch_shapes=[
            pltpu.VMEM((hid, width), bf16),
            pltpu.VMEM((flight * CAP, hid), bf16),
            pltpu.SemaphoreType.DMA((width // block,)),
        ],
        compiler_params=params(),
        name="expert_forward",
    )(scale, hidden, quant, tie)


def backward_kernel(flight, block, gate_up_ref, weight_ref, *refs):
    in_refs, (out_ref, grads, acc) = refs[:flight], refs[flight:]
    hid, width = weight_ref.shape
    me = lax.axis_index("expert")
    for j in range(flight):
        grads[pl.ds(pl.multiple_of((me ^ j) * CAP, CAP), CAP), :] = in_refs[j][...]
    for c, cols in enumerate(chunks(width, block)):
        part = lax.dot_general(
            grads[:, cols], weight_ref[:, cols], (((1,), (1,)), ((), ())), preferred_element_type=f32
        )
        if c == 0:
            acc[...] = part
        else:
            acc[...] += part
    gate = gate_up_ref[:, :hid].astype(f32)
    up = gate_up_ref[:, hid:].astype(f32)
    sig = jax.nn.sigmoid(gate)
    d_hidden = acc[...]
    out_ref[:, :hid] = (d_hidden * up * sig * (1.0 + gate * (1.0 - sig))).astype(bf16)
    out_ref[:, hid:] = (d_hidden * (gate * sig)).astype(bf16)


def backward(gate_up, weight, arrived, block=1024):
    slots, double = gate_up.shape
    hid, width = weight.shape
    flight = len(arrived)
    return pl.pallas_call(
        functools.partial(backward_kernel, flight, block),
        out_shape=jax.ShapeDtypeStruct((slots, double), bf16),
        in_specs=[VMEM] * (2 + flight),
        out_specs=VMEM,
        scratch_shapes=[pltpu.VMEM((slots, width), bf16), pltpu.VMEM((slots, hid), f32)],
        compiler_params=params(),
        name="expert_backward",
    )(gate_up, weight, *arrived)


def combine_kernel(flight, block, ids_ref, own_ref, dout_ref, *refs):
    ret_refs, (out_ref, dprobs_ref, ret) = refs[:flight], refs[flight:]
    topk, tokens = ids_ref.shape
    width = dout_ref.shape[1]
    slots = flight * CAP
    me = lax.axis_index("expert")
    for j in range(flight):
        ret[pl.ds(j * CAP, CAP), :] = ret_refs[j][...]
    own = own_ref[...]
    turned = own.T
    high = turned.astype(bf16)
    low = (turned - high.astype(f32)).astype(bf16)
    total = jnp.zeros((slots, tokens), f32)
    for cols in chunks(width, block):
        here = ret[:, cols]
        out = jnp.dot(high, here, preferred_element_type=f32)
        out = out + jnp.dot(low, here, preferred_element_type=f32)
        out_ref[:, cols] = out.astype(bf16)
        total = total + lax.dot_general(
            here, dout_ref[:, cols], (((1,), (1,)), ((), ())), preferred_element_type=f32
        )
    inner = jnp.where(own > 0.0, total, 0.0)
    row_expert = (lax.broadcasted_iota(jnp.int32, (slots, 1), 0) // CAP) ^ me
    for k in range(topk):
        mine = jnp.where(ids_ref[k : k + 1, :] == row_expert, inner, 0.0)
        dprobs_ref[k : k + 1, :] = jnp.sum(mine, axis=0, keepdims=True)


def combine(ids, own, d_out, returned, block=1024):
    tokens, width = d_out.shape
    slots = own.shape[0]
    flight = len(returned)
    return pl.pallas_call(
        functools.partial(combine_kernel, flight, block),
        out_shape=(
            jax.ShapeDtypeStruct((tokens, width), bf16),
            jax.ShapeDtypeStruct(ids.shape, f32),
        ),
        in_specs=[VMEM] * (3 + flight),
        out_specs=(VMEM, VMEM),
        scratch_shapes=[pltpu.VMEM((slots, width), bf16)],
        compiler_params=params(),
        name="combine",
    )(ids, own, d_out, *returned)


def weight_grad_kernel(groups, block, grads_ref, *refs):
    hid_refs, (out_ref, hidden) = refs[:groups], refs[groups:]
    rows, share = grads_ref.shape
    slots = rows // groups
    me = lax.axis_index("dp")
    for j in range(groups):
        hidden[pl.ds(pl.multiple_of((me ^ j) * slots, slots), slots), :] = hid_refs[j][...]
    for cols in chunks(share, block):
        out_ref[cols, :] = lax.dot_general(
            grads_ref[:, cols], hidden[...], (((0,), (0,)), ((), ())), preferred_element_type=f32
        ).astype(bf16)


def weight_grad(grads, hiddens, block=256):
    rows, share = grads.shape
    hid = hiddens[0].shape[1]
    groups = len(hiddens)
    return pl.pallas_call(
        functools.partial(weight_grad_kernel, groups, block),
        out_shape=jax.ShapeDtypeStruct((share, hid), bf16),
        in_specs=[VMEM] * (1 + groups),
        out_specs=VMEM,
        scratch_shapes=[pltpu.VMEM((rows, hid), bf16)],
        compiler_params=params(),
        name="weight_grad",
    )(grads, *hiddens)


def swap(value, axis, j):
    size = lax.axis_size(axis)
    return lax.ppermute(value, axis, [(i, i ^ j) for i in range(size)])


def shards(route_ids, route_probs, capacity, hot_lists, gate_up, w_quant, w_scale, d_out):
    flight = lax.axis_size("expert")
    groups = lax.axis_size("dp")
    slots = flight * CAP
    width = d_out.shape[1]
    gate_up = gate_up[0, 0]
    ids, probs = route_ids.T, route_probs.T
    hidden = make_hidden(gate_up)
    hiddens = [hidden] + [swap(hidden, "dp", j) for j in range(1, groups)]
    own, parts, *full = dispatch(capacity, hot_lists, ids, probs, d_out, flight, groups)
    crossed = lax.all_to_all(
        parts.reshape(groups * flight, CAP, width // groups),
        ("dp", "expert"),
        split_axis=0,
        concat_axis=0,
        tiled=True,
    )
    arrived = [full[0]] + [swap(full[j], "expert", j) for j in range(1, flight)]
    weight, *expert_out = forward(
        w_scale.transpose(1, 0, 2), hidden, w_quant[0], own, flight
    )
    returned = [expert_out[0]] + [swap(expert_out[j], "expert", j) for j in range(1, flight)]
    d_gate_up = backward(gate_up, weight, arrived)
    combined, d_probs = combine(ids, own, d_out, returned)
    d_weight = weight_grad(crossed.reshape(groups * slots, width // groups), hiddens)
    return (combined, d_probs.T, d_gate_up[None, None], d_weight[None])


def solution(mesh):
    placed = (
        P(("dp", "expert"), None),
        P(("dp", "expert"), None),
        P(),
        P("dp", None),
        P("dp", "expert", None, None),
        P("expert", None, None),
        P("expert", None, None),
        P(("dp", "expert"), None),
    )
    return jax.shard_map(
        shards,
        mesh=mesh,
        in_specs=placed,
        out_specs=(
            P(("dp", "expert"), None),
            P(("dp", "expert"), None),
            P("dp", "expert", None, None),
            P("expert", "dp", None),
        ),
        check_vma=False,
    )
```

```python
import functools

import jax
import jax.numpy as jnp
from jax import lax
from jax.experimental import pallas as pl
from jax.experimental.pallas import tpu as pltpu
from jax.sharding import PartitionSpec as P

QB = 128
CAP = 16
VMEM_LIMIT = 40 * 1024 * 1024

bf16 = jnp.bfloat16
f32 = jnp.float32

VMEM = pl.BlockSpec(memory_space=pltpu.VMEM)
ANY = pl.BlockSpec(memory_space=pl.ANY)
HBM = pl.BlockSpec(memory_space=pltpu.HBM)


def params():
    return pltpu.CompilerParams(vmem_limit_bytes=VMEM_LIMIT)


def hbm(value):
    return pltpu.with_memory_space_constraint(value, pltpu.HBM)


def chunks(total, size):
    return [pl.ds(start, size) for start in range(0, total, size)]


def hidden_kernel(gate_up_ref, tie_ref, out_ref, gate_up, sem):
    copy = pltpu.make_async_copy(gate_up_ref, gate_up, sem)
    copy.start()
    copy.wait()
    hid = out_ref.shape[1]
    gate = gate_up[:, :hid].astype(f32)
    up = gate_up[:, hid:].astype(f32)
    out_ref[...] = (gate * jax.nn.sigmoid(gate) * up).astype(bf16)


def make_hidden(gate_up, tie):
    slots, double = gate_up.shape
    return pl.pallas_call(
        hidden_kernel,
        out_shape=pltpu.HBM((slots, double // 2), bf16),
        in_specs=[HBM, ANY],
        out_specs=VMEM,
        scratch_shapes=[pltpu.VMEM((slots, double), bf16), pltpu.SemaphoreType.DMA],
        compiler_params=params(),
        name="hidden",
    )(hbm(gate_up), tie)


def dispatch_kernel(
    flight, groups, cap_hbm, hot_hbm, ids_hbm, probs_hbm, dout_hbm, own_ref, rows_hbm,
    cap_ref, hot_ref, ids_ref, probs_ref, dout, rows, small_sems, in_sems, out_sems
):
    topk, tokens = ids_ref.shape
    slots = flight * CAP
    group = lax.axis_index("dp")
    share = dout_hbm.shape[1] // groups
    small = [
        pltpu.make_async_copy(src, dst, small_sems.at[i])
        for i, (src, dst) in enumerate(
            [(ids_hbm, ids_ref), (probs_hbm, probs_ref), (cap_hbm, cap_ref), (hot_hbm, hot_ref)]
        )
    ]
    loads = [
        pltpu.make_async_copy(
            dout_hbm.at[:, pl.ds(pl.multiple_of((group ^ j) * share, share), share)],
            dout.at[j],
            in_sems.at[j],
        )
        for j in range(groups)
    ]
    for copy in small + loads:
        copy.start()
    for copy in small:
        copy.wait()
    row = lax.broadcasted_iota(jnp.int32, (slots, 1), 0)
    row_expert = row // CAP
    row_rank = (row % CAP).astype(f32)
    limit = jnp.zeros((slots, 1), jnp.int32)
    for e in range(flight):
        hot = hot_ref[0, 0] == e
        for h in range(1, hot_ref.shape[1]):
            hot = jnp.logical_or(hot, hot_ref[0, h] == e)
        limit = jnp.where(row_expert == e, jnp.where(hot, CAP, cap_ref[e]), limit)
    limit = limit.astype(f32)
    named = jnp.zeros((slots, tokens), f32)
    weight = jnp.zeros((slots, tokens), f32)
    for k in range(topk):
        hit = ids_ref[k : k + 1, :] == row_expert
        named = jnp.where(hit, 1.0, named)
        weight = jnp.where(hit, probs_ref[k : k + 1, :], weight)
    first = lax.broadcasted_iota(jnp.int32, (tokens, tokens), 0)
    second = lax.broadcasted_iota(jnp.int32, (tokens, tokens), 1)
    before = (first < second).astype(f32).astype(bf16)
    rank = jnp.dot(named.astype(bf16), before, preferred_element_type=f32)
    owns = (named > 0.0) & (rank == row_rank) & (rank < limit)
    own_weight = jnp.where(owns, weight, 0.0)
    own_ref[...] = own_weight
    owner = jnp.where(owns, 1.0, 0.0).astype(bf16)
    slot_weight = jnp.sum(own_weight, axis=1, keepdims=True)
    stores = []
    for j in range(groups):
        loads[j].wait()
        part = jnp.dot(owner, dout[j], preferred_element_type=f32)
        rows[j] = (part * slot_weight).astype(bf16).reshape(flight, CAP, share)
        stores.append(pltpu.make_async_copy(rows.at[j], rows_hbm.at[:, j], out_sems.at[j]))
        stores[j].start()
    for copy in stores:
        copy.wait()


def dispatch(capacity, hot_row, ids, probs, d_out, flight, groups):
    tokens, width = d_out.shape
    slots = flight * CAP
    share = width // groups
    return pl.pallas_call(
        functools.partial(dispatch_kernel, flight, groups),
        out_shape=(
            jax.ShapeDtypeStruct((slots, tokens), f32),
            pltpu.HBM((flight, groups, CAP, share), bf16),
        ),
        in_specs=[HBM] * 5,
        out_specs=(VMEM, HBM),
        scratch_shapes=[
            pltpu.SMEM(capacity.shape, jnp.int32),
            pltpu.SMEM(hot_row.shape, jnp.int32),
            pltpu.VMEM(ids.shape, jnp.int32),
            pltpu.VMEM(probs.shape, f32),
            pltpu.VMEM((groups, tokens, share), bf16),
            pltpu.VMEM((groups, flight, CAP, share), bf16),
            pltpu.SemaphoreType.DMA((4,)),
            pltpu.SemaphoreType.DMA((groups,)),
            pltpu.SemaphoreType.DMA((groups,)),
        ],
        compiler_params=params(),
        name="dispatch",
    )(hbm(capacity), hbm(hot_row), hbm(ids), hbm(probs), hbm(d_out))


def forward_kernel(
    flight, block, scale_hbm, hidden_hbm, quant_hbm, weight_ref, out_hbm,
    scale_ref, hidden, quant, out, small_sems, in_sems, out_sems
):
    hid, width = quant.shape
    steps = chunks(width, block)
    small = [
        pltpu.make_async_copy(scale_hbm, scale_ref, small_sems.at[0]),
        pltpu.make_async_copy(hidden_hbm, hidden, small_sems.at[1]),
    ]
    loads = [
        pltpu.make_async_copy(quant_hbm.at[:, cols], quant.at[:, cols], in_sems.at[c])
        for c, cols in enumerate(steps)
    ]
    for copy in small + loads:
        copy.start()
    for copy in small:
        copy.wait()
    stores = []
    for c, cols in enumerate(steps):
        loads[c].wait()
        for i in range(hid // QB):
            for j in range(block // QB):
                at = (pl.ds(i * QB, QB), pl.ds(c * block + j * QB, QB))
                scale = scale_ref[i, 0, c * (block // QB) + j]
                weight_ref[at] = (quant[at].astype(f32) * scale).astype(bf16)
        part = jnp.dot(hidden[...], weight_ref[:, cols], preferred_element_type=f32)
        out[:, :, cols] = part.astype(bf16).reshape(flight, CAP, block)
        stores.append(
            pltpu.make_async_copy(out.at[:, :, cols], out_hbm.at[:, :, cols], out_sems.at[c])
        )
        stores[c].start()
    for copy in stores:
        copy.wait()


def forward(scale, hidden, quant, flight, block=512):
    hid, width = quant.shape
    return pl.pallas_call(
        functools.partial(forward_kernel, flight, block),
        out_shape=(
            jax.ShapeDtypeStruct((hid, width), bf16),
            pltpu.HBM((flight, CAP, width), bf16),
        ),
        in_specs=[HBM, HBM, HBM],
        out_specs=(VMEM, HBM),
        scratch_shapes=[
            pltpu.SMEM(scale.shape, f32),
            pltpu.VMEM(hidden.shape, bf16),
            pltpu.VMEM((hid, width), bf16),
            pltpu.VMEM((flight, CAP, width), bf16),
            pltpu.SemaphoreType.DMA((2,)),
            pltpu.SemaphoreType.DMA((width // block,)),
            pltpu.SemaphoreType.DMA((width // block,)),
        ],
        compiler_params=params(),
        name="expert_forward",
    )(hbm(scale), hbm(hidden), hbm(quant))


def split_kernel(groups, rows_ref, tie_ref, *refs):
    outs, sems = refs[:-1], refs[-1]
    copies = [
        pltpu.make_async_copy(rows_ref.at[:, j], outs[j - 1], sems.at[j - 1])
        for j in range(1, groups)
    ]
    for copy in copies:
        copy.start()
    for copy in copies:
        copy.wait()


def split(rows, tie):
    flight, groups, cap, share = rows.shape
    return pl.pallas_call(
        functools.partial(split_kernel, groups),
        out_shape=(pltpu.HBM((flight, cap, share), bf16),) * (groups - 1),
        in_specs=[ANY, ANY],
        out_specs=(HBM,) * (groups - 1),
        scratch_shapes=[pltpu.SemaphoreType.DMA((groups - 1,))],
        compiler_params=params(),
        name="split",
    )(rows, hbm(tie))


def backward_kernel(gate_up_hbm, weight_ref, rows_ref, tie_ref, out_ref, gate_up, acc, sem):
    copy = pltpu.make_async_copy(gate_up_hbm, gate_up, sem)
    copy.start()
    hid = weight_ref.shape[0]
    flight, groups, cap, share = rows_ref.shape
    group = lax.axis_index("dp")
    for j in range(groups):
        cols = pl.ds(pl.multiple_of((group ^ j) * share, share), share)
        part = lax.dot_general(
            rows_ref[:, j].reshape(flight * cap, share),
            weight_ref[:, cols],
            (((1,), (1,)), ((), ())),
            preferred_element_type=f32,
        )
        if j == 0:
            acc[...] = part
        else:
            acc[...] += part
    copy.wait()
    gate = gate_up[:, :hid].astype(f32)
    up = gate_up[:, hid:].astype(f32)
    sig = jax.nn.sigmoid(gate)
    d_hidden = acc[...]
    out_ref[:, :hid] = (d_hidden * up * sig * (1.0 + gate * (1.0 - sig))).astype(bf16)
    out_ref[:, hid:] = (d_hidden * (gate * sig)).astype(bf16)


def backward(gate_up, weight, rows, tie):
    slots, double = gate_up.shape
    hid = weight.shape[0]
    return pl.pallas_call(
        backward_kernel,
        out_shape=jax.ShapeDtypeStruct((slots, double), bf16),
        in_specs=[HBM, VMEM, VMEM, ANY],
        out_specs=VMEM,
        scratch_shapes=[
            pltpu.VMEM((slots, double), bf16),
            pltpu.VMEM((slots, hid), f32),
            pltpu.SemaphoreType.DMA,
        ],
        compiler_params=params(),
        name="expert_backward",
    )(hbm(gate_up), weight, rows, hbm(tie))


def combine_kernel(
    block, ids_hbm, own_ref, dout_hbm, ret_ref, out_ref, dprobs_ref, ids_ref, dout, sems
):
    copies = [
        pltpu.make_async_copy(ids_hbm, ids_ref, sems.at[0]),
        pltpu.make_async_copy(dout_hbm, dout, sems.at[1]),
    ]
    for copy in copies:
        copy.start()
    topk, tokens = ids_ref.shape
    slots = own_ref.shape[0]
    width = dout.shape[1]
    own = own_ref[...]
    turned = own.T
    high = turned.astype(bf16)
    low = (turned - high.astype(f32)).astype(bf16)
    total = jnp.zeros((slots, tokens), f32)
    for copy in copies:
        copy.wait()
    for cols in chunks(width, block):
        here = ret_ref[:, :, cols].reshape(slots, block)
        out = jnp.dot(high, here, preferred_element_type=f32)
        out = out + jnp.dot(low, here, preferred_element_type=f32)
        out_ref[:, cols] = out.astype(bf16)
        total = total + lax.dot_general(
            here, dout[:, cols], (((1,), (1,)), ((), ())), preferred_element_type=f32
        )
    inner = jnp.where(own > 0.0, total, 0.0)
    row_expert = lax.broadcasted_iota(jnp.int32, (slots, 1), 0) // CAP
    for k in range(topk):
        mine = jnp.where(ids_ref[k : k + 1, :] == row_expert, inner, 0.0)
        dprobs_ref[k : k + 1, :] = jnp.sum(mine, axis=0, keepdims=True)


def combine(ids, own, d_out, returned, block=1024):
    tokens, width = d_out.shape
    return pl.pallas_call(
        functools.partial(combine_kernel, block),
        out_shape=(
            jax.ShapeDtypeStruct((tokens, width), bf16),
            jax.ShapeDtypeStruct(ids.shape, f32),
        ),
        in_specs=[HBM, VMEM, HBM, VMEM],
        out_specs=(VMEM, VMEM),
        scratch_shapes=[
            pltpu.VMEM(ids.shape, jnp.int32),
            pltpu.VMEM((tokens, width), bf16),
            pltpu.SemaphoreType.DMA((2,)),
        ],
        compiler_params=params(),
        name="combine",
    )(hbm(ids), own, hbm(d_out), returned)


def weight_grad_kernel(groups, block, rows_ref, *refs):
    part_refs, hid_refs = refs[: groups - 1], refs[groups - 1 : 2 * groups - 1]
    out_hbm, grads, hidden, out, sems, out_sems = refs[2 * groups - 1 :]
    flight, cap, share = part_refs[0].shape
    slots = flight * cap
    copies = []
    for j in range(groups):
        src = rows_ref.at[:, 0] if j == 0 else part_refs[j - 1]
        copies.append(
            pltpu.make_async_copy(src, grads.at[pl.ds(j * flight, flight)], sems.at[2 * j])
        )
        copies.append(
            pltpu.make_async_copy(
                hid_refs[j], hidden.at[pl.ds(j * slots, slots)], sems.at[2 * j + 1]
            )
        )
    for copy in copies:
        copy.start()
    for copy in copies:
        copy.wait()
    stores = []
    for c, cols in enumerate(chunks(share, block)):
        out[cols, :] = lax.dot_general(
            grads[:, :, cols].reshape(groups * slots, block),
            hidden[...],
            (((0,), (0,)), ((), ())),
            preferred_element_type=f32,
        ).astype(bf16)
        stores.append(pltpu.make_async_copy(out.at[cols], out_hbm.at[cols], out_sems.at[c]))
        stores[c].start()
    for copy in stores:
        copy.wait()


def weight_grad(rows, parts, hiddens, block=256):
    flight, groups, cap, share = rows.shape
    slots, hid = hiddens[0].shape
    return pl.pallas_call(
        functools.partial(weight_grad_kernel, groups, block),
        out_shape=pltpu.HBM((share, hid), bf16),
        in_specs=[ANY] * (2 * groups),
        out_specs=HBM,
        scratch_shapes=[
            pltpu.VMEM((groups * flight, cap, share), bf16),
            pltpu.VMEM((groups * slots, hid), bf16),
            pltpu.VMEM((share, hid), bf16),
            pltpu.SemaphoreType.DMA((2 * groups,)),
            pltpu.SemaphoreType.DMA((share // block,)),
        ],
        compiler_params=params(),
        name="weight_grad",
    )(rows, *parts, hbm(hiddens[0]), *hiddens[1:])


def swap(value, axis, j):
    size = lax.axis_size(axis)
    return lax.ppermute(value, axis, [(i, i ^ j) for i in range(size)])


def exchange(value):
    return lax.all_to_all(value, "expert", split_axis=0, concat_axis=0, tiled=True)


def shards(route_ids, route_probs, capacity, hot_lists, gate_up, w_quant, w_scale, d_out):
    flight = lax.axis_size("expert")
    groups = lax.axis_size("dp")
    gate_up = gate_up[0, 0]
    ids, probs = route_ids.T, route_probs.T
    own, rows = dispatch(capacity, hot_lists, ids, probs, d_out, flight, groups)
    arrived = exchange(rows)
    hidden = make_hidden(gate_up, own)
    hiddens = [hidden] + [swap(hidden, "dp", j) for j in range(1, groups)]
    weight, expert_out = forward(w_scale.transpose(1, 0, 2), hidden, w_quant[0], flight)
    returned = exchange(expert_out)
    pieces = split(arrived, expert_out)
    parts = [swap(pieces[j - 1], "dp", j) for j in range(1, groups)]
    d_gate_up = backward(gate_up, weight, arrived, pieces[0])
    combined, d_probs = combine(ids, own, d_out, returned)
    d_weight = weight_grad(arrived, parts, hiddens)
    return (combined, d_probs.T, d_gate_up[None, None], d_weight[None])


def solution(mesh):
    placed = (
        P(("dp", "expert"), None),
        P(("dp", "expert"), None),
        P(),
        P("dp", None),
        P("dp", "expert", None, None),
        P("expert", None, None),
        P("expert", None, None),
        P(("dp", "expert"), None),
    )
    return jax.shard_map(
        shards,
        mesh=mesh,
        in_specs=placed,
        out_specs=(
            P(("dp", "expert"), None),
            P(("dp", "expert"), None),
            P("dp", "expert", None, None),
            P("expert", "dp", None),
        ),
        check_vma=False,
    )
```

```python
import functools

import jax
import jax.numpy as jnp
from jax import lax
from jax.experimental import pallas as pl
from jax.experimental.pallas import tpu as pltpu
from jax.sharding import PartitionSpec as P

QB = 128
CAP = 16
VMEM_LIMIT = 24 * 1024 * 1024

bf16 = jnp.bfloat16
f32 = jnp.float32

SMALL = pl.CostEstimate(flops=1024, bytes_accessed=1024, transcendentals=0)

VMEM = pl.BlockSpec(memory_space=pltpu.VMEM)
ANY = pl.BlockSpec(memory_space=pl.ANY)
HBM = pl.BlockSpec(memory_space=pltpu.HBM)


def params():
    return pltpu.CompilerParams(vmem_limit_bytes=VMEM_LIMIT)


def hbm(value):
    return pltpu.with_memory_space_constraint(value, pltpu.HBM)


def chunks(total, size):
    return [pl.ds(start, size) for start in range(0, total, size)]


def dispatch_kernel(
    flight, groups, gate_up_hbm, cap_hbm, hot_hbm, ids_hbm, probs_hbm, dout_hbm,
    hidden_hbm, own_ref, rows_hbm,
    gate_up, cap_ref, hot_ref, ids_ref, probs_ref, dout, hidden, rows,
    gate_sem, hidden_sem, small_sems, in_sems, out_sems
):
    topk, tokens = ids_ref.shape
    slots = flight * CAP
    group = lax.axis_index("dp")
    share = dout_hbm.shape[1] // groups
    small = [
        pltpu.make_async_copy(src, dst, small_sems.at[i])
        for i, (src, dst) in enumerate(
            [(ids_hbm, ids_ref), (probs_hbm, probs_ref), (cap_hbm, cap_ref), (hot_hbm, hot_ref)]
        )
    ]
    loads = [
        pltpu.make_async_copy(
            dout_hbm.at[:, pl.ds(pl.multiple_of((group ^ j) * share, share), share)],
            dout.at[j],
            in_sems.at[j],
        )
        for j in range(groups)
    ]
    gate_copy = pltpu.make_async_copy(gate_up_hbm, gate_up, gate_sem)
    for copy in [gate_copy] + small + loads:
        copy.start()
    gate_copy.wait()
    hid = hidden.shape[1]
    gate = gate_up[:, :hid].astype(f32)
    up = gate_up[:, hid:].astype(f32)
    hidden[...] = (gate * jax.nn.sigmoid(gate) * up).astype(bf16)
    hidden_copy = pltpu.make_async_copy(hidden, hidden_hbm, hidden_sem)
    hidden_copy.start()
    for copy in small:
        copy.wait()
    row = lax.broadcasted_iota(jnp.int32, (slots, 1), 0)
    row_expert = row // CAP
    row_rank = (row % CAP).astype(f32)
    limit = jnp.zeros((slots, 1), jnp.int32)
    for e in range(flight):
        hot = hot_ref[0, 0] == e
        for h in range(1, hot_ref.shape[1]):
            hot = jnp.logical_or(hot, hot_ref[0, h] == e)
        limit = jnp.where(row_expert == e, jnp.where(hot, CAP, cap_ref[e]), limit)
    limit = limit.astype(f32)
    named = jnp.zeros((slots, tokens), f32)
    weight = jnp.zeros((slots, tokens), f32)
    for k in range(topk):
        hit = ids_ref[k : k + 1, :] == row_expert
        named = jnp.where(hit, 1.0, named)
        weight = jnp.where(hit, probs_ref[k : k + 1, :], weight)
    first = lax.broadcasted_iota(jnp.int32, (tokens, tokens), 0)
    second = lax.broadcasted_iota(jnp.int32, (tokens, tokens), 1)
    before = (first < second).astype(f32).astype(bf16)
    rank = jnp.dot(named.astype(bf16), before, preferred_element_type=f32)
    owns = (named > 0.0) & (rank == row_rank) & (rank < limit)
    own_weight = jnp.where(owns, weight, 0.0)
    own_ref[...] = own_weight
    owner = jnp.where(owns, 1.0, 0.0).astype(bf16)
    slot_weight = jnp.sum(own_weight, axis=1, keepdims=True)
    stores = []
    for j in range(groups):
        loads[j].wait()
        part = jnp.dot(owner, dout[j], preferred_element_type=f32)
        rows[j] = (part * slot_weight).astype(bf16).reshape(flight, CAP, share)
        stores.append(pltpu.make_async_copy(rows.at[j], rows_hbm.at[:, j], out_sems.at[j]))
        stores[j].start()
    for copy in stores:
        copy.wait()
    hidden_copy.wait()


def dispatch(gate_up, capacity, hot_row, ids, probs, d_out, flight, groups):
    tokens, width = d_out.shape
    rows, double = gate_up.shape
    slots = flight * CAP
    share = width // groups
    return pl.pallas_call(
        functools.partial(dispatch_kernel, flight, groups),
        out_shape=(
            pltpu.HBM((rows, double // 2), bf16),
            jax.ShapeDtypeStruct((slots, tokens), f32),
            pltpu.HBM((flight, groups, CAP, share), bf16),
        ),
        in_specs=[HBM] * 6,
        out_specs=(HBM, VMEM, HBM),
        scratch_shapes=[
            pltpu.VMEM((rows, double), bf16),
            pltpu.SMEM(capacity.shape, jnp.int32),
            pltpu.SMEM(hot_row.shape, jnp.int32),
            pltpu.VMEM(ids.shape, jnp.int32),
            pltpu.VMEM(probs.shape, f32),
            pltpu.VMEM((groups, tokens, share), bf16),
            pltpu.VMEM((rows, double // 2), bf16),
            pltpu.VMEM((groups, flight, CAP, share), bf16),
            pltpu.SemaphoreType.DMA,
            pltpu.SemaphoreType.DMA,
            pltpu.SemaphoreType.DMA((4,)),
            pltpu.SemaphoreType.DMA((groups,)),
            pltpu.SemaphoreType.DMA((groups,)),
        ],
        compiler_params=params(),
        cost_estimate=SMALL,
        name="dispatch",
    )(hbm(gate_up), hbm(capacity), hbm(hot_row), hbm(ids), hbm(probs), hbm(d_out))


def forward_kernel(
    flight, block, scale_hbm, hidden_hbm, quant_hbm, weight_ref, out_hbm,
    scale_ref, hidden, quant, out, small_sems, in_sems, out_sems
):
    hid, width = quant.shape
    steps = chunks(width, block)
    small = [
        pltpu.make_async_copy(scale_hbm, scale_ref, small_sems.at[0]),
        pltpu.make_async_copy(hidden_hbm, hidden, small_sems.at[1]),
    ]
    loads = [
        pltpu.make_async_copy(quant_hbm.at[:, cols], quant.at[:, cols], in_sems.at[c])
        for c, cols in enumerate(steps)
    ]
    for copy in small + loads:
        copy.start()
    for copy in small:
        copy.wait()
    stores = []
    for c, cols in enumerate(steps):
        loads[c].wait()
        for i in range(hid // QB):
            for j in range(block // QB):
                at = (pl.ds(i * QB, QB), pl.ds(c * block + j * QB, QB))
                scale = scale_ref[i, 0, c * (block // QB) + j]
                weight_ref[at] = (quant[at].astype(f32) * scale).astype(bf16)
        part = jnp.dot(hidden[...], weight_ref[:, cols], preferred_element_type=f32)
        out[:, :, cols] = part.astype(bf16).reshape(flight, CAP, block)
        stores.append(
            pltpu.make_async_copy(out.at[:, :, cols], out_hbm.at[:, :, cols], out_sems.at[c])
        )
        stores[c].start()
    for copy in stores:
        copy.wait()


def forward(scale, hidden, quant, flight, block=512):
    hid, width = quant.shape
    return pl.pallas_call(
        functools.partial(forward_kernel, flight, block),
        out_shape=(
            jax.ShapeDtypeStruct((hid, width), bf16),
            pltpu.HBM((flight, CAP, width), bf16),
        ),
        in_specs=[HBM, HBM, HBM],
        out_specs=(VMEM, HBM),
        scratch_shapes=[
            pltpu.SMEM(scale.shape, f32),
            pltpu.VMEM(hidden.shape, bf16),
            pltpu.VMEM((hid, width), bf16),
            pltpu.VMEM((flight, CAP, width), bf16),
            pltpu.SemaphoreType.DMA((2,)),
            pltpu.SemaphoreType.DMA((width // block,)),
            pltpu.SemaphoreType.DMA((width // block,)),
        ],
        compiler_params=params(),
        cost_estimate=SMALL,
        name="expert_forward",
    )(hbm(scale), hbm(hidden), hbm(quant))


def split_kernel(groups, rows_ref, *refs):
    outs, sems = refs[groups:-1], refs[-1]
    copies = [
        pltpu.make_async_copy(rows_ref.at[:, j], outs[j - 1], sems.at[j - 1])
        for j in range(1, groups)
    ]
    for copy in copies:
        copy.start()
    for copy in copies:
        copy.wait()


def split(rows, ties):
    flight, groups, cap, share = rows.shape
    return pl.pallas_call(
        functools.partial(split_kernel, groups),
        out_shape=(pltpu.HBM((flight, cap, share), bf16),) * (groups - 1),
        in_specs=[ANY] * (1 + groups),
        out_specs=(HBM,) * (groups - 1),
        scratch_shapes=[pltpu.SemaphoreType.DMA((groups - 1,))],
        compiler_params=params(),
        cost_estimate=SMALL,
        name="split",
    )(rows, *ties)


def backward_kernel(gate_up_hbm, weight_ref, rows_ref, tie_ref, out_ref, gate_up, acc, sem):
    copy = pltpu.make_async_copy(gate_up_hbm, gate_up, sem)
    copy.start()
    hid = weight_ref.shape[0]
    flight, groups, cap, share = rows_ref.shape
    group = lax.axis_index("dp")
    for j in range(groups):
        cols = pl.ds(pl.multiple_of((group ^ j) * share, share), share)
        part = lax.dot_general(
            rows_ref[:, j].reshape(flight * cap, share),
            weight_ref[:, cols],
            (((1,), (1,)), ((), ())),
            preferred_element_type=f32,
        )
        if j == 0:
            acc[...] = part
        else:
            acc[...] += part
    copy.wait()
    gate = gate_up[:, :hid].astype(f32)
    up = gate_up[:, hid:].astype(f32)
    sig = jax.nn.sigmoid(gate)
    d_hidden = acc[...]
    out_ref[:, :hid] = (d_hidden * up * sig * (1.0 + gate * (1.0 - sig))).astype(bf16)
    out_ref[:, hid:] = (d_hidden * (gate * sig)).astype(bf16)


def backward(gate_up, weight, rows, tie):
    slots, double = gate_up.shape
    hid = weight.shape[0]
    return pl.pallas_call(
        backward_kernel,
        out_shape=jax.ShapeDtypeStruct((slots, double), bf16),
        in_specs=[HBM, VMEM, VMEM, ANY],
        out_specs=VMEM,
        scratch_shapes=[
            pltpu.VMEM((slots, double), bf16),
            pltpu.VMEM((slots, hid), f32),
            pltpu.SemaphoreType.DMA,
        ],
        compiler_params=params(),
        cost_estimate=SMALL,
        name="expert_backward",
    )(hbm(gate_up), weight, rows, hbm(tie))


def combine_kernel(
    block, ids_hbm, own_ref, dout_hbm, ret_ref, out_ref, dprobs_ref, ids_ref, dout, sems
):
    copies = [
        pltpu.make_async_copy(ids_hbm, ids_ref, sems.at[0]),
        pltpu.make_async_copy(dout_hbm, dout, sems.at[1]),
    ]
    for copy in copies:
        copy.start()
    topk, tokens = ids_ref.shape
    slots = own_ref.shape[0]
    width = dout.shape[1]
    own = own_ref[...]
    turned = own.T
    high = turned.astype(bf16)
    low = (turned - high.astype(f32)).astype(bf16)
    total = jnp.zeros((slots, tokens), f32)
    for copy in copies:
        copy.wait()
    for cols in chunks(width, block):
        here = ret_ref[:, :, cols].reshape(slots, block)
        out = jnp.dot(high, here, preferred_element_type=f32)
        out = out + jnp.dot(low, here, preferred_element_type=f32)
        out_ref[:, cols] = out.astype(bf16)
        total = total + lax.dot_general(
            here, dout[:, cols], (((1,), (1,)), ((), ())), preferred_element_type=f32
        )
    inner = jnp.where(own > 0.0, total, 0.0)
    row_expert = lax.broadcasted_iota(jnp.int32, (slots, 1), 0) // CAP
    for k in range(topk):
        mine = jnp.where(ids_ref[k : k + 1, :] == row_expert, inner, 0.0)
        dprobs_ref[k : k + 1, :] = jnp.sum(mine, axis=0, keepdims=True)


def combine(ids, own, d_out, returned, block=1024):
    tokens, width = d_out.shape
    return pl.pallas_call(
        functools.partial(combine_kernel, block),
        out_shape=(
            jax.ShapeDtypeStruct((tokens, width), bf16),
            jax.ShapeDtypeStruct(ids.shape, f32),
        ),
        in_specs=[HBM, VMEM, HBM, VMEM],
        out_specs=(VMEM, VMEM),
        scratch_shapes=[
            pltpu.VMEM(ids.shape, jnp.int32),
            pltpu.VMEM((tokens, width), bf16),
            pltpu.SemaphoreType.DMA((2,)),
        ],
        compiler_params=params(),
        cost_estimate=SMALL,
        name="combine",
    )(hbm(ids), own, hbm(d_out), returned)


def weight_grad_kernel(groups, block, rows_ref, *refs):
    part_refs, hid_refs = refs[: groups - 1], refs[groups - 1 : 2 * groups - 1]
    out_hbm, grads, hidden, out, sems, out_sems = refs[2 * groups - 1 :]
    flight, cap, share = part_refs[0].shape
    slots = flight * cap
    copies = []
    for j in range(groups):
        src = rows_ref.at[:, 0] if j == 0 else part_refs[j - 1]
        copies.append(
            pltpu.make_async_copy(src, grads.at[pl.ds(j * flight, flight)], sems.at[2 * j])
        )
        copies.append(
            pltpu.make_async_copy(
                hid_refs[j], hidden.at[pl.ds(j * slots, slots)], sems.at[2 * j + 1]
            )
        )
    for copy in copies:
        copy.start()
    for copy in copies:
        copy.wait()
    stores = []
    for c, cols in enumerate(chunks(share, block)):
        out[cols, :] = lax.dot_general(
            grads[:, :, cols].reshape(groups * slots, block),
            hidden[...],
            (((0,), (0,)), ((), ())),
            preferred_element_type=f32,
        ).astype(bf16)
        stores.append(pltpu.make_async_copy(out.at[cols], out_hbm.at[cols], out_sems.at[c]))
        stores[c].start()
    for copy in stores:
        copy.wait()


def weight_grad(rows, parts, hiddens, block=256):
    flight, groups, cap, share = rows.shape
    slots, hid = hiddens[0].shape
    return pl.pallas_call(
        functools.partial(weight_grad_kernel, groups, block),
        out_shape=pltpu.HBM((share, hid), bf16),
        in_specs=[ANY] * (2 * groups),
        out_specs=HBM,
        scratch_shapes=[
            pltpu.VMEM((groups * flight, cap, share), bf16),
            pltpu.VMEM((groups * slots, hid), bf16),
            pltpu.VMEM((share, hid), bf16),
            pltpu.SemaphoreType.DMA((2 * groups,)),
            pltpu.SemaphoreType.DMA((share // block,)),
        ],
        compiler_params=params(),
        cost_estimate=SMALL,
        name="weight_grad",
    )(rows, *parts, hbm(hiddens[0]), *hiddens[1:])


def swap(value, axis, j):
    size = lax.axis_size(axis)
    return lax.ppermute(value, axis, [(i, i ^ j) for i in range(size)])


def exchange(value):
    return lax.all_to_all(value, "expert", split_axis=0, concat_axis=0, tiled=True)


def shards(route_ids, route_probs, capacity, hot_lists, gate_up, w_quant, w_scale, d_out):
    flight = lax.axis_size("expert")
    groups = lax.axis_size("dp")
    gate_up = gate_up[0, 0]
    ids, probs = route_ids.T, route_probs.T
    hidden, own, rows = dispatch(gate_up, capacity, hot_lists, ids, probs, d_out, flight, groups)
    arrived = exchange(rows)
    hiddens = [hidden] + [swap(hidden, "dp", j) for j in range(1, groups)]
    weight, expert_out = forward(w_scale.transpose(1, 0, 2), hidden, w_quant[0], flight)
    returned = exchange(expert_out)
    pieces = split(arrived, [hbm(expert_out)] + hiddens[1:])
    parts = [swap(pieces[j - 1], "dp", j) for j in range(1, groups)]
    d_gate_up = backward(gate_up, weight, arrived, pieces[0])
    combined, d_probs = combine(ids, own, d_out, returned)
    d_weight = weight_grad(arrived, parts, hiddens)
    return (combined, d_probs.T, d_gate_up[None, None], d_weight[None])


def solution(mesh):
    placed = (
        P(("dp", "expert"), None),
        P(("dp", "expert"), None),
        P(),
        P("dp", None),
        P("dp", "expert", None, None),
        P("expert", None, None),
        P("expert", None, None),
        P(("dp", "expert"), None),
    )
    return jax.shard_map(
        shards,
        mesh=mesh,
        in_specs=placed,
        out_specs=(
            P(("dp", "expert"), None),
            P(("dp", "expert"), None),
            P("dp", "expert", None, None),
            P("expert", "dp", None),
        ),
        check_vma=False,
    )
```

```python
import functools

import jax
import jax.numpy as jnp
from jax import lax
from jax.experimental import pallas as pl
from jax.experimental.pallas import tpu as pltpu
from jax.sharding import PartitionSpec as P

QB = 128
CAP = 16
VMEM_LIMIT = 24 * 1024 * 1024

bf16 = jnp.bfloat16
f32 = jnp.float32

SMALL = pl.CostEstimate(flops=1024, bytes_accessed=1024, transcendentals=0)

VMEM = pl.BlockSpec(memory_space=pltpu.VMEM)
ANY = pl.BlockSpec(memory_space=pl.ANY)
HBM = pl.BlockSpec(memory_space=pltpu.HBM)


def params():
    return pltpu.CompilerParams(vmem_limit_bytes=VMEM_LIMIT)


def hbm(value):
    return pltpu.with_memory_space_constraint(value, pltpu.HBM)


def chunks(total, size):
    return [pl.ds(start, size) for start in range(0, total, size)]


def dispatch_kernel(
    flight, groups, gate_up_hbm, cap_hbm, hot_hbm, ids_hbm, probs_hbm, dout_hbm,
    hidden_hbm, own_ref, rows_hbm,
    gate_up, cap_ref, hot_ref, ids_ref, probs_ref, dout, hidden, rows,
    gate_sem, hidden_sem, small_sems, in_sems, out_sems
):
    topk, tokens = ids_ref.shape
    slots = flight * CAP
    group = lax.axis_index("dp")
    share = dout_hbm.shape[1] // groups
    small = [
        pltpu.make_async_copy(src, dst, small_sems.at[i])
        for i, (src, dst) in enumerate(
            [(ids_hbm, ids_ref), (probs_hbm, probs_ref), (cap_hbm, cap_ref), (hot_hbm, hot_ref)]
        )
    ]
    loads = [
        pltpu.make_async_copy(
            dout_hbm.at[:, pl.ds(pl.multiple_of((group ^ j) * share, share), share)],
            dout.at[j],
            in_sems.at[j],
        )
        for j in range(groups)
    ]
    gate_copy = pltpu.make_async_copy(gate_up_hbm, gate_up, gate_sem)
    for copy in [gate_copy] + small + loads:
        copy.start()
    gate_copy.wait()
    hid = hidden.shape[1]
    gate = gate_up[:, :hid].astype(f32)
    up = gate_up[:, hid:].astype(f32)
    hidden[...] = (gate * jax.nn.sigmoid(gate) * up).astype(bf16)
    hidden_copy = pltpu.make_async_copy(hidden, hidden_hbm, hidden_sem)
    hidden_copy.start()
    for copy in small:
        copy.wait()
    row = lax.broadcasted_iota(jnp.int32, (slots, 1), 0)
    row_expert = row // CAP
    row_rank = (row % CAP).astype(f32)
    limit = jnp.zeros((slots, 1), jnp.int32)
    for e in range(flight):
        hot = hot_ref[0, 0] == e
        for h in range(1, hot_ref.shape[1]):
            hot = jnp.logical_or(hot, hot_ref[0, h] == e)
        limit = jnp.where(row_expert == e, jnp.where(hot, CAP, cap_ref[e]), limit)
    limit = limit.astype(f32)
    named = jnp.zeros((slots, tokens), f32)
    weight = jnp.zeros((slots, tokens), f32)
    for k in range(topk):
        hit = ids_ref[k : k + 1, :] == row_expert
        named = jnp.where(hit, 1.0, named)
        weight = jnp.where(hit, probs_ref[k : k + 1, :], weight)
    first = lax.broadcasted_iota(jnp.int32, (tokens, tokens), 0)
    second = lax.broadcasted_iota(jnp.int32, (tokens, tokens), 1)
    before = (first < second).astype(f32).astype(bf16)
    rank = jnp.dot(named.astype(bf16), before, preferred_element_type=f32)
    owns = (named > 0.0) & (rank == row_rank) & (rank < limit)
    own_weight = jnp.where(owns, weight, 0.0)
    own_ref[...] = own_weight
    owner = jnp.where(owns, 1.0, 0.0).astype(bf16)
    slot_weight = jnp.sum(own_weight, axis=1, keepdims=True)
    stores = []
    for j in range(groups):
        loads[j].wait()
        part = jnp.dot(owner, dout[j], preferred_element_type=f32)
        rows[j] = (part * slot_weight).astype(bf16).reshape(flight, CAP, share)
        stores.append(pltpu.make_async_copy(rows.at[j], rows_hbm.at[:, j], out_sems.at[j]))
        stores[j].start()
    for copy in stores:
        copy.wait()
    hidden_copy.wait()


def dispatch(gate_up, capacity, hot_row, ids, probs, d_out, flight, groups):
    tokens, width = d_out.shape
    rows, double = gate_up.shape
    slots = flight * CAP
    share = width // groups
    return pl.pallas_call(
        functools.partial(dispatch_kernel, flight, groups),
        out_shape=(
            pltpu.HBM((rows, double // 2), bf16),
            jax.ShapeDtypeStruct((slots, tokens), f32),
            pltpu.HBM((flight, groups, CAP, share), bf16),
        ),
        in_specs=[HBM] * 6,
        out_specs=(HBM, VMEM, HBM),
        scratch_shapes=[
            pltpu.VMEM((rows, double), bf16),
            pltpu.SMEM(capacity.shape, jnp.int32),
            pltpu.SMEM(hot_row.shape, jnp.int32),
            pltpu.VMEM(ids.shape, jnp.int32),
            pltpu.VMEM(probs.shape, f32),
            pltpu.VMEM((groups, tokens, share), bf16),
            pltpu.VMEM((rows, double // 2), bf16),
            pltpu.VMEM((groups, flight, CAP, share), bf16),
            pltpu.SemaphoreType.DMA,
            pltpu.SemaphoreType.DMA,
            pltpu.SemaphoreType.DMA((4,)),
            pltpu.SemaphoreType.DMA((groups,)),
            pltpu.SemaphoreType.DMA((groups,)),
        ],
        compiler_params=params(),
        cost_estimate=SMALL,
        name="dispatch",
    )(hbm(gate_up), hbm(capacity), hbm(hot_row), hbm(ids), hbm(probs), hbm(d_out))


def forward_kernel(
    flight, block, scale_hbm, hidden_hbm, quant_hbm, weight_hbm, out_hbm,
    scale_ref, hidden, quant, weight, out, small_sems, in_sems, out_sems, weight_sems
):
    hid, width = quant.shape
    steps = chunks(width, block)
    small = [
        pltpu.make_async_copy(scale_hbm, scale_ref, small_sems.at[0]),
        pltpu.make_async_copy(hidden_hbm, hidden, small_sems.at[1]),
    ]
    loads = [
        pltpu.make_async_copy(quant_hbm.at[:, cols], quant.at[:, cols], in_sems.at[c])
        for c, cols in enumerate(steps)
    ]
    for copy in small + loads:
        copy.start()
    for copy in small:
        copy.wait()
    stores = []
    for c, cols in enumerate(steps):
        loads[c].wait()
        for i in range(hid // QB):
            for j in range(block // QB):
                at = (pl.ds(i * QB, QB), pl.ds(c * block + j * QB, QB))
                scale = scale_ref[i, 0, c * (block // QB) + j]
                weight[at] = (quant[at].astype(f32) * scale).astype(bf16)
        stores.append(
            pltpu.make_async_copy(weight.at[:, cols], weight_hbm.at[:, cols], weight_sems.at[c])
        )
        stores[-1].start()
        part = jnp.dot(hidden[...], weight[:, cols], preferred_element_type=f32)
        out[:, :, cols] = part.astype(bf16).reshape(flight, CAP, block)
        stores.append(
            pltpu.make_async_copy(out.at[:, :, cols], out_hbm.at[:, :, cols], out_sems.at[c])
        )
        stores[-1].start()
    for copy in stores:
        copy.wait()


def forward(scale, hidden, quant, flight, block=512):
    hid, width = quant.shape
    return pl.pallas_call(
        functools.partial(forward_kernel, flight, block),
        out_shape=(
            pltpu.HBM((hid, width), bf16),
            pltpu.HBM((flight, CAP, width), bf16),
        ),
        in_specs=[HBM, HBM, HBM],
        out_specs=(HBM, HBM),
        scratch_shapes=[
            pltpu.SMEM(scale.shape, f32),
            pltpu.VMEM(hidden.shape, bf16),
            pltpu.VMEM((hid, width), bf16),
            pltpu.VMEM((hid, width), bf16),
            pltpu.VMEM((flight, CAP, width), bf16),
            pltpu.SemaphoreType.DMA((2,)),
            pltpu.SemaphoreType.DMA((width // block,)),
            pltpu.SemaphoreType.DMA((width // block,)),
            pltpu.SemaphoreType.DMA((width // block,)),
        ],
        compiler_params=params(),
        cost_estimate=SMALL,
        name="expert_forward",
    )(hbm(scale), hbm(hidden), hbm(quant))


def split_kernel(groups, out_ref, rows_ref, *refs):
    pieces, sems = refs[groups:-1], refs[-1]
    copies = [
        pltpu.make_async_copy(rows_ref.at[:, j], pieces[j - 1], sems.at[j - 1])
        for j in range(1, groups)
    ]
    for copy in copies:
        copy.start()
    for copy in copies:
        copy.wait()


def split(expert_out, rows, ties):
    flight, groups, cap, share = rows.shape
    return pl.pallas_call(
        functools.partial(split_kernel, groups),
        out_shape=(pltpu.HBM(expert_out.shape, bf16),)
        + (pltpu.HBM((flight, cap, share), bf16),) * (groups - 1),
        in_specs=[HBM] + [ANY] * groups,
        out_specs=(HBM,) * groups,
        scratch_shapes=[pltpu.SemaphoreType.DMA((groups - 1,))],
        input_output_aliases={0: 0},
        compiler_params=params(),
        cost_estimate=SMALL,
        name="split",
    )(hbm(expert_out), rows, *ties)


def backward_kernel(
    gate_up_hbm, weight_hbm, rows_ref, tie_ref, out_ref, gate_up, weight, acc, gate_sem, sems
):
    flight, groups, cap, share = rows_ref.shape
    group = lax.axis_index("dp")
    loads = [
        pltpu.make_async_copy(
            weight_hbm.at[:, pl.ds(pl.multiple_of((group ^ j) * share, share), share)],
            weight.at[j],
            sems.at[j],
        )
        for j in range(groups)
    ]
    gate_copy = pltpu.make_async_copy(gate_up_hbm, gate_up, gate_sem)
    for copy in loads + [gate_copy]:
        copy.start()
    hid = acc.shape[1]
    for j in range(groups):
        loads[j].wait()
        part = lax.dot_general(
            rows_ref[:, j].reshape(flight * cap, share),
            weight[j],
            (((1,), (1,)), ((), ())),
            preferred_element_type=f32,
        )
        if j == 0:
            acc[...] = part
        else:
            acc[...] += part
    gate_copy.wait()
    gate = gate_up[:, :hid].astype(f32)
    up = gate_up[:, hid:].astype(f32)
    sig = jax.nn.sigmoid(gate)
    d_hidden = acc[...]
    out_ref[:, :hid] = (d_hidden * up * sig * (1.0 + gate * (1.0 - sig))).astype(bf16)
    out_ref[:, hid:] = (d_hidden * (gate * sig)).astype(bf16)


def backward(gate_up, weight, rows, tie):
    slots, double = gate_up.shape
    hid, width = weight.shape
    groups = rows.shape[1]
    return pl.pallas_call(
        backward_kernel,
        out_shape=jax.ShapeDtypeStruct((slots, double), bf16),
        in_specs=[HBM, HBM, VMEM, ANY],
        out_specs=VMEM,
        scratch_shapes=[
            pltpu.VMEM((slots, double), bf16),
            pltpu.VMEM((groups, hid, width // groups), bf16),
            pltpu.VMEM((slots, hid), f32),
            pltpu.SemaphoreType.DMA,
            pltpu.SemaphoreType.DMA((groups,)),
        ],
        compiler_params=params(),
        cost_estimate=SMALL,
        name="expert_backward",
    )(hbm(gate_up), hbm(weight), rows, hbm(tie))


def combine_kernel(
    block, ids_hbm, own_ref, dout_hbm, ret_ref, out_ref, dprobs_ref, ids_ref, dout, sems
):
    copies = [
        pltpu.make_async_copy(ids_hbm, ids_ref, sems.at[0]),
        pltpu.make_async_copy(dout_hbm, dout, sems.at[1]),
    ]
    for copy in copies:
        copy.start()
    topk, tokens = ids_ref.shape
    slots = own_ref.shape[0]
    width = dout.shape[1]
    own = own_ref[...]
    turned = own.T
    high = turned.astype(bf16)
    low = (turned - high.astype(f32)).astype(bf16)
    total = jnp.zeros((slots, tokens), f32)
    for copy in copies:
        copy.wait()
    for cols in chunks(width, block):
        here = ret_ref[:, :, cols].reshape(slots, block)
        out = jnp.dot(high, here, preferred_element_type=f32)
        out = out + jnp.dot(low, here, preferred_element_type=f32)
        out_ref[:, cols] = out.astype(bf16)
        total = total + lax.dot_general(
            here, dout[:, cols], (((1,), (1,)), ((), ())), preferred_element_type=f32
        )
    inner = jnp.where(own > 0.0, total, 0.0)
    row_expert = lax.broadcasted_iota(jnp.int32, (slots, 1), 0) // CAP
    for k in range(topk):
        mine = jnp.where(ids_ref[k : k + 1, :] == row_expert, inner, 0.0)
        dprobs_ref[k : k + 1, :] = jnp.sum(mine, axis=0, keepdims=True)


def combine(ids, own, d_out, returned, block=1024):
    tokens, width = d_out.shape
    return pl.pallas_call(
        functools.partial(combine_kernel, block),
        out_shape=(
            jax.ShapeDtypeStruct((tokens, width), bf16),
            jax.ShapeDtypeStruct(ids.shape, f32),
        ),
        in_specs=[HBM, VMEM, HBM, VMEM],
        out_specs=(VMEM, VMEM),
        scratch_shapes=[
            pltpu.VMEM(ids.shape, jnp.int32),
            pltpu.VMEM((tokens, width), bf16),
            pltpu.SemaphoreType.DMA((2,)),
        ],
        compiler_params=params(),
        cost_estimate=SMALL,
        name="combine",
    )(hbm(ids), own, hbm(d_out), returned)


def weight_grad_kernel(groups, block, rows_ref, *refs):
    part_refs, hid_refs = refs[: groups - 1], refs[groups - 1 : 2 * groups - 1]
    out_hbm, grads, hidden, out, sems, out_sems = refs[2 * groups - 1 :]
    flight, cap, share = part_refs[0].shape
    slots = flight * cap
    copies = []
    for j in range(groups):
        src = rows_ref.at[:, 0] if j == 0 else part_refs[j - 1]
        copies.append(
            pltpu.make_async_copy(src, grads.at[pl.ds(j * flight, flight)], sems.at[2 * j])
        )
        copies.append(
            pltpu.make_async_copy(
                hid_refs[j], hidden.at[pl.ds(j * slots, slots)], sems.at[2 * j + 1]
            )
        )
    for copy in copies:
        copy.start()
    for copy in copies:
        copy.wait()
    stores = []
    for c, cols in enumerate(chunks(share, block)):
        out[cols, :] = lax.dot_general(
            grads[:, :, cols].reshape(groups * slots, block),
            hidden[...],
            (((0,), (0,)), ((), ())),
            preferred_element_type=f32,
        ).astype(bf16)
        stores.append(pltpu.make_async_copy(out.at[cols], out_hbm.at[cols], out_sems.at[c]))
        stores[c].start()
    for copy in stores:
        copy.wait()


def weight_grad(rows, parts, hiddens, block=256):
    flight, groups, cap, share = rows.shape
    slots, hid = hiddens[0].shape
    return pl.pallas_call(
        functools.partial(weight_grad_kernel, groups, block),
        out_shape=pltpu.HBM((share, hid), bf16),
        in_specs=[ANY] * (2 * groups),
        out_specs=HBM,
        scratch_shapes=[
            pltpu.VMEM((groups * flight, cap, share), bf16),
            pltpu.VMEM((groups * slots, hid), bf16),
            pltpu.VMEM((share, hid), bf16),
            pltpu.SemaphoreType.DMA((2 * groups,)),
            pltpu.SemaphoreType.DMA((share // block,)),
        ],
        compiler_params=params(),
        cost_estimate=SMALL,
        name="weight_grad",
    )(rows, *parts, hbm(hiddens[0]), *hiddens[1:])


def swap(value, axis, j):
    size = lax.axis_size(axis)
    return lax.ppermute(value, axis, [(i, i ^ j) for i in range(size)])


def exchange(value):
    return lax.all_to_all(value, "expert", split_axis=0, concat_axis=0, tiled=True)


def shards(route_ids, route_probs, capacity, hot_lists, gate_up, w_quant, w_scale, d_out):
    flight = lax.axis_size("expert")
    groups = lax.axis_size("dp")
    gate_up = gate_up[0, 0]
    ids, probs = route_ids.T, route_probs.T
    hidden, own, rows = dispatch(gate_up, capacity, hot_lists, ids, probs, d_out, flight, groups)
    arrived = exchange(rows)
    hiddens = [hidden] + [swap(hidden, "dp", j) for j in range(1, groups)]
    weight, expert_out = forward(w_scale.transpose(1, 0, 2), hidden, w_quant[0], flight)
    expert_out, *pieces = split(expert_out, arrived, hiddens[1:])
    returned = exchange(expert_out)
    parts = [swap(pieces[j - 1], "dp", j) for j in range(1, groups)]
    d_gate_up = backward(gate_up, weight, arrived, pieces[0])
    combined, d_probs = combine(ids, own, d_out, returned)
    d_weight = weight_grad(arrived, parts, hiddens)
    return (combined, d_probs.T, d_gate_up[None, None], d_weight[None])


def solution(mesh):
    placed = (
        P(("dp", "expert"), None),
        P(("dp", "expert"), None),
        P(),
        P("dp", None),
        P("dp", "expert", None, None),
        P("expert", None, None),
        P("expert", None, None),
        P(("dp", "expert"), None),
    )
    return jax.shard_map(
        shards,
        mesh=mesh,
        in_specs=placed,
        out_specs=(
            P(("dp", "expert"), None),
            P(("dp", "expert"), None),
            P("dp", "expert", None, None),
            P("expert", "dp", None),
        ),
        check_vma=False,
    )
```

```python
import functools

import jax
import jax.numpy as jnp
from jax import lax
from jax.experimental import pallas as pl
from jax.experimental.pallas import tpu as pltpu
from jax.sharding import PartitionSpec as P

QB = 128
CAP = 16
VMEM_LIMIT = 24 * 1024 * 1024

bf16 = jnp.bfloat16
f32 = jnp.float32

SMALL = pl.CostEstimate(flops=1024, bytes_accessed=1024, transcendentals=0)

VMEM = pl.BlockSpec(memory_space=pltpu.VMEM)
ANY = pl.BlockSpec(memory_space=pl.ANY)
HBM = pl.BlockSpec(memory_space=pltpu.HBM)


def params():
    return pltpu.CompilerParams(vmem_limit_bytes=VMEM_LIMIT)


def hbm(value):
    return pltpu.with_memory_space_constraint(value, pltpu.HBM)


def chunks(total, size):
    return [pl.ds(start, size) for start in range(0, total, size)]


def dispatch_kernel(
    flight, groups, gate_up_hbm, cap_hbm, hot_hbm, ids_hbm, probs_hbm, dout_hbm,
    hidden_hbm, own_ref, rows_hbm,
    gate_up, cap_ref, hot_ref, ids_ref, probs_ref, dout, hidden, rows,
    gate_sem, hidden_sem, small_sems, in_sems, out_sems
):
    topk, tokens = ids_ref.shape
    slots = flight * CAP
    group = lax.axis_index("dp")
    share = dout_hbm.shape[1] // groups
    small = [
        pltpu.make_async_copy(src, dst, small_sems.at[i])
        for i, (src, dst) in enumerate(
            [(ids_hbm, ids_ref), (probs_hbm, probs_ref), (cap_hbm, cap_ref), (hot_hbm, hot_ref)]
        )
    ]
    loads = [
        pltpu.make_async_copy(
            dout_hbm.at[:, pl.ds(pl.multiple_of((group ^ j) * share, share), share)],
            dout.at[j],
            in_sems.at[j],
        )
        for j in range(groups)
    ]
    gate_copy = pltpu.make_async_copy(gate_up_hbm, gate_up, gate_sem)
    for copy in [gate_copy] + small + loads:
        copy.start()
    gate_copy.wait()
    hid = hidden.shape[1]
    gate = gate_up[:, :hid].astype(f32)
    up = gate_up[:, hid:].astype(f32)
    hidden[...] = (gate * jax.nn.sigmoid(gate) * up).astype(bf16)
    hidden_copy = pltpu.make_async_copy(hidden, hidden_hbm, hidden_sem)
    hidden_copy.start()
    for copy in small:
        copy.wait()
    row = lax.broadcasted_iota(jnp.int32, (slots, 1), 0)
    row_expert = row // CAP
    row_rank = (row % CAP).astype(f32)
    limit = jnp.zeros((slots, 1), jnp.int32)
    for e in range(flight):
        hot = hot_ref[0, 0] == e
        for h in range(1, hot_ref.shape[1]):
            hot = jnp.logical_or(hot, hot_ref[0, h] == e)
        limit = jnp.where(row_expert == e, jnp.where(hot, CAP, cap_ref[e]), limit)
    limit = limit.astype(f32)
    named = jnp.zeros((slots, tokens), f32)
    weight = jnp.zeros((slots, tokens), f32)
    for k in range(topk):
        hit = ids_ref[k : k + 1, :] == row_expert
        named = jnp.where(hit, 1.0, named)
        weight = jnp.where(hit, probs_ref[k : k + 1, :], weight)
    first = lax.broadcasted_iota(jnp.int32, (tokens, tokens), 0)
    second = lax.broadcasted_iota(jnp.int32, (tokens, tokens), 1)
    before = (first < second).astype(f32).astype(bf16)
    rank = jnp.dot(named.astype(bf16), before, preferred_element_type=f32)
    owns = (named > 0.0) & (rank == row_rank) & (rank < limit)
    own_weight = jnp.where(owns, weight, 0.0)
    own_ref[...] = own_weight
    owner = jnp.where(owns, 1.0, 0.0).astype(bf16)
    slot_weight = jnp.sum(own_weight, axis=1, keepdims=True)
    stores = []
    for j in range(groups):
        loads[j].wait()
        part = jnp.dot(owner, dout[j], preferred_element_type=f32)
        rows[j] = (part * slot_weight).astype(bf16).reshape(flight, CAP, share)
        stores.append(pltpu.make_async_copy(rows.at[j], rows_hbm.at[:, j], out_sems.at[j]))
        stores[j].start()
    for copy in stores:
        copy.wait()
    hidden_copy.wait()


def dispatch(gate_up, capacity, hot_row, ids, probs, d_out, flight, groups):
    tokens, width = d_out.shape
    rows, double = gate_up.shape
    slots = flight * CAP
    share = width // groups
    return pl.pallas_call(
        functools.partial(dispatch_kernel, flight, groups),
        out_shape=(
            pltpu.HBM((rows, double // 2), bf16),
            jax.ShapeDtypeStruct((slots, tokens), f32),
            pltpu.HBM((flight, groups, CAP, share), bf16),
        ),
        in_specs=[HBM] * 6,
        out_specs=(HBM, VMEM, HBM),
        scratch_shapes=[
            pltpu.VMEM((rows, double), bf16),
            pltpu.SMEM(capacity.shape, jnp.int32),
            pltpu.SMEM(hot_row.shape, jnp.int32),
            pltpu.VMEM(ids.shape, jnp.int32),
            pltpu.VMEM(probs.shape, f32),
            pltpu.VMEM((groups, tokens, share), bf16),
            pltpu.VMEM((rows, double // 2), bf16),
            pltpu.VMEM((groups, flight, CAP, share), bf16),
            pltpu.SemaphoreType.DMA,
            pltpu.SemaphoreType.DMA,
            pltpu.SemaphoreType.DMA((4,)),
            pltpu.SemaphoreType.DMA((groups,)),
            pltpu.SemaphoreType.DMA((groups,)),
        ],
        compiler_params=params(),
        cost_estimate=SMALL,
        name="dispatch",
    )(hbm(gate_up), hbm(capacity), hbm(hot_row), hbm(ids), hbm(probs), hbm(d_out))


def forward_kernel(
    flight, block, scale_hbm, hidden_hbm, quant_hbm, weight_hbm, out_hbm,
    scale_ref, hidden, quant, weight, out, small_sems, in_sems, out_sems, weight_sems
):
    hid, width = quant.shape
    steps = chunks(width, block)
    small = [
        pltpu.make_async_copy(scale_hbm, scale_ref, small_sems.at[0]),
        pltpu.make_async_copy(hidden_hbm, hidden, small_sems.at[1]),
    ]
    loads = [
        pltpu.make_async_copy(quant_hbm.at[:, cols], quant.at[:, cols], in_sems.at[c])
        for c, cols in enumerate(steps)
    ]
    for copy in small + loads:
        copy.start()
    for copy in small:
        copy.wait()
    stores = []
    for c, cols in enumerate(steps):
        loads[c].wait()
        for i in range(hid // QB):
            for j in range(block // QB):
                at = (pl.ds(i * QB, QB), pl.ds(c * block + j * QB, QB))
                scale = scale_ref[i, 0, c * (block // QB) + j]
                weight[at] = (quant[at].astype(f32) * scale).astype(bf16)
        stores.append(
            pltpu.make_async_copy(weight.at[:, cols], weight_hbm.at[:, cols], weight_sems.at[c])
        )
        stores[-1].start()
        part = jnp.dot(hidden[...], weight[:, cols], preferred_element_type=f32)
        out[:, :, cols] = part.astype(bf16).reshape(flight, CAP, block)
        stores.append(
            pltpu.make_async_copy(out.at[:, :, cols], out_hbm.at[:, :, cols], out_sems.at[c])
        )
        stores[-1].start()
    for copy in stores:
        copy.wait()


def forward(scale, hidden, quant, flight, block=512):
    hid, width = quant.shape
    return pl.pallas_call(
        functools.partial(forward_kernel, flight, block),
        out_shape=(
            pltpu.HBM((hid, width), bf16),
            pltpu.HBM((flight, CAP, width), bf16),
        ),
        in_specs=[HBM, HBM, HBM],
        out_specs=(HBM, HBM),
        scratch_shapes=[
            pltpu.SMEM(scale.shape, f32),
            pltpu.VMEM(hidden.shape, bf16),
            pltpu.VMEM((hid, width), bf16),
            pltpu.VMEM((hid, width), bf16),
            pltpu.VMEM((flight, CAP, width), bf16),
            pltpu.SemaphoreType.DMA((2,)),
            pltpu.SemaphoreType.DMA((width // block,)),
            pltpu.SemaphoreType.DMA((width // block,)),
            pltpu.SemaphoreType.DMA((width // block,)),
        ],
        compiler_params=params(),
        cost_estimate=SMALL,
        name="expert_forward",
    )(hbm(scale), hbm(hidden), hbm(quant))


def split_kernel(groups, ties, out_ref, rows_ref, *refs):
    pieces, sems = refs[ties + 1 : -1], refs[-1]
    copies = [
        pltpu.make_async_copy(rows_ref.at[:, j], pieces[j - 1], sems.at[j - 1])
        for j in range(1, groups)
    ]
    for copy in copies:
        copy.start()
    for copy in copies:
        copy.wait()


def split(expert_out, rows, ties):
    flight, groups, cap, share = rows.shape
    return pl.pallas_call(
        functools.partial(split_kernel, groups, len(ties)),
        out_shape=(pltpu.HBM(expert_out.shape, bf16),)
        + (pltpu.HBM((flight, cap, share), bf16),) * (groups - 1),
        in_specs=[HBM] + [ANY] * (1 + len(ties)),
        out_specs=(HBM,) * groups,
        scratch_shapes=[pltpu.SemaphoreType.DMA((groups - 1,))],
        input_output_aliases={0: 0},
        compiler_params=params(),
        cost_estimate=SMALL,
        name="split",
    )(hbm(expert_out), rows, *ties)


def backward_kernel(
    gate_up_hbm, weight_hbm, rows_ref, tie_ref, out_ref, gate_up, weight, acc, gate_sem, sems
):
    flight, groups, cap, share = rows_ref.shape
    group = lax.axis_index("dp")
    loads = [
        pltpu.make_async_copy(
            weight_hbm.at[:, pl.ds(pl.multiple_of((group ^ j) * share, share), share)],
            weight.at[j],
            sems.at[j],
        )
        for j in range(groups)
    ]
    gate_copy = pltpu.make_async_copy(gate_up_hbm, gate_up, gate_sem)
    for copy in loads + [gate_copy]:
        copy.start()
    hid = acc.shape[1]
    for j in range(groups):
        loads[j].wait()
        part = lax.dot_general(
            rows_ref[:, j].reshape(flight * cap, share),
            weight[j],
            (((1,), (1,)), ((), ())),
            preferred_element_type=f32,
        )
        if j == 0:
            acc[...] = part
        else:
            acc[...] += part
    gate_copy.wait()
    gate = gate_up[:, :hid].astype(f32)
    up = gate_up[:, hid:].astype(f32)
    sig = jax.nn.sigmoid(gate)
    d_hidden = acc[...]
    out_ref[:, :hid] = (d_hidden * up * sig * (1.0 + gate * (1.0 - sig))).astype(bf16)
    out_ref[:, hid:] = (d_hidden * (gate * sig)).astype(bf16)


def backward(gate_up, weight, rows, tie):
    slots, double = gate_up.shape
    hid, width = weight.shape
    groups = rows.shape[1]
    return pl.pallas_call(
        backward_kernel,
        out_shape=pltpu.HBM((slots, double), bf16),
        in_specs=[HBM, HBM, VMEM, ANY],
        out_specs=VMEM,
        scratch_shapes=[
            pltpu.VMEM((slots, double), bf16),
            pltpu.VMEM((groups, hid, width // groups), bf16),
            pltpu.VMEM((slots, hid), f32),
            pltpu.SemaphoreType.DMA,
            pltpu.SemaphoreType.DMA((groups,)),
        ],
        compiler_params=params(),
        cost_estimate=SMALL,
        name="expert_backward",
    )(hbm(gate_up), hbm(weight), rows, hbm(tie))


def combine_kernel(
    block, ids_hbm, own_ref, dout_hbm, ret_ref, out_ref, dprobs_ref, ids_ref, dout, sems
):
    copies = [
        pltpu.make_async_copy(ids_hbm, ids_ref, sems.at[0]),
        pltpu.make_async_copy(dout_hbm, dout, sems.at[1]),
    ]
    for copy in copies:
        copy.start()
    topk, tokens = ids_ref.shape
    slots = own_ref.shape[0]
    width = dout.shape[1]
    own = own_ref[...]
    turned = own.T
    high = turned.astype(bf16)
    low = (turned - high.astype(f32)).astype(bf16)
    total = jnp.zeros((slots, tokens), f32)
    for copy in copies:
        copy.wait()
    for cols in chunks(width, block):
        here = ret_ref[:, :, cols].reshape(slots, block)
        out = jnp.dot(high, here, preferred_element_type=f32)
        out = out + jnp.dot(low, here, preferred_element_type=f32)
        out_ref[:, cols] = out.astype(bf16)
        total = total + lax.dot_general(
            here, dout[:, cols], (((1,), (1,)), ((), ())), preferred_element_type=f32
        )
    inner = jnp.where(own > 0.0, total, 0.0)
    row_expert = lax.broadcasted_iota(jnp.int32, (slots, 1), 0) // CAP
    for k in range(topk):
        mine = jnp.where(ids_ref[k : k + 1, :] == row_expert, inner, 0.0)
        dprobs_ref[k : k + 1, :] = jnp.sum(mine, axis=0, keepdims=True)


def combine(ids, own, d_out, returned, block=1024):
    tokens, width = d_out.shape
    return pl.pallas_call(
        functools.partial(combine_kernel, block),
        out_shape=(
            pltpu.HBM((tokens, width), bf16),
            pltpu.HBM(ids.shape, f32),
        ),
        in_specs=[HBM, VMEM, HBM, VMEM],
        out_specs=(VMEM, VMEM),
        scratch_shapes=[
            pltpu.VMEM(ids.shape, jnp.int32),
            pltpu.VMEM((tokens, width), bf16),
            pltpu.SemaphoreType.DMA((2,)),
        ],
        compiler_params=params(),
        cost_estimate=SMALL,
        name="combine",
    )(hbm(ids), own, hbm(d_out), returned)


def weight_grad_kernel(groups, block, tie_ref, rows_ref, *refs):
    part_refs, hid_refs = refs[: groups - 1], refs[groups - 1 : 2 * groups - 1]
    out_hbm, grads, hidden, out, sems, out_sems = refs[2 * groups - 1 :]
    flight, cap, share = part_refs[0].shape
    slots = flight * cap
    copies = []
    for j in range(groups):
        src = rows_ref.at[:, 0] if j == 0 else part_refs[j - 1]
        copies.append(
            pltpu.make_async_copy(src, grads.at[pl.ds(j * flight, flight)], sems.at[2 * j])
        )
        copies.append(
            pltpu.make_async_copy(
                hid_refs[j], hidden.at[pl.ds(j * slots, slots)], sems.at[2 * j + 1]
            )
        )
    for copy in copies:
        copy.start()
    for copy in copies:
        copy.wait()
    stores = []
    for c, cols in enumerate(chunks(share, block)):
        out[cols, :] = lax.dot_general(
            grads[:, :, cols].reshape(groups * slots, block),
            hidden[...],
            (((0,), (0,)), ((), ())),
            preferred_element_type=f32,
        ).astype(bf16)
        stores.append(pltpu.make_async_copy(out.at[cols], out_hbm.at[cols], out_sems.at[c]))
        stores[c].start()
    for copy in stores:
        copy.wait()


def weight_grad(tie, rows, parts, hiddens, block=256):
    flight, groups, cap, share = rows.shape
    slots, hid = hiddens[0].shape
    return pl.pallas_call(
        functools.partial(weight_grad_kernel, groups, block),
        out_shape=pltpu.HBM((share, hid), bf16),
        in_specs=[ANY] * (1 + 2 * groups),
        out_specs=HBM,
        scratch_shapes=[
            pltpu.VMEM((groups * flight, cap, share), bf16),
            pltpu.VMEM((groups * slots, hid), bf16),
            pltpu.VMEM((share, hid), bf16),
            pltpu.SemaphoreType.DMA((2 * groups,)),
            pltpu.SemaphoreType.DMA((share // block,)),
        ],
        compiler_params=params(),
        cost_estimate=SMALL,
        name="weight_grad",
    )(tie, rows, *parts, hbm(hiddens[0]), *hiddens[1:])


def swap(value, axis, j):
    size = lax.axis_size(axis)
    return lax.ppermute(value, axis, [(i, i ^ j) for i in range(size)])


def exchange(value):
    return lax.all_to_all(value, "expert", split_axis=0, concat_axis=0, tiled=True)


def shards(route_ids, route_probs, capacity, hot_lists, gate_up, w_quant, w_scale, d_out):
    flight = lax.axis_size("expert")
    groups = lax.axis_size("dp")
    gate_up = gate_up[0, 0]
    ids, probs = route_ids.T, route_probs.T
    hidden, own, rows = dispatch(gate_up, capacity, hot_lists, ids, probs, d_out, flight, groups)
    arrived = exchange(rows)
    hiddens, late = {0: hidden}, set()
    bit = groups // 2
    while bit:
        for j in sorted(hiddens):
            hiddens[j ^ bit] = swap(hiddens[j], "dp", bit)
            if j:
                late.add(j ^ bit)
        bit //= 2
    early = [hiddens[j] for j in range(1, groups) if j not in late]
    hiddens = [hiddens[j] for j in range(groups)]
    weight, expert_out = forward(w_scale.transpose(1, 0, 2), hidden, w_quant[0], flight)
    expert_out, *pieces = split(expert_out, arrived, early)
    returned = exchange(expert_out)
    parts = [swap(pieces[j - 1], "dp", j) for j in range(1, groups)]
    d_gate_up = backward(gate_up, weight, arrived, pieces[0])
    combined, d_probs = combine(ids, own, d_out, returned)
    d_weight = weight_grad(d_probs, arrived, parts, hiddens)
    return (combined, d_probs.T, d_gate_up[None, None], d_weight[None])


def solution(mesh):
    placed = (
        P(("dp", "expert"), None),
        P(("dp", "expert"), None),
        P(),
        P("dp", None),
        P("dp", "expert", None, None),
        P("expert", None, None),
        P("expert", None, None),
        P(("dp", "expert"), None),
    )
    return jax.shard_map(
        shards,
        mesh=mesh,
        in_specs=placed,
        out_specs=(
            P(("dp", "expert"), None),
            P(("dp", "expert"), None),
            P("dp", "expert", None, None),
            P("expert", "dp", None),
        ),
        check_vma=False,
    )
```

```python
import functools

import jax
import jax.numpy as jnp
from jax import lax
from jax.experimental import pallas as pl
from jax.experimental.pallas import tpu as pltpu
from jax.sharding import PartitionSpec as P

QB = 128
CAP = 16
VMEM_LIMIT = 30 * 1024 * 1024

bf16 = jnp.bfloat16
f32 = jnp.float32

SMALL = pl.CostEstimate(flops=1024, bytes_accessed=1024, transcendentals=0)

VMEM = pl.BlockSpec(memory_space=pltpu.VMEM)
ANY = pl.BlockSpec(memory_space=pl.ANY)
HBM = pl.BlockSpec(memory_space=pltpu.HBM)


def params():
    return pltpu.CompilerParams(vmem_limit_bytes=VMEM_LIMIT)


def hbm(value):
    return pltpu.with_memory_space_constraint(value, pltpu.HBM)


def chunks(total, size):
    return [pl.ds(start, size) for start in range(0, total, size)]


def block_place(me, r, flight):
    half = flight // 2
    return me ^ (2 * (r % half) + r // half)


def dispatch_kernel(flight, groups, gate_up_hbm, cap_hbm, hot_hbm, ids_hbm, probs_hbm, dout_hbm, *refs):
    half = flight // 2
    hidden_hbm, own_ref, *chips = refs[: 2 + half]
    gate_up, cap_ref, hot_ref, ids_ref, probs_ref, dout, hidden, rows = refs[2 + half : 10 + half]
    gate_sems, hidden_sem, small_sems, in_sems, out_sems = refs[10 + half :]
    topk, tokens = ids_ref.shape
    slots = flight * CAP
    me, group = lax.axis_index("expert"), lax.axis_index("dp")
    share = dout_hbm.shape[1] // groups
    small = [
        pltpu.make_async_copy(src, dst, small_sems.at[i])
        for i, (src, dst) in enumerate(
            [(ids_hbm, ids_ref), (probs_hbm, probs_ref), (cap_hbm, cap_ref), (hot_hbm, hot_ref)]
        )
    ]
    loads = [
        pltpu.make_async_copy(
            dout_hbm.at[:, pl.ds(pl.multiple_of((group ^ j) * share, share), share)],
            dout.at[j],
            in_sems.at[j],
        )
        for j in range(groups)
    ]
    gates = [
        pltpu.make_async_copy(
            gate_up_hbm.at[pl.ds(pl.multiple_of(block_place(me, r, flight) * CAP, CAP), CAP)],
            gate_up.at[pl.ds(r * CAP, CAP)],
            gate_sems.at[r],
        )
        for r in range(flight)
    ]
    for copy in gates + small + loads:
        copy.start()
    for copy in gates:
        copy.wait()
    hid = hidden.shape[1]
    gate = gate_up[:, :hid].astype(f32)
    up = gate_up[:, hid:].astype(f32)
    hidden[...] = (gate * jax.nn.sigmoid(gate) * up).astype(bf16)
    hidden_copy = pltpu.make_async_copy(hidden, hidden_hbm, hidden_sem)
    hidden_copy.start()
    for copy in small:
        copy.wait()
    row = lax.broadcasted_iota(jnp.int32, (slots, 1), 0)
    row_expert = row // CAP
    row_rank = (row % CAP).astype(f32)
    limit = jnp.zeros((slots, 1), jnp.int32)
    for e in range(flight):
        hot = hot_ref[0, 0] == e
        for h in range(1, hot_ref.shape[1]):
            hot = jnp.logical_or(hot, hot_ref[0, h] == e)
        limit = jnp.where(row_expert == e, jnp.where(hot, CAP, cap_ref[e]), limit)
    limit = limit.astype(f32)
    named = jnp.zeros((slots, tokens), f32)
    weight = jnp.zeros((slots, tokens), f32)
    for k in range(topk):
        hit = ids_ref[k : k + 1, :] == row_expert
        named = jnp.where(hit, 1.0, named)
        weight = jnp.where(hit, probs_ref[k : k + 1, :], weight)
    first = lax.broadcasted_iota(jnp.int32, (tokens, tokens), 0)
    second = lax.broadcasted_iota(jnp.int32, (tokens, tokens), 1)
    before = (first < second).astype(f32).astype(bf16)
    rank = jnp.dot(named.astype(bf16), before, preferred_element_type=f32)
    owns = (named > 0.0) & (rank == row_rank) & (rank < limit)
    own_weight = jnp.where(owns, weight, 0.0)
    own_ref[...] = own_weight
    owner = jnp.where(owns, 1.0, 0.0).astype(bf16)
    slot_weight = jnp.sum(own_weight, axis=1, keepdims=True)
    stores = []
    for j in range(groups):
        loads[j].wait()
        part = jnp.dot(owner, dout[j], preferred_element_type=f32)
        rows[j] = (part * slot_weight).astype(bf16).reshape(flight, CAP, share)
        for c in range(half):
            for k in range(2):
                copy = pltpu.make_async_copy(
                    rows.at[j, me ^ (2 * c + k)], chips[c].at[k, j], out_sems.at[j, 2 * c + k]
                )
                copy.start()
                stores.append(copy)
    for copy in stores:
        copy.wait()
    hidden_copy.wait()


def dispatch(gate_up, capacity, hot_row, ids, probs, d_out, flight, groups):
    tokens, width = d_out.shape
    rows, double = gate_up.shape
    slots = flight * CAP
    share = width // groups
    half = flight // 2
    return pl.pallas_call(
        functools.partial(dispatch_kernel, flight, groups),
        out_shape=(
            pltpu.HBM((rows, double // 2), bf16),
            jax.ShapeDtypeStruct((slots, tokens), f32),
        )
        + (pltpu.HBM((2, groups, CAP, share), bf16),) * half,
        in_specs=[HBM] * 6,
        out_specs=(HBM, VMEM) + (HBM,) * half,
        scratch_shapes=[
            pltpu.VMEM((rows, double), bf16),
            pltpu.SMEM(capacity.shape, jnp.int32),
            pltpu.SMEM(hot_row.shape, jnp.int32),
            pltpu.VMEM(ids.shape, jnp.int32),
            pltpu.VMEM(probs.shape, f32),
            pltpu.VMEM((groups, tokens, share), bf16),
            pltpu.VMEM((rows, double // 2), bf16),
            pltpu.VMEM((groups, flight, CAP, share), bf16),
            pltpu.SemaphoreType.DMA((flight,)),
            pltpu.SemaphoreType.DMA,
            pltpu.SemaphoreType.DMA((4,)),
            pltpu.SemaphoreType.DMA((groups,)),
            pltpu.SemaphoreType.DMA((groups, flight)),
        ],
        compiler_params=params(),
        cost_estimate=SMALL,
        name="dispatch",
    )(hbm(gate_up), hbm(capacity), hbm(hot_row), hbm(ids), hbm(probs), hbm(d_out))


def dequant(weight, quant, scale, first):
    hid, block = quant.shape
    for i in range(hid // QB):
        for j in range(block // QB):
            at = (pl.ds(i * QB, QB), pl.ds(j * QB, QB))
            weight[at] = (quant[at].astype(f32) * scale[i, 0, first + j]).astype(bf16)


def forward_kernel(
    flight, block, scale_hbm, hidden_hbm, quant_hbm, out_hbm,
    scale, hidden, quant, weight, out, scale_sem, hidden_sems, in_sems, out_sems
):
    steps, hid, _ = quant.shape
    me = lax.axis_index("expert")
    loads = [
        pltpu.make_async_copy(quant_hbm.at[:, pl.ds(c * block, block)], quant.at[c], in_sems.at[c])
        for c in range(steps)
    ]
    small = [pltpu.make_async_copy(scale_hbm, scale, scale_sem)]
    for r in range(flight):
        place = pl.multiple_of(block_place(me, r, flight) * CAP, CAP)
        small.append(
            pltpu.make_async_copy(
                hidden_hbm.at[pl.ds(r * CAP, CAP)], hidden.at[pl.ds(place, CAP)], hidden_sems.at[r]
            )
        )
    for copy in loads[:1] + small + loads[1:]:
        copy.start()
    for copy in small:
        copy.wait()
    stores = []
    for c in range(steps + 1):
        if c < steps:
            loads[c].wait()
            dequant(weight.at[c], quant.at[c], scale, c * (block // QB))
        if c > 0:
            cols = pl.ds((c - 1) * block, block)
            part = jnp.dot(hidden[...], weight[c - 1], preferred_element_type=f32)
            out[:, :, cols] = part.astype(bf16).reshape(flight, CAP, block)
            copy = pltpu.make_async_copy(
                out.at[:, :, cols], out_hbm.at[:, :, cols], out_sems.at[c - 1]
            )
            copy.start()
            stores.append(copy)
    for copy in stores:
        copy.wait()


def forward(scale, hidden, quant, flight, block=512):
    hid, width = quant.shape
    steps = width // block
    return pl.pallas_call(
        functools.partial(forward_kernel, flight, block),
        out_shape=pltpu.HBM((flight, CAP, width), bf16),
        in_specs=[HBM, HBM, HBM],
        out_specs=HBM,
        scratch_shapes=[
            pltpu.SMEM(scale.shape, f32),
            pltpu.VMEM(hidden.shape, bf16),
            pltpu.VMEM((steps, hid, block), bf16),
            pltpu.VMEM((steps, hid, block), bf16),
            pltpu.VMEM((flight, CAP, width), bf16),
            pltpu.SemaphoreType.DMA,
            pltpu.SemaphoreType.DMA((flight,)),
            pltpu.SemaphoreType.DMA((steps,)),
            pltpu.SemaphoreType.DMA((steps,)),
        ],
        compiler_params=params(),
        cost_estimate=SMALL,
        name="expert_forward",
    )(hbm(scale), hbm(hidden), hbm(quant))


def copy_all(pairs, sems):
    copies = [pltpu.make_async_copy(src, dst, sems.at[i]) for i, (src, dst) in enumerate(pairs)]
    for copy in copies:
        copy.start()
    for copy in copies:
        copy.wait()


def sibling_kernel(half, *refs):
    chips, ties, (out_ref, sems) = refs[:half], refs[half:-2], refs[-2:]
    copy_all([(chips[c].at[1], out_ref.at[c]) for c in range(half)], sems)


def sibling_rows(chips, ties):
    half = len(chips)
    return pl.pallas_call(
        functools.partial(sibling_kernel, half),
        out_shape=pltpu.HBM((half,) + chips[0].shape[1:], bf16),
        in_specs=[ANY] * (half + len(ties)),
        out_specs=HBM,
        scratch_shapes=[pltpu.SemaphoreType.DMA((half,))],
        compiler_params=params(),
        cost_estimate=SMALL,
        name="sibling_rows",
    )(hbm(chips[0]), *chips[1:], *ties)


def split_kernel(half, groups, *refs):
    chips, swapped = refs[:half], refs[half]
    pieces, sems = refs[half + 1 : -1], refs[-1]
    pairs = []
    for j in range(1, groups):
        pairs.append((swapped.at[:, j], pieces[j - 1].at[pl.ds(half, half)]))
        for c in range(half):
            pairs.append((chips[c].at[0, j], pieces[j - 1].at[c]))
    copy_all(pairs, sems)


def split(chips, swapped):
    half, groups, cap, share = swapped.shape
    return pl.pallas_call(
        functools.partial(split_kernel, half, groups),
        out_shape=(pltpu.HBM((2 * half, cap, share), bf16),) * (groups - 1),
        in_specs=[ANY] * (half + 1),
        out_specs=(HBM,) * (groups - 1),
        scratch_shapes=[pltpu.SemaphoreType.DMA(((groups - 1) * (half + 1),))],
        compiler_params=params(),
        cost_estimate=SMALL,
        name="split",
    )(hbm(chips[0]), *chips[1:], swapped)


def backward_kernel(flight, groups, scale_hbm, gate_up_hbm, quant_hbm, tie_ref, swapped, *refs):
    half = flight // 2
    chips, out_hbm = refs[:half], refs[half]
    scale, gate_up, rows, quant, weight, acc, out = refs[half + 1 : half + 8]
    scale_sem, gate_sems, row_sems, in_sems, out_sems = refs[half + 8 :]
    me, group = lax.axis_index("expert"), lax.axis_index("dp")
    slots, hid = acc.shape
    share = quant.shape[2]

    def place(r):
        return pl.ds(pl.multiple_of(block_place(me, r, flight) * CAP, CAP), CAP)

    loads = [
        pltpu.make_async_copy(
            quant_hbm.at[:, pl.ds(pl.multiple_of((group ^ j) * share, share), share)],
            quant.at[j],
            in_sems.at[j],
        )
        for j in range(groups)
    ]
    gates = [
        pltpu.make_async_copy(
            gate_up_hbm.at[place(r)], gate_up.at[pl.ds(r * CAP, CAP)], gate_sems.at[r]
        )
        for r in range(flight)
    ]
    small = [pltpu.make_async_copy(scale_hbm, scale, scale_sem)]
    for r in range(flight):
        src = chips[r].at[0] if r < half else swapped.at[r - half]
        small.append(
            pltpu.make_async_copy(src, rows.at[:, pl.ds(r * CAP, CAP), :], row_sems.at[r])
        )
    for copy in loads[:1] + small + loads[1:] + gates:
        copy.start()
    for copy in small:
        copy.wait()
    for j in range(groups + 1):
        if j < groups:
            loads[j].wait()
            dequant(weight.at[j], quant.at[j], scale, (group ^ j) * (share // QB))
        if j > 0:
            part = lax.dot_general(
                rows[j - 1], weight[j - 1], (((1,), (1,)), ((), ())), preferred_element_type=f32
            )
            if j == 1:
                acc[...] = part
            else:
                acc[...] += part
    for copy in gates:
        copy.wait()
    gate = gate_up[:, :hid].astype(f32)
    up = gate_up[:, hid:].astype(f32)
    sig = jax.nn.sigmoid(gate)
    d_hidden = acc[...]
    out[:, :hid] = (d_hidden * up * sig * (1.0 + gate * (1.0 - sig))).astype(bf16)
    out[:, hid:] = (d_hidden * (gate * sig)).astype(bf16)
    copy_all([(out.at[pl.ds(r * CAP, CAP)], out_hbm.at[place(r)]) for r in range(flight)], out_sems)


def backward(scale, gate_up, quant, tie, chips, swapped):
    slots, double = gate_up.shape
    hid, width = quant.shape
    half, groups, cap, share = swapped.shape
    flight = 2 * half
    return pl.pallas_call(
        functools.partial(backward_kernel, flight, groups),
        out_shape=pltpu.HBM((slots, double), bf16),
        in_specs=[HBM, HBM, HBM, HBM] + [ANY] * (1 + half),
        out_specs=HBM,
        scratch_shapes=[
            pltpu.SMEM(scale.shape, f32),
            pltpu.VMEM((slots, double), bf16),
            pltpu.VMEM((groups, slots, share), bf16),
            pltpu.VMEM((groups, hid, share), bf16),
            pltpu.VMEM((groups, hid, share), bf16),
            pltpu.VMEM((slots, hid), f32),
            pltpu.VMEM((slots, double), bf16),
            pltpu.SemaphoreType.DMA,
            pltpu.SemaphoreType.DMA((flight,)),
            pltpu.SemaphoreType.DMA((flight,)),
            pltpu.SemaphoreType.DMA((groups,)),
            pltpu.SemaphoreType.DMA((flight,)),
        ],
        compiler_params=params(),
        cost_estimate=SMALL,
        name="expert_backward",
    )(hbm(scale), hbm(gate_up), hbm(quant), hbm(tie), swapped, hbm(chips[0]), *chips[1:])


def combine_kernel(
    block, ids_hbm, own_ref, dout_hbm, ret_ref, out_ref, dprobs_ref, ids_ref, dout, sems
):
    copies = [
        pltpu.make_async_copy(ids_hbm, ids_ref, sems.at[0]),
        pltpu.make_async_copy(dout_hbm, dout, sems.at[1]),
    ]
    for copy in copies:
        copy.start()
    topk, tokens = ids_ref.shape
    slots = own_ref.shape[0]
    width = dout.shape[1]
    own = own_ref[...]
    turned = own.T
    high = turned.astype(bf16)
    low = (turned - high.astype(f32)).astype(bf16)
    total = jnp.zeros((slots, tokens), f32)
    for copy in copies:
        copy.wait()
    for cols in chunks(width, block):
        here = ret_ref[:, :, cols].reshape(slots, block)
        out = jnp.dot(high, here, preferred_element_type=f32)
        out = out + jnp.dot(low, here, preferred_element_type=f32)
        out_ref[:, cols] = out.astype(bf16)
        total = total + lax.dot_general(
            here, dout[:, cols], (((1,), (1,)), ((), ())), preferred_element_type=f32
        )
    inner = jnp.where(own > 0.0, total, 0.0)
    row_expert = lax.broadcasted_iota(jnp.int32, (slots, 1), 0) // CAP
    for k in range(topk):
        mine = jnp.where(ids_ref[k : k + 1, :] == row_expert, inner, 0.0)
        dprobs_ref[k : k + 1, :] = jnp.sum(mine, axis=0, keepdims=True)


def combine(ids, own, d_out, returned, block=1024):
    tokens, width = d_out.shape
    return pl.pallas_call(
        functools.partial(combine_kernel, block),
        out_shape=(
            pltpu.HBM((tokens, width), bf16),
            pltpu.HBM(ids.shape, f32),
        ),
        in_specs=[HBM, VMEM, HBM, VMEM],
        out_specs=(VMEM, VMEM),
        scratch_shapes=[
            pltpu.VMEM(ids.shape, jnp.int32),
            pltpu.VMEM((tokens, width), bf16),
            pltpu.SemaphoreType.DMA((2,)),
        ],
        compiler_params=params(),
        cost_estimate=SMALL,
        name="combine",
    )(hbm(ids), own, hbm(d_out), returned)


def weight_grad_kernel(half, groups, block, tie_ref, swapped, *refs):
    chips, parts = refs[:half], refs[half : half + groups - 1]
    hid_refs = refs[half + groups - 1 : half + 2 * groups - 1]
    out_hbm, grads, hidden, out, sems, out_sems = refs[half + 2 * groups - 1 :]
    cap, share = parts[0].shape[1:]
    slots = 2 * half * cap
    pairs = [(chips[c].at[0, 0], grads.at[c]) for c in range(half)]
    pairs.append((swapped.at[:, 0], grads.at[pl.ds(half, half)]))
    for j in range(groups):
        pairs.append((hid_refs[j], hidden.at[pl.ds(j * slots, slots)]))
        if j:
            pairs.append((parts[j - 1], grads.at[pl.ds(2 * half * j, 2 * half)]))
    copy_all(pairs, sems)
    stores = []
    for c, cols in enumerate(chunks(share, block)):
        out[cols, :] = lax.dot_general(
            grads[:, :, cols].reshape(groups * slots, block),
            hidden[...],
            (((0,), (0,)), ((), ())),
            preferred_element_type=f32,
        ).astype(bf16)
        stores.append(pltpu.make_async_copy(out.at[cols], out_hbm.at[cols], out_sems.at[c]))
        stores[c].start()
    for copy in stores:
        copy.wait()


def weight_grad(tie, chips, swapped, parts, hiddens, block=256):
    half, groups, cap, share = swapped.shape
    slots, hid = hiddens[0].shape
    return pl.pallas_call(
        functools.partial(weight_grad_kernel, half, groups, block),
        out_shape=pltpu.HBM((share, hid), bf16),
        in_specs=[HBM] + [ANY] * (half + 2 * groups),
        out_specs=HBM,
        scratch_shapes=[
            pltpu.VMEM((groups * 2 * half, cap, share), bf16),
            pltpu.VMEM((groups * slots, hid), bf16),
            pltpu.VMEM((share, hid), bf16),
            pltpu.SemaphoreType.DMA((half + 2 * groups,)),
            pltpu.SemaphoreType.DMA((share // block,)),
        ],
        compiler_params=params(),
        cost_estimate=SMALL,
        name="weight_grad",
    )(hbm(tie), swapped, hbm(chips[0]), *chips[1:], *parts, hbm(hiddens[0]), *hiddens[1:])


def swap(value, axis, j):
    size = lax.axis_size(axis)
    return lax.ppermute(value, axis, [(i, i ^ j) for i in range(size)])


def shards(route_ids, route_probs, capacity, hot_lists, gate_up, w_quant, w_scale, d_out):
    flight = lax.axis_size("expert")
    groups = lax.axis_size("dp")
    gate_up = gate_up[0, 0]
    ids, probs = route_ids.T, route_probs.T
    scale = w_scale.transpose(1, 0, 2)
    hidden, own, *chips = dispatch(
        gate_up, capacity, hot_lists, ids, probs, d_out, flight, groups
    )
    chips = chips[:1] + [swap(chips[c], "expert", 2 * c) for c in range(1, flight // 2)]
    hiddens, late = {0: hidden}, set()
    bit = groups // 2
    while bit:
        for j in sorted(hiddens):
            hiddens[j ^ bit] = swap(hiddens[j], "dp", bit)
            if j:
                late.add(j ^ bit)
        bit //= 2
    early = [hiddens[j] for j in range(1, groups) if j not in late]
    hiddens = [hiddens[j] for j in range(groups)]
    expert_out = forward(scale, hidden, w_quant[0], flight)
    returned = lax.all_to_all(expert_out, "expert", split_axis=0, concat_axis=0, tiled=True)
    swapped = swap(sibling_rows(chips, [hbm(expert_out)] + early), "expert", 1)
    pieces = split(chips, swapped)
    parts = [swap(pieces[j - 1], "dp", j) for j in range(1, groups)]
    d_gate_up = backward(scale, gate_up, w_quant[0], pieces[0], chips, swapped)
    combined, d_probs = combine(ids, own, d_out, returned)
    d_weight = weight_grad(d_probs, chips, swapped, parts, hiddens)
    return (combined, d_probs.T, d_gate_up[None, None], d_weight[None])


def solution(mesh):
    placed = (
        P(("dp", "expert"), None),
        P(("dp", "expert"), None),
        P(),
        P("dp", None),
        P("dp", "expert", None, None),
        P("expert", None, None),
        P("expert", None, None),
        P(("dp", "expert"), None),
    )
    return jax.shard_map(
        shards,
        mesh=mesh,
        in_specs=placed,
        out_specs=(
            P(("dp", "expert"), None),
            P(("dp", "expert"), None),
            P("dp", "expert", None, None),
            P("expert", "dp", None),
        ),
        check_vma=False,
    )
```

```python
import functools

import jax
import jax.numpy as jnp
from jax import lax
from jax.experimental import pallas as pl
from jax.experimental.pallas import tpu as pltpu
from jax.sharding import PartitionSpec as P

QB = 128
CAP = 16
VMEM_LIMIT = 30 * 1024 * 1024

bf16 = jnp.bfloat16
f32 = jnp.float32

SMALL = pl.CostEstimate(flops=1024, bytes_accessed=1024, transcendentals=0)

VMEM = pl.BlockSpec(memory_space=pltpu.VMEM)
ANY = pl.BlockSpec(memory_space=pl.ANY)
HBM = pl.BlockSpec(memory_space=pltpu.HBM)


def params():
    return pltpu.CompilerParams(vmem_limit_bytes=VMEM_LIMIT)


def hbm(value):
    return pltpu.with_memory_space_constraint(value, pltpu.HBM)


def chunks(total, size):
    return [pl.ds(start, size) for start in range(0, total, size)]


def block_place(me, r, flight):
    half = flight // 2
    return me ^ (2 * (r % half) + r // half)


def dispatch_kernel(flight, groups, gate_up_hbm, cap_hbm, hot_hbm, ids_hbm, probs_hbm, dout_hbm, *refs):
    half = flight // 2
    hidden_hbm, own_hbm, *chips = refs[: 2 + half]
    gate_up, cap_ref, hot_ref, ids_ref, probs_ref, dout = refs[2 + half : 8 + half]
    hidden, own_ref, rows = refs[8 + half : 11 + half]
    gate_sems, keep_sems, small_sems, in_sems, out_sems = refs[11 + half :]
    topk, tokens = ids_ref.shape
    slots = flight * CAP
    me, group = lax.axis_index("expert"), lax.axis_index("dp")
    share = dout_hbm.shape[1] // groups
    small = [
        pltpu.make_async_copy(src, dst, small_sems.at[i])
        for i, (src, dst) in enumerate(
            [(ids_hbm, ids_ref), (probs_hbm, probs_ref), (cap_hbm, cap_ref), (hot_hbm, hot_ref)]
        )
    ]
    loads = [
        pltpu.make_async_copy(
            dout_hbm.at[:, pl.ds(pl.multiple_of((group ^ j) * share, share), share)],
            dout.at[j],
            in_sems.at[j],
        )
        for j in range(groups)
    ]
    gates = [
        pltpu.make_async_copy(
            gate_up_hbm.at[pl.ds(pl.multiple_of(block_place(me, r, flight) * CAP, CAP), CAP)],
            gate_up.at[pl.ds(r * CAP, CAP)],
            gate_sems.at[r],
        )
        for r in range(flight)
    ]
    for copy in gates + small + loads:
        copy.start()
    for copy in gates:
        copy.wait()
    hid = hidden.shape[1]
    gate = gate_up[:, :hid].astype(f32)
    up = gate_up[:, hid:].astype(f32)
    hidden[...] = (gate * jax.nn.sigmoid(gate) * up).astype(bf16)
    hidden_copy = pltpu.make_async_copy(hidden, hidden_hbm, keep_sems.at[0])
    hidden_copy.start()
    for copy in small:
        copy.wait()
    row = lax.broadcasted_iota(jnp.int32, (slots, 1), 0)
    row_expert = row // CAP
    row_rank = (row % CAP).astype(f32)
    limit = jnp.zeros((slots, 1), jnp.int32)
    for e in range(flight):
        hot = hot_ref[0, 0] == e
        for h in range(1, hot_ref.shape[1]):
            hot = jnp.logical_or(hot, hot_ref[0, h] == e)
        limit = jnp.where(row_expert == e, jnp.where(hot, CAP, cap_ref[e]), limit)
    limit = limit.astype(f32)
    named = jnp.zeros((slots, tokens), f32)
    weight = jnp.zeros((slots, tokens), f32)
    for k in range(topk):
        hit = ids_ref[k : k + 1, :] == row_expert
        named = jnp.where(hit, 1.0, named)
        weight = jnp.where(hit, probs_ref[k : k + 1, :], weight)
    first = lax.broadcasted_iota(jnp.int32, (tokens, tokens), 0)
    second = lax.broadcasted_iota(jnp.int32, (tokens, tokens), 1)
    before = (first < second).astype(f32).astype(bf16)
    rank = jnp.dot(named.astype(bf16), before, preferred_element_type=f32)
    owns = (named > 0.0) & (rank == row_rank) & (rank < limit)
    own_weight = jnp.where(owns, weight, 0.0)
    own_ref[...] = own_weight
    own_copy = pltpu.make_async_copy(own_ref, own_hbm, keep_sems.at[1])
    own_copy.start()
    owner = jnp.where(owns, 1.0, 0.0).astype(bf16)
    slot_weight = jnp.sum(own_weight, axis=1, keepdims=True)
    stores = []
    for j in range(groups):
        loads[j].wait()
        part = jnp.dot(owner, dout[j], preferred_element_type=f32)
        rows[j] = (part * slot_weight).astype(bf16).reshape(flight, CAP, share)
        for c in range(half):
            for k in range(2):
                copy = pltpu.make_async_copy(
                    rows.at[j, me ^ (2 * c + k)], chips[c].at[k, j], out_sems.at[j, 2 * c + k]
                )
                copy.start()
                stores.append(copy)
    for copy in stores:
        copy.wait()
    hidden_copy.wait()
    own_copy.wait()


def dispatch(gate_up, capacity, hot_row, ids, probs, d_out, flight, groups):
    tokens, width = d_out.shape
    rows, double = gate_up.shape
    slots = flight * CAP
    share = width // groups
    half = flight // 2
    return pl.pallas_call(
        functools.partial(dispatch_kernel, flight, groups),
        out_shape=(
            pltpu.HBM((rows, double // 2), bf16),
            pltpu.HBM((slots, tokens), f32),
        )
        + (pltpu.HBM((2, groups, CAP, share), bf16),) * half,
        in_specs=[HBM] * 6,
        out_specs=(HBM, HBM) + (HBM,) * half,
        scratch_shapes=[
            pltpu.VMEM((rows, double), bf16),
            pltpu.SMEM(capacity.shape, jnp.int32),
            pltpu.SMEM(hot_row.shape, jnp.int32),
            pltpu.VMEM(ids.shape, jnp.int32),
            pltpu.VMEM(probs.shape, f32),
            pltpu.VMEM((groups, tokens, share), bf16),
            pltpu.VMEM((rows, double // 2), bf16),
            pltpu.VMEM((slots, tokens), f32),
            pltpu.VMEM((groups, flight, CAP, share), bf16),
            pltpu.SemaphoreType.DMA((flight,)),
            pltpu.SemaphoreType.DMA((2,)),
            pltpu.SemaphoreType.DMA((4,)),
            pltpu.SemaphoreType.DMA((groups,)),
            pltpu.SemaphoreType.DMA((groups, flight)),
        ],
        compiler_params=params(),
        cost_estimate=SMALL,
        name="dispatch",
    )(hbm(gate_up), hbm(capacity), hbm(hot_row), hbm(ids), hbm(probs), hbm(d_out))


def dequant(weight, quant, scale, first):
    hid, block = quant.shape
    for i in range(hid // QB):
        for j in range(block // QB):
            at = (pl.ds(i * QB, QB), pl.ds(j * QB, QB))
            factor = jnp.full((CAP, QB), scale[i, 0, first + j], f32).astype(bf16)
            part = quant[at].reshape(QB // CAP, CAP, QB) * factor[None]
            weight[at] = part.reshape(QB, QB)


def forward_kernel(
    flight, block, scale_hbm, hidden_hbm, quant_hbm, out_hbm,
    scale, hidden, quant, weight, out, scale_sem, hidden_sems, in_sems, out_sems
):
    steps, hid, _ = quant.shape
    me = lax.axis_index("expert")
    loads = [
        pltpu.make_async_copy(quant_hbm.at[:, pl.ds(c * block, block)], quant.at[c], in_sems.at[c])
        for c in range(steps)
    ]
    small = [pltpu.make_async_copy(scale_hbm, scale, scale_sem)]
    for r in range(flight):
        place = pl.multiple_of(block_place(me, r, flight) * CAP, CAP)
        small.append(
            pltpu.make_async_copy(
                hidden_hbm.at[pl.ds(r * CAP, CAP)], hidden.at[pl.ds(place, CAP)], hidden_sems.at[r]
            )
        )
    for copy in loads[:1] + small + loads[1:]:
        copy.start()
    for copy in small:
        copy.wait()
    stores = []
    for c in range(steps + 1):
        if c < steps:
            loads[c].wait()
            dequant(weight.at[c], quant.at[c], scale, c * (block // QB))
        if c > 0:
            cols = pl.ds((c - 1) * block, block)
            part = jnp.dot(hidden[...], weight[c - 1], preferred_element_type=f32)
            out[:, :, cols] = part.astype(bf16).reshape(flight, CAP, block)
            copy = pltpu.make_async_copy(
                out.at[:, :, cols], out_hbm.at[:, :, cols], out_sems.at[c - 1]
            )
            copy.start()
            stores.append(copy)
    for copy in stores:
        copy.wait()


def forward(scale, hidden, quant, flight, block=512):
    hid, width = quant.shape
    steps = width // block
    return pl.pallas_call(
        functools.partial(forward_kernel, flight, block),
        out_shape=pltpu.HBM((flight, CAP, width), bf16),
        in_specs=[HBM, HBM, HBM],
        out_specs=HBM,
        scratch_shapes=[
            pltpu.SMEM(scale.shape, f32),
            pltpu.VMEM(hidden.shape, bf16),
            pltpu.VMEM((steps, hid, block), bf16),
            pltpu.VMEM((steps, hid, block), bf16),
            pltpu.VMEM((flight, CAP, width), bf16),
            pltpu.SemaphoreType.DMA,
            pltpu.SemaphoreType.DMA((flight,)),
            pltpu.SemaphoreType.DMA((steps,)),
            pltpu.SemaphoreType.DMA((steps,)),
        ],
        compiler_params=params(),
        cost_estimate=SMALL,
        name="expert_forward",
    )(hbm(scale), hbm(hidden), hbm(quant))


def copy_all(pairs, sems):
    copies = [pltpu.make_async_copy(src, dst, sems.at[i]) for i, (src, dst) in enumerate(pairs)]
    for copy in copies:
        copy.start()
    for copy in copies:
        copy.wait()


def sibling_kernel(half, *refs):
    chips, ties, (out_ref, sems) = refs[:half], refs[half:-2], refs[-2:]
    copy_all([(chips[c].at[1], out_ref.at[c]) for c in range(half)], sems)


def sibling_rows(chips, ties):
    half = len(chips)
    return pl.pallas_call(
        functools.partial(sibling_kernel, half),
        out_shape=pltpu.VMEM((half,) + chips[0].shape[1:], bf16),
        in_specs=[ANY] * (half + len(ties)),
        out_specs=VMEM,
        scratch_shapes=[pltpu.SemaphoreType.DMA((half,))],
        compiler_params=params(),
        cost_estimate=SMALL,
        name="sibling_rows",
    )(hbm(chips[0]), *chips[1:], *ties)


def split_kernel(half, groups, *refs):
    chips, swapped = refs[:half], refs[half]
    pieces, sems = refs[half + 1 : -1], refs[-1]
    pairs = []
    for j in range(1, groups):
        pairs.append((swapped.at[:, j], pieces[j - 1].at[pl.ds(half, half)]))
        for c in range(half):
            pairs.append((chips[c].at[0, j], pieces[j - 1].at[c]))
    copy_all(pairs, sems)


def split(chips, swapped):
    half, groups, cap, share = swapped.shape
    return pl.pallas_call(
        functools.partial(split_kernel, half, groups),
        out_shape=(pltpu.VMEM((2 * half, cap, share), bf16),) * (groups - 1),
        in_specs=[ANY] * (half + 1),
        out_specs=(VMEM,) * (groups - 1),
        scratch_shapes=[pltpu.SemaphoreType.DMA(((groups - 1) * (half + 1),))],
        compiler_params=params(),
        cost_estimate=SMALL,
        name="split",
    )(hbm(chips[0]), *chips[1:], swapped)


def backward_kernel(flight, groups, scale_hbm, gate_up_hbm, quant_hbm, tie_ref, swapped, *refs):
    half = flight // 2
    chips, out_hbm = refs[:half], refs[half]
    scale, gate_up, rows, quant, weight, acc, out = refs[half + 1 : half + 8]
    scale_sem, gate_sems, row_sems, in_sems, out_sems = refs[half + 8 :]
    me, group = lax.axis_index("expert"), lax.axis_index("dp")
    slots, hid = acc.shape
    share = quant.shape[2]

    def place(r):
        return pl.ds(pl.multiple_of(block_place(me, r, flight) * CAP, CAP), CAP)

    loads = [
        pltpu.make_async_copy(
            quant_hbm.at[:, pl.ds(pl.multiple_of((group ^ j) * share, share), share)],
            quant.at[j],
            in_sems.at[j],
        )
        for j in range(groups)
    ]
    gates = [
        pltpu.make_async_copy(
            gate_up_hbm.at[place(r)], gate_up.at[pl.ds(r * CAP, CAP)], gate_sems.at[r]
        )
        for r in range(flight)
    ]
    small = [pltpu.make_async_copy(scale_hbm, scale, scale_sem)]
    for r in range(flight):
        src = chips[r].at[0] if r < half else swapped.at[r - half]
        small.append(
            pltpu.make_async_copy(src, rows.at[:, pl.ds(r * CAP, CAP), :], row_sems.at[r])
        )
    for copy in loads[:1] + small + loads[1:] + gates:
        copy.start()
    for copy in small:
        copy.wait()
    for j in range(groups + 1):
        if j < groups:
            loads[j].wait()
            dequant(weight.at[j], quant.at[j], scale, (group ^ j) * (share // QB))
        if j > 0:
            part = lax.dot_general(
                rows[j - 1], weight[j - 1], (((1,), (1,)), ((), ())), preferred_element_type=f32
            )
            if j == 1:
                acc[...] = part
            else:
                acc[...] += part
    for copy in gates:
        copy.wait()
    gate = gate_up[:, :hid].astype(f32)
    up = gate_up[:, hid:].astype(f32)
    sig = jax.nn.sigmoid(gate)
    d_hidden = acc[...]
    out[:, :hid] = (d_hidden * up * sig * (1.0 + gate * (1.0 - sig))).astype(bf16)
    out[:, hid:] = (d_hidden * (gate * sig)).astype(bf16)
    copy_all([(out.at[pl.ds(r * CAP, CAP)], out_hbm.at[place(r)]) for r in range(flight)], out_sems)


def backward(scale, gate_up, quant, tie, chips, swapped):
    slots, double = gate_up.shape
    hid, width = quant.shape
    half, groups, cap, share = swapped.shape
    flight = 2 * half
    return pl.pallas_call(
        functools.partial(backward_kernel, flight, groups),
        out_shape=pltpu.HBM((slots, double), bf16),
        in_specs=[HBM, HBM, HBM] + [ANY] * (2 + half),
        out_specs=HBM,
        scratch_shapes=[
            pltpu.SMEM(scale.shape, f32),
            pltpu.VMEM((slots, double), bf16),
            pltpu.VMEM((groups, slots, share), bf16),
            pltpu.VMEM((groups, hid, share), bf16),
            pltpu.VMEM((groups, hid, share), bf16),
            pltpu.VMEM((slots, hid), f32),
            pltpu.VMEM((slots, double), bf16),
            pltpu.SemaphoreType.DMA,
            pltpu.SemaphoreType.DMA((flight,)),
            pltpu.SemaphoreType.DMA((flight,)),
            pltpu.SemaphoreType.DMA((groups,)),
            pltpu.SemaphoreType.DMA((flight,)),
        ],
        compiler_params=params(),
        cost_estimate=SMALL,
        name="expert_backward",
    )(hbm(scale), hbm(gate_up), hbm(quant), tie, swapped, hbm(chips[0]), *chips[1:])


def combine_kernel(
    block, ids_hbm, own_hbm, dout_hbm, ret_ref, out_ref, dprobs_ref, ids_ref, own_ref, dout, sems
):
    copies = [
        pltpu.make_async_copy(ids_hbm, ids_ref, sems.at[0]),
        pltpu.make_async_copy(own_hbm, own_ref, sems.at[1]),
        pltpu.make_async_copy(dout_hbm, dout, sems.at[2]),
    ]
    for copy in copies:
        copy.start()
    topk, tokens = ids_ref.shape
    slots = own_ref.shape[0]
    width = dout.shape[1]
    copies[1].wait()
    own = own_ref[...]
    turned = own.T
    high = turned.astype(bf16)
    low = (turned - high.astype(f32)).astype(bf16)
    total = jnp.zeros((slots, tokens), f32)
    copies[0].wait()
    copies[2].wait()
    for cols in chunks(width, block):
        here = ret_ref[:, :, cols].reshape(slots, block)
        out = jnp.dot(high, here, preferred_element_type=f32)
        out = out + jnp.dot(low, here, preferred_element_type=f32)
        out_ref[:, cols] = out.astype(bf16)
        total = total + lax.dot_general(
            here, dout[:, cols], (((1,), (1,)), ((), ())), preferred_element_type=f32
        )
    inner = jnp.where(own > 0.0, total, 0.0)
    row_expert = lax.broadcasted_iota(jnp.int32, (slots, 1), 0) // CAP
    for k in range(topk):
        mine = jnp.where(ids_ref[k : k + 1, :] == row_expert, inner, 0.0)
        dprobs_ref[k : k + 1, :] = jnp.sum(mine, axis=0, keepdims=True)


def combine(ids, own, d_out, returned, block=1024):
    tokens, width = d_out.shape
    return pl.pallas_call(
        functools.partial(combine_kernel, block),
        out_shape=(
            pltpu.HBM((tokens, width), bf16),
            pltpu.HBM(ids.shape, f32),
        ),
        in_specs=[HBM, HBM, HBM, VMEM],
        out_specs=(VMEM, VMEM),
        scratch_shapes=[
            pltpu.VMEM(ids.shape, jnp.int32),
            pltpu.VMEM(own.shape, f32),
            pltpu.VMEM((tokens, width), bf16),
            pltpu.SemaphoreType.DMA((3,)),
        ],
        compiler_params=params(),
        cost_estimate=SMALL,
        name="combine",
    )(hbm(ids), hbm(own), hbm(d_out), returned)


def weight_grad_kernel(half, groups, block, tie_ref, swapped, *refs):
    chips, parts = refs[:half], refs[half : half + groups - 1]
    hid_refs = refs[half + groups - 1 : half + 2 * groups - 1]
    out_hbm, grads, hidden, out, sems, out_sems = refs[half + 2 * groups - 1 :]
    cap, share = parts[0].shape[1:]
    slots = 2 * half * cap
    pairs = [(chips[c].at[0, 0], grads.at[c]) for c in range(half)]
    pairs.append((swapped.at[:, 0], grads.at[pl.ds(half, half)]))
    for j in range(groups):
        pairs.append((hid_refs[j], hidden.at[pl.ds(j * slots, slots)]))
        if j:
            pairs.append((parts[j - 1], grads.at[pl.ds(2 * half * j, 2 * half)]))
    copy_all(pairs, sems)
    stores = []
    for c, cols in enumerate(chunks(share, block)):
        out[cols, :] = lax.dot_general(
            grads[:, :, cols].reshape(groups * slots, block),
            hidden[...],
            (((0,), (0,)), ((), ())),
            preferred_element_type=f32,
        ).astype(bf16)
        stores.append(pltpu.make_async_copy(out.at[cols], out_hbm.at[cols], out_sems.at[c]))
        stores[c].start()
    for copy in stores:
        copy.wait()


def weight_grad(tie, chips, swapped, parts, hiddens, block=256):
    half, groups, cap, share = swapped.shape
    slots, hid = hiddens[0].shape
    return pl.pallas_call(
        functools.partial(weight_grad_kernel, half, groups, block),
        out_shape=pltpu.HBM((share, hid), bf16),
        in_specs=[HBM] + [ANY] * (half + 2 * groups),
        out_specs=HBM,
        scratch_shapes=[
            pltpu.VMEM((groups * 2 * half, cap, share), bf16),
            pltpu.VMEM((groups * slots, hid), bf16),
            pltpu.VMEM((share, hid), bf16),
            pltpu.SemaphoreType.DMA((half + 2 * groups,)),
            pltpu.SemaphoreType.DMA((share // block,)),
        ],
        compiler_params=params(),
        cost_estimate=SMALL,
        name="weight_grad",
    )(hbm(tie), swapped, hbm(chips[0]), *chips[1:], *parts, hbm(hiddens[0]), *hiddens[1:])


def swap(value, axis, j):
    size = lax.axis_size(axis)
    return lax.ppermute(value, axis, [(i, i ^ j) for i in range(size)])


def shards(route_ids, route_probs, capacity, hot_lists, gate_up, w_quant, w_scale, d_out):
    flight = lax.axis_size("expert")
    groups = lax.axis_size("dp")
    gate_up = gate_up[0, 0]
    ids, probs = route_ids.T, route_probs.T
    scale = w_scale.transpose(1, 0, 2)
    hidden, own, *chips = dispatch(
        gate_up, capacity, hot_lists, ids, probs, d_out, flight, groups
    )
    chips = chips[:1] + [swap(chips[c], "expert", 2 * c) for c in range(1, flight // 2)]
    hiddens, late = {0: hidden}, set()
    bit = groups // 2
    while bit:
        for j in sorted(hiddens):
            hiddens[j ^ bit] = swap(hiddens[j], "dp", bit)
            if j:
                late.add(j ^ bit)
        bit //= 2
    early = [hiddens[j] for j in range(1, groups) if j not in late]
    hiddens = [hiddens[j] for j in range(groups)]
    expert_out = forward(scale, hidden, w_quant[0], flight)
    returned = lax.all_to_all(expert_out, "expert", split_axis=0, concat_axis=0, tiled=True)
    swapped = swap(sibling_rows(chips, [hbm(expert_out)] + early), "expert", 1)
    pieces = split(chips, swapped)
    parts = [swap(pieces[j - 1], "dp", j) for j in range(1, groups)]
    d_gate_up = backward(scale, gate_up, w_quant[0], pieces[0], chips, swapped)
    combined, d_probs = combine(ids, own, d_out, returned)
    d_weight = weight_grad(d_probs, chips, swapped, parts, hiddens)
    return (combined, d_probs.T, d_gate_up[None, None], d_weight[None])


def solution(mesh):
    placed = (
        P(("dp", "expert"), None),
        P(("dp", "expert"), None),
        P(),
        P("dp", None),
        P("dp", "expert", None, None),
        P("expert", None, None),
        P("expert", None, None),
        P(("dp", "expert"), None),
    )
    return jax.shard_map(
        shards,
        mesh=mesh,
        in_specs=placed,
        out_specs=(
            P(("dp", "expert"), None),
            P(("dp", "expert"), None),
            P("dp", "expert", None, None),
            P("expert", "dp", None),
        ),
        check_vma=False,
    )
```

```python
import functools

import jax
import jax.numpy as jnp
from jax import lax
from jax.experimental import pallas as pl
from jax.experimental.pallas import tpu as pltpu
from jax.sharding import PartitionSpec as P

QB = 128
CAP = 16
VMEM_LIMIT = 24 * 1024 * 1024

bf16 = jnp.bfloat16
f32 = jnp.float32

SMALL = pl.CostEstimate(flops=1024, bytes_accessed=1024, transcendentals=0)

VMEM = pl.BlockSpec(memory_space=pltpu.VMEM)
ANY = pl.BlockSpec(memory_space=pl.ANY)
HBM = pl.BlockSpec(memory_space=pltpu.HBM)


def params():
    return pltpu.CompilerParams(vmem_limit_bytes=VMEM_LIMIT)


def hbm(value):
    return pltpu.with_memory_space_constraint(value, pltpu.HBM)


def chunks(total, size):
    return [pl.ds(start, size) for start in range(0, total, size)]


def block_place(me, r, flight):
    half = flight // 2
    return me ^ (2 * (r % half) + r // half)


def dispatch_kernel(flight, groups, gate_up_hbm, cap_hbm, hot_hbm, ids_hbm, probs_hbm, dout_hbm, *refs):
    half = flight // 2
    own_hbm, hidden_ref, *chips = refs[: 2 + half]
    gate_up, cap_ref, hot_ref, ids_ref, probs_ref, dout, own_ref = refs[2 + half : 9 + half]
    gate_sems, own_sem, small_sems, in_sems = refs[9 + half :]
    topk, tokens = ids_ref.shape
    slots = flight * CAP
    me, group = lax.axis_index("expert"), lax.axis_index("dp")
    share = dout_hbm.shape[1] // groups
    small = [
        pltpu.make_async_copy(src, dst, small_sems.at[i])
        for i, (src, dst) in enumerate(
            [(ids_hbm, ids_ref), (probs_hbm, probs_ref), (cap_hbm, cap_ref), (hot_hbm, hot_ref)]
        )
    ]
    loads = [
        pltpu.make_async_copy(
            dout_hbm.at[:, pl.ds(pl.multiple_of((group ^ j) * share, share), share)],
            dout.at[j],
            in_sems.at[j],
        )
        for j in range(groups)
    ]
    gates = [
        pltpu.make_async_copy(
            gate_up_hbm.at[pl.ds(pl.multiple_of(block_place(me, r, flight) * CAP, CAP), CAP)],
            gate_up.at[pl.ds(r * CAP, CAP)],
            gate_sems.at[r],
        )
        for r in range(flight)
    ]
    for copy in small + loads + gates:
        copy.start()
    for copy in small:
        copy.wait()
    row = lax.broadcasted_iota(jnp.int32, (slots, 1), 0)
    row_expert = block_place(me, row // CAP, flight)
    row_rank = (row % CAP).astype(f32)
    limit = jnp.zeros((slots, 1), jnp.int32)
    for e in range(flight):
        hot = hot_ref[0, 0] == e
        for h in range(1, hot_ref.shape[1]):
            hot = jnp.logical_or(hot, hot_ref[0, h] == e)
        limit = jnp.where(row_expert == e, jnp.where(hot, CAP, cap_ref[e]), limit)
    limit = limit.astype(f32)
    named = jnp.zeros((slots, tokens), f32)
    weight = jnp.zeros((slots, tokens), f32)
    for k in range(topk):
        hit = ids_ref[k : k + 1, :] == row_expert
        named = jnp.where(hit, 1.0, named)
        weight = jnp.where(hit, probs_ref[k : k + 1, :], weight)
    first = lax.broadcasted_iota(jnp.int32, (tokens, tokens), 0)
    second = lax.broadcasted_iota(jnp.int32, (tokens, tokens), 1)
    before = (first < second).astype(f32).astype(bf16)
    rank = jnp.dot(named.astype(bf16), before, preferred_element_type=f32)
    owns = (named > 0.0) & (rank == row_rank) & (rank < limit)
    own_weight = jnp.where(owns, weight, 0.0)
    own_ref[...] = own_weight
    own_copy = pltpu.make_async_copy(own_ref, own_hbm, own_sem)
    own_copy.start()
    owner = jnp.where(owns, 1.0, 0.0).astype(bf16)
    slot_weight = jnp.sum(own_weight, axis=1, keepdims=True)
    for copy in loads:
        copy.wait()
    for j in range(groups):
        part = jnp.dot(owner, dout[j], preferred_element_type=f32)
        part = (part * slot_weight).astype(bf16)
        for r in range(flight):
            chips[r % half][r // half, j] = part[r * CAP : (r + 1) * CAP, :]
    for copy in gates:
        copy.wait()
    hid = hidden_ref.shape[1]
    gate = gate_up[:, :hid].astype(f32)
    up = gate_up[:, hid:].astype(f32)
    hidden_ref[...] = (gate * jax.nn.sigmoid(gate) * up).astype(bf16)
    own_copy.wait()


def dispatch(gate_up, capacity, hot_row, ids, probs, d_out, flight, groups):
    tokens, width = d_out.shape
    rows, double = gate_up.shape
    slots = flight * CAP
    share = width // groups
    half = flight // 2
    return pl.pallas_call(
        functools.partial(dispatch_kernel, flight, groups),
        out_shape=(pltpu.HBM((slots, tokens), f32), pltpu.VMEM((rows, double // 2), bf16))
        + (pltpu.VMEM((2, groups, CAP, share), bf16),) * half,
        in_specs=[HBM] * 6,
        out_specs=(HBM, VMEM) + (VMEM,) * half,
        scratch_shapes=[
            pltpu.VMEM((rows, double), bf16),
            pltpu.SMEM(capacity.shape, jnp.int32),
            pltpu.SMEM(hot_row.shape, jnp.int32),
            pltpu.VMEM(ids.shape, jnp.int32),
            pltpu.VMEM(probs.shape, f32),
            pltpu.VMEM((groups, tokens, share), bf16),
            pltpu.VMEM((slots, tokens), f32),
            pltpu.SemaphoreType.DMA((flight,)),
            pltpu.SemaphoreType.DMA,
            pltpu.SemaphoreType.DMA((4,)),
            pltpu.SemaphoreType.DMA((groups,)),
        ],
        compiler_params=params(),
        cost_estimate=SMALL,
        name="dispatch",
    )(hbm(gate_up), hbm(capacity), hbm(hot_row), hbm(ids), hbm(probs), hbm(d_out))


def forward_kernel(
    flight, block, hidden_ref, scale_hbm, quant_hbm, out_hbm,
    scale, hidden, quant, out, scale_sem, in_sems, out_sems
):
    steps, hid, _ = quant.shape
    me = lax.axis_index("expert")
    loads = [
        pltpu.make_async_copy(quant_hbm.at[:, pl.ds(c * block, block)], quant.at[c], in_sems.at[c])
        for c in range(steps)
    ]
    small = pltpu.make_async_copy(scale_hbm, scale, scale_sem)
    for copy in [small] + loads:
        copy.start()
    for r in range(flight):
        place = pl.multiple_of(block_place(me, r, flight) * CAP, CAP)
        hidden[pl.ds(place, CAP), :] = hidden_ref[pl.ds(r * CAP, CAP), :]
    small.wait()
    stores = []
    for c in range(steps):
        cols = pl.ds(c * block, block)
        loads[c].wait()
        total = [None] * (block // QB)
        for i in range(hid // QB):
            part = jnp.dot(
                hidden[:, i * QB : (i + 1) * QB],
                quant[c, i * QB : (i + 1) * QB, :],
                preferred_element_type=f32,
            )
            for j in range(block // QB):
                scaled = part[:, j * QB : (j + 1) * QB] * scale[i, 0, c * (block // QB) + j]
                total[j] = scaled if i == 0 else total[j] + scaled
        for j in range(block // QB):
            at = pl.ds(c * block + j * QB, QB)
            out[:, :, at] = total[j].astype(bf16).reshape(flight, CAP, QB)
        stores.append(
            pltpu.make_async_copy(out.at[:, :, cols], out_hbm.at[:, :, cols], out_sems.at[c])
        )
        stores[c].start()
    for copy in stores:
        copy.wait()


def forward(scale, hidden, quant, flight, block=512):
    hid, width = quant.shape
    steps = width // block
    return pl.pallas_call(
        functools.partial(forward_kernel, flight, block),
        out_shape=pltpu.HBM((flight, CAP, width), bf16),
        in_specs=[VMEM, HBM, HBM],
        out_specs=HBM,
        scratch_shapes=[
            pltpu.SMEM(scale.shape, f32),
            pltpu.VMEM(hidden.shape, bf16),
            pltpu.VMEM((steps, hid, block), bf16),
            pltpu.VMEM((flight, CAP, width), bf16),
            pltpu.SemaphoreType.DMA,
            pltpu.SemaphoreType.DMA((steps,)),
            pltpu.SemaphoreType.DMA((steps,)),
        ],
        compiler_params=params(),
        cost_estimate=SMALL,
        name="expert_forward",
    )(hidden, hbm(scale), hbm(quant))


def sibling_kernel(half, *refs):
    chips, out_ref = refs[:half], refs[-1]
    for c in range(half):
        out_ref[c] = chips[c][1]


def sibling_rows(chips, ties):
    half = len(chips)
    return pl.pallas_call(
        functools.partial(sibling_kernel, half),
        out_shape=pltpu.VMEM((half,) + chips[0].shape[1:], bf16),
        in_specs=[VMEM] * half + [ANY] * len(ties),
        out_specs=VMEM,
        compiler_params=params(),
        cost_estimate=SMALL,
        name="sibling_rows",
    )(*chips, *ties)


def split_kernel(half, groups, *refs):
    chips, swapped, pieces = refs[:half], refs[half], refs[half + 1 :]
    for j in range(1, groups):
        for c in range(half):
            pieces[j - 1][c] = chips[c][0, j]
            pieces[j - 1][half + c] = swapped[c, j]


def split(chips, swapped):
    half, groups, cap, share = swapped.shape
    return pl.pallas_call(
        functools.partial(split_kernel, half, groups),
        out_shape=(pltpu.VMEM((2 * half, cap, share), bf16),) * (groups - 1),
        in_specs=[VMEM] * (half + 1),
        out_specs=(VMEM,) * (groups - 1),
        compiler_params=params(),
        cost_estimate=SMALL,
        name="split",
    )(*chips, swapped)


def backward_kernel(flight, groups, scale_hbm, gate_up_hbm, quant_hbm, tie_ref, swapped, *refs):
    half = flight // 2
    chips, out_hbm = refs[:half], refs[half]
    scale, gate_up, rows, quant, acc, out = refs[half + 1 : half + 7]
    scale_sem, gate_sems, in_sems, out_sems = refs[half + 7 :]
    me, group = lax.axis_index("expert"), lax.axis_index("dp")
    slots, hid = acc.shape
    share = quant.shape[2]

    def place(r):
        return pl.ds(pl.multiple_of(block_place(me, r, flight) * CAP, CAP), CAP)

    loads = [
        pltpu.make_async_copy(
            quant_hbm.at[:, pl.ds(pl.multiple_of((group ^ j) * share, share), share)],
            quant.at[j],
            in_sems.at[j],
        )
        for j in range(groups)
    ]
    gates = [
        pltpu.make_async_copy(
            gate_up_hbm.at[place(r)], gate_up.at[pl.ds(r * CAP, CAP)], gate_sems.at[r]
        )
        for r in range(flight)
    ]
    small = pltpu.make_async_copy(scale_hbm, scale, scale_sem)
    for copy in [small] + loads + gates:
        copy.start()
    for c in range(half):
        rows[:, c * CAP : (c + 1) * CAP, :] = chips[c][0]
        rows[:, (half + c) * CAP : (half + c + 1) * CAP, :] = swapped[c]
    small.wait()
    for j in range(groups):
        loads[j].wait()
        for b in range(share // QB):
            cols = slice(b * QB, (b + 1) * QB)
            part = lax.dot_general(
                rows[j, :, cols],
                quant[j, :, cols],
                (((1,), (1,)), ((), ())),
                preferred_element_type=f32,
            )
            for i in range(hid // QB):
                at = (slice(None), slice(i * QB, (i + 1) * QB))
                scaled = part[at] * scale[i, 0, (group ^ j) * (share // QB) + b]
                if j == 0 and b == 0:
                    acc[at] = scaled
                else:
                    acc[at] += scaled
    for copy in gates:
        copy.wait()
    gate = gate_up[:, :hid].astype(f32)
    up = gate_up[:, hid:].astype(f32)
    sig = jax.nn.sigmoid(gate)
    d_hidden = acc[...]
    out[:, :hid] = (d_hidden * up * sig * (1.0 + gate * (1.0 - sig))).astype(bf16)
    out[:, hid:] = (d_hidden * (gate * sig)).astype(bf16)
    stores = [
        pltpu.make_async_copy(out.at[pl.ds(r * CAP, CAP)], out_hbm.at[place(r)], out_sems.at[r])
        for r in range(flight)
    ]
    for copy in stores:
        copy.start()
    for copy in stores:
        copy.wait()


def backward(scale, gate_up, quant, tie, chips, swapped):
    slots, double = gate_up.shape
    hid, width = quant.shape
    half, groups, cap, share = swapped.shape
    flight = 2 * half
    return pl.pallas_call(
        functools.partial(backward_kernel, flight, groups),
        out_shape=pltpu.HBM((slots, double), bf16),
        in_specs=[HBM, HBM, HBM, ANY] + [VMEM] * (1 + half),
        out_specs=HBM,
        scratch_shapes=[
            pltpu.SMEM(scale.shape, f32),
            pltpu.VMEM((slots, double), bf16),
            pltpu.VMEM((groups, slots, share), bf16),
            pltpu.VMEM((groups, hid, share), bf16),
            pltpu.VMEM((slots, hid), f32),
            pltpu.VMEM((slots, double), bf16),
            pltpu.SemaphoreType.DMA,
            pltpu.SemaphoreType.DMA((flight,)),
            pltpu.SemaphoreType.DMA((groups,)),
            pltpu.SemaphoreType.DMA((flight,)),
        ],
        compiler_params=params(),
        cost_estimate=SMALL,
        name="expert_backward",
    )(hbm(scale), hbm(gate_up), hbm(quant), tie, swapped, *chips)


def combine_kernel(
    block, ids_hbm, own_hbm, dout_hbm, ret_ref, out_ref, dprobs_ref, ids_ref, own_ref, dout, sems
):
    copies = [
        pltpu.make_async_copy(ids_hbm, ids_ref, sems.at[0]),
        pltpu.make_async_copy(own_hbm, own_ref, sems.at[1]),
        pltpu.make_async_copy(dout_hbm, dout, sems.at[2]),
    ]
    for copy in copies:
        copy.start()
    topk, tokens = ids_ref.shape
    slots = own_ref.shape[0]
    width = dout.shape[1]
    flight = slots // CAP
    me = lax.axis_index("expert")
    copies[1].wait()
    own = own_ref[...]
    turned = own.T
    high = turned.astype(bf16)
    low = (turned - high.astype(f32)).astype(bf16)
    total = jnp.zeros((slots, tokens), f32)
    copies[0].wait()
    copies[2].wait()
    for cols in chunks(width, block):
        here = jnp.concatenate(
            [ret_ref[block_place(me, r, flight), :, cols] for r in range(flight)], axis=0
        )
        out = jnp.dot(high, here, preferred_element_type=f32)
        out = out + jnp.dot(low, here, preferred_element_type=f32)
        out_ref[:, cols] = out.astype(bf16)
        total = total + lax.dot_general(
            here, dout[:, cols], (((1,), (1,)), ((), ())), preferred_element_type=f32
        )
    inner = jnp.where(own > 0.0, total, 0.0)
    row_expert = block_place(me, lax.broadcasted_iota(jnp.int32, (slots, 1), 0) // CAP, flight)
    for k in range(topk):
        mine = jnp.where(ids_ref[k : k + 1, :] == row_expert, inner, 0.0)
        dprobs_ref[k : k + 1, :] = jnp.sum(mine, axis=0, keepdims=True)


def combine(ids, own, d_out, returned, block=1024):
    tokens, width = d_out.shape
    return pl.pallas_call(
        functools.partial(combine_kernel, block),
        out_shape=(
            pltpu.HBM((tokens, width), bf16),
            pltpu.HBM(ids.shape, f32),
        ),
        in_specs=[HBM, HBM, HBM, VMEM],
        out_specs=(VMEM, VMEM),
        scratch_shapes=[
            pltpu.VMEM(ids.shape, jnp.int32),
            pltpu.VMEM(own.shape, f32),
            pltpu.VMEM((tokens, width), bf16),
            pltpu.SemaphoreType.DMA((3,)),
        ],
        compiler_params=params(),
        cost_estimate=SMALL,
        name="combine",
    )(hbm(ids), hbm(own), hbm(d_out), returned)


def weight_grad_kernel(half, groups, block, tie_ref, swapped, *refs):
    chips, parts = refs[:half], refs[half : half + groups - 1]
    hid_refs = refs[half + groups - 1 : half + 2 * groups - 1]
    out_hbm, hidden, out, out_sems = refs[half + 2 * groups - 1 :]
    cap, share = parts[0].shape[1:]
    slots = 2 * half * cap
    for j in range(groups):
        hidden[j * slots : (j + 1) * slots, :] = hid_refs[j][...]
    stores = []
    for n, cols in enumerate(chunks(share, block)):
        grads = [chips[c][0, 0, :, cols] for c in range(half)]
        grads += [swapped[c, 0, :, cols] for c in range(half)]
        grads += [part[:, :, cols].reshape(slots, block) for part in parts]
        out[cols, :] = lax.dot_general(
            jnp.concatenate(grads, axis=0),
            hidden[...],
            (((0,), (0,)), ((), ())),
            preferred_element_type=f32,
        ).astype(bf16)
        stores.append(pltpu.make_async_copy(out.at[cols], out_hbm.at[cols], out_sems.at[n]))
        stores[n].start()
    for copy in stores:
        copy.wait()


def weight_grad(tie, chips, swapped, parts, hiddens, block=256):
    half, groups, cap, share = swapped.shape
    slots, hid = hiddens[0].shape
    return pl.pallas_call(
        functools.partial(weight_grad_kernel, half, groups, block),
        out_shape=pltpu.HBM((share, hid), bf16),
        in_specs=[HBM] + [VMEM] * (half + 2 * groups),
        out_specs=HBM,
        scratch_shapes=[
            pltpu.VMEM((groups * slots, hid), bf16),
            pltpu.VMEM((share, hid), bf16),
            pltpu.SemaphoreType.DMA((share // block,)),
        ],
        compiler_params=params(),
        cost_estimate=SMALL,
        name="weight_grad",
    )(hbm(tie), swapped, *chips, *parts, *hiddens)


def swap(value, axis, j):
    size = lax.axis_size(axis)
    return lax.ppermute(value, axis, [(i, i ^ j) for i in range(size)])


def shards(route_ids, route_probs, capacity, hot_lists, gate_up, w_quant, w_scale, d_out):
    flight = lax.axis_size("expert")
    groups = lax.axis_size("dp")
    gate_up = gate_up[0, 0]
    ids, probs = route_ids.T, route_probs.T
    scale = w_scale.transpose(1, 0, 2)
    own, hidden, *chips = dispatch(
        gate_up, capacity, hot_lists, ids, probs, d_out, flight, groups
    )
    chips = chips[:1] + [swap(chips[c], "expert", 2 * c) for c in range(1, flight // 2)]
    hiddens, late = {0: hidden}, set()
    bit = groups // 2
    while bit:
        for j in sorted(hiddens):
            hiddens[j ^ bit] = swap(hiddens[j], "dp", bit)
            if j:
                late.add(j ^ bit)
        bit //= 2
    early = [hiddens[j] for j in range(1, groups) if j not in late]
    hiddens = [hiddens[j] for j in range(groups)]
    expert_out = forward(scale, hidden, w_quant[0], flight)
    returned = lax.all_to_all(expert_out, "expert", split_axis=0, concat_axis=0, tiled=True)
    swapped = swap(sibling_rows(chips, [hbm(expert_out)] + early), "expert", 1)
    pieces = split(chips, swapped)
    parts = [swap(pieces[j - 1], "dp", j) for j in range(1, groups)]
    d_gate_up = backward(scale, gate_up, w_quant[0], pieces[0], chips, swapped)
    combined, d_probs = combine(ids, own, d_out, returned)
    d_weight = weight_grad(d_probs, chips, swapped, parts, hiddens)
    return (combined, d_probs.T, d_gate_up[None, None], d_weight[None])


def solution(mesh):
    placed = (
        P(("dp", "expert"), None),
        P(("dp", "expert"), None),
        P(),
        P("dp", None),
        P("dp", "expert", None, None),
        P("expert", None, None),
        P("expert", None, None),
        P(("dp", "expert"), None),
    )
    return jax.shard_map(
        shards,
        mesh=mesh,
        in_specs=placed,
        out_specs=(
            P(("dp", "expert"), None),
            P(("dp", "expert"), None),
            P("dp", "expert", None, None),
            P("expert", "dp", None),
        ),
        check_vma=False,
    )
```

```python
import functools

import jax
import jax.numpy as jnp
from jax import lax
from jax.experimental import pallas as pl
from jax.experimental.pallas import tpu as pltpu
from jax.sharding import PartitionSpec as P

QB = 128
CAP = 16
TILE = 256

bf16 = jnp.bfloat16
f32 = jnp.float32

SMALL = pl.CostEstimate(flops=1024, bytes_accessed=1024, transcendentals=0)

VMEM = pl.BlockSpec(memory_space=pltpu.VMEM)
ANY = pl.BlockSpec(memory_space=pl.ANY)
HBM = pl.BlockSpec(memory_space=pltpu.HBM)


def params(slots):
    return pltpu.CompilerParams(vmem_limit_bytes=(12 + slots // 32) * 1024 * 1024)


def hbm(value):
    return pltpu.with_memory_space_constraint(value, pltpu.HBM)


def chunks(total, size):
    return [pl.ds(start, size) for start in range(0, total, size)]


def bits_of(groups):
    bits = []
    while groups > 1:
        groups //= 2
        bits.append(groups)
    return bits


def block_place(me, r, flight):
    half = flight // 2
    return me ^ (2 * (r % half) + r // half)


def dispatch_kernel(flight, groups, gate_up_hbm, cap_hbm, hot_hbm, ids_hbm, probs_hbm, dout_hbm, *refs):
    half = flight // 2
    bits = bits_of(groups)
    outs = 2 + half + len(bits)
    own_hbm, hidden_ref, *chips = refs[: 2 + half]
    messages = dict(zip(bits, refs[2 + half : outs]))
    gate_up, cap_ref, hot_ref, ids_ref, probs_ref, dout, own_ref = refs[outs : outs + 7]
    gate_sems, own_sem, small_sems, in_sems = refs[outs + 7 :]
    topk, tokens = ids_ref.shape
    slots = flight * CAP
    me, group = lax.axis_index("expert"), lax.axis_index("dp")
    share = dout_hbm.shape[1] // groups
    hid = hidden_ref.shape[1]
    small = [
        pltpu.make_async_copy(src, dst, small_sems.at[i])
        for i, (src, dst) in enumerate(
            [(ids_hbm, ids_ref), (probs_hbm, probs_ref), (cap_hbm, cap_ref), (hot_hbm, hot_ref)]
        )
    ]
    loads = [
        pltpu.make_async_copy(
            dout_hbm.at[:, pl.ds(pl.multiple_of((group ^ j) * share, share), share)],
            dout.at[j],
            in_sems.at[j],
        )
        for j in range(groups)
    ]
    gates = [
        pltpu.make_async_copy(
            gate_up_hbm.at[pl.ds(pl.multiple_of(block_place(me, r, flight) * CAP, CAP), CAP)],
            gate_up.at[pl.ds(r * CAP, CAP)],
            gate_sems.at[r],
        )
        for r in range(flight)
    ]
    for copy in small + loads + gates:
        copy.start()
    for copy in small:
        copy.wait()
    row = lax.broadcasted_iota(jnp.int32, (slots, 1), 0)
    row_expert = block_place(me, row // CAP, flight)
    row_rank = (row % CAP).astype(f32)
    limit = jnp.zeros((slots, 1), jnp.int32)
    for e in range(flight):
        hot = hot_ref[0, 0] == e
        for h in range(1, hot_ref.shape[1]):
            hot = jnp.logical_or(hot, hot_ref[0, h] == e)
        limit = jnp.where(row_expert == e, jnp.where(hot, CAP, cap_ref[e]), limit)
    limit = limit.astype(f32)
    named = jnp.zeros((slots, tokens), f32)
    weight = jnp.zeros((slots, tokens), f32)
    for k in range(topk):
        hit = ids_ref[k : k + 1, :] == row_expert
        named = jnp.where(hit, 1.0, named)
        weight = jnp.where(hit, probs_ref[k : k + 1, :], weight)
    earlier = lax.broadcasted_iota(jnp.int32, (tokens, tokens), 0)
    later = lax.broadcasted_iota(jnp.int32, (tokens, tokens), 1)
    before = (earlier < later).astype(f32).astype(bf16)
    rank = jnp.dot(named.astype(bf16), before, preferred_element_type=f32)
    owns = (named > 0.0) & (rank == row_rank) & (rank < limit)
    own_weight = jnp.where(owns, weight, 0.0)
    own_ref[...] = own_weight
    own_copy = pltpu.make_async_copy(own_ref, own_hbm, own_sem)
    own_copy.start()
    owner = jnp.where(owns, 1.0, 0.0).astype(bf16)
    slot_weight = jnp.sum(own_weight, axis=1, keepdims=True)
    for copy in loads:
        copy.wait()
    for j in range(groups):
        part = jnp.dot(owner, dout[j], preferred_element_type=f32)
        part = (part * slot_weight).astype(bf16)
        for r in range(flight):
            chips[r % half][r // half, j] = part[r * CAP : (r + 1) * CAP, :]
        for bit in bits:
            if bit <= j < 2 * bit:
                first = flight * (hid // TILE) + (j - bit) * (share // TILE)
                for q in range(share // TILE):
                    messages[bit][first + q] = part[:CAP, q * TILE : (q + 1) * TILE]
    for copy in gates:
        copy.wait()
    for r in range(flight):
        at = slice(r * CAP, (r + 1) * CAP)
        gate = gate_up[at, :hid].astype(f32)
        up = gate_up[at, hid:].astype(f32)
        block = (gate * jax.nn.sigmoid(gate) * up).astype(bf16)
        hidden_ref[at, :] = block
        for bit in bits:
            for q in range(hid // TILE):
                messages[bit][r * (hid // TILE) + q] = block[:, q * TILE : (q + 1) * TILE]
    own_copy.wait()


def dispatch(gate_up, capacity, hot_row, ids, probs, d_out, flight, groups):
    tokens, width = d_out.shape
    rows, double = gate_up.shape
    slots = flight * CAP
    share = width // groups
    half = flight // 2
    return pl.pallas_call(
        functools.partial(dispatch_kernel, flight, groups),
        out_shape=(pltpu.HBM((slots, tokens), f32), pltpu.VMEM((rows, double // 2), bf16))
        + (pltpu.VMEM((2, groups, CAP, share), bf16),) * half
        + tuple(
            pltpu.VMEM((flight * (double // 2 // TILE) + bit * (share // TILE), CAP, TILE), bf16)
            for bit in bits_of(groups)
        ),
        in_specs=[HBM] * 6,
        out_specs=(HBM, VMEM) + (VMEM,) * (half + len(bits_of(groups))),
        scratch_shapes=[
            pltpu.VMEM((rows, double), bf16),
            pltpu.SMEM(capacity.shape, jnp.int32),
            pltpu.SMEM(hot_row.shape, jnp.int32),
            pltpu.VMEM(ids.shape, jnp.int32),
            pltpu.VMEM(probs.shape, f32),
            pltpu.VMEM((groups, tokens, share), bf16),
            pltpu.VMEM((slots, tokens), f32),
            pltpu.SemaphoreType.DMA((flight,)),
            pltpu.SemaphoreType.DMA,
            pltpu.SemaphoreType.DMA((4,)),
            pltpu.SemaphoreType.DMA((groups,)),
        ],
        compiler_params=params(slots),
        cost_estimate=SMALL,
        name="dispatch",
    )(hbm(gate_up), hbm(capacity), hbm(hot_row), hbm(ids), hbm(probs), hbm(d_out))


def forward_kernel(
    flight, block, hidden_ref, scale_hbm, quant_hbm, out_hbm,
    scale, hidden, quant, out, scale_sem, in_sems, out_sems
):
    steps, hid, _ = quant.shape
    me = lax.axis_index("expert")
    loads = [
        pltpu.make_async_copy(quant_hbm.at[:, pl.ds(c * block, block)], quant.at[c], in_sems.at[c])
        for c in range(steps)
    ]
    small = pltpu.make_async_copy(scale_hbm, scale, scale_sem)
    for copy in [small] + loads:
        copy.start()
    for r in range(flight):
        place = pl.multiple_of(block_place(me, r, flight) * CAP, CAP)
        hidden[pl.ds(place, CAP), :] = hidden_ref[pl.ds(r * CAP, CAP), :]
    small.wait()
    stores = []
    for c in range(steps):
        cols = pl.ds(c * block, block)
        loads[c].wait()
        total = [None] * (block // QB)
        for i in range(hid // QB):
            part = jnp.dot(
                hidden[:, i * QB : (i + 1) * QB],
                quant[c, i * QB : (i + 1) * QB, :],
                preferred_element_type=f32,
            )
            for j in range(block // QB):
                scaled = part[:, j * QB : (j + 1) * QB] * scale[i, 0, c * (block // QB) + j]
                total[j] = scaled if i == 0 else total[j] + scaled
        for j in range(block // QB):
            at = pl.ds(c * block + j * QB, QB)
            out[:, :, at] = total[j].astype(bf16).reshape(flight, CAP, QB)
        stores.append(
            pltpu.make_async_copy(out.at[:, :, cols], out_hbm.at[:, :, cols], out_sems.at[c])
        )
        stores[c].start()
    for copy in stores:
        copy.wait()


def forward(scale, hidden, quant, flight, block=512):
    hid, width = quant.shape
    steps = width // block
    return pl.pallas_call(
        functools.partial(forward_kernel, flight, block),
        out_shape=pltpu.HBM((flight, CAP, width), bf16),
        in_specs=[VMEM, HBM, HBM],
        out_specs=HBM,
        scratch_shapes=[
            pltpu.SMEM(scale.shape, f32),
            pltpu.VMEM(hidden.shape, bf16),
            pltpu.VMEM((steps, hid, block), bf16),
            pltpu.VMEM((flight, CAP, width), bf16),
            pltpu.SemaphoreType.DMA,
            pltpu.SemaphoreType.DMA((steps,)),
            pltpu.SemaphoreType.DMA((steps,)),
        ],
        compiler_params=params(flight * CAP),
        cost_estimate=SMALL,
        name="expert_forward",
    )(hidden, hbm(scale), hbm(quant))


def sibling_kernel(half, *refs):
    chips, out_ref = refs[:half], refs[-1]
    for c in range(half):
        out_ref[c] = chips[c][1]


def sibling_rows(chips, ties):
    half = len(chips)
    return pl.pallas_call(
        functools.partial(sibling_kernel, half),
        out_shape=pltpu.VMEM((half,) + chips[0].shape[1:], bf16),
        in_specs=[VMEM] * half + [ANY] * len(ties),
        out_specs=VMEM,
        compiler_params=params(2 * half * CAP),
        cost_estimate=SMALL,
        name="sibling_rows",
    )(*chips, *ties)


def split_kernel(half, groups, *refs):
    chips, swapped, pieces = refs[: half - 1], refs[half - 1], refs[1 - groups :]
    for j in range(1, groups):
        for c in range(half):
            if c:
                pieces[j - 1][c - 1] = chips[c - 1][0, j]
            pieces[j - 1][half - 1 + c] = swapped[c, j]


def split(chips, swapped):
    half, groups, cap, share = swapped.shape
    return pl.pallas_call(
        functools.partial(split_kernel, half, groups),
        out_shape=(pltpu.VMEM((2 * half - 1, cap, share), bf16),) * (groups - 1),
        in_specs=[VMEM] * half,
        out_specs=(VMEM,) * (groups - 1),
        compiler_params=params(2 * half * CAP),
        cost_estimate=SMALL,
        name="split",
    )(*chips[1:], swapped)


def backward_kernel(flight, groups, scale_hbm, gate_up_hbm, quant_hbm, tie_ref, swapped, *refs):
    half = flight // 2
    chips, out_hbm = refs[:half], refs[half]
    scale, gate_up, rows, quant, acc, out = refs[half + 1 : half + 7]
    scale_sem, gate_sems, in_sems, out_sems = refs[half + 7 :]
    me, group = lax.axis_index("expert"), lax.axis_index("dp")
    slots, hid = acc.shape
    share = quant.shape[2]

    def place(r):
        return pl.ds(pl.multiple_of(block_place(me, r, flight) * CAP, CAP), CAP)

    loads = [
        pltpu.make_async_copy(
            quant_hbm.at[:, pl.ds(pl.multiple_of((group ^ j) * share, share), share)],
            quant.at[j],
            in_sems.at[j],
        )
        for j in range(groups)
    ]
    gates = [
        pltpu.make_async_copy(
            gate_up_hbm.at[place(r)], gate_up.at[pl.ds(r * CAP, CAP)], gate_sems.at[r]
        )
        for r in range(flight)
    ]
    small = pltpu.make_async_copy(scale_hbm, scale, scale_sem)
    for copy in [small] + loads + gates:
        copy.start()
    for c in range(half):
        rows[:, c * CAP : (c + 1) * CAP, :] = chips[c][0]
        rows[:, (half + c) * CAP : (half + c + 1) * CAP, :] = swapped[c]
    small.wait()
    for j in range(groups):
        loads[j].wait()
        for b in range(share // QB):
            cols = slice(b * QB, (b + 1) * QB)
            part = lax.dot_general(
                rows[j, :, cols],
                quant[j, :, cols],
                (((1,), (1,)), ((), ())),
                preferred_element_type=f32,
            )
            for i in range(hid // QB):
                at = (slice(None), slice(i * QB, (i + 1) * QB))
                scaled = part[at] * scale[i, 0, (group ^ j) * (share // QB) + b]
                if j == 0 and b == 0:
                    acc[at] = scaled
                else:
                    acc[at] += scaled
    for copy in gates:
        copy.wait()
    gate = gate_up[:, :hid].astype(f32)
    up = gate_up[:, hid:].astype(f32)
    sig = jax.nn.sigmoid(gate)
    d_hidden = acc[...]
    out[:, :hid] = (d_hidden * up * sig * (1.0 + gate * (1.0 - sig))).astype(bf16)
    out[:, hid:] = (d_hidden * (gate * sig)).astype(bf16)
    stores = [
        pltpu.make_async_copy(out.at[pl.ds(r * CAP, CAP)], out_hbm.at[place(r)], out_sems.at[r])
        for r in range(flight)
    ]
    for copy in stores:
        copy.start()
    for copy in stores:
        copy.wait()


def backward(scale, gate_up, quant, tie, chips, swapped):
    slots, double = gate_up.shape
    hid, width = quant.shape
    half, groups, cap, share = swapped.shape
    flight = 2 * half
    return pl.pallas_call(
        functools.partial(backward_kernel, flight, groups),
        out_shape=pltpu.HBM((slots, double), bf16),
        in_specs=[HBM, HBM, HBM, ANY] + [VMEM] * (1 + half),
        out_specs=HBM,
        scratch_shapes=[
            pltpu.SMEM(scale.shape, f32),
            pltpu.VMEM((slots, double), bf16),
            pltpu.VMEM((groups, slots, share), bf16),
            pltpu.VMEM((groups, hid, share), bf16),
            pltpu.VMEM((slots, hid), f32),
            pltpu.VMEM((slots, double), bf16),
            pltpu.SemaphoreType.DMA,
            pltpu.SemaphoreType.DMA((flight,)),
            pltpu.SemaphoreType.DMA((groups,)),
            pltpu.SemaphoreType.DMA((flight,)),
        ],
        compiler_params=params(slots),
        cost_estimate=SMALL,
        name="expert_backward",
    )(hbm(scale), hbm(gate_up), hbm(quant), tie, swapped, *chips)


def combine_kernel(
    block, ids_hbm, own_hbm, dout_hbm, ret_ref, out_ref, dprobs_ref, ids_ref, own_ref, dout, sems
):
    copies = [
        pltpu.make_async_copy(ids_hbm, ids_ref, sems.at[0]),
        pltpu.make_async_copy(own_hbm, own_ref, sems.at[1]),
        pltpu.make_async_copy(dout_hbm, dout, sems.at[2]),
    ]
    for copy in copies:
        copy.start()
    topk, tokens = ids_ref.shape
    slots = own_ref.shape[0]
    width = dout.shape[1]
    flight = slots // CAP
    me = lax.axis_index("expert")
    copies[1].wait()
    own = own_ref[...]
    turned = own.T
    high = turned.astype(bf16)
    low = (turned - high.astype(f32)).astype(bf16)
    total = jnp.zeros((slots, tokens), f32)
    copies[0].wait()
    copies[2].wait()
    for cols in chunks(width, block):
        here = jnp.concatenate(
            [ret_ref[block_place(me, r, flight), :, cols] for r in range(flight)], axis=0
        )
        out = jnp.dot(high, here, preferred_element_type=f32)
        out = out + jnp.dot(low, here, preferred_element_type=f32)
        out_ref[:, cols] = out.astype(bf16)
        total = total + lax.dot_general(
            here, dout[:, cols], (((1,), (1,)), ((), ())), preferred_element_type=f32
        )
    inner = jnp.where(own > 0.0, total, 0.0)
    row_expert = block_place(me, lax.broadcasted_iota(jnp.int32, (slots, 1), 0) // CAP, flight)
    for k in range(topk):
        mine = jnp.where(ids_ref[k : k + 1, :] == row_expert, inner, 0.0)
        dprobs_ref[k : k + 1, :] = jnp.sum(mine, axis=0, keepdims=True)


def combine(ids, own, d_out, returned, block=1024):
    tokens, width = d_out.shape
    return pl.pallas_call(
        functools.partial(combine_kernel, block),
        out_shape=(
            pltpu.HBM((tokens, width), bf16),
            pltpu.HBM(ids.shape, f32),
        ),
        in_specs=[HBM, HBM, HBM, VMEM],
        out_specs=(VMEM, VMEM),
        scratch_shapes=[
            pltpu.VMEM(ids.shape, jnp.int32),
            pltpu.VMEM(own.shape, f32),
            pltpu.VMEM((tokens, width), bf16),
            pltpu.SemaphoreType.DMA((3,)),
        ],
        compiler_params=params(own.shape[0]),
        cost_estimate=SMALL,
        name="combine",
    )(hbm(ids), hbm(own), hbm(d_out), returned)


def weight_grad_kernel(half, groups, block, tie_ref, swapped, hidden_ref, *refs):
    chips, parts = refs[:half], refs[half : half + groups - 1]
    messages = refs[half + groups - 1 : half + 2 * groups - 2]
    out_hbm, hidden, own, out, out_sems = refs[half + 2 * groups - 2 :]
    cap, share = parts[0].shape[1:]
    flight = 2 * half
    slots = flight * cap
    wide = hidden_ref.shape[1] // TILE
    hidden[:slots, :] = hidden_ref[...]
    for j in range(1, groups):
        bit = max(b for b in bits_of(groups) if b <= j)
        message = messages[j - 1]
        for r in range(flight):
            for q in range(wide):
                hidden[
                    j * slots + r * cap : j * slots + (r + 1) * cap, q * TILE : (q + 1) * TILE
                ] = message[r * wide + q]
        for q in range(share // TILE):
            own[j - 1, :, q * TILE : (q + 1) * TILE] = message[
                flight * wide + (j - bit) * (share // TILE) + q
            ]
    stores = []
    for n, cols in enumerate(chunks(share, block)):
        grads = [chips[c][0, 0, :, cols] for c in range(half)]
        grads += [swapped[c, 0, :, cols] for c in range(half)]
        for j in range(1, groups):
            grads.append(own[j - 1, :, cols])
            grads.append(parts[j - 1][:, :, cols].reshape(slots - cap, block))
        out[cols, :] = lax.dot_general(
            jnp.concatenate(grads, axis=0),
            hidden[...],
            (((0,), (0,)), ((), ())),
            preferred_element_type=f32,
        ).astype(bf16)
        stores.append(pltpu.make_async_copy(out.at[cols], out_hbm.at[cols], out_sems.at[n]))
        stores[n].start()
    for copy in stores:
        copy.wait()


def weight_grad(tie, chips, swapped, hidden, parts, messages, block=256):
    half, groups, cap, share = swapped.shape
    slots, hid = hidden.shape
    return pl.pallas_call(
        functools.partial(weight_grad_kernel, half, groups, block),
        out_shape=pltpu.HBM((share, hid), bf16),
        in_specs=[HBM] + [VMEM] * (half + 2 * groups),
        out_specs=HBM,
        scratch_shapes=[
            pltpu.VMEM((groups * slots, hid), bf16),
            pltpu.VMEM((groups - 1, cap, share), bf16),
            pltpu.VMEM((share, hid), bf16),
            pltpu.SemaphoreType.DMA((share // block,)),
        ],
        compiler_params=params(slots),
        cost_estimate=SMALL,
        name="weight_grad",
    )(hbm(tie), swapped, hidden, *chips, *parts, *messages)


def swap(value, axis, j):
    size = lax.axis_size(axis)
    return lax.ppermute(value, axis, [(i, i ^ j) for i in range(size)])


def shards(route_ids, route_probs, capacity, hot_lists, gate_up, w_quant, w_scale, d_out):
    flight = lax.axis_size("expert")
    groups = lax.axis_size("dp")
    gate_up = gate_up[0, 0]
    ids, probs = route_ids.T, route_probs.T
    scale = w_scale.transpose(1, 0, 2)
    own, hidden, *rest = dispatch(
        gate_up, capacity, hot_lists, ids, probs, d_out, flight, groups
    )
    half, bits = flight // 2, bits_of(groups)
    chips = rest[:1] + [swap(rest[c], "expert", 2 * c) for c in range(1, half)]
    messages, early = {}, []
    for bit, message in zip(bits, rest[half:]):
        for j in sorted(messages):
            messages[j ^ bit] = swap(messages[j], "dp", bit)
        messages[bit] = swap(message, "dp", bit)
        early.append(messages[bit])
    messages = [messages[j] for j in range(1, groups)]
    expert_out = forward(scale, hidden, w_quant[0], flight)
    returned = lax.all_to_all(expert_out, "expert", split_axis=0, concat_axis=0, tiled=True)
    swapped = swap(sibling_rows(chips, [hbm(expert_out)] + early), "expert", 1)
    pieces = split(chips, swapped)
    parts = [swap(pieces[j - 1], "dp", j) for j in range(1, groups)]
    d_gate_up = backward(scale, gate_up, w_quant[0], pieces[0], chips, swapped)
    combined, d_probs = combine(ids, own, d_out, returned)
    d_weight = weight_grad(d_probs, chips, swapped, hidden, parts, messages)
    return (combined, d_probs.T, d_gate_up[None, None], d_weight[None])


def solution(mesh):
    placed = (
        P(("dp", "expert"), None),
        P(("dp", "expert"), None),
        P(),
        P("dp", None),
        P("dp", "expert", None, None),
        P("expert", None, None),
        P("expert", None, None),
        P(("dp", "expert"), None),
    )
    return jax.shard_map(
        shards,
        mesh=mesh,
        in_specs=placed,
        out_specs=(
            P(("dp", "expert"), None),
            P(("dp", "expert"), None),
            P("dp", "expert", None, None),
            P("expert", "dp", None),
        ),
        check_vma=False,
    )
```

```python
import functools

import jax
import jax.numpy as jnp
from jax import lax
from jax.experimental import pallas as pl
from jax.experimental.pallas import tpu as pltpu
from jax.sharding import PartitionSpec as P

QB = 128
CAP = 16
TILE = 256

bf16 = jnp.bfloat16
f32 = jnp.float32

SMALL = pl.CostEstimate(flops=1024, bytes_accessed=1024, transcendentals=0)

VMEM = pl.BlockSpec(memory_space=pltpu.VMEM)
ANY = pl.BlockSpec(memory_space=pl.ANY)
HBM = pl.BlockSpec(memory_space=pltpu.HBM)


def params(slots):
    return pltpu.CompilerParams(vmem_limit_bytes=(12 + slots // 32) * 1024 * 1024)


def hbm(value):
    return pltpu.with_memory_space_constraint(value, pltpu.HBM)


def chunks(total, size):
    return [pl.ds(start, size) for start in range(0, total, size)]


def bits_of(groups):
    bits = []
    while groups > 1:
        groups //= 2
        bits.append(groups)
    return bits


def block_place(me, r, flight):
    half = flight // 2
    return me ^ (2 * (r % half) + r // half)


def dispatch_kernel(flight, groups, gate_up_hbm, cap_hbm, hot_hbm, ids_hbm, probs_hbm, dout_hbm, *refs):
    half = flight // 2
    bits = bits_of(groups)
    outs = 2 + half + len(bits)
    own_hbm, hidden_ref, *chips = refs[: 2 + half]
    messages = dict(zip(bits, refs[2 + half : outs]))
    gate_up, cap_ref, hot_ref, ids_ref, probs_ref, dout, own_ref = refs[outs : outs + 7]
    gate_sems, own_sem, small_sems, in_sems = refs[outs + 7 :]
    topk, tokens = ids_ref.shape
    slots = flight * CAP
    me, group = lax.axis_index("expert"), lax.axis_index("dp")
    share = dout_hbm.shape[1] // groups
    hid = hidden_ref.shape[1]
    small = [
        pltpu.make_async_copy(src, dst, small_sems.at[i])
        for i, (src, dst) in enumerate(
            [(ids_hbm, ids_ref), (probs_hbm, probs_ref), (cap_hbm, cap_ref), (hot_hbm, hot_ref)]
        )
    ]
    loads = [
        pltpu.make_async_copy(
            dout_hbm.at[:, pl.ds(pl.multiple_of((group ^ j) * share, share), share)],
            dout.at[j],
            in_sems.at[j],
        )
        for j in range(groups)
    ]
    gates = [
        pltpu.make_async_copy(
            gate_up_hbm.at[pl.ds(pl.multiple_of(block_place(me, r, flight) * CAP, CAP), CAP)],
            gate_up.at[pl.ds(r * CAP, CAP)],
            gate_sems.at[r],
        )
        for r in range(flight)
    ]
    for copy in small + loads + gates:
        copy.start()
    for copy in small:
        copy.wait()
    row = lax.broadcasted_iota(jnp.int32, (slots, 1), 0)
    row_expert = block_place(me, row // CAP, flight)
    row_rank = (row % CAP).astype(f32)
    limit = jnp.zeros((slots, 1), jnp.int32)
    for e in range(flight):
        hot = hot_ref[0, 0] == e
        for h in range(1, hot_ref.shape[1]):
            hot = jnp.logical_or(hot, hot_ref[0, h] == e)
        limit = jnp.where(row_expert == e, jnp.where(hot, CAP, cap_ref[e]), limit)
    limit = limit.astype(f32)
    named = jnp.zeros((slots, tokens), f32)
    weight = jnp.zeros((slots, tokens), f32)
    for k in range(topk):
        hit = ids_ref[k : k + 1, :] == row_expert
        named = jnp.where(hit, 1.0, named)
        weight = jnp.where(hit, probs_ref[k : k + 1, :], weight)
    earlier = lax.broadcasted_iota(jnp.int32, (tokens, tokens), 0)
    later = lax.broadcasted_iota(jnp.int32, (tokens, tokens), 1)
    before = (earlier < later).astype(f32).astype(bf16)
    rank = jnp.dot(named.astype(bf16), before, preferred_element_type=f32)
    owns = (named > 0.0) & (rank == row_rank) & (rank < limit)
    own_weight = jnp.where(owns, weight, 0.0)
    own_ref[...] = own_weight
    own_copy = pltpu.make_async_copy(own_ref, own_hbm, own_sem)
    own_copy.start()
    owner = jnp.where(owns, 1.0, 0.0).astype(bf16)
    slot_weight = jnp.sum(own_weight, axis=1, keepdims=True)
    for copy in loads:
        copy.wait()
    for j in range(groups):
        part = jnp.dot(owner, dout[j], preferred_element_type=f32)
        part = (part * slot_weight).astype(bf16)
        for r in range(flight):
            chips[r % half][r // half, j] = part[r * CAP : (r + 1) * CAP, :]
        for bit in bits:
            if bit <= j < 2 * bit:
                first = flight * (hid // TILE) + (j - bit) * (share // TILE)
                for q in range(share // TILE):
                    messages[bit][first + q] = part[:CAP, q * TILE : (q + 1) * TILE]
    for copy in gates:
        copy.wait()
    for r in range(flight):
        at = slice(r * CAP, (r + 1) * CAP)
        gate = gate_up[at, :hid].astype(f32)
        up = gate_up[at, hid:].astype(f32)
        block = (gate * jax.nn.sigmoid(gate) * up).astype(bf16)
        hidden_ref[at, :] = block
        for bit in bits:
            for q in range(hid // TILE):
                messages[bit][r * (hid // TILE) + q] = block[:, q * TILE : (q + 1) * TILE]
    own_copy.wait()


def dispatch(gate_up, capacity, hot_row, ids, probs, d_out, flight, groups):
    tokens, width = d_out.shape
    rows, double = gate_up.shape
    slots = flight * CAP
    share = width // groups
    half = flight // 2
    return pl.pallas_call(
        functools.partial(dispatch_kernel, flight, groups),
        out_shape=(pltpu.HBM((slots, tokens), f32), pltpu.VMEM((rows, double // 2), bf16))
        + (pltpu.VMEM((2, groups, CAP, share), bf16),) * half
        + tuple(
            pltpu.VMEM((flight * (double // 2 // TILE) + bit * (share // TILE), CAP, TILE), bf16)
            for bit in bits_of(groups)
        ),
        in_specs=[HBM] * 6,
        out_specs=(HBM, VMEM) + (VMEM,) * (half + len(bits_of(groups))),
        scratch_shapes=[
            pltpu.VMEM((rows, double), bf16),
            pltpu.SMEM(capacity.shape, jnp.int32),
            pltpu.SMEM(hot_row.shape, jnp.int32),
            pltpu.VMEM(ids.shape, jnp.int32),
            pltpu.VMEM(probs.shape, f32),
            pltpu.VMEM((groups, tokens, share), bf16),
            pltpu.VMEM((slots, tokens), f32),
            pltpu.SemaphoreType.DMA((flight,)),
            pltpu.SemaphoreType.DMA,
            pltpu.SemaphoreType.DMA((4,)),
            pltpu.SemaphoreType.DMA((groups,)),
        ],
        compiler_params=params(slots),
        cost_estimate=SMALL,
        name="dispatch",
    )(hbm(gate_up), hbm(capacity), hbm(hot_row), hbm(ids), hbm(probs), hbm(d_out))


def forward_kernel(
    flight, block, hidden_ref, scale_hbm, quant_hbm, out_hbm,
    scale, hidden, quant, out, scale_sem, in_sems, out_sems
):
    steps, hid, _ = quant.shape
    me = lax.axis_index("expert")
    loads = [
        pltpu.make_async_copy(quant_hbm.at[:, pl.ds(c * block, block)], quant.at[c], in_sems.at[c])
        for c in range(steps)
    ]
    small = pltpu.make_async_copy(scale_hbm, scale, scale_sem)
    for copy in [small] + loads:
        copy.start()
    for r in range(flight):
        place = pl.multiple_of(block_place(me, r, flight) * CAP, CAP)
        hidden[pl.ds(place, CAP), :] = hidden_ref[pl.ds(r * CAP, CAP), :]
    small.wait()
    stores = []
    for c in range(steps):
        cols = pl.ds(c * block, block)
        loads[c].wait()
        total = [None] * (block // QB)
        for i in range(hid // QB):
            part = jnp.dot(
                hidden[:, i * QB : (i + 1) * QB],
                quant[c, i * QB : (i + 1) * QB, :],
                preferred_element_type=f32,
            )
            for j in range(block // QB):
                scaled = part[:, j * QB : (j + 1) * QB] * scale[i, 0, c * (block // QB) + j]
                total[j] = scaled if i == 0 else total[j] + scaled
        for j in range(block // QB):
            at = pl.ds(c * block + j * QB, QB)
            out[:, :, at] = total[j].astype(bf16).reshape(flight, CAP, QB)
        stores.append(
            pltpu.make_async_copy(out.at[:, :, cols], out_hbm.at[:, :, cols], out_sems.at[c])
        )
        stores[c].start()
    for copy in stores:
        copy.wait()


def forward(scale, hidden, quant, flight, block=512):
    hid, width = quant.shape
    steps = width // block
    return pl.pallas_call(
        functools.partial(forward_kernel, flight, block),
        out_shape=pltpu.HBM((flight, CAP, width), bf16),
        in_specs=[VMEM, HBM, HBM],
        out_specs=HBM,
        scratch_shapes=[
            pltpu.SMEM(scale.shape, f32),
            pltpu.VMEM(hidden.shape, bf16),
            pltpu.VMEM((steps, hid, block), bf16),
            pltpu.VMEM((flight, CAP, width), bf16),
            pltpu.SemaphoreType.DMA,
            pltpu.SemaphoreType.DMA((steps,)),
            pltpu.SemaphoreType.DMA((steps,)),
        ],
        compiler_params=params(flight * CAP),
        cost_estimate=SMALL,
        name="expert_forward",
    )(hidden, hbm(scale), hbm(quant))


def sort_kernel(half, groups, ties, *refs):
    chips, (sibling, *pieces) = refs[:half], refs[half + ties :]
    for c in range(half):
        sibling[c] = chips[c][1]
        for j in range(1, groups):
            if c:
                pieces[j - 1][c - 1] = chips[c][0, j]


def sort_rows(chips, ties):
    half = len(chips)
    _, groups, cap, share = chips[0].shape
    return pl.pallas_call(
        functools.partial(sort_kernel, half, groups, len(ties)),
        out_shape=(pltpu.VMEM((half, groups, cap, share), bf16),)
        + (pltpu.VMEM((half - 1, cap, share), bf16),) * (groups - 1),
        in_specs=[VMEM] * half + [ANY] * len(ties),
        out_specs=(VMEM,) * groups,
        compiler_params=params(2 * half * CAP),
        cost_estimate=SMALL,
        name="sort_rows",
    )(*chips, *ties)


def split_kernel(groups, swapped, *pieces):
    for j in range(1, groups):
        pieces[j - 1][...] = swapped[:, j]


def split(swapped):
    half, groups, cap, share = swapped.shape
    return pl.pallas_call(
        functools.partial(split_kernel, groups),
        out_shape=(pltpu.VMEM((half, cap, share), bf16),) * (groups - 1),
        in_specs=[VMEM],
        out_specs=(VMEM,) * (groups - 1),
        compiler_params=params(2 * half * CAP),
        cost_estimate=SMALL,
        name="split",
    )(swapped)


def backward_kernel(flight, groups, scale_hbm, gate_up_hbm, quant_hbm, tie_ref, swapped, *refs):
    half = flight // 2
    chips, out_hbm = refs[:half], refs[half]
    scale, gate_up, rows, quant, acc, out = refs[half + 1 : half + 7]
    scale_sem, gate_sems, in_sems, out_sems = refs[half + 7 :]
    me, group = lax.axis_index("expert"), lax.axis_index("dp")
    slots, hid = acc.shape
    share = quant.shape[2]

    def place(r):
        return pl.ds(pl.multiple_of(block_place(me, r, flight) * CAP, CAP), CAP)

    loads = [
        pltpu.make_async_copy(
            quant_hbm.at[:, pl.ds(pl.multiple_of((group ^ j) * share, share), share)],
            quant.at[j],
            in_sems.at[j],
        )
        for j in range(groups)
    ]
    gates = [
        pltpu.make_async_copy(
            gate_up_hbm.at[place(r)], gate_up.at[pl.ds(r * CAP, CAP)], gate_sems.at[r]
        )
        for r in range(flight)
    ]
    small = pltpu.make_async_copy(scale_hbm, scale, scale_sem)
    for copy in [small] + loads + gates:
        copy.start()
    for c in range(half):
        rows[:, c * CAP : (c + 1) * CAP, :] = chips[c][0]
        rows[:, (half + c) * CAP : (half + c + 1) * CAP, :] = swapped[c]
    small.wait()
    for j in range(groups):
        loads[j].wait()
        for b in range(share // QB):
            cols = slice(b * QB, (b + 1) * QB)
            part = lax.dot_general(
                rows[j, :, cols],
                quant[j, :, cols],
                (((1,), (1,)), ((), ())),
                preferred_element_type=f32,
            )
            for i in range(hid // QB):
                at = (slice(None), slice(i * QB, (i + 1) * QB))
                scaled = part[at] * scale[i, 0, (group ^ j) * (share // QB) + b]
                if j == 0 and b == 0:
                    acc[at] = scaled
                else:
                    acc[at] += scaled
    for copy in gates:
        copy.wait()
    gate = gate_up[:, :hid].astype(f32)
    up = gate_up[:, hid:].astype(f32)
    sig = jax.nn.sigmoid(gate)
    d_hidden = acc[...]
    out[:, :hid] = (d_hidden * up * sig * (1.0 + gate * (1.0 - sig))).astype(bf16)
    out[:, hid:] = (d_hidden * (gate * sig)).astype(bf16)
    stores = [
        pltpu.make_async_copy(out.at[pl.ds(r * CAP, CAP)], out_hbm.at[place(r)], out_sems.at[r])
        for r in range(flight)
    ]
    for copy in stores:
        copy.start()
    for copy in stores:
        copy.wait()


def backward(scale, gate_up, quant, tie, chips, swapped):
    slots, double = gate_up.shape
    hid, width = quant.shape
    half, groups, cap, share = swapped.shape
    flight = 2 * half
    return pl.pallas_call(
        functools.partial(backward_kernel, flight, groups),
        out_shape=pltpu.HBM((slots, double), bf16),
        in_specs=[HBM, HBM, HBM, ANY] + [VMEM] * (1 + half),
        out_specs=HBM,
        scratch_shapes=[
            pltpu.SMEM(scale.shape, f32),
            pltpu.VMEM((slots, double), bf16),
            pltpu.VMEM((groups, slots, share), bf16),
            pltpu.VMEM((groups, hid, share), bf16),
            pltpu.VMEM((slots, hid), f32),
            pltpu.VMEM((slots, double), bf16),
            pltpu.SemaphoreType.DMA,
            pltpu.SemaphoreType.DMA((flight,)),
            pltpu.SemaphoreType.DMA((groups,)),
            pltpu.SemaphoreType.DMA((flight,)),
        ],
        compiler_params=params(slots),
        cost_estimate=SMALL,
        name="expert_backward",
    )(hbm(scale), hbm(gate_up), hbm(quant), tie, swapped, *chips)


def combine_kernel(
    block, ids_hbm, own_hbm, dout_hbm, ret_hbm, out_ref, dprobs_ref, ids_ref, own_ref, dout, ret_ref, sems
):
    copies = [
        pltpu.make_async_copy(ids_hbm, ids_ref, sems.at[0]),
        pltpu.make_async_copy(own_hbm, own_ref, sems.at[1]),
        pltpu.make_async_copy(dout_hbm, dout, sems.at[2]),
        pltpu.make_async_copy(ret_hbm, ret_ref, sems.at[3]),
    ]
    for copy in copies:
        copy.start()
    topk, tokens = ids_ref.shape
    slots = own_ref.shape[0]
    width = dout.shape[1]
    flight = slots // CAP
    me = lax.axis_index("expert")
    copies[1].wait()
    own = own_ref[...]
    turned = own.T
    high = turned.astype(bf16)
    low = (turned - high.astype(f32)).astype(bf16)
    total = jnp.zeros((slots, tokens), f32)
    for copy in (copies[0], copies[2], copies[3]):
        copy.wait()
    for cols in chunks(width, block):
        here = jnp.concatenate(
            [ret_ref[block_place(me, r, flight), :, cols] for r in range(flight)], axis=0
        )
        out = jnp.dot(high, here, preferred_element_type=f32)
        out = out + jnp.dot(low, here, preferred_element_type=f32)
        out_ref[:, cols] = out.astype(bf16)
        total = total + lax.dot_general(
            here, dout[:, cols], (((1,), (1,)), ((), ())), preferred_element_type=f32
        )
    inner = jnp.where(own > 0.0, total, 0.0)
    row_expert = block_place(me, lax.broadcasted_iota(jnp.int32, (slots, 1), 0) // CAP, flight)
    for k in range(topk):
        mine = jnp.where(ids_ref[k : k + 1, :] == row_expert, inner, 0.0)
        dprobs_ref[k : k + 1, :] = jnp.sum(mine, axis=0, keepdims=True)


def combine(ids, own, d_out, returned, block=1024):
    tokens, width = d_out.shape
    return pl.pallas_call(
        functools.partial(combine_kernel, block),
        out_shape=(
            pltpu.HBM((tokens, width), bf16),
            pltpu.HBM(ids.shape, f32),
        ),
        in_specs=[HBM, HBM, HBM, HBM],
        out_specs=(VMEM, VMEM),
        scratch_shapes=[
            pltpu.VMEM(ids.shape, jnp.int32),
            pltpu.VMEM(own.shape, f32),
            pltpu.VMEM((tokens, width), bf16),
            pltpu.VMEM(returned.shape, bf16),
            pltpu.SemaphoreType.DMA((4,)),
        ],
        compiler_params=params(own.shape[0]),
        cost_estimate=SMALL,
        name="combine",
    )(hbm(ids), hbm(own), hbm(d_out), hbm(returned))


def weight_grad_kernel(half, groups, block, tie_ref, swapped, hidden_ref, *refs):
    others = groups - 1
    chips, parts, refs = refs[:half], refs[half : half + 2 * others], refs[half + 2 * others :]
    messages, (out_hbm, hidden, own, out, out_sems) = refs[:others], refs[others:]
    cap, share = parts[0].shape[1:]
    flight = 2 * half
    slots = flight * cap
    wide = hidden_ref.shape[1] // TILE
    hidden[:slots, :] = hidden_ref[...]
    for j in range(1, groups):
        bit = max(b for b in bits_of(groups) if b <= j)
        message = messages[j - 1]
        for r in range(flight):
            for q in range(wide):
                hidden[
                    j * slots + r * cap : j * slots + (r + 1) * cap, q * TILE : (q + 1) * TILE
                ] = message[r * wide + q]
        for q in range(share // TILE):
            own[j - 1, :, q * TILE : (q + 1) * TILE] = message[
                flight * wide + (j - bit) * (share // TILE) + q
            ]
    stores = []
    for n, cols in enumerate(chunks(share, block)):
        grads = [chips[c][0, 0, :, cols] for c in range(half)]
        grads += [swapped[c, 0, :, cols] for c in range(half)]
        for j in range(1, groups):
            grads.append(own[j - 1, :, cols])
            grads.append(parts[j - 1][:, :, cols].reshape(slots // 2 - cap, block))
            grads.append(parts[others + j - 1][:, :, cols].reshape(slots // 2, block))
        out[cols, :] = lax.dot_general(
            jnp.concatenate(grads, axis=0),
            hidden[...],
            (((0,), (0,)), ((), ())),
            preferred_element_type=f32,
        ).astype(bf16)
        stores.append(pltpu.make_async_copy(out.at[cols], out_hbm.at[cols], out_sems.at[n]))
        stores[n].start()
    for copy in stores:
        copy.wait()


def weight_grad(tie, chips, swapped, hidden, parts, messages, block=256):
    half, groups, cap, share = swapped.shape
    slots, hid = hidden.shape
    return pl.pallas_call(
        functools.partial(weight_grad_kernel, half, groups, block),
        out_shape=pltpu.HBM((share, hid), bf16),
        in_specs=[HBM] + [VMEM] * (half + 3 * groups - 1),
        out_specs=HBM,
        scratch_shapes=[
            pltpu.VMEM((groups * slots, hid), bf16),
            pltpu.VMEM((groups - 1, cap, share), bf16),
            pltpu.VMEM((share, hid), bf16),
            pltpu.SemaphoreType.DMA((share // block,)),
        ],
        compiler_params=params(slots),
        cost_estimate=SMALL,
        name="weight_grad",
    )(hbm(tie), swapped, hidden, *chips, *parts, *messages)


def swap(value, axis, j):
    size = lax.axis_size(axis)
    return lax.ppermute(value, axis, [(i, i ^ j) for i in range(size)])


def shards(route_ids, route_probs, capacity, hot_lists, gate_up, w_quant, w_scale, d_out):
    flight = lax.axis_size("expert")
    groups = lax.axis_size("dp")
    gate_up = gate_up[0, 0]
    ids, probs = route_ids.T, route_probs.T
    scale = w_scale.transpose(1, 0, 2)
    own, hidden, *rest = dispatch(
        gate_up, capacity, hot_lists, ids, probs, d_out, flight, groups
    )
    half, bits = flight // 2, bits_of(groups)
    chips = rest[:1] + [swap(rest[c], "expert", 2 * c) for c in range(1, half)]
    messages, early = {}, []
    for bit, message in zip(bits, rest[half:]):
        for j in sorted(messages):
            messages[j ^ bit] = swap(messages[j], "dp", bit)
        messages[bit] = swap(message, "dp", bit)
        early.append(messages[bit])
    messages = [messages[j] for j in range(1, groups)]
    expert_out = forward(scale, hidden, w_quant[0], flight)
    returned = lax.all_to_all(expert_out, "expert", split_axis=0, concat_axis=0, tiled=True)
    sibling, *direct = sort_rows(chips, [hbm(expert_out)] + early)
    swapped = swap(sibling, "expert", 1)
    handed = split(swapped)
    parts = [swap(direct[j - 1], "dp", j) for j in range(1, groups)]
    parts += [swap(handed[j - 1], "dp", j) for j in range(1, groups)]
    d_gate_up = backward(scale, gate_up, w_quant[0], handed[0], chips, swapped)
    combined, d_probs = combine(ids, own, d_out, returned)
    d_weight = weight_grad(d_probs, chips, swapped, hidden, parts, messages)
    return (combined, d_probs.T, d_gate_up[None, None], d_weight[None])


def solution(mesh):
    placed = (
        P(("dp", "expert"), None),
        P(("dp", "expert"), None),
        P(),
        P("dp", None),
        P("dp", "expert", None, None),
        P("expert", None, None),
        P("expert", None, None),
        P(("dp", "expert"), None),
    )
    return jax.shard_map(
        shards,
        mesh=mesh,
        in_specs=placed,
        out_specs=(
            P(("dp", "expert"), None),
            P(("dp", "expert"), None),
            P("dp", "expert", None, None),
            P("expert", "dp", None),
        ),
        check_vma=False,
    )
```

```python
import functools

import jax
import jax.numpy as jnp
from jax import lax
from jax.experimental import pallas as pl
from jax.experimental.pallas import tpu as pltpu
from jax.sharding import PartitionSpec as P

QB = 128
CAP = 16
TILE = 256

bf16 = jnp.bfloat16
f32 = jnp.float32

SMALL = pl.CostEstimate(flops=1024, bytes_accessed=1024, transcendentals=0)

VMEM = pl.BlockSpec(memory_space=pltpu.VMEM)
ANY = pl.BlockSpec(memory_space=pl.ANY)
HBM = pl.BlockSpec(memory_space=pltpu.HBM)


def params(slots):
    return pltpu.CompilerParams(vmem_limit_bytes=(12 + slots // 32) * 1024 * 1024)


def hbm(value):
    return pltpu.with_memory_space_constraint(value, pltpu.HBM)


def chunks(total, size):
    return [pl.ds(start, size) for start in range(0, total, size)]


def bits_of(groups):
    bits = []
    while groups > 1:
        groups //= 2
        bits.append(groups)
    return bits


def block_place(me, r, flight):
    half = flight // 2
    return me ^ (2 * (r % half) + r // half)


def dispatch_kernel(flight, groups, gate_up_hbm, cap_hbm, hot_hbm, ids_hbm, probs_hbm, dout_hbm, *refs):
    half = flight // 2
    bits = bits_of(groups)
    outs = 2 + half + len(bits)
    own_hbm, hidden_ref, *chips = refs[: 2 + half]
    messages = dict(zip(bits, refs[2 + half : outs]))
    gate_up, cap_ref, hot_ref, ids_ref, probs_ref, dout, own_ref = refs[outs : outs + 7]
    gate_sems, own_sem, small_sems, in_sems = refs[outs + 7 :]
    topk, tokens = ids_ref.shape
    slots = flight * CAP
    me, group = lax.axis_index("expert"), lax.axis_index("dp")
    share = dout_hbm.shape[1] // groups
    hid = hidden_ref.shape[1]
    small = [
        pltpu.make_async_copy(src, dst, small_sems.at[i])
        for i, (src, dst) in enumerate(
            [(ids_hbm, ids_ref), (probs_hbm, probs_ref), (cap_hbm, cap_ref), (hot_hbm, hot_ref)]
        )
    ]
    loads = [
        pltpu.make_async_copy(
            dout_hbm.at[:, pl.ds(pl.multiple_of((group ^ j) * share, share), share)],
            dout.at[j],
            in_sems.at[j],
        )
        for j in range(groups)
    ]
    gates = [
        pltpu.make_async_copy(
            gate_up_hbm.at[pl.ds(pl.multiple_of(block_place(me, r, flight) * CAP, CAP), CAP)],
            gate_up.at[pl.ds(r * CAP, CAP)],
            gate_sems.at[r],
        )
        for r in range(flight)
    ]
    for copy in small + loads + gates:
        copy.start()
    for copy in small:
        copy.wait()
    row = lax.broadcasted_iota(jnp.int32, (slots, 1), 0)
    row_expert = block_place(me, row // CAP, flight)
    row_rank = (row % CAP).astype(f32)
    limit = jnp.zeros((slots, 1), jnp.int32)
    for e in range(flight):
        hot = hot_ref[0, 0] == e
        for h in range(1, hot_ref.shape[1]):
            hot = jnp.logical_or(hot, hot_ref[0, h] == e)
        limit = jnp.where(row_expert == e, jnp.where(hot, CAP, cap_ref[e]), limit)
    limit = limit.astype(f32)
    named = jnp.zeros((slots, tokens), f32)
    weight = jnp.zeros((slots, tokens), f32)
    for k in range(topk):
        hit = ids_ref[k : k + 1, :] == row_expert
        named = jnp.where(hit, 1.0, named)
        weight = jnp.where(hit, probs_ref[k : k + 1, :], weight)
    earlier = lax.broadcasted_iota(jnp.int32, (tokens, tokens), 0)
    later = lax.broadcasted_iota(jnp.int32, (tokens, tokens), 1)
    before = (earlier < later).astype(f32).astype(bf16)
    rank = jnp.dot(named.astype(bf16), before, preferred_element_type=f32)
    owns = (named > 0.0) & (rank == row_rank) & (rank < limit)
    own_weight = jnp.where(owns, weight, 0.0)
    own_ref[...] = own_weight
    own_copy = pltpu.make_async_copy(own_ref, own_hbm, own_sem)
    own_copy.start()
    owner = jnp.where(owns, 1.0, 0.0).astype(bf16)
    slot_weight = jnp.sum(own_weight, axis=1, keepdims=True)
    for copy in loads:
        copy.wait()
    for j in range(groups):
        part = jnp.dot(owner, dout[j], preferred_element_type=f32)
        part = (part * slot_weight).astype(bf16)
        for r in range(flight):
            chips[r % half][r // half, j] = part[r * CAP : (r + 1) * CAP, :]
        for bit in bits:
            if bit <= j < 2 * bit:
                first = flight * (hid // TILE) + (j - bit) * (share // TILE)
                for q in range(share // TILE):
                    messages[bit][first + q] = part[:CAP, q * TILE : (q + 1) * TILE]
    for copy in gates:
        copy.wait()
    for r in range(flight):
        at = slice(r * CAP, (r + 1) * CAP)
        gate = gate_up[at, :hid].astype(f32)
        up = gate_up[at, hid:].astype(f32)
        block = (gate * jax.nn.sigmoid(gate) * up).astype(bf16)
        hidden_ref[at, :] = block
        for bit in bits:
            for q in range(hid // TILE):
                messages[bit][r * (hid // TILE) + q] = block[:, q * TILE : (q + 1) * TILE]
    own_copy.wait()


def dispatch(gate_up, capacity, hot_row, ids, probs, d_out, flight, groups):
    tokens, width = d_out.shape
    rows, double = gate_up.shape
    slots = flight * CAP
    share = width // groups
    half = flight // 2
    return pl.pallas_call(
        functools.partial(dispatch_kernel, flight, groups),
        out_shape=(pltpu.HBM((slots, tokens), f32), pltpu.VMEM((rows, double // 2), bf16))
        + (pltpu.VMEM((2, groups, CAP, share), bf16),) * half
        + tuple(
            pltpu.VMEM((flight * (double // 2 // TILE) + bit * (share // TILE), CAP, TILE), bf16)
            for bit in bits_of(groups)
        ),
        in_specs=[HBM] * 6,
        out_specs=(HBM, VMEM) + (VMEM,) * (half + len(bits_of(groups))),
        scratch_shapes=[
            pltpu.VMEM((rows, double), bf16),
            pltpu.SMEM(capacity.shape, jnp.int32),
            pltpu.SMEM(hot_row.shape, jnp.int32),
            pltpu.VMEM(ids.shape, jnp.int32),
            pltpu.VMEM(probs.shape, f32),
            pltpu.VMEM((groups, tokens, share), bf16),
            pltpu.VMEM((slots, tokens), f32),
            pltpu.SemaphoreType.DMA((flight,)),
            pltpu.SemaphoreType.DMA,
            pltpu.SemaphoreType.DMA((4,)),
            pltpu.SemaphoreType.DMA((groups,)),
        ],
        compiler_params=params(slots),
        cost_estimate=SMALL,
        name="dispatch",
    )(hbm(gate_up), hbm(capacity), hbm(hot_row), hbm(ids), hbm(probs), hbm(d_out))


def forward_kernel(
    flight, block, hidden_ref, scale_hbm, quant_hbm, out_hbm,
    scale, hidden, quant, out, scale_sem, in_sems, out_sems
):
    steps, hid, _ = quant.shape
    me = lax.axis_index("expert")
    loads = [
        pltpu.make_async_copy(quant_hbm.at[:, pl.ds(c * block, block)], quant.at[c], in_sems.at[c])
        for c in range(steps)
    ]
    small = pltpu.make_async_copy(scale_hbm, scale, scale_sem)
    for copy in [small] + loads:
        copy.start()
    for r in range(flight):
        place = pl.multiple_of(block_place(me, r, flight) * CAP, CAP)
        hidden[pl.ds(place, CAP), :] = hidden_ref[pl.ds(r * CAP, CAP), :]
    small.wait()
    stores = []
    for c in range(steps):
        cols = pl.ds(c * block, block)
        loads[c].wait()
        total = [None] * (block // QB)
        for i in range(hid // QB):
            part = jnp.dot(
                hidden[:, i * QB : (i + 1) * QB],
                quant[c, i * QB : (i + 1) * QB, :],
                preferred_element_type=f32,
            )
            for j in range(block // QB):
                scaled = part[:, j * QB : (j + 1) * QB] * scale[i, 0, c * (block // QB) + j]
                total[j] = scaled if i == 0 else total[j] + scaled
        for j in range(block // QB):
            at = pl.ds(c * block + j * QB, QB)
            out[:, :, at] = total[j].astype(bf16).reshape(flight, CAP, QB)
        stores.append(
            pltpu.make_async_copy(out.at[:, :, cols], out_hbm.at[:, :, cols], out_sems.at[c])
        )
        stores[c].start()
    for copy in stores:
        copy.wait()


def forward(scale, hidden, quant, flight, block=512):
    hid, width = quant.shape
    steps = width // block
    return pl.pallas_call(
        functools.partial(forward_kernel, flight, block),
        out_shape=pltpu.HBM((flight, CAP, width), bf16),
        in_specs=[VMEM, HBM, HBM],
        out_specs=HBM,
        scratch_shapes=[
            pltpu.SMEM(scale.shape, f32),
            pltpu.VMEM(hidden.shape, bf16),
            pltpu.VMEM((steps, hid, block), bf16),
            pltpu.VMEM((flight, CAP, width), bf16),
            pltpu.SemaphoreType.DMA,
            pltpu.SemaphoreType.DMA((steps,)),
            pltpu.SemaphoreType.DMA((steps,)),
        ],
        compiler_params=params(flight * CAP),
        cost_estimate=SMALL,
        name="expert_forward",
    )(hidden, hbm(scale), hbm(quant))


def sort_kernel(half, groups, ties, *refs):
    chips, (sibling, *pieces) = refs[:half], refs[half + ties :]
    for c in range(half):
        sibling[c] = chips[c][1]
        for j in range(2, groups):
            if c:
                pieces[j - 2][c - 1] = chips[c][0, j]


def sort_rows(chips, ties):
    half = len(chips)
    _, groups, cap, share = chips[0].shape
    return pl.pallas_call(
        functools.partial(sort_kernel, half, groups, len(ties)),
        out_shape=(pltpu.VMEM((half, groups, cap, share), bf16),)
        + (pltpu.VMEM((half - 1, cap, share), bf16),) * (groups - 2),
        in_specs=[VMEM] * half + [ANY] * len(ties),
        out_specs=(VMEM,) * (groups - 1),
        compiler_params=params(2 * half * CAP),
        cost_estimate=SMALL,
        name="sort_rows",
    )(*chips, *ties)


def split_kernel(half, groups, count, swapped, *refs):
    chips, messages = refs[: half - 1], refs[half - 1 : half - 1 + count]
    near, *pieces = refs[half - 1 + count :]
    wide = swapped.shape[3] // TILE
    for j in range(2, groups):
        pieces[j - 2][...] = swapped[:, j]
    for r in range(2 * half - 1):
        for q in range(wide):
            cols = slice(q * TILE, (q + 1) * TILE)
            near[r * wide + q] = (
                chips[r][0, 1, :, cols] if r < half - 1 else swapped[r - half + 1, 1, :, cols]
            )
    first = (2 * half - 1) * wide
    for message in messages:
        near[first : first + message.shape[0]] = message[...]
        first += message.shape[0]


def split(swapped, chips, messages):
    half, groups, cap, share = swapped.shape
    tiles = (2 * half - 1) * (share // TILE) + sum(message.shape[0] for message in messages)
    return pl.pallas_call(
        functools.partial(split_kernel, half, groups, len(messages)),
        out_shape=(pltpu.VMEM((tiles, cap, TILE), bf16),)
        + (pltpu.VMEM((half, cap, share), bf16),) * (groups - 2),
        in_specs=[VMEM] * (half + len(messages)),
        out_specs=(VMEM,) * (groups - 1),
        compiler_params=params(2 * half * CAP),
        cost_estimate=SMALL,
        name="split",
    )(swapped, *chips[1:], *messages)


def backward_kernel(flight, groups, scale_hbm, gate_up_hbm, quant_hbm, tie_ref, swapped, *refs):
    half = flight // 2
    chips, out_hbm = refs[:half], refs[half]
    scale, gate_up, rows, quant, acc, out = refs[half + 1 : half + 7]
    scale_sem, gate_sems, in_sems, out_sems = refs[half + 7 :]
    me, group = lax.axis_index("expert"), lax.axis_index("dp")
    slots, hid = acc.shape
    share = quant.shape[2]

    def place(r):
        return pl.ds(pl.multiple_of(block_place(me, r, flight) * CAP, CAP), CAP)

    loads = [
        pltpu.make_async_copy(
            quant_hbm.at[:, pl.ds(pl.multiple_of((group ^ j) * share, share), share)],
            quant.at[j],
            in_sems.at[j],
        )
        for j in range(groups)
    ]
    gates = [
        pltpu.make_async_copy(
            gate_up_hbm.at[place(r)], gate_up.at[pl.ds(r * CAP, CAP)], gate_sems.at[r]
        )
        for r in range(flight)
    ]
    small = pltpu.make_async_copy(scale_hbm, scale, scale_sem)
    for copy in [small] + loads + gates:
        copy.start()
    for c in range(half):
        rows[:, c * CAP : (c + 1) * CAP, :] = chips[c][0]
        rows[:, (half + c) * CAP : (half + c + 1) * CAP, :] = swapped[c]
    small.wait()
    for j in range(groups):
        loads[j].wait()
        for b in range(share // QB):
            cols = slice(b * QB, (b + 1) * QB)
            part = lax.dot_general(
                rows[j, :, cols],
                quant[j, :, cols],
                (((1,), (1,)), ((), ())),
                preferred_element_type=f32,
            )
            for i in range(hid // QB):
                at = (slice(None), slice(i * QB, (i + 1) * QB))
                scaled = part[at] * scale[i, 0, (group ^ j) * (share // QB) + b]
                if j == 0 and b == 0:
                    acc[at] = scaled
                else:
                    acc[at] += scaled
    for copy in gates:
        copy.wait()
    gate = gate_up[:, :hid].astype(f32)
    up = gate_up[:, hid:].astype(f32)
    sig = jax.nn.sigmoid(gate)
    d_hidden = acc[...]
    out[:, :hid] = (d_hidden * up * sig * (1.0 + gate * (1.0 - sig))).astype(bf16)
    out[:, hid:] = (d_hidden * (gate * sig)).astype(bf16)
    stores = [
        pltpu.make_async_copy(out.at[pl.ds(r * CAP, CAP)], out_hbm.at[place(r)], out_sems.at[r])
        for r in range(flight)
    ]
    for copy in stores:
        copy.start()
    for copy in stores:
        copy.wait()


def backward(scale, gate_up, quant, tie, chips, swapped):
    slots, double = gate_up.shape
    hid, width = quant.shape
    half, groups, cap, share = swapped.shape
    flight = 2 * half
    return pl.pallas_call(
        functools.partial(backward_kernel, flight, groups),
        out_shape=pltpu.HBM((slots, double), bf16),
        in_specs=[HBM, HBM, HBM, ANY] + [VMEM] * (1 + half),
        out_specs=HBM,
        scratch_shapes=[
            pltpu.SMEM(scale.shape, f32),
            pltpu.VMEM((slots, double), bf16),
            pltpu.VMEM((groups, slots, share), bf16),
            pltpu.VMEM((groups, hid, share), bf16),
            pltpu.VMEM((slots, hid), f32),
            pltpu.VMEM((slots, double), bf16),
            pltpu.SemaphoreType.DMA,
            pltpu.SemaphoreType.DMA((flight,)),
            pltpu.SemaphoreType.DMA((groups,)),
            pltpu.SemaphoreType.DMA((flight,)),
        ],
        compiler_params=params(slots),
        cost_estimate=SMALL,
        name="expert_backward",
    )(hbm(scale), hbm(gate_up), hbm(quant), tie, swapped, *chips)


def combine_kernel(
    block, ids_hbm, own_hbm, dout_hbm, ret_hbm, out_ref, dprobs_ref, ids_ref, own_ref, dout, ret_ref, sems
):
    copies = [
        pltpu.make_async_copy(ids_hbm, ids_ref, sems.at[0]),
        pltpu.make_async_copy(own_hbm, own_ref, sems.at[1]),
        pltpu.make_async_copy(dout_hbm, dout, sems.at[2]),
        pltpu.make_async_copy(ret_hbm, ret_ref, sems.at[3]),
    ]
    for copy in copies:
        copy.start()
    topk, tokens = ids_ref.shape
    slots = own_ref.shape[0]
    width = dout.shape[1]
    flight = slots // CAP
    me = lax.axis_index("expert")
    copies[1].wait()
    own = own_ref[...]
    turned = own.T
    high = turned.astype(bf16)
    low = (turned - high.astype(f32)).astype(bf16)
    total = jnp.zeros((slots, tokens), f32)
    for copy in (copies[0], copies[2], copies[3]):
        copy.wait()
    for cols in chunks(width, block):
        here = jnp.concatenate(
            [ret_ref[block_place(me, r, flight), :, cols] for r in range(flight)], axis=0
        )
        out = jnp.dot(high, here, preferred_element_type=f32)
        out = out + jnp.dot(low, here, preferred_element_type=f32)
        out_ref[:, cols] = out.astype(bf16)
        total = total + lax.dot_general(
            here, dout[:, cols], (((1,), (1,)), ((), ())), preferred_element_type=f32
        )
    inner = jnp.where(own > 0.0, total, 0.0)
    row_expert = block_place(me, lax.broadcasted_iota(jnp.int32, (slots, 1), 0) // CAP, flight)
    for k in range(topk):
        mine = jnp.where(ids_ref[k : k + 1, :] == row_expert, inner, 0.0)
        dprobs_ref[k : k + 1, :] = jnp.sum(mine, axis=0, keepdims=True)


def combine(ids, own, d_out, returned, block=1024):
    tokens, width = d_out.shape
    return pl.pallas_call(
        functools.partial(combine_kernel, block),
        out_shape=(
            pltpu.HBM((tokens, width), bf16),
            pltpu.HBM(ids.shape, f32),
        ),
        in_specs=[HBM, HBM, HBM, HBM],
        out_specs=(VMEM, VMEM),
        scratch_shapes=[
            pltpu.VMEM(ids.shape, jnp.int32),
            pltpu.VMEM(own.shape, f32),
            pltpu.VMEM((tokens, width), bf16),
            pltpu.VMEM(returned.shape, bf16),
            pltpu.SemaphoreType.DMA((4,)),
        ],
        compiler_params=params(own.shape[0]),
        cost_estimate=SMALL,
        name="combine",
    )(hbm(ids), hbm(own), hbm(d_out), hbm(returned))


def weight_grad_kernel(half, groups, block, tie_ref, swapped, hidden_ref, near, *refs):
    chips, refs = refs[:half], refs[half:]
    direct, handed, refs = refs[: groups - 2], refs[groups - 2 : 2 * groups - 4], refs[2 * groups - 4 :]
    messages, (out_hbm, hidden, own, rows, out, out_sems) = refs[: groups // 2], refs[groups // 2 :]
    cap, share = rows.shape[1:]
    flight = 2 * half
    slots = flight * cap
    wide, tall = hidden_ref.shape[1] // TILE, share // TILE
    for r in range(flight - 1):
        for q in range(tall):
            rows[r, :, q * TILE : (q + 1) * TILE] = near[r * tall + q]
    hidden[:slots, :] = hidden_ref[...]
    passed = (flight - 1) * tall
    for j in range(1, groups):
        bit = max(b for b in bits_of(groups) if b <= j)
        message, first = messages[j // 2], 0
        if j > 1 and j % 2:
            message, first = near, passed
            passed += messages[j // 2].shape[0]
        for r in range(flight):
            for q in range(wide):
                hidden[
                    j * slots + r * cap : j * slots + (r + 1) * cap, q * TILE : (q + 1) * TILE
                ] = message[first + r * wide + q]
        for q in range(tall):
            own[j - 1, :, q * TILE : (q + 1) * TILE] = message[
                first + flight * wide + (j - bit) * tall + q
            ]
    stores = []
    for n, cols in enumerate(chunks(share, block)):
        grads = [chips[c][0, 0, :, cols] for c in range(half)]
        grads += [swapped[c, 0, :, cols] for c in range(half)]
        for j in range(1, groups):
            grads.append(own[j - 1, :, cols])
            if j == 1:
                grads.append(rows[:, :, cols].reshape(slots - cap, block))
            else:
                grads.append(direct[j - 2][:, :, cols].reshape(slots // 2 - cap, block))
                grads.append(handed[j - 2][:, :, cols].reshape(slots // 2, block))
        out[cols, :] = lax.dot_general(
            jnp.concatenate(grads, axis=0),
            hidden[...],
            (((0,), (0,)), ((), ())),
            preferred_element_type=f32,
        ).astype(bf16)
        stores.append(pltpu.make_async_copy(out.at[cols], out_hbm.at[cols], out_sems.at[n]))
        stores[n].start()
    for copy in stores:
        copy.wait()


def weight_grad(tie, chips, swapped, hidden, near, direct, handed, messages, block=256):
    half, groups, cap, share = swapped.shape
    slots, hid = hidden.shape
    operands = [swapped, hidden, near, *chips, *direct, *handed, *messages]
    return pl.pallas_call(
        functools.partial(weight_grad_kernel, half, groups, block),
        out_shape=pltpu.HBM((share, hid), bf16),
        in_specs=[HBM] + [VMEM] * len(operands),
        out_specs=HBM,
        scratch_shapes=[
            pltpu.VMEM((groups * slots, hid), bf16),
            pltpu.VMEM((groups - 1, cap, share), bf16),
            pltpu.VMEM((2 * half - 1, cap, share), bf16),
            pltpu.VMEM((share, hid), bf16),
            pltpu.SemaphoreType.DMA((share // block,)),
        ],
        compiler_params=params(slots),
        cost_estimate=SMALL,
        name="weight_grad",
    )(hbm(tie), *operands)


def swap(value, axis, j):
    size = lax.axis_size(axis)
    return lax.ppermute(value, axis, [(i, i ^ j) for i in range(size)])


def shards(route_ids, route_probs, capacity, hot_lists, gate_up, w_quant, w_scale, d_out):
    flight = lax.axis_size("expert")
    groups = lax.axis_size("dp")
    gate_up = gate_up[0, 0]
    ids, probs = route_ids.T, route_probs.T
    scale = w_scale.transpose(1, 0, 2)
    own, hidden, *rest = dispatch(
        gate_up, capacity, hot_lists, ids, probs, d_out, flight, groups
    )
    half, bits = flight // 2, bits_of(groups)
    chips = rest[:1] + [swap(rest[c], "expert", 2 * c) for c in range(1, half)]
    messages, early = {}, []
    for bit, message in zip(bits, rest[half:]):
        if bit > 1:
            for j in sorted(messages):
                messages[j ^ bit] = swap(messages[j], "dp", bit)
        messages[bit] = swap(message, "dp", bit)
        early.append(messages[bit])
    passed = [messages[j] for j in range(2, groups, 2)]
    expert_out = forward(scale, hidden, w_quant[0], flight)
    returned = lax.all_to_all(expert_out, "expert", split_axis=0, concat_axis=0, tiled=True)
    sibling, *direct = sort_rows(chips, [hbm(expert_out)] + early)
    swapped = swap(sibling, "expert", 1)
    near, *handed = split(swapped, chips, passed)
    tie = near
    near = swap(near, "dp", 1)
    direct = [swap(direct[j - 2], "dp", j) for j in range(2, groups)]
    handed = [swap(handed[j - 2], "dp", j) for j in range(2, groups)]
    d_gate_up = backward(scale, gate_up, w_quant[0], tie, chips, swapped)
    combined, d_probs = combine(ids, own, d_out, returned)
    d_weight = weight_grad(
        d_probs, chips, swapped, hidden, near, direct, handed, [messages[1]] + passed
    )
    return (combined, d_probs.T, d_gate_up[None, None], d_weight[None])


def solution(mesh):
    placed = (
        P(("dp", "expert"), None),
        P(("dp", "expert"), None),
        P(),
        P("dp", None),
        P("dp", "expert", None, None),
        P("expert", None, None),
        P("expert", None, None),
        P(("dp", "expert"), None),
    )
    return jax.shard_map(
        shards,
        mesh=mesh,
        in_specs=placed,
        out_specs=(
            P(("dp", "expert"), None),
            P(("dp", "expert"), None),
            P("dp", "expert", None, None),
            P("expert", "dp", None),
        ),
        check_vma=False,
    )
```

```python
import functools

import jax
import jax.numpy as jnp
from jax import lax
from jax.experimental import pallas as pl
from jax.experimental.pallas import tpu as pltpu
from jax.sharding import PartitionSpec as P

QB = 128
CAP = 16
TILE = 256

bf16 = jnp.bfloat16
f32 = jnp.float32

SMALL = pl.CostEstimate(flops=1024, bytes_accessed=1024, transcendentals=0)

VMEM = pl.BlockSpec(memory_space=pltpu.VMEM)
ANY = pl.BlockSpec(memory_space=pl.ANY)
HBM = pl.BlockSpec(memory_space=pltpu.HBM)


def params(slots):
    return pltpu.CompilerParams(vmem_limit_bytes=(12 + slots // 32) * 1024 * 1024)


def hbm(value):
    return pltpu.with_memory_space_constraint(value, pltpu.HBM)


def chunks(total, size):
    return [pl.ds(start, size) for start in range(0, total, size)]


def bits_of(groups):
    bits = []
    while groups > 1:
        groups //= 2
        bits.append(groups)
    return bits


def block_place(me, r, flight):
    half = flight // 2
    return me ^ (2 * (r % half) + r // half)


def dispatch_kernel(flight, groups, gate_up_hbm, cap_hbm, hot_hbm, ids_hbm, probs_hbm, dout_hbm, *refs):
    half = flight // 2
    bits = bits_of(groups)
    outs = 2 + half + len(bits)
    own_hbm, hidden_ref, *chips = refs[: 2 + half]
    messages = dict(zip(bits, refs[2 + half : outs]))
    gate_up, cap_ref, hot_ref, ids_ref, probs_ref, dout, own_ref = refs[outs : outs + 7]
    gate_sems, own_sem, small_sems, in_sems = refs[outs + 7 :]
    topk, tokens = ids_ref.shape
    slots = flight * CAP
    me, group = lax.axis_index("expert"), lax.axis_index("dp")
    share = dout_hbm.shape[1] // groups
    hid = hidden_ref.shape[1]
    small = [
        pltpu.make_async_copy(src, dst, small_sems.at[i])
        for i, (src, dst) in enumerate(
            [(ids_hbm, ids_ref), (probs_hbm, probs_ref), (cap_hbm, cap_ref), (hot_hbm, hot_ref)]
        )
    ]
    loads = [
        pltpu.make_async_copy(
            dout_hbm.at[:, pl.ds(pl.multiple_of((group ^ j) * share, share), share)],
            dout.at[j],
            in_sems.at[j],
        )
        for j in range(groups)
    ]
    gates = [
        pltpu.make_async_copy(
            gate_up_hbm.at[pl.ds(pl.multiple_of(block_place(me, r, flight) * CAP, CAP), CAP)],
            gate_up.at[pl.ds(r * CAP, CAP)],
            gate_sems.at[r],
        )
        for r in range(flight)
    ]
    for copy in small + loads + gates:
        copy.start()
    for copy in small:
        copy.wait()
    row = lax.broadcasted_iota(jnp.int32, (slots, 1), 0)
    row_expert = block_place(me, row // CAP, flight)
    row_rank = (row % CAP).astype(f32)
    limit = jnp.zeros((slots, 1), jnp.int32)
    for e in range(flight):
        hot = hot_ref[0, 0] == e
        for h in range(1, hot_ref.shape[1]):
            hot = jnp.logical_or(hot, hot_ref[0, h] == e)
        limit = jnp.where(row_expert == e, jnp.where(hot, CAP, cap_ref[e]), limit)
    limit = limit.astype(f32)
    named = jnp.zeros((slots, tokens), f32)
    weight = jnp.zeros((slots, tokens), f32)
    for k in range(topk):
        hit = ids_ref[k : k + 1, :] == row_expert
        named = jnp.where(hit, 1.0, named)
        weight = jnp.where(hit, probs_ref[k : k + 1, :], weight)
    earlier = lax.broadcasted_iota(jnp.int32, (tokens, tokens), 0)
    later = lax.broadcasted_iota(jnp.int32, (tokens, tokens), 1)
    before = (earlier < later).astype(f32).astype(bf16)
    rank = jnp.dot(named.astype(bf16), before, preferred_element_type=f32)
    owns = (named > 0.0) & (rank == row_rank) & (rank < limit)
    own_weight = jnp.where(owns, weight, 0.0)
    own_ref[...] = own_weight
    own_copy = pltpu.make_async_copy(own_ref, own_hbm, own_sem)
    own_copy.start()
    owner = jnp.where(owns, 1.0, 0.0).astype(bf16)
    slot_weight = jnp.sum(own_weight, axis=1, keepdims=True)
    for copy in loads:
        copy.wait()
    for j in range(groups):
        part = jnp.dot(owner, dout[j], preferred_element_type=f32)
        part = (part * slot_weight).astype(bf16)
        for r in range(flight):
            chips[r % half][r // half, j] = part[r * CAP : (r + 1) * CAP, :]
        if j in bits:
            for q in range(share // TILE):
                at = flight * (hid // TILE) + q
                messages[j][at] = part[:CAP, q * TILE : (q + 1) * TILE]
    for copy in gates:
        copy.wait()
    for r in range(flight):
        at = slice(r * CAP, (r + 1) * CAP)
        gate = gate_up[at, :hid].astype(f32)
        up = gate_up[at, hid:].astype(f32)
        block = (gate * jax.nn.sigmoid(gate) * up).astype(bf16)
        hidden_ref[at, :] = block
        for bit in bits:
            for q in range(hid // TILE):
                messages[bit][r * (hid // TILE) + q] = block[:, q * TILE : (q + 1) * TILE]
    own_copy.wait()


def dispatch(gate_up, capacity, hot_row, ids, probs, d_out, flight, groups):
    tokens, width = d_out.shape
    rows, double = gate_up.shape
    slots = flight * CAP
    share = width // groups
    half = flight // 2
    return pl.pallas_call(
        functools.partial(dispatch_kernel, flight, groups),
        out_shape=(pltpu.HBM((slots, tokens), f32), pltpu.VMEM((rows, double // 2), bf16))
        + (pltpu.VMEM((2, groups, CAP, share), bf16),) * half
        + tuple(
            pltpu.VMEM((flight * (double // 2 // TILE) + share // TILE, CAP, TILE), bf16)
            for _ in bits_of(groups)
        ),
        in_specs=[HBM] * 6,
        out_specs=(HBM, VMEM) + (VMEM,) * (half + len(bits_of(groups))),
        scratch_shapes=[
            pltpu.VMEM((rows, double), bf16),
            pltpu.SMEM(capacity.shape, jnp.int32),
            pltpu.SMEM(hot_row.shape, jnp.int32),
            pltpu.VMEM(ids.shape, jnp.int32),
            pltpu.VMEM(probs.shape, f32),
            pltpu.VMEM((groups, tokens, share), bf16),
            pltpu.VMEM((slots, tokens), f32),
            pltpu.SemaphoreType.DMA((flight,)),
            pltpu.SemaphoreType.DMA,
            pltpu.SemaphoreType.DMA((4,)),
            pltpu.SemaphoreType.DMA((groups,)),
        ],
        compiler_params=params(slots),
        cost_estimate=SMALL,
        name="dispatch",
    )(hbm(gate_up), hbm(capacity), hbm(hot_row), hbm(ids), hbm(probs), hbm(d_out))


def forward_kernel(
    flight, block, hidden_ref, scale_hbm, quant_hbm, out_hbm,
    scale, hidden, quant, out, scale_sem, in_sems, out_sems
):
    steps, hid, _ = quant.shape
    me = lax.axis_index("expert")
    loads = [
        pltpu.make_async_copy(quant_hbm.at[:, pl.ds(c * block, block)], quant.at[c], in_sems.at[c])
        for c in range(steps)
    ]
    small = pltpu.make_async_copy(scale_hbm, scale, scale_sem)
    for copy in [small] + loads:
        copy.start()
    for r in range(flight):
        place = pl.multiple_of(block_place(me, r, flight) * CAP, CAP)
        hidden[pl.ds(place, CAP), :] = hidden_ref[pl.ds(r * CAP, CAP), :]
    small.wait()
    stores = []
    for c in range(steps):
        cols = pl.ds(c * block, block)
        loads[c].wait()
        total = [None] * (block // QB)
        for i in range(hid // QB):
            part = jnp.dot(
                hidden[:, i * QB : (i + 1) * QB],
                quant[c, i * QB : (i + 1) * QB, :],
                preferred_element_type=f32,
            )
            for j in range(block // QB):
                scaled = part[:, j * QB : (j + 1) * QB] * scale[i, 0, c * (block // QB) + j]
                total[j] = scaled if i == 0 else total[j] + scaled
        for j in range(block // QB):
            at = pl.ds(c * block + j * QB, QB)
            out[:, :, at] = total[j].astype(bf16).reshape(flight, CAP, QB)
        stores.append(
            pltpu.make_async_copy(out.at[:, :, cols], out_hbm.at[:, :, cols], out_sems.at[c])
        )
        stores[c].start()
    for copy in stores:
        copy.wait()


def forward(scale, hidden, quant, flight, block=512):
    hid, width = quant.shape
    steps = width // block
    return pl.pallas_call(
        functools.partial(forward_kernel, flight, block),
        out_shape=pltpu.HBM((flight, CAP, width), bf16),
        in_specs=[VMEM, HBM, HBM],
        out_specs=HBM,
        scratch_shapes=[
            pltpu.SMEM(scale.shape, f32),
            pltpu.VMEM(hidden.shape, bf16),
            pltpu.VMEM((steps, hid, block), bf16),
            pltpu.VMEM((flight, CAP, width), bf16),
            pltpu.SemaphoreType.DMA,
            pltpu.SemaphoreType.DMA((steps,)),
            pltpu.SemaphoreType.DMA((steps,)),
        ],
        compiler_params=params(flight * CAP),
        cost_estimate=SMALL,
        name="expert_forward",
    )(hidden, hbm(scale), hbm(quant))


def sort_kernel(half, groups, ties, *refs):
    chips, (sibling, *pieces) = refs[:half], refs[half + ties :]
    for c in range(half):
        sibling[c] = chips[c][1]
        for j in range(2, groups):
            if j not in bits_of(groups):
                pieces[j - 2][c] = chips[c][0, j]
            elif c:
                pieces[j - 2][c - 1] = chips[c][0, j]


def sort_rows(chips, ties):
    half = len(chips)
    _, groups, cap, share = chips[0].shape
    return pl.pallas_call(
        functools.partial(sort_kernel, half, groups, len(ties)),
        out_shape=(pltpu.VMEM((half, groups, cap, share), bf16),)
        + tuple(
            pltpu.VMEM((half - (j in bits_of(groups)), cap, share), bf16) for j in range(2, groups)
        ),
        in_specs=[VMEM] * half + [ANY] * len(ties),
        out_specs=(VMEM,) * (groups - 1),
        compiler_params=params(2 * half * CAP),
        cost_estimate=SMALL,
        name="sort_rows",
    )(*chips, *ties)


def split_kernel(half, groups, count, swapped, *refs):
    chips, messages = refs[: half - 1], refs[half - 1 : half - 1 + count]
    near, *pieces = refs[half - 1 + count :]
    wide = swapped.shape[3] // TILE
    for j in range(2, groups):
        pieces[j - 2][...] = swapped[:, j]
    for r in range(2 * half - 1):
        for q in range(wide):
            cols = slice(q * TILE, (q + 1) * TILE)
            near[r * wide + q] = (
                chips[r][0, 1, :, cols] if r < half - 1 else swapped[r - half + 1, 1, :, cols]
            )
    first = (2 * half - 1) * wide
    for message in messages:
        near[first : first + message.shape[0]] = message[...]
        first += message.shape[0]


def split(swapped, chips, messages):
    half, groups, cap, share = swapped.shape
    tiles = (2 * half - 1) * (share // TILE) + sum(message.shape[0] for message in messages)
    return pl.pallas_call(
        functools.partial(split_kernel, half, groups, len(messages)),
        out_shape=(pltpu.VMEM((tiles, cap, TILE), bf16),)
        + (pltpu.VMEM((half, cap, share), bf16),) * (groups - 2),
        in_specs=[VMEM] * (half + len(messages)),
        out_specs=(VMEM,) * (groups - 1),
        compiler_params=params(2 * half * CAP),
        cost_estimate=SMALL,
        name="split",
    )(swapped, *chips[1:], *messages)


def backward_kernel(flight, groups, ties, scale_hbm, gate_up_hbm, quant_hbm, *refs):
    half = flight // 2
    swapped, *refs = refs[ties:]
    chips, out_hbm = refs[:half], refs[half]
    scale, gate_up, rows, quant, acc, out = refs[half + 1 : half + 7]
    scale_sem, gate_sems, in_sems, out_sems = refs[half + 7 :]
    me, group = lax.axis_index("expert"), lax.axis_index("dp")
    slots, hid = acc.shape
    share = quant.shape[2]

    def place(r):
        return pl.ds(pl.multiple_of(block_place(me, r, flight) * CAP, CAP), CAP)

    loads = [
        pltpu.make_async_copy(
            quant_hbm.at[:, pl.ds(pl.multiple_of((group ^ j) * share, share), share)],
            quant.at[j],
            in_sems.at[j],
        )
        for j in range(groups)
    ]
    gates = [
        pltpu.make_async_copy(
            gate_up_hbm.at[place(r)], gate_up.at[pl.ds(r * CAP, CAP)], gate_sems.at[r]
        )
        for r in range(flight)
    ]
    small = pltpu.make_async_copy(scale_hbm, scale, scale_sem)
    for copy in [small] + loads + gates:
        copy.start()
    for c in range(half):
        rows[:, c * CAP : (c + 1) * CAP, :] = chips[c][0]
        rows[:, (half + c) * CAP : (half + c + 1) * CAP, :] = swapped[c]
    small.wait()
    for j in range(groups):
        loads[j].wait()
        for b in range(share // QB):
            cols = slice(b * QB, (b + 1) * QB)
            part = lax.dot_general(
                rows[j, :, cols],
                quant[j, :, cols],
                (((1,), (1,)), ((), ())),
                preferred_element_type=f32,
            )
            for i in range(hid // QB):
                at = (slice(None), slice(i * QB, (i + 1) * QB))
                scaled = part[at] * scale[i, 0, (group ^ j) * (share // QB) + b]
                if j == 0 and b == 0:
                    acc[at] = scaled
                else:
                    acc[at] += scaled
    for copy in gates:
        copy.wait()
    gate = gate_up[:, :hid].astype(f32)
    up = gate_up[:, hid:].astype(f32)
    sig = jax.nn.sigmoid(gate)
    d_hidden = acc[...]
    out[:, :hid] = (d_hidden * up * sig * (1.0 + gate * (1.0 - sig))).astype(bf16)
    out[:, hid:] = (d_hidden * (gate * sig)).astype(bf16)
    stores = [
        pltpu.make_async_copy(out.at[pl.ds(r * CAP, CAP)], out_hbm.at[place(r)], out_sems.at[r])
        for r in range(flight)
    ]
    for copy in stores:
        copy.start()
    for copy in stores:
        copy.wait()


def backward(scale, gate_up, quant, ties, chips, swapped):
    slots, double = gate_up.shape
    hid, width = quant.shape
    half, groups, cap, share = swapped.shape
    flight = 2 * half
    return pl.pallas_call(
        functools.partial(backward_kernel, flight, groups, len(ties)),
        out_shape=pltpu.HBM((slots, double), bf16),
        in_specs=[HBM] * 3 + [ANY] * len(ties) + [VMEM] * (1 + half),
        out_specs=HBM,
        scratch_shapes=[
            pltpu.SMEM(scale.shape, f32),
            pltpu.VMEM((slots, double), bf16),
            pltpu.VMEM((groups, slots, share), bf16),
            pltpu.VMEM((groups, hid, share), bf16),
            pltpu.VMEM((slots, hid), f32),
            pltpu.VMEM((slots, double), bf16),
            pltpu.SemaphoreType.DMA,
            pltpu.SemaphoreType.DMA((flight,)),
            pltpu.SemaphoreType.DMA((groups,)),
            pltpu.SemaphoreType.DMA((flight,)),
        ],
        compiler_params=params(slots),
        cost_estimate=SMALL,
        name="expert_backward",
    )(hbm(scale), hbm(gate_up), hbm(quant), *ties, swapped, *chips)


def combine_kernel(
    block, ids_hbm, own_hbm, dout_hbm, ret_hbm, out_ref, dprobs_ref, ids_ref, own_ref, dout, ret_ref, sems
):
    copies = [
        pltpu.make_async_copy(ids_hbm, ids_ref, sems.at[0]),
        pltpu.make_async_copy(own_hbm, own_ref, sems.at[1]),
        pltpu.make_async_copy(dout_hbm, dout, sems.at[2]),
        pltpu.make_async_copy(ret_hbm, ret_ref, sems.at[3]),
    ]
    for copy in copies:
        copy.start()
    topk, tokens = ids_ref.shape
    slots = own_ref.shape[0]
    width = dout.shape[1]
    flight = slots // CAP
    me = lax.axis_index("expert")
    copies[1].wait()
    own = own_ref[...]
    turned = own.T
    high = turned.astype(bf16)
    low = (turned - high.astype(f32)).astype(bf16)
    total = jnp.zeros((slots, tokens), f32)
    for copy in (copies[0], copies[2], copies[3]):
        copy.wait()
    for cols in chunks(width, block):
        here = jnp.concatenate(
            [ret_ref[block_place(me, r, flight), :, cols] for r in range(flight)], axis=0
        )
        out = jnp.dot(high, here, preferred_element_type=f32)
        out = out + jnp.dot(low, here, preferred_element_type=f32)
        out_ref[:, cols] = out.astype(bf16)
        total = total + lax.dot_general(
            here, dout[:, cols], (((1,), (1,)), ((), ())), preferred_element_type=f32
        )
    inner = jnp.where(own > 0.0, total, 0.0)
    row_expert = block_place(me, lax.broadcasted_iota(jnp.int32, (slots, 1), 0) // CAP, flight)
    for k in range(topk):
        mine = jnp.where(ids_ref[k : k + 1, :] == row_expert, inner, 0.0)
        dprobs_ref[k : k + 1, :] = jnp.sum(mine, axis=0, keepdims=True)


def combine(ids, own, d_out, returned, block=1024):
    tokens, width = d_out.shape
    return pl.pallas_call(
        functools.partial(combine_kernel, block),
        out_shape=(
            pltpu.HBM((tokens, width), bf16),
            pltpu.HBM(ids.shape, f32),
        ),
        in_specs=[HBM, HBM, HBM, HBM],
        out_specs=(VMEM, VMEM),
        scratch_shapes=[
            pltpu.VMEM(ids.shape, jnp.int32),
            pltpu.VMEM(own.shape, f32),
            pltpu.VMEM((tokens, width), bf16),
            pltpu.VMEM(returned.shape, bf16),
            pltpu.SemaphoreType.DMA((4,)),
        ],
        compiler_params=params(own.shape[0]),
        cost_estimate=SMALL,
        name="combine",
    )(hbm(ids), hbm(own), hbm(d_out), hbm(returned))


def weight_grad_kernel(half, groups, block, tie_ref, swapped, hidden_ref, near, *refs):
    chips, refs = refs[:half], refs[half:]
    direct, handed, refs = refs[: groups - 2], refs[groups - 2 : 2 * groups - 4], refs[2 * groups - 4 :]
    messages, (out_hbm, hidden, own, rows, out, out_sems) = refs[: groups // 2], refs[groups // 2 :]
    cap, share = rows.shape[1:]
    flight = 2 * half
    slots = flight * cap
    wide, tall = hidden_ref.shape[1] // TILE, share // TILE
    for r in range(flight - 1):
        for q in range(tall):
            rows[r, :, q * TILE : (q + 1) * TILE] = near[r * tall + q]
    hidden[:slots, :] = hidden_ref[...]
    passed = (flight - 1) * tall
    for j in range(1, groups):
        message, first = messages[j // 2], 0
        if j > 1 and j % 2:
            message, first = near, passed
            passed += messages[j // 2].shape[0]
        for r in range(flight):
            for q in range(wide):
                hidden[
                    j * slots + r * cap : j * slots + (r + 1) * cap, q * TILE : (q + 1) * TILE
                ] = message[first + r * wide + q]
        for q in range(tall if j in bits_of(groups) else 0):
            own[j - 1, :, q * TILE : (q + 1) * TILE] = message[first + flight * wide + q]
    stores = []
    for n, cols in enumerate(chunks(share, block)):
        grads = [chips[c][0, 0, :, cols] for c in range(half)]
        grads += [swapped[c, 0, :, cols] for c in range(half)]
        for j in range(1, groups):
            if j in bits_of(groups):
                grads.append(own[j - 1, :, cols])
            if j == 1:
                grads.append(rows[:, :, cols].reshape(slots - cap, block))
            else:
                count = direct[j - 2].shape[0] * cap
                grads.append(direct[j - 2][:, :, cols].reshape(count, block))
                grads.append(handed[j - 2][:, :, cols].reshape(slots // 2, block))
        out[cols, :] = lax.dot_general(
            jnp.concatenate(grads, axis=0),
            hidden[...],
            (((0,), (0,)), ((), ())),
            preferred_element_type=f32,
        ).astype(bf16)
        stores.append(pltpu.make_async_copy(out.at[cols], out_hbm.at[cols], out_sems.at[n]))
        stores[n].start()
    for copy in stores:
        copy.wait()


def weight_grad(tie, chips, swapped, hidden, near, direct, handed, messages, block=256):
    half, groups, cap, share = swapped.shape
    slots, hid = hidden.shape
    operands = [swapped, hidden, near, *chips, *direct, *handed, *messages]
    return pl.pallas_call(
        functools.partial(weight_grad_kernel, half, groups, block),
        out_shape=pltpu.HBM((share, hid), bf16),
        in_specs=[HBM] + [VMEM] * len(operands),
        out_specs=HBM,
        scratch_shapes=[
            pltpu.VMEM((groups * slots, hid), bf16),
            pltpu.VMEM((groups - 1, cap, share), bf16),
            pltpu.VMEM((2 * half - 1, cap, share), bf16),
            pltpu.VMEM((share, hid), bf16),
            pltpu.SemaphoreType.DMA((share // block,)),
        ],
        compiler_params=params(slots),
        cost_estimate=SMALL,
        name="weight_grad",
    )(hbm(tie), *operands)


def swap(value, axis, j):
    size = lax.axis_size(axis)
    return lax.ppermute(value, axis, [(i, i ^ j) for i in range(size)])


def shards(route_ids, route_probs, capacity, hot_lists, gate_up, w_quant, w_scale, d_out):
    flight = lax.axis_size("expert")
    groups = lax.axis_size("dp")
    gate_up = gate_up[0, 0]
    ids, probs = route_ids.T, route_probs.T
    scale = w_scale.transpose(1, 0, 2)
    own, hidden, *rest = dispatch(
        gate_up, capacity, hot_lists, ids, probs, d_out, flight, groups
    )
    half, bits = flight // 2, bits_of(groups)
    chips = rest[:1] + [swap(rest[c], "expert", 2 * c) for c in range(1, half)]
    messages, early = {}, []
    for bit, message in zip(bits, rest[half:]):
        if bit > 1:
            for j in sorted(messages):
                messages[j ^ bit] = swap(messages[j], "dp", bit)
        messages[bit] = swap(message, "dp", bit)
        early.append(messages[bit])
    passed = [messages[j] for j in range(2, groups, 2)]
    expert_out = forward(scale, hidden, w_quant[0], flight)
    returned = lax.all_to_all(expert_out, "expert", split_axis=0, concat_axis=0, tiled=True)
    sibling, *direct = sort_rows(chips, [hbm(expert_out)] + early)
    swapped = swap(sibling, "expert", 1)
    near, *handed = split(swapped, chips, passed)
    tie = near
    near = swap(near, "dp", 1)
    direct = [swap(direct[j - 2], "dp", j) for j in range(2, groups)]
    handed = [swap(handed[j - 2], "dp", j) for j in range(2, groups)]
    d_gate_up = backward(scale, gate_up, w_quant[0], [tie] + direct, chips, swapped)
    combined, d_probs = combine(ids, own, d_out, returned)
    d_weight = weight_grad(
        d_probs, chips, swapped, hidden, near, direct, handed, [messages[1]] + passed
    )
    return (combined, d_probs.T, d_gate_up[None, None], d_weight[None])


def solution(mesh):
    placed = (
        P(("dp", "expert"), None),
        P(("dp", "expert"), None),
        P(),
        P("dp", None),
        P("dp", "expert", None, None),
        P("expert", None, None),
        P("expert", None, None),
        P(("dp", "expert"), None),
    )
    return jax.shard_map(
        shards,
        mesh=mesh,
        in_specs=placed,
        out_specs=(
            P(("dp", "expert"), None),
            P(("dp", "expert"), None),
            P("dp", "expert", None, None),
            P("expert", "dp", None),
        ),
        check_vma=False,
    )
```

```python
import functools

import jax
import jax.numpy as jnp
from jax import lax
from jax.experimental import pallas as pl
from jax.experimental.pallas import tpu as pltpu
from jax.sharding import PartitionSpec as P

QB = 128
CAP = 16
TILE = 256

bf16 = jnp.bfloat16
f32 = jnp.float32

SMALL = pl.CostEstimate(flops=1024, bytes_accessed=1024, transcendentals=0)

VMEM = pl.BlockSpec(memory_space=pltpu.VMEM)
ANY = pl.BlockSpec(memory_space=pl.ANY)
HBM = pl.BlockSpec(memory_space=pltpu.HBM)


def params(slots):
    return pltpu.CompilerParams(vmem_limit_bytes=(12 + slots // 32) * 1024 * 1024)


def hbm(value):
    return pltpu.with_memory_space_constraint(value, pltpu.HBM)


def chunks(total, size):
    return [pl.ds(start, size) for start in range(0, total, size)]


def bits_of(groups):
    bits = []
    while groups > 1:
        groups //= 2
        bits.append(groups)
    return bits


def block_place(me, r, flight):
    half = flight // 2
    return me ^ (2 * (r % half) + r // half)


def dispatch_kernel(flight, groups, gate_up_hbm, cap_hbm, hot_hbm, ids_hbm, probs_hbm, dout_hbm, *refs):
    half = flight // 2
    bits = bits_of(groups)
    outs = 2 + half + len(bits)
    own_hbm, hidden_ref, *chips = refs[: 2 + half]
    messages = dict(zip(bits, refs[2 + half : outs]))
    gate_up, cap_ref, hot_ref, ids_ref, probs_ref, dout, own_ref = refs[outs : outs + 7]
    gate_sems, own_sem, small_sems, in_sems = refs[outs + 7 :]
    topk, tokens = ids_ref.shape
    slots = flight * CAP
    me, group = lax.axis_index("expert"), lax.axis_index("dp")
    share = dout_hbm.shape[1] // groups
    hid = hidden_ref.shape[1]
    small = [
        pltpu.make_async_copy(src, dst, small_sems.at[i])
        for i, (src, dst) in enumerate(
            [(ids_hbm, ids_ref), (probs_hbm, probs_ref), (cap_hbm, cap_ref), (hot_hbm, hot_ref)]
        )
    ]
    loads = [
        pltpu.make_async_copy(
            dout_hbm.at[:, pl.ds(pl.multiple_of((group ^ j) * share, share), share)],
            dout.at[j],
            in_sems.at[j],
        )
        for j in range(groups)
    ]
    gates = [
        pltpu.make_async_copy(
            gate_up_hbm.at[pl.ds(pl.multiple_of(block_place(me, r, flight) * CAP, CAP), CAP)],
            gate_up.at[pl.ds(r * CAP, CAP)],
            gate_sems.at[r],
        )
        for r in range(flight)
    ]
    for copy in small + loads + gates:
        copy.start()
    for copy in small:
        copy.wait()
    row = lax.broadcasted_iota(jnp.int32, (slots, 1), 0)
    row_expert = block_place(me, row // CAP, flight)
    row_rank = (row % CAP).astype(f32)
    limit = jnp.zeros((slots, 1), jnp.int32)
    for e in range(flight):
        hot = hot_ref[0, 0] == e
        for h in range(1, hot_ref.shape[1]):
            hot = jnp.logical_or(hot, hot_ref[0, h] == e)
        limit = jnp.where(row_expert == e, jnp.where(hot, CAP, cap_ref[e]), limit)
    limit = limit.astype(f32)
    named = jnp.zeros((slots, tokens), f32)
    weight = jnp.zeros((slots, tokens), f32)
    for k in range(topk):
        hit = ids_ref[k : k + 1, :] == row_expert
        named = jnp.where(hit, 1.0, named)
        weight = jnp.where(hit, probs_ref[k : k + 1, :], weight)
    earlier = lax.broadcasted_iota(jnp.int32, (tokens, tokens), 0)
    later = lax.broadcasted_iota(jnp.int32, (tokens, tokens), 1)
    before = (earlier < later).astype(f32).astype(bf16)
    rank = jnp.dot(named.astype(bf16), before, preferred_element_type=f32)
    owns = (named > 0.0) & (rank == row_rank) & (rank < limit)
    own_weight = jnp.where(owns, weight, 0.0)
    own_ref[...] = own_weight
    own_copy = pltpu.make_async_copy(own_ref, own_hbm, own_sem)
    own_copy.start()
    owner = jnp.where(owns, 1.0, 0.0).astype(bf16)
    slot_weight = jnp.sum(own_weight, axis=1, keepdims=True)
    for copy in loads:
        copy.wait()
    for j in range(groups):
        part = jnp.dot(owner, dout[j], preferred_element_type=f32)
        part = (part * slot_weight).astype(bf16)
        for r in range(flight):
            chips[r % half][r // half, j] = part[r * CAP : (r + 1) * CAP, :]
        for bit in bits:
            if bit <= j < 2 * bit:
                first = flight * (hid // TILE) + (j - bit) * (share // TILE)
                for q in range(share // TILE):
                    messages[bit][first + q] = part[:CAP, q * TILE : (q + 1) * TILE]
    for copy in gates:
        copy.wait()
    for r in range(flight):
        at = slice(r * CAP, (r + 1) * CAP)
        gate = gate_up[at, :hid].astype(f32)
        up = gate_up[at, hid:].astype(f32)
        block = (gate * jax.nn.sigmoid(gate) * up).astype(bf16)
        hidden_ref[at, :] = block
        for bit in bits:
            for q in range(hid // TILE):
                messages[bit][r * (hid // TILE) + q] = block[:, q * TILE : (q + 1) * TILE]
    own_copy.wait()


def dispatch(gate_up, capacity, hot_row, ids, probs, d_out, flight, groups):
    tokens, width = d_out.shape
    rows, double = gate_up.shape
    slots = flight * CAP
    share = width // groups
    half = flight // 2
    return pl.pallas_call(
        functools.partial(dispatch_kernel, flight, groups),
        out_shape=(pltpu.HBM((slots, tokens), f32), pltpu.VMEM((rows, double // 2), bf16))
        + (pltpu.VMEM((2, groups, CAP, share), bf16),) * half
        + tuple(
            pltpu.VMEM((flight * (double // 2 // TILE) + bit * (share // TILE), CAP, TILE), bf16)
            for bit in bits_of(groups)
        ),
        in_specs=[HBM] * 6,
        out_specs=(HBM, VMEM) + (VMEM,) * (half + len(bits_of(groups))),
        scratch_shapes=[
            pltpu.VMEM((rows, double), bf16),
            pltpu.SMEM(capacity.shape, jnp.int32),
            pltpu.SMEM(hot_row.shape, jnp.int32),
            pltpu.VMEM(ids.shape, jnp.int32),
            pltpu.VMEM(probs.shape, f32),
            pltpu.VMEM((groups, tokens, share), bf16),
            pltpu.VMEM((slots, tokens), f32),
            pltpu.SemaphoreType.DMA((flight,)),
            pltpu.SemaphoreType.DMA,
            pltpu.SemaphoreType.DMA((4,)),
            pltpu.SemaphoreType.DMA((groups,)),
        ],
        compiler_params=params(slots),
        cost_estimate=SMALL,
        name="dispatch",
    )(hbm(gate_up), hbm(capacity), hbm(hot_row), hbm(ids), hbm(probs), hbm(d_out))


def forward_kernel(
    flight, block, hidden_ref, scale_hbm, quant_hbm, out_hbm,
    scale, hidden, quant, out, scale_sem, in_sems, out_sems
):
    steps, hid, _ = quant.shape
    me = lax.axis_index("expert")
    loads = [
        pltpu.make_async_copy(quant_hbm.at[:, pl.ds(c * block, block)], quant.at[c], in_sems.at[c])
        for c in range(steps)
    ]
    small = pltpu.make_async_copy(scale_hbm, scale, scale_sem)
    for copy in [small] + loads:
        copy.start()
    for r in range(flight):
        place = pl.multiple_of(block_place(me, r, flight) * CAP, CAP)
        hidden[pl.ds(place, CAP), :] = hidden_ref[pl.ds(r * CAP, CAP), :]
    small.wait()
    stores = []
    for c in range(steps):
        cols = pl.ds(c * block, block)
        loads[c].wait()
        total = [None] * (block // QB)
        for i in range(hid // QB):
            part = jnp.dot(
                hidden[:, i * QB : (i + 1) * QB],
                quant[c, i * QB : (i + 1) * QB, :],
                preferred_element_type=f32,
            )
            for j in range(block // QB):
                scaled = part[:, j * QB : (j + 1) * QB] * scale[i, 0, c * (block // QB) + j]
                total[j] = scaled if i == 0 else total[j] + scaled
        for j in range(block // QB):
            at = pl.ds(c * block + j * QB, QB)
            out[:, :, at] = total[j].astype(bf16).reshape(flight, CAP, QB)
        stores.append(
            pltpu.make_async_copy(out.at[:, :, cols], out_hbm.at[:, :, cols], out_sems.at[c])
        )
        stores[c].start()
    for copy in stores:
        copy.wait()


def forward(scale, hidden, quant, flight, block=512):
    hid, width = quant.shape
    steps = width // block
    return pl.pallas_call(
        functools.partial(forward_kernel, flight, block),
        out_shape=pltpu.HBM((flight, CAP, width), bf16),
        in_specs=[VMEM, HBM, HBM],
        out_specs=HBM,
        scratch_shapes=[
            pltpu.SMEM(scale.shape, f32),
            pltpu.VMEM(hidden.shape, bf16),
            pltpu.VMEM((steps, hid, block), bf16),
            pltpu.VMEM((flight, CAP, width), bf16),
            pltpu.SemaphoreType.DMA,
            pltpu.SemaphoreType.DMA((steps,)),
            pltpu.SemaphoreType.DMA((steps,)),
        ],
        compiler_params=params(flight * CAP),
        cost_estimate=SMALL,
        name="expert_forward",
    )(hidden, hbm(scale), hbm(quant))


def sibling_kernel(half, *refs):
    chips, out_ref = refs[:half], refs[-1]
    for c in range(half):
        out_ref[c] = chips[c][1]


def sibling_rows(chips, ties):
    half = len(chips)
    return pl.pallas_call(
        functools.partial(sibling_kernel, half),
        out_shape=pltpu.VMEM((half,) + chips[0].shape[1:], bf16),
        in_specs=[VMEM] * half + [ANY] * len(ties),
        out_specs=VMEM,
        compiler_params=params(2 * half * CAP),
        cost_estimate=SMALL,
        name="sibling_rows",
    )(*chips, *ties)


def split_kernel(half, groups, *refs):
    chips, swapped, pieces = refs[: half - 1], refs[half - 1], refs[1 - groups :]
    for j in range(1, groups):
        for c in range(half):
            if c:
                pieces[j - 1][c - 1] = chips[c - 1][0, j]
            pieces[j - 1][half - 1 + c] = swapped[c, j]


def split(chips, swapped):
    half, groups, cap, share = swapped.shape
    return pl.pallas_call(
        functools.partial(split_kernel, half, groups),
        out_shape=(pltpu.VMEM((2 * half - 1, cap, share), bf16),) * (groups - 1),
        in_specs=[VMEM] * half,
        out_specs=(VMEM,) * (groups - 1),
        compiler_params=params(2 * half * CAP),
        cost_estimate=SMALL,
        name="split",
    )(*chips[1:], swapped)


def backward_kernel(flight, groups, scale_hbm, gate_up_hbm, quant_hbm, tie_ref, swapped, *refs):
    half = flight // 2
    chips, out_hbm = refs[:half], refs[half]
    scale, gate_up, rows, quant, acc, out = refs[half + 1 : half + 7]
    scale_sem, gate_sems, in_sems, out_sems = refs[half + 7 :]
    me, group = lax.axis_index("expert"), lax.axis_index("dp")
    slots, hid = acc.shape
    share = quant.shape[2]

    def place(r):
        return pl.ds(pl.multiple_of(block_place(me, r, flight) * CAP, CAP), CAP)

    loads = [
        pltpu.make_async_copy(
            quant_hbm.at[:, pl.ds(pl.multiple_of((group ^ j) * share, share), share)],
            quant.at[j],
            in_sems.at[j],
        )
        for j in range(groups)
    ]
    gates = [
        pltpu.make_async_copy(
            gate_up_hbm.at[place(r)], gate_up.at[pl.ds(r * CAP, CAP)], gate_sems.at[r]
        )
        for r in range(flight)
    ]
    small = pltpu.make_async_copy(scale_hbm, scale, scale_sem)
    for copy in [small] + loads + gates:
        copy.start()
    for c in range(half):
        rows[:, c * CAP : (c + 1) * CAP, :] = chips[c][0]
        rows[:, (half + c) * CAP : (half + c + 1) * CAP, :] = swapped[c]
    small.wait()
    for j in range(groups):
        loads[j].wait()
        for b in range(share // QB):
            cols = slice(b * QB, (b + 1) * QB)
            part = lax.dot_general(
                rows[j, :, cols],
                quant[j, :, cols],
                (((1,), (1,)), ((), ())),
                preferred_element_type=f32,
            )
            for i in range(hid // QB):
                at = (slice(None), slice(i * QB, (i + 1) * QB))
                scaled = part[at] * scale[i, 0, (group ^ j) * (share // QB) + b]
                if j == 0 and b == 0:
                    acc[at] = scaled
                else:
                    acc[at] += scaled
    for copy in gates:
        copy.wait()
    gate = gate_up[:, :hid].astype(f32)
    up = gate_up[:, hid:].astype(f32)
    sig = jax.nn.sigmoid(gate)
    d_hidden = acc[...]
    out[:, :hid] = (d_hidden * up * sig * (1.0 + gate * (1.0 - sig))).astype(bf16)
    out[:, hid:] = (d_hidden * (gate * sig)).astype(bf16)
    stores = [
        pltpu.make_async_copy(out.at[pl.ds(r * CAP, CAP)], out_hbm.at[place(r)], out_sems.at[r])
        for r in range(flight)
    ]
    for copy in stores:
        copy.start()
    for copy in stores:
        copy.wait()


def backward(scale, gate_up, quant, tie, chips, swapped):
    slots, double = gate_up.shape
    hid, width = quant.shape
    half, groups, cap, share = swapped.shape
    flight = 2 * half
    return pl.pallas_call(
        functools.partial(backward_kernel, flight, groups),
        out_shape=pltpu.HBM((slots, double), bf16),
        in_specs=[HBM, HBM, HBM, ANY] + [VMEM] * (1 + half),
        out_specs=HBM,
        scratch_shapes=[
            pltpu.SMEM(scale.shape, f32),
            pltpu.VMEM((slots, double), bf16),
            pltpu.VMEM((groups, slots, share), bf16),
            pltpu.VMEM((groups, hid, share), bf16),
            pltpu.VMEM((slots, hid), f32),
            pltpu.VMEM((slots, double), bf16),
            pltpu.SemaphoreType.DMA,
            pltpu.SemaphoreType.DMA((flight,)),
            pltpu.SemaphoreType.DMA((groups,)),
            pltpu.SemaphoreType.DMA((flight,)),
        ],
        compiler_params=params(slots),
        cost_estimate=SMALL,
        name="expert_backward",
    )(hbm(scale), hbm(gate_up), hbm(quant), tie, swapped, *chips)


def combine_kernel(
    block, ids_hbm, own_hbm, dout_hbm, ret_hbm, out_ref, dprobs_ref, ids_ref, own_ref, dout, ret_ref, sems
):
    copies = [
        pltpu.make_async_copy(ids_hbm, ids_ref, sems.at[0]),
        pltpu.make_async_copy(own_hbm, own_ref, sems.at[1]),
        pltpu.make_async_copy(dout_hbm, dout, sems.at[2]),
        pltpu.make_async_copy(ret_hbm, ret_ref, sems.at[3]),
    ]
    for copy in copies:
        copy.start()
    topk, tokens = ids_ref.shape
    slots = own_ref.shape[0]
    width = dout.shape[1]
    flight = slots // CAP
    me = lax.axis_index("expert")
    copies[1].wait()
    own = own_ref[...]
    turned = own.T
    high = turned.astype(bf16)
    low = (turned - high.astype(f32)).astype(bf16)
    total = jnp.zeros((slots, tokens), f32)
    for copy in (copies[0], copies[2], copies[3]):
        copy.wait()
    for cols in chunks(width, block):
        here = jnp.concatenate(
            [ret_ref[block_place(me, r, flight), :, cols] for r in range(flight)], axis=0
        )
        out = jnp.dot(high, here, preferred_element_type=f32)
        out = out + jnp.dot(low, here, preferred_element_type=f32)
        out_ref[:, cols] = out.astype(bf16)
        total = total + lax.dot_general(
            here, dout[:, cols], (((1,), (1,)), ((), ())), preferred_element_type=f32
        )
    inner = jnp.where(own > 0.0, total, 0.0)
    row_expert = block_place(me, lax.broadcasted_iota(jnp.int32, (slots, 1), 0) // CAP, flight)
    for k in range(topk):
        mine = jnp.where(ids_ref[k : k + 1, :] == row_expert, inner, 0.0)
        dprobs_ref[k : k + 1, :] = jnp.sum(mine, axis=0, keepdims=True)


def combine(ids, own, d_out, returned, block=1024):
    tokens, width = d_out.shape
    return pl.pallas_call(
        functools.partial(combine_kernel, block),
        out_shape=(
            pltpu.HBM((tokens, width), bf16),
            pltpu.HBM(ids.shape, f32),
        ),
        in_specs=[HBM, HBM, HBM, HBM],
        out_specs=(VMEM, VMEM),
        scratch_shapes=[
            pltpu.VMEM(ids.shape, jnp.int32),
            pltpu.VMEM(own.shape, f32),
            pltpu.VMEM((tokens, width), bf16),
            pltpu.VMEM(returned.shape, bf16),
            pltpu.SemaphoreType.DMA((4,)),
        ],
        compiler_params=params(own.shape[0]),
        cost_estimate=SMALL,
        name="combine",
    )(hbm(ids), hbm(own), hbm(d_out), hbm(returned))


def weight_grad_kernel(half, groups, block, tie_ref, swapped, hidden_ref, *refs):
    chips, parts = refs[:half], refs[half : half + groups - 1]
    messages = refs[half + groups - 1 : half + 2 * groups - 2]
    out_hbm, hidden, own, out, out_sems = refs[half + 2 * groups - 2 :]
    cap, share = parts[0].shape[1:]
    flight = 2 * half
    slots = flight * cap
    wide = hidden_ref.shape[1] // TILE
    hidden[:slots, :] = hidden_ref[...]
    for j in range(1, groups):
        bit = max(b for b in bits_of(groups) if b <= j)
        message = messages[j - 1]
        for r in range(flight):
            for q in range(wide):
                hidden[
                    j * slots + r * cap : j * slots + (r + 1) * cap, q * TILE : (q + 1) * TILE
                ] = message[r * wide + q]
        for q in range(share // TILE):
            own[j - 1, :, q * TILE : (q + 1) * TILE] = message[
                flight * wide + (j - bit) * (share // TILE) + q
            ]
    stores = []
    for n, cols in enumerate(chunks(share, block)):
        grads = [chips[c][0, 0, :, cols] for c in range(half)]
        grads += [swapped[c, 0, :, cols] for c in range(half)]
        for j in range(1, groups):
            grads.append(own[j - 1, :, cols])
            grads.append(parts[j - 1][:, :, cols].reshape(slots - cap, block))
        out[cols, :] = lax.dot_general(
            jnp.concatenate(grads, axis=0),
            hidden[...],
            (((0,), (0,)), ((), ())),
            preferred_element_type=f32,
        ).astype(bf16)
        stores.append(pltpu.make_async_copy(out.at[cols], out_hbm.at[cols], out_sems.at[n]))
        stores[n].start()
    for copy in stores:
        copy.wait()


def weight_grad(tie, chips, swapped, hidden, parts, messages, block=256):
    half, groups, cap, share = swapped.shape
    slots, hid = hidden.shape
    return pl.pallas_call(
        functools.partial(weight_grad_kernel, half, groups, block),
        out_shape=pltpu.HBM((share, hid), bf16),
        in_specs=[HBM] + [VMEM] * (half + 2 * groups),
        out_specs=HBM,
        scratch_shapes=[
            pltpu.VMEM((groups * slots, hid), bf16),
            pltpu.VMEM((groups - 1, cap, share), bf16),
            pltpu.VMEM((share, hid), bf16),
            pltpu.SemaphoreType.DMA((share // block,)),
        ],
        compiler_params=params(slots),
        cost_estimate=SMALL,
        name="weight_grad",
    )(hbm(tie), swapped, hidden, *chips, *parts, *messages)


def swap(value, axis, j):
    size = lax.axis_size(axis)
    return lax.ppermute(value, axis, [(i, i ^ j) for i in range(size)])


def shards(route_ids, route_probs, capacity, hot_lists, gate_up, w_quant, w_scale, d_out):
    flight = lax.axis_size("expert")
    groups = lax.axis_size("dp")
    gate_up = gate_up[0, 0]
    ids, probs = route_ids.T, route_probs.T
    scale = w_scale.transpose(1, 0, 2)
    own, hidden, *rest = dispatch(
        gate_up, capacity, hot_lists, ids, probs, d_out, flight, groups
    )
    half, bits = flight // 2, bits_of(groups)
    chips = rest[:1] + [swap(rest[c], "expert", 2 * c) for c in range(1, half)]
    messages, early = {}, []
    for bit, message in zip(bits, rest[half:]):
        for j in sorted(messages):
            messages[j ^ bit] = swap(messages[j], "dp", bit)
        messages[bit] = swap(message, "dp", bit)
        early.append(messages[bit])
    messages = [messages[j] for j in range(1, groups)]
    expert_out = forward(scale, hidden, w_quant[0], flight)
    returned = lax.all_to_all(expert_out, "expert", split_axis=0, concat_axis=0, tiled=True)
    swapped = swap(sibling_rows(chips, [hbm(expert_out)] + early), "expert", 1)
    pieces = split(chips, swapped)
    parts = [swap(pieces[j - 1], "dp", j) for j in range(1, groups)]
    d_gate_up = backward(scale, gate_up, w_quant[0], pieces[0], chips, swapped)
    combined, d_probs = combine(ids, own, d_out, returned)
    d_weight = weight_grad(d_probs, chips, swapped, hidden, parts, messages)
    return (combined, d_probs.T, d_gate_up[None, None], d_weight[None])


def solution(mesh):
    placed = (
        P(("dp", "expert"), None),
        P(("dp", "expert"), None),
        P(),
        P("dp", None),
        P("dp", "expert", None, None),
        P("expert", None, None),
        P("expert", None, None),
        P(("dp", "expert"), None),
    )
    return jax.shard_map(
        shards,
        mesh=mesh,
        in_specs=placed,
        out_specs=(
            P(("dp", "expert"), None),
            P(("dp", "expert"), None),
            P("dp", "expert", None, None),
            P("expert", "dp", None),
        ),
        check_vma=False,
    )
```

```python
import functools

import jax
import jax.numpy as jnp
from jax import lax
from jax.experimental import pallas as pl
from jax.experimental.pallas import tpu as pltpu
from jax.sharding import PartitionSpec as P

QB = 128
CAP = 16
TILE = 256

bf16 = jnp.bfloat16
f32 = jnp.float32

SMALL = pl.CostEstimate(flops=1024, bytes_accessed=1024, transcendentals=0)

VMEM = pl.BlockSpec(memory_space=pltpu.VMEM)
ANY = pl.BlockSpec(memory_space=pl.ANY)
HBM = pl.BlockSpec(memory_space=pltpu.HBM)


def params(slots):
    return pltpu.CompilerParams(vmem_limit_bytes=(12 + slots // 32) * 1024 * 1024)


def hbm(value):
    return pltpu.with_memory_space_constraint(value, pltpu.HBM)


def chunks(total, size):
    return [pl.ds(start, size) for start in range(0, total, size)]


def bits_of(groups):
    bits = []
    while groups > 1:
        groups //= 2
        bits.append(groups)
    return bits


def block_place(me, r, flight):
    half = flight // 2
    return me ^ (2 * (r % half) + r // half)


def dispatch_kernel(flight, groups, gate_up_hbm, cap_hbm, hot_hbm, ids_hbm, probs_hbm, dout_hbm, *refs):
    half = flight // 2
    bits = bits_of(groups)
    outs = 2 + half + len(bits)
    own_hbm, hidden_ref, *chips = refs[: 2 + half]
    messages = dict(zip(bits, refs[2 + half : outs]))
    gate_up, cap_ref, hot_ref, ids_ref, probs_ref, dout, own_ref = refs[outs : outs + 7]
    gate_sems, own_sem, small_sems, in_sems = refs[outs + 7 :]
    topk, tokens = ids_ref.shape
    slots = flight * CAP
    me, group = lax.axis_index("expert"), lax.axis_index("dp")
    share = dout_hbm.shape[1] // groups
    hid = hidden_ref.shape[1]
    small = [
        pltpu.make_async_copy(src, dst, small_sems.at[i])
        for i, (src, dst) in enumerate(
            [(ids_hbm, ids_ref), (probs_hbm, probs_ref), (cap_hbm, cap_ref), (hot_hbm, hot_ref)]
        )
    ]
    loads = [
        pltpu.make_async_copy(
            dout_hbm.at[:, pl.ds(pl.multiple_of((group ^ j) * share, share), share)],
            dout.at[j],
            in_sems.at[j],
        )
        for j in range(groups)
    ]
    gates = [
        pltpu.make_async_copy(
            gate_up_hbm.at[pl.ds(pl.multiple_of(block_place(me, r, flight) * CAP, CAP), CAP)],
            gate_up.at[pl.ds(r * CAP, CAP)],
            gate_sems.at[r],
        )
        for r in range(flight)
    ]
    for copy in small + loads + gates:
        copy.start()
    for copy in small:
        copy.wait()
    row = lax.broadcasted_iota(jnp.int32, (slots, 1), 0)
    row_expert = block_place(me, row // CAP, flight)
    row_rank = (row % CAP).astype(f32)
    limit = jnp.zeros((slots, 1), jnp.int32)
    for e in range(flight):
        hot = hot_ref[0, 0] == e
        for h in range(1, hot_ref.shape[1]):
            hot = jnp.logical_or(hot, hot_ref[0, h] == e)
        limit = jnp.where(row_expert == e, jnp.where(hot, CAP, cap_ref[e]), limit)
    limit = limit.astype(f32)
    named = jnp.zeros((slots, tokens), f32)
    weight = jnp.zeros((slots, tokens), f32)
    for k in range(topk):
        hit = ids_ref[k : k + 1, :] == row_expert
        named = jnp.where(hit, 1.0, named)
        weight = jnp.where(hit, probs_ref[k : k + 1, :], weight)
    earlier = lax.broadcasted_iota(jnp.int32, (tokens, tokens), 0)
    later = lax.broadcasted_iota(jnp.int32, (tokens, tokens), 1)
    before = (earlier < later).astype(f32).astype(bf16)
    rank = jnp.dot(named.astype(bf16), before, preferred_element_type=f32)
    owns = (named > 0.0) & (rank == row_rank) & (rank < limit)
    own_weight = jnp.where(owns, weight, 0.0)
    own_ref[...] = own_weight
    own_copy = pltpu.make_async_copy(own_ref, own_hbm, own_sem)
    own_copy.start()
    owner = jnp.where(owns, 1.0, 0.0).astype(bf16)
    slot_weight = jnp.sum(own_weight, axis=1, keepdims=True)
    for copy in loads:
        copy.wait()
    for j in range(groups):
        part = jnp.dot(owner, dout[j], preferred_element_type=f32)
        part = (part * slot_weight).astype(bf16)
        for r in range(flight):
            chips[r % half][r // half, j] = part[r * CAP : (r + 1) * CAP, :]
        for bit in bits:
            if bit <= j < 2 * bit:
                first = flight * (hid // TILE) + (j - bit) * (share // TILE)
                for q in range(share // TILE):
                    messages[bit][first + q] = part[:CAP, q * TILE : (q + 1) * TILE]
    for copy in gates:
        copy.wait()
    for r in range(flight):
        at = slice(r * CAP, (r + 1) * CAP)
        gate = gate_up[at, :hid].astype(f32)
        up = gate_up[at, hid:].astype(f32)
        block = (gate * jax.nn.sigmoid(gate) * up).astype(bf16)
        hidden_ref[at, :] = block
        for bit in bits:
            for q in range(hid // TILE):
                messages[bit][r * (hid // TILE) + q] = block[:, q * TILE : (q + 1) * TILE]
    own_copy.wait()


def dispatch(gate_up, capacity, hot_row, ids, probs, d_out, flight, groups):
    tokens, width = d_out.shape
    rows, double = gate_up.shape
    slots = flight * CAP
    share = width // groups
    half = flight // 2
    return pl.pallas_call(
        functools.partial(dispatch_kernel, flight, groups),
        out_shape=(pltpu.HBM((slots, tokens), f32), pltpu.VMEM((rows, double // 2), bf16))
        + (pltpu.VMEM((2, groups, CAP, share), bf16),) * half
        + tuple(
            pltpu.VMEM((flight * (double // 2 // TILE) + bit * (share // TILE), CAP, TILE), bf16)
            for bit in bits_of(groups)
        ),
        in_specs=[HBM] * 6,
        out_specs=(HBM, VMEM) + (VMEM,) * (half + len(bits_of(groups))),
        scratch_shapes=[
            pltpu.VMEM((rows, double), bf16),
            pltpu.SMEM(capacity.shape, jnp.int32),
            pltpu.SMEM(hot_row.shape, jnp.int32),
            pltpu.VMEM(ids.shape, jnp.int32),
            pltpu.VMEM(probs.shape, f32),
            pltpu.VMEM((groups, tokens, share), bf16),
            pltpu.VMEM((slots, tokens), f32),
            pltpu.SemaphoreType.DMA((flight,)),
            pltpu.SemaphoreType.DMA,
            pltpu.SemaphoreType.DMA((4,)),
            pltpu.SemaphoreType.DMA((groups,)),
        ],
        compiler_params=params(slots),
        cost_estimate=SMALL,
        name="dispatch",
    )(hbm(gate_up), hbm(capacity), hbm(hot_row), hbm(ids), hbm(probs), hbm(d_out))


def forward_kernel(
    flight, block, hidden_ref, scale_hbm, quant_hbm, out_hbm,
    scale, hidden, quant, out, scale_sem, in_sems, out_sems
):
    steps, hid, _ = quant.shape
    me = lax.axis_index("expert")
    loads = [
        pltpu.make_async_copy(quant_hbm.at[:, pl.ds(c * block, block)], quant.at[c], in_sems.at[c])
        for c in range(steps)
    ]
    small = pltpu.make_async_copy(scale_hbm, scale, scale_sem)
    for copy in [small] + loads:
        copy.start()
    for r in range(flight):
        place = pl.multiple_of(block_place(me, r, flight) * CAP, CAP)
        hidden[pl.ds(place, CAP), :] = hidden_ref[pl.ds(r * CAP, CAP), :]
    small.wait()
    stores = []
    for c in range(steps):
        cols = pl.ds(c * block, block)
        loads[c].wait()
        total = [None] * (block // QB)
        for i in range(hid // QB):
            part = jnp.dot(
                hidden[:, i * QB : (i + 1) * QB],
                quant[c, i * QB : (i + 1) * QB, :],
                preferred_element_type=f32,
            )
            for j in range(block // QB):
                scaled = part[:, j * QB : (j + 1) * QB] * scale[i, 0, c * (block // QB) + j]
                total[j] = scaled if i == 0 else total[j] + scaled
        for j in range(block // QB):
            at = pl.ds(c * block + j * QB, QB)
            out[:, :, at] = total[j].astype(bf16).reshape(flight, CAP, QB)
        stores.append(
            pltpu.make_async_copy(out.at[:, :, cols], out_hbm.at[:, :, cols], out_sems.at[c])
        )
        stores[c].start()
    for copy in stores:
        copy.wait()


def forward(scale, hidden, quant, flight, block=512):
    hid, width = quant.shape
    steps = width // block
    return pl.pallas_call(
        functools.partial(forward_kernel, flight, block),
        out_shape=pltpu.HBM((flight, CAP, width), bf16),
        in_specs=[VMEM, HBM, HBM],
        out_specs=HBM,
        scratch_shapes=[
            pltpu.SMEM(scale.shape, f32),
            pltpu.VMEM(hidden.shape, bf16),
            pltpu.VMEM((steps, hid, block), bf16),
            pltpu.VMEM((flight, CAP, width), bf16),
            pltpu.SemaphoreType.DMA,
            pltpu.SemaphoreType.DMA((steps,)),
            pltpu.SemaphoreType.DMA((steps,)),
        ],
        compiler_params=params(flight * CAP),
        cost_estimate=SMALL,
        name="expert_forward",
    )(hidden, hbm(scale), hbm(quant))


def sort_kernel(half, *refs):
    chips, (sibling, mine) = refs[:half], refs[-2:]
    for c in range(half):
        sibling[c] = chips[c][1]
        mine[c] = chips[c][0]


def sort_rows(chips, ties):
    half = len(chips)
    return pl.pallas_call(
        functools.partial(sort_kernel, half),
        out_shape=(pltpu.VMEM((half,) + chips[0].shape[1:], bf16),) * 2,
        in_specs=[VMEM] * half + [ANY] * len(ties),
        out_specs=(VMEM, VMEM),
        compiler_params=params(2 * half * CAP),
        cost_estimate=SMALL,
        name="sort_rows",
    )(*chips, *ties)


def split_kernel(mine, swapped, *pieces):
    half = mine.shape[0]
    for j, piece in enumerate(pieces, 1):
        piece[: half - 1] = mine[1:, j]
        piece[half - 1 :] = swapped[:, j]


def split(mine, swapped):
    half, groups, cap, share = swapped.shape
    return pl.pallas_call(
        split_kernel,
        out_shape=(pltpu.VMEM((2 * half - 1, cap, share), bf16),) * (groups - 1),
        in_specs=[VMEM, VMEM],
        out_specs=(VMEM,) * (groups - 1),
        compiler_params=params(2 * half * CAP),
        cost_estimate=SMALL,
        name="split",
    )(mine, swapped)


def backward_kernel(
    flight, groups, scale_hbm, gate_up_hbm, quant_hbm, tie_ref, mine, swapped, out_hbm,
    scale, gate_up, rows, quant, acc, out, scale_sem, gate_sems, in_sems, out_sems
):
    half = flight // 2
    me, group = lax.axis_index("expert"), lax.axis_index("dp")
    slots, hid = acc.shape
    share = quant.shape[2]

    def place(r):
        return pl.ds(pl.multiple_of(block_place(me, r, flight) * CAP, CAP), CAP)

    loads = [
        pltpu.make_async_copy(
            quant_hbm.at[:, pl.ds(pl.multiple_of((group ^ j) * share, share), share)],
            quant.at[j],
            in_sems.at[j],
        )
        for j in range(groups)
    ]
    gates = [
        pltpu.make_async_copy(
            gate_up_hbm.at[place(r)], gate_up.at[pl.ds(r * CAP, CAP)], gate_sems.at[r]
        )
        for r in range(flight)
    ]
    small = pltpu.make_async_copy(scale_hbm, scale, scale_sem)
    for copy in [small] + loads + gates:
        copy.start()
    for c in range(half):
        rows[:, c * CAP : (c + 1) * CAP, :] = mine[c]
        rows[:, (half + c) * CAP : (half + c + 1) * CAP, :] = swapped[c]
    small.wait()
    for j in range(groups):
        loads[j].wait()
        for b in range(share // QB):
            cols = slice(b * QB, (b + 1) * QB)
            part = lax.dot_general(
                rows[j, :, cols],
                quant[j, :, cols],
                (((1,), (1,)), ((), ())),
                preferred_element_type=f32,
            )
            for i in range(hid // QB):
                at = (slice(None), slice(i * QB, (i + 1) * QB))
                scaled = part[at] * scale[i, 0, (group ^ j) * (share // QB) + b]
                if j == 0 and b == 0:
                    acc[at] = scaled
                else:
                    acc[at] += scaled
    for copy in gates:
        copy.wait()
    gate = gate_up[:, :hid].astype(f32)
    up = gate_up[:, hid:].astype(f32)
    sig = jax.nn.sigmoid(gate)
    d_hidden = acc[...]
    out[:, :hid] = (d_hidden * up * sig * (1.0 + gate * (1.0 - sig))).astype(bf16)
    out[:, hid:] = (d_hidden * (gate * sig)).astype(bf16)
    stores = [
        pltpu.make_async_copy(out.at[pl.ds(r * CAP, CAP)], out_hbm.at[place(r)], out_sems.at[r])
        for r in range(flight)
    ]
    for copy in stores:
        copy.start()
    for copy in stores:
        copy.wait()


def backward(scale, gate_up, quant, tie, mine, swapped):
    slots, double = gate_up.shape
    hid, width = quant.shape
    half, groups, cap, share = swapped.shape
    flight = 2 * half
    return pl.pallas_call(
        functools.partial(backward_kernel, flight, groups),
        out_shape=pltpu.HBM((slots, double), bf16),
        in_specs=[HBM, HBM, HBM, ANY, VMEM, VMEM],
        out_specs=HBM,
        scratch_shapes=[
            pltpu.SMEM(scale.shape, f32),
            pltpu.VMEM((slots, double), bf16),
            pltpu.VMEM((groups, slots, share), bf16),
            pltpu.VMEM((groups, hid, share), bf16),
            pltpu.VMEM((slots, hid), f32),
            pltpu.VMEM((slots, double), bf16),
            pltpu.SemaphoreType.DMA,
            pltpu.SemaphoreType.DMA((flight,)),
            pltpu.SemaphoreType.DMA((groups,)),
            pltpu.SemaphoreType.DMA((flight,)),
        ],
        compiler_params=params(slots),
        cost_estimate=SMALL,
        name="expert_backward",
    )(hbm(scale), hbm(gate_up), hbm(quant), tie, mine, swapped)


def combine_kernel(
    block, ids_hbm, own_hbm, dout_hbm, ret_hbm, out_ref, dprobs_ref, ids_ref, own_ref, dout, ret_ref, sems
):
    copies = [
        pltpu.make_async_copy(ids_hbm, ids_ref, sems.at[0]),
        pltpu.make_async_copy(own_hbm, own_ref, sems.at[1]),
        pltpu.make_async_copy(dout_hbm, dout, sems.at[2]),
        pltpu.make_async_copy(ret_hbm, ret_ref, sems.at[3]),
    ]
    for copy in copies:
        copy.start()
    topk, tokens = ids_ref.shape
    slots = own_ref.shape[0]
    width = dout.shape[1]
    flight = slots // CAP
    me = lax.axis_index("expert")
    copies[1].wait()
    own = own_ref[...]
    turned = own.T
    high = turned.astype(bf16)
    low = (turned - high.astype(f32)).astype(bf16)
    total = jnp.zeros((slots, tokens), f32)
    for copy in (copies[0], copies[2], copies[3]):
        copy.wait()
    for cols in chunks(width, block):
        here = jnp.concatenate(
            [ret_ref[block_place(me, r, flight), :, cols] for r in range(flight)], axis=0
        )
        out = jnp.dot(high, here, preferred_element_type=f32)
        out = out + jnp.dot(low, here, preferred_element_type=f32)
        out_ref[:, cols] = out.astype(bf16)
        total = total + lax.dot_general(
            here, dout[:, cols], (((1,), (1,)), ((), ())), preferred_element_type=f32
        )
    inner = jnp.where(own > 0.0, total, 0.0)
    row_expert = block_place(me, lax.broadcasted_iota(jnp.int32, (slots, 1), 0) // CAP, flight)
    for k in range(topk):
        mine = jnp.where(ids_ref[k : k + 1, :] == row_expert, inner, 0.0)
        dprobs_ref[k : k + 1, :] = jnp.sum(mine, axis=0, keepdims=True)


def combine(ids, own, d_out, returned, block=1024):
    tokens, width = d_out.shape
    return pl.pallas_call(
        functools.partial(combine_kernel, block),
        out_shape=(
            pltpu.HBM((tokens, width), bf16),
            pltpu.HBM(ids.shape, f32),
        ),
        in_specs=[HBM, HBM, HBM, HBM],
        out_specs=(VMEM, VMEM),
        scratch_shapes=[
            pltpu.VMEM(ids.shape, jnp.int32),
            pltpu.VMEM(own.shape, f32),
            pltpu.VMEM((tokens, width), bf16),
            pltpu.VMEM(returned.shape, bf16),
            pltpu.SemaphoreType.DMA((4,)),
        ],
        compiler_params=params(own.shape[0]),
        cost_estimate=SMALL,
        name="combine",
    )(hbm(ids), hbm(own), hbm(d_out), hbm(returned))


def weight_grad_kernel(groups, block, tie_ref, mine, swapped, hidden_ref, *refs):
    parts, messages = refs[: groups - 1], refs[groups - 1 : 2 * groups - 2]
    out_hbm, hidden, own, out, out_sems = refs[2 * groups - 2 :]
    half = mine.shape[0]
    cap, share = parts[0].shape[1:]
    flight = 2 * half
    slots = flight * cap
    wide = hidden_ref.shape[1] // TILE
    hidden[:slots, :] = hidden_ref[...]
    for j in range(1, groups):
        bit = max(b for b in bits_of(groups) if b <= j)
        message = messages[j - 1]
        for r in range(flight):
            for q in range(wide):
                hidden[
                    j * slots + r * cap : j * slots + (r + 1) * cap, q * TILE : (q + 1) * TILE
                ] = message[r * wide + q]
        for q in range(share // TILE):
            own[j - 1, :, q * TILE : (q + 1) * TILE] = message[
                flight * wide + (j - bit) * (share // TILE) + q
            ]
    stores = []
    for n, cols in enumerate(chunks(share, block)):
        grads = [mine[c, 0, :, cols] for c in range(half)]
        grads += [swapped[c, 0, :, cols] for c in range(half)]
        for j in range(1, groups):
            grads.append(own[j - 1, :, cols])
            grads.append(parts[j - 1][:, :, cols].reshape(slots - cap, block))
        out[cols, :] = lax.dot_general(
            jnp.concatenate(grads, axis=0),
            hidden[...],
            (((0,), (0,)), ((), ())),
            preferred_element_type=f32,
        ).astype(bf16)
        stores.append(pltpu.make_async_copy(out.at[cols], out_hbm.at[cols], out_sems.at[n]))
        stores[n].start()
    for copy in stores:
        copy.wait()


def weight_grad(tie, mine, swapped, hidden, parts, messages, block=256):
    half, groups, cap, share = swapped.shape
    slots, hid = hidden.shape
    return pl.pallas_call(
        functools.partial(weight_grad_kernel, groups, block),
        out_shape=pltpu.HBM((share, hid), bf16),
        in_specs=[HBM] + [VMEM] * (1 + 2 * groups),
        out_specs=HBM,
        scratch_shapes=[
            pltpu.VMEM((groups * slots, hid), bf16),
            pltpu.VMEM((groups - 1, cap, share), bf16),
            pltpu.VMEM((share, hid), bf16),
            pltpu.SemaphoreType.DMA((share // block,)),
        ],
        compiler_params=params(slots),
        cost_estimate=SMALL,
        name="weight_grad",
    )(hbm(tie), mine, swapped, hidden, *parts, *messages)


def swap(value, axis, j):
    size = lax.axis_size(axis)
    return lax.ppermute(value, axis, [(i, i ^ j) for i in range(size)])


def shards(route_ids, route_probs, capacity, hot_lists, gate_up, w_quant, w_scale, d_out):
    flight = lax.axis_size("expert")
    groups = lax.axis_size("dp")
    gate_up = gate_up[0, 0]
    ids, probs = route_ids.T, route_probs.T
    scale = w_scale.transpose(1, 0, 2)
    own, hidden, *rest = dispatch(
        gate_up, capacity, hot_lists, ids, probs, d_out, flight, groups
    )
    half, bits = flight // 2, bits_of(groups)
    chips = rest[:1] + [swap(rest[c], "expert", 2 * c) for c in range(1, half)]
    messages, early = {}, []
    for bit, message in zip(bits, rest[half:]):
        for j in sorted(messages):
            messages[j ^ bit] = swap(messages[j], "dp", bit)
        messages[bit] = swap(message, "dp", bit)
        early.append(messages[bit])
    messages = [messages[j] for j in range(1, groups)]
    expert_out = forward(scale, hidden, w_quant[0], flight)
    returned = lax.all_to_all(expert_out, "expert", split_axis=0, concat_axis=0, tiled=True)
    sibling, mine = sort_rows(chips, [hbm(expert_out)] + early)
    swapped = swap(sibling, "expert", 1)
    pieces = split(mine, swapped)
    parts = [swap(pieces[j - 1], "dp", j) for j in range(1, groups)]
    d_gate_up = backward(scale, gate_up, w_quant[0], pieces[0], mine, swapped)
    combined, d_probs = combine(ids, own, d_out, returned)
    d_weight = weight_grad(d_probs, mine, swapped, hidden, parts, messages)
    return (combined, d_probs.T, d_gate_up[None, None], d_weight[None])


def solution(mesh):
    placed = (
        P(("dp", "expert"), None),
        P(("dp", "expert"), None),
        P(),
        P("dp", None),
        P("dp", "expert", None, None),
        P("expert", None, None),
        P("expert", None, None),
        P(("dp", "expert"), None),
    )
    return jax.shard_map(
        shards,
        mesh=mesh,
        in_specs=placed,
        out_specs=(
            P(("dp", "expert"), None),
            P(("dp", "expert"), None),
            P("dp", "expert", None, None),
            P("expert", "dp", None),
        ),
        check_vma=False,
    )
```

```python
import functools

import jax
import jax.numpy as jnp
from jax import lax
from jax.experimental import pallas as pl
from jax.experimental.pallas import tpu as pltpu
from jax.sharding import PartitionSpec as P

QB = 128
CAP = 16
TILE = 256
AHEAD = 3

bf16 = jnp.bfloat16
f32 = jnp.float32

SMALL = pl.CostEstimate(flops=1024, bytes_accessed=1024, transcendentals=0)

VMEM = pl.BlockSpec(memory_space=pltpu.VMEM)
ANY = pl.BlockSpec(memory_space=pl.ANY)
HBM = pl.BlockSpec(memory_space=pltpu.HBM)


def params(slots):
    return pltpu.CompilerParams(vmem_limit_bytes=(12 + slots // 32) * 1024 * 1024)


def hbm(value):
    return pltpu.with_memory_space_constraint(value, pltpu.HBM)


def chunks(total, size):
    return [pl.ds(start, size) for start in range(0, total, size)]


def bits_of(groups):
    bits = []
    while groups > 1:
        groups //= 2
        bits.append(groups)
    return bits


def message_tiles(flight, groups, bit, hid, share):
    far = 1 if 2 * bit == groups else 0
    return flight * (hid // TILE) + bit * (share // TILE) + far


def block_place(me, r, flight):
    half = flight // 2
    return me ^ (2 * (r % half) + r // half)


def dispatch_kernel(flight, groups, gate_up_hbm, cap_hbm, hot_hbm, ids_hbm, probs_hbm, dout_hbm, *refs):
    half = flight // 2
    bits = bits_of(groups)
    outs = 2 + half + len(bits)
    own_hbm, hidden_ref, *chips = refs[: 2 + half]
    messages = dict(zip(bits, refs[2 + half : outs]))
    gate_up, cap_ref, hot_ref, ids_ref, probs_ref, dout, own_ref = refs[outs : outs + 7]
    gate_sems, own_sem, small_sems, in_sems = refs[outs + 7 :]
    topk, tokens = ids_ref.shape
    slots = flight * CAP
    me, group = lax.axis_index("expert"), lax.axis_index("dp")
    share = dout_hbm.shape[1] // groups
    hid = hidden_ref.shape[1]
    small = [
        pltpu.make_async_copy(src, dst, small_sems.at[i])
        for i, (src, dst) in enumerate(
            [(ids_hbm, ids_ref), (probs_hbm, probs_ref), (cap_hbm, cap_ref), (hot_hbm, hot_ref)]
        )
    ]
    loads = [
        pltpu.make_async_copy(
            dout_hbm.at[:, pl.ds(pl.multiple_of((group ^ j) * share, share), share)],
            dout.at[j],
            in_sems.at[j],
        )
        for j in range(groups)
    ]
    gates = [
        pltpu.make_async_copy(
            gate_up_hbm.at[pl.ds(pl.multiple_of(block_place(me, r, flight) * CAP, CAP), CAP)],
            gate_up.at[pl.ds(r * CAP, CAP)],
            gate_sems.at[r],
        )
        for r in range(flight)
    ]
    for copy in small + loads + gates:
        copy.start()
    for copy in small:
        copy.wait()
    row = lax.broadcasted_iota(jnp.int32, (slots, 1), 0)
    row_expert = block_place(me, row // CAP, flight)
    row_rank = (row % CAP).astype(f32)
    limit = jnp.zeros((slots, 1), jnp.int32)
    for e in range(flight):
        hot = hot_ref[0, 0] == e
        for h in range(1, hot_ref.shape[1]):
            hot = jnp.logical_or(hot, hot_ref[0, h] == e)
        limit = jnp.where(row_expert == e, jnp.where(hot, CAP, cap_ref[e]), limit)
    limit = limit.astype(f32)
    named = jnp.zeros((slots, tokens), f32)
    weight = jnp.zeros((slots, tokens), f32)
    for k in range(topk):
        hit = ids_ref[k : k + 1, :] == row_expert
        named = jnp.where(hit, 1.0, named)
        weight = jnp.where(hit, probs_ref[k : k + 1, :], weight)
    earlier = lax.broadcasted_iota(jnp.int32, (tokens, tokens), 0)
    later = lax.broadcasted_iota(jnp.int32, (tokens, tokens), 1)
    before = (earlier < later).astype(f32).astype(bf16)
    rank = jnp.dot(named.astype(bf16), before, preferred_element_type=f32)
    owns = (named > 0.0) & (rank == row_rank) & (rank < limit)
    own_weight = jnp.where(owns, weight, 0.0)
    own_ref[...] = own_weight
    own_copy = pltpu.make_async_copy(own_ref, own_hbm, own_sem)
    own_copy.start()
    owner = jnp.where(owns, 1.0, 0.0).astype(bf16)
    slot_weight = jnp.sum(own_weight, axis=1, keepdims=True)
    for copy in loads:
        copy.wait()
    for j in range(groups):
        part = jnp.dot(owner, dout[j], preferred_element_type=f32)
        part = (part * slot_weight).astype(bf16)
        for r in range(flight):
            chips[r % half][r // half, j] = part[r * CAP : (r + 1) * CAP, :]
        for bit in bits:
            if bit <= j < 2 * bit:
                first = flight * (hid // TILE) + (j - bit) * (share // TILE)
                for q in range(share // TILE):
                    messages[bit][first + q] = part[:CAP, q * TILE : (q + 1) * TILE]
    messages[bits[0]][messages[bits[0]].shape[0] - 1] = jnp.zeros((CAP, TILE), bf16)
    for copy in gates:
        copy.wait()
    for r in range(flight):
        at = slice(r * CAP, (r + 1) * CAP)
        gate = gate_up[at, :hid].astype(f32)
        up = gate_up[at, hid:].astype(f32)
        block = (gate * jax.nn.sigmoid(gate) * up).astype(bf16)
        hidden_ref[at, :] = block
        for bit in bits:
            for q in range(hid // TILE):
                messages[bit][r * (hid // TILE) + q] = block[:, q * TILE : (q + 1) * TILE]
    own_copy.wait()


def dispatch(gate_up, capacity, hot_row, ids, probs, d_out, flight, groups):
    tokens, width = d_out.shape
    rows, double = gate_up.shape
    slots = flight * CAP
    share = width // groups
    half = flight // 2
    return pl.pallas_call(
        functools.partial(dispatch_kernel, flight, groups),
        out_shape=(pltpu.HBM((slots, tokens), f32), pltpu.VMEM((rows, double // 2), bf16))
        + (pltpu.VMEM((2, groups, CAP, share), bf16),) * half
        + tuple(
            pltpu.VMEM((message_tiles(flight, groups, bit, double // 2, share), CAP, TILE), bf16)
            for bit in bits_of(groups)
        ),
        in_specs=[HBM] * 6,
        out_specs=(HBM, VMEM) + (VMEM,) * (half + len(bits_of(groups))),
        scratch_shapes=[
            pltpu.VMEM((rows, double), bf16),
            pltpu.SMEM(capacity.shape, jnp.int32),
            pltpu.SMEM(hot_row.shape, jnp.int32),
            pltpu.VMEM(ids.shape, jnp.int32),
            pltpu.VMEM(probs.shape, f32),
            pltpu.VMEM((groups, tokens, share), bf16),
            pltpu.VMEM((slots, tokens), f32),
            pltpu.SemaphoreType.DMA((flight,)),
            pltpu.SemaphoreType.DMA,
            pltpu.SemaphoreType.DMA((4,)),
            pltpu.SemaphoreType.DMA((groups,)),
        ],
        compiler_params=params(slots),
        cost_estimate=SMALL,
        name="dispatch",
    )(hbm(gate_up), hbm(capacity), hbm(hot_row), hbm(ids), hbm(probs), hbm(d_out))


def forward_kernel(
    flight, block, hidden_ref, scale_hbm, quant_hbm, out_hbm,
    scale, hidden, quant, out, scale_sem, in_sems, out_sems
):
    steps, hid, _ = quant.shape
    me = lax.axis_index("expert")
    loads = [
        pltpu.make_async_copy(quant_hbm.at[:, pl.ds(c * block, block)], quant.at[c], in_sems.at[c])
        for c in range(steps)
    ]
    small = pltpu.make_async_copy(scale_hbm, scale, scale_sem)
    for copy in [small] + loads[:AHEAD]:
        copy.start()
    for r in range(flight):
        place = pl.multiple_of(block_place(me, r, flight) * CAP, CAP)
        hidden[pl.ds(place, CAP), :] = hidden_ref[pl.ds(r * CAP, CAP), :]
    small.wait()
    stores = []
    for c in range(steps):
        cols = pl.ds(c * block, block)
        loads[c].wait()
        if c + AHEAD < steps:
            loads[c + AHEAD].start()
        total = [None] * (block // QB)
        for i in range(hid // QB):
            part = jnp.dot(
                hidden[:, i * QB : (i + 1) * QB],
                quant[c, i * QB : (i + 1) * QB, :],
                preferred_element_type=f32,
            )
            for j in range(block // QB):
                scaled = part[:, j * QB : (j + 1) * QB] * scale[i, 0, c * (block // QB) + j]
                total[j] = scaled if i == 0 else total[j] + scaled
        for j in range(block // QB):
            at = pl.ds(c * block + j * QB, QB)
            out[:, :, at] = total[j].astype(bf16).reshape(flight, CAP, QB)
        stores.append(
            pltpu.make_async_copy(out.at[:, :, cols], out_hbm.at[:, :, cols], out_sems.at[c])
        )
        stores[c].start()
    for copy in stores:
        copy.wait()


def forward(scale, hidden, quant, flight, block=512):
    hid, width = quant.shape
    steps = width // block
    return pl.pallas_call(
        functools.partial(forward_kernel, flight, block),
        out_shape=pltpu.HBM((flight, CAP, width), bf16),
        in_specs=[VMEM, HBM, HBM],
        out_specs=HBM,
        scratch_shapes=[
            pltpu.SMEM(scale.shape, f32),
            pltpu.VMEM(hidden.shape, bf16),
            pltpu.VMEM((steps, hid, block), bf16),
            pltpu.VMEM((flight, CAP, width), bf16),
            pltpu.SemaphoreType.DMA,
            pltpu.SemaphoreType.DMA((steps,)),
            pltpu.SemaphoreType.DMA((steps,)),
        ],
        compiler_params=params(flight * CAP),
        cost_estimate=SMALL,
        name="expert_forward",
    )(hidden, hbm(scale), hbm(quant))


def sort_kernel(half, *refs):
    chips, (sibling, mine) = refs[:half], refs[-2:]
    for c in range(half):
        sibling[c] = chips[c][1]
        mine[c] = chips[c][0]


def sort_rows(chips, ties):
    half = len(chips)
    return pl.pallas_call(
        functools.partial(sort_kernel, half),
        out_shape=(pltpu.VMEM((half,) + chips[0].shape[1:], bf16),) * 2,
        in_specs=[VMEM] * half + [ANY] * len(ties),
        out_specs=(VMEM, VMEM),
        compiler_params=params(2 * half * CAP),
        cost_estimate=SMALL,
        name="sort_rows",
    )(*chips, *ties)


def split_kernel(mine, swapped, *pieces):
    half = mine.shape[0]
    for j, piece in enumerate(pieces, 1):
        piece[: half - 1] = mine[1:, j]
        piece[half - 1 :] = swapped[:, j]


def split(mine, swapped):
    half, groups, cap, share = swapped.shape
    return pl.pallas_call(
        split_kernel,
        out_shape=(pltpu.VMEM((2 * half - 1, cap, share), bf16),) * (groups - 1),
        in_specs=[VMEM, VMEM],
        out_specs=(VMEM,) * (groups - 1),
        compiler_params=params(2 * half * CAP),
        cost_estimate=SMALL,
        name="split",
    )(mine, swapped)


def backward_kernel(
    flight, groups, scale_hbm, gate_up_hbm, quant_hbm, tie_ref, mine, swapped, out_hbm,
    scale, gate_up, rows, quant, acc, out, scale_sem, gate_sems, in_sems, out_sems
):
    half = flight // 2
    me, group = lax.axis_index("expert"), lax.axis_index("dp")
    slots, hid = acc.shape
    share = quant.shape[2]

    def place(r):
        return pl.ds(pl.multiple_of(block_place(me, r, flight) * CAP, CAP), CAP)

    loads = [
        pltpu.make_async_copy(
            quant_hbm.at[:, pl.ds(pl.multiple_of((group ^ j) * share, share), share)],
            quant.at[j],
            in_sems.at[j],
        )
        for j in range(groups)
    ]
    gates = [
        pltpu.make_async_copy(
            gate_up_hbm.at[place(r)], gate_up.at[pl.ds(r * CAP, CAP)], gate_sems.at[r]
        )
        for r in range(flight)
    ]
    small = pltpu.make_async_copy(scale_hbm, scale, scale_sem)
    for copy in [small] + loads + gates:
        copy.start()
    for c in range(half):
        rows[:, c * CAP : (c + 1) * CAP, :] = mine[c]
        rows[:, (half + c) * CAP : (half + c + 1) * CAP, :] = swapped[c]
    small.wait()
    for j in range(groups):
        loads[j].wait()
        for b in range(share // QB):
            cols = slice(b * QB, (b + 1) * QB)
            part = lax.dot_general(
                rows[j, :, cols],
                quant[j, :, cols],
                (((1,), (1,)), ((), ())),
                preferred_element_type=f32,
            )
            for i in range(hid // QB):
                at = (slice(None), slice(i * QB, (i + 1) * QB))
                scaled = part[at] * scale[i, 0, (group ^ j) * (share // QB) + b]
                if j == 0 and b == 0:
                    acc[at] = scaled
                else:
                    acc[at] += scaled
    for copy in gates:
        copy.wait()
    gate = gate_up[:, :hid].astype(f32)
    up = gate_up[:, hid:].astype(f32)
    sig = jax.nn.sigmoid(gate)
    d_hidden = acc[...]
    out[:, :hid] = (d_hidden * up * sig * (1.0 + gate * (1.0 - sig))).astype(bf16)
    out[:, hid:] = (d_hidden * (gate * sig)).astype(bf16)
    stores = [
        pltpu.make_async_copy(out.at[pl.ds(r * CAP, CAP)], out_hbm.at[place(r)], out_sems.at[r])
        for r in range(flight)
    ]
    for copy in stores:
        copy.start()
    for copy in stores:
        copy.wait()


def backward(scale, gate_up, quant, tie, mine, swapped):
    slots, double = gate_up.shape
    hid, width = quant.shape
    half, groups, cap, share = swapped.shape
    flight = 2 * half
    return pl.pallas_call(
        functools.partial(backward_kernel, flight, groups),
        out_shape=pltpu.HBM((slots, double), bf16),
        in_specs=[HBM, HBM, HBM, ANY, VMEM, VMEM],
        out_specs=HBM,
        scratch_shapes=[
            pltpu.SMEM(scale.shape, f32),
            pltpu.VMEM((slots, double), bf16),
            pltpu.VMEM((groups, slots, share), bf16),
            pltpu.VMEM((groups, hid, share), bf16),
            pltpu.VMEM((slots, hid), f32),
            pltpu.VMEM((slots, double), bf16),
            pltpu.SemaphoreType.DMA,
            pltpu.SemaphoreType.DMA((flight,)),
            pltpu.SemaphoreType.DMA((groups,)),
            pltpu.SemaphoreType.DMA((flight,)),
        ],
        compiler_params=params(slots),
        cost_estimate=SMALL,
        name="expert_backward",
    )(hbm(scale), hbm(gate_up), hbm(quant), tie, mine, swapped)


def combine_kernel(
    block, ids_hbm, own_hbm, dout_hbm, ret_hbm, out_ref, dprobs_ref, ids_ref, own_ref, dout, ret_ref, sems
):
    copies = [
        pltpu.make_async_copy(ids_hbm, ids_ref, sems.at[0]),
        pltpu.make_async_copy(own_hbm, own_ref, sems.at[1]),
        pltpu.make_async_copy(dout_hbm, dout, sems.at[2]),
        pltpu.make_async_copy(ret_hbm, ret_ref, sems.at[3]),
    ]
    for copy in copies:
        copy.start()
    topk, tokens = ids_ref.shape
    slots = own_ref.shape[0]
    width = dout.shape[1]
    flight = slots // CAP
    me = lax.axis_index("expert")
    copies[1].wait()
    own = own_ref[...]
    turned = own.T
    high = turned.astype(bf16)
    low = (turned - high.astype(f32)).astype(bf16)
    total = jnp.zeros((slots, tokens), f32)
    for copy in (copies[0], copies[2], copies[3]):
        copy.wait()
    for cols in chunks(width, block):
        here = jnp.concatenate(
            [ret_ref[block_place(me, r, flight), :, cols] for r in range(flight)], axis=0
        )
        out = jnp.dot(high, here, preferred_element_type=f32)
        out = out + jnp.dot(low, here, preferred_element_type=f32)
        out_ref[:, cols] = out.astype(bf16)
        total = total + lax.dot_general(
            here, dout[:, cols], (((1,), (1,)), ((), ())), preferred_element_type=f32
        )
    inner = jnp.where(own > 0.0, total, 0.0)
    row_expert = block_place(me, lax.broadcasted_iota(jnp.int32, (slots, 1), 0) // CAP, flight)
    for k in range(topk):
        mine = jnp.where(ids_ref[k : k + 1, :] == row_expert, inner, 0.0)
        dprobs_ref[k : k + 1, :] = jnp.sum(mine, axis=0, keepdims=True)


def combine(ids, own, d_out, returned, block=1024):
    tokens, width = d_out.shape
    return pl.pallas_call(
        functools.partial(combine_kernel, block),
        out_shape=(
            pltpu.HBM((tokens, width), bf16),
            pltpu.HBM(ids.shape, f32),
        ),
        in_specs=[HBM, HBM, HBM, HBM],
        out_specs=(VMEM, VMEM),
        scratch_shapes=[
            pltpu.VMEM(ids.shape, jnp.int32),
            pltpu.VMEM(own.shape, f32),
            pltpu.VMEM((tokens, width), bf16),
            pltpu.VMEM(returned.shape, bf16),
            pltpu.SemaphoreType.DMA((4,)),
        ],
        compiler_params=params(own.shape[0]),
        cost_estimate=SMALL,
        name="combine",
    )(hbm(ids), hbm(own), hbm(d_out), hbm(returned))


def weight_grad_kernel(groups, block, tie_ref, mine, swapped, hidden_ref, *refs):
    parts, messages = refs[: groups - 1], refs[groups - 1 : 2 * groups - 2]
    out_hbm, hidden, own, out, out_sems = refs[2 * groups - 2 :]
    half = mine.shape[0]
    cap, share = parts[0].shape[1:]
    flight = 2 * half
    slots = flight * cap
    wide = hidden_ref.shape[1] // TILE
    hidden[:slots, :] = hidden_ref[...]
    for j in range(1, groups):
        bit = max(b for b in bits_of(groups) if b <= j)
        message = messages[j - 1]
        for r in range(flight):
            for q in range(wide):
                hidden[
                    j * slots + r * cap : j * slots + (r + 1) * cap, q * TILE : (q + 1) * TILE
                ] = message[r * wide + q]
        for q in range(share // TILE):
            own[j - 1, :, q * TILE : (q + 1) * TILE] = message[
                flight * wide + (j - bit) * (share // TILE) + q
            ]
    stores = []
    for n, cols in enumerate(chunks(share, block)):
        grads = [mine[c, 0, :, cols] for c in range(half)]
        grads += [swapped[c, 0, :, cols] for c in range(half)]
        for j in range(1, groups):
            grads.append(own[j - 1, :, cols])
            grads.append(parts[j - 1][:, :, cols].reshape(slots - cap, block))
        out[cols, :] = lax.dot_general(
            jnp.concatenate(grads, axis=0),
            hidden[...],
            (((0,), (0,)), ((), ())),
            preferred_element_type=f32,
        ).astype(bf16)
        stores.append(pltpu.make_async_copy(out.at[cols], out_hbm.at[cols], out_sems.at[n]))
        stores[n].start()
    for copy in stores:
        copy.wait()


def weight_grad(tie, mine, swapped, hidden, parts, messages, block=256):
    half, groups, cap, share = swapped.shape
    slots, hid = hidden.shape
    return pl.pallas_call(
        functools.partial(weight_grad_kernel, groups, block),
        out_shape=pltpu.HBM((share, hid), bf16),
        in_specs=[HBM] + [VMEM] * (1 + 2 * groups),
        out_specs=HBM,
        scratch_shapes=[
            pltpu.VMEM((groups * slots, hid), bf16),
            pltpu.VMEM((groups - 1, cap, share), bf16),
            pltpu.VMEM((share, hid), bf16),
            pltpu.SemaphoreType.DMA((share // block,)),
        ],
        compiler_params=params(slots),
        cost_estimate=SMALL,
        name="weight_grad",
    )(hbm(tie), mine, swapped, hidden, *parts, *messages)


def swap(value, axis, j):
    size = lax.axis_size(axis)
    return lax.ppermute(value, axis, [(i, i ^ j) for i in range(size)])


def shards(route_ids, route_probs, capacity, hot_lists, gate_up, w_quant, w_scale, d_out):
    flight = lax.axis_size("expert")
    groups = lax.axis_size("dp")
    gate_up = gate_up[0, 0]
    ids, probs = route_ids.T, route_probs.T
    scale = w_scale.transpose(1, 0, 2)
    own, hidden, *rest = dispatch(
        gate_up, capacity, hot_lists, ids, probs, d_out, flight, groups
    )
    half, bits = flight // 2, bits_of(groups)
    chips = rest[:1] + [swap(rest[c], "expert", 2 * c) for c in range(1, half)]
    messages, early = {}, []
    for bit, message in zip(bits, rest[half:]):
        for j in sorted(messages):
            messages[j ^ bit] = swap(messages[j], "dp", bit)
        messages[bit] = swap(message, "dp", bit)
        early.append(messages[bit])
    messages = [messages[j] for j in range(1, groups)]
    expert_out = forward(scale, hidden, w_quant[0], flight)
    returned = lax.all_to_all(expert_out, "expert", split_axis=0, concat_axis=0, tiled=True)
    sibling, mine = sort_rows(chips, [hbm(expert_out)] + early)
    swapped = swap(sibling, "expert", 1)
    pieces = split(mine, swapped)
    parts = [swap(pieces[j - 1], "dp", j) for j in range(1, groups)]
    d_gate_up = backward(scale, gate_up, w_quant[0], pieces[0], mine, swapped)
    combined, d_probs = combine(ids, own, d_out, returned)
    d_weight = weight_grad(d_probs, mine, swapped, hidden, parts, messages)
    return (combined, d_probs.T, d_gate_up[None, None], d_weight[None])


def solution(mesh):
    placed = (
        P(("dp", "expert"), None),
        P(("dp", "expert"), None),
        P(),
        P("dp", None),
        P("dp", "expert", None, None),
        P("expert", None, None),
        P("expert", None, None),
        P(("dp", "expert"), None),
    )
    return jax.shard_map(
        shards,
        mesh=mesh,
        in_specs=placed,
        out_specs=(
            P(("dp", "expert"), None),
            P(("dp", "expert"), None),
            P("dp", "expert", None, None),
            P("expert", "dp", None),
        ),
        check_vma=False,
    )
```

```python
import functools

import jax
import jax.numpy as jnp
from jax import lax
from jax.experimental import pallas as pl
from jax.experimental.pallas import tpu as pltpu
from jax.sharding import PartitionSpec as P

QB = 128
CAP = 16
TILE = 256
PART = 256

bf16 = jnp.bfloat16
f32 = jnp.float32

SMALL = pl.CostEstimate(flops=1024, bytes_accessed=1024, transcendentals=0)

VMEM = pl.BlockSpec(memory_space=pltpu.VMEM)
ANY = pl.BlockSpec(memory_space=pl.ANY)
HBM = pl.BlockSpec(memory_space=pltpu.HBM)


def params(slots):
    return pltpu.CompilerParams(vmem_limit_bytes=(12 + slots // 32) * 1024 * 1024)


def hbm(value):
    return pltpu.with_memory_space_constraint(value, pltpu.HBM)


def chunks(total, size):
    return [pl.ds(start, size) for start in range(0, total, size)]


def bits_of(groups):
    bits = []
    while groups > 1:
        groups //= 2
        bits.append(groups)
    return bits


def message_tiles(flight, groups, bit, hid, share):
    far = 1 if 2 * bit == groups else 0
    return flight * (hid // TILE) + bit * (share // TILE) + far


def block_place(me, r, flight):
    half = flight // 2
    return me ^ (2 * (r % half) + r // half)


def dispatch_kernel(flight, groups, gate_up_hbm, cap_hbm, hot_hbm, ids_hbm, probs_hbm, dout_hbm, *refs):
    half = flight // 2
    bits = bits_of(groups)
    outs = 2 + half + len(bits)
    own_hbm, hidden_ref, *chips = refs[: 2 + half]
    messages = dict(zip(bits, refs[2 + half : outs]))
    gate_up, cap_ref, hot_ref, ids_ref, probs_ref, dout, own_ref = refs[outs : outs + 7]
    gate_sems, own_sem, small_sems, in_sems = refs[outs + 7 :]
    topk, tokens = ids_ref.shape
    slots = flight * CAP
    me, group = lax.axis_index("expert"), lax.axis_index("dp")
    share = dout_hbm.shape[1] // groups
    hid = hidden_ref.shape[1]
    small = [
        pltpu.make_async_copy(src, dst, small_sems.at[i])
        for i, (src, dst) in enumerate(
            [(ids_hbm, ids_ref), (probs_hbm, probs_ref), (cap_hbm, cap_ref), (hot_hbm, hot_ref)]
        )
    ]
    loads = [
        pltpu.make_async_copy(
            dout_hbm.at[:, pl.ds(pl.multiple_of((group ^ j) * share, share), share)],
            dout.at[j],
            in_sems.at[j],
        )
        for j in range(groups)
    ]
    gates = [
        pltpu.make_async_copy(
            gate_up_hbm.at[pl.ds(pl.multiple_of(block_place(me, r, flight) * CAP, CAP), CAP)],
            gate_up.at[pl.ds(r * CAP, CAP)],
            gate_sems.at[r],
        )
        for r in range(flight)
    ]
    for copy in small + loads + gates:
        copy.start()
    for copy in small:
        copy.wait()
    row = lax.broadcasted_iota(jnp.int32, (slots, 1), 0)
    row_expert = block_place(me, row // CAP, flight)
    row_rank = (row % CAP).astype(f32)
    limit = jnp.zeros((slots, 1), jnp.int32)
    for e in range(flight):
        hot = hot_ref[0, 0] == e
        for h in range(1, hot_ref.shape[1]):
            hot = jnp.logical_or(hot, hot_ref[0, h] == e)
        limit = jnp.where(row_expert == e, jnp.where(hot, CAP, cap_ref[e]), limit)
    limit = limit.astype(f32)
    named = jnp.zeros((slots, tokens), f32)
    weight = jnp.zeros((slots, tokens), f32)
    for k in range(topk):
        hit = ids_ref[k : k + 1, :] == row_expert
        named = jnp.where(hit, 1.0, named)
        weight = jnp.where(hit, probs_ref[k : k + 1, :], weight)
    earlier = lax.broadcasted_iota(jnp.int32, (tokens, tokens), 0)
    later = lax.broadcasted_iota(jnp.int32, (tokens, tokens), 1)
    before = (earlier < later).astype(f32).astype(bf16)
    rank = jnp.dot(named.astype(bf16), before, preferred_element_type=f32)
    owns = (named > 0.0) & (rank == row_rank) & (rank < limit)
    own_weight = jnp.where(owns, weight, 0.0)
    own_ref[...] = own_weight
    own_copy = pltpu.make_async_copy(own_ref, own_hbm, own_sem)
    own_copy.start()
    owner = jnp.where(owns, 1.0, 0.0).astype(bf16)
    slot_weight = jnp.sum(own_weight, axis=1, keepdims=True)
    for copy in loads:
        copy.wait()
    for j in range(groups):
        part = jnp.dot(owner, dout[j], preferred_element_type=f32)
        part = (part * slot_weight).astype(bf16)
        for r in range(flight):
            chips[r % half][r // half, j] = part[r * CAP : (r + 1) * CAP, :]
        for bit in bits:
            if bit <= j < 2 * bit:
                first = flight * (hid // TILE) + (j - bit) * (share // TILE)
                for q in range(share // TILE):
                    messages[bit][first + q] = part[:CAP, q * TILE : (q + 1) * TILE]
    messages[bits[0]][messages[bits[0]].shape[0] - 1] = jnp.zeros((CAP, TILE), bf16)
    for copy in gates:
        copy.wait()
    for r in range(flight):
        at = slice(r * CAP, (r + 1) * CAP)
        gate = gate_up[at, :hid].astype(f32)
        up = gate_up[at, hid:].astype(f32)
        block = (gate * jax.nn.sigmoid(gate) * up).astype(bf16)
        hidden_ref[at, :] = block
        for bit in bits:
            for q in range(hid // TILE):
                messages[bit][r * (hid // TILE) + q] = block[:, q * TILE : (q + 1) * TILE]
    own_copy.wait()


def dispatch(gate_up, capacity, hot_row, ids, probs, d_out, flight, groups):
    tokens, width = d_out.shape
    rows, double = gate_up.shape
    slots = flight * CAP
    share = width // groups
    half = flight // 2
    return pl.pallas_call(
        functools.partial(dispatch_kernel, flight, groups),
        out_shape=(pltpu.HBM((slots, tokens), f32), pltpu.VMEM((rows, double // 2), bf16))
        + (pltpu.VMEM((2, groups, CAP, share), bf16),) * half
        + tuple(
            pltpu.VMEM((message_tiles(flight, groups, bit, double // 2, share), CAP, TILE), bf16)
            for bit in bits_of(groups)
        ),
        in_specs=[HBM] * 6,
        out_specs=(HBM, VMEM) + (VMEM,) * (half + len(bits_of(groups))),
        scratch_shapes=[
            pltpu.VMEM((rows, double), bf16),
            pltpu.SMEM(capacity.shape, jnp.int32),
            pltpu.SMEM(hot_row.shape, jnp.int32),
            pltpu.VMEM(ids.shape, jnp.int32),
            pltpu.VMEM(probs.shape, f32),
            pltpu.VMEM((groups, tokens, share), bf16),
            pltpu.VMEM((slots, tokens), f32),
            pltpu.SemaphoreType.DMA((flight,)),
            pltpu.SemaphoreType.DMA,
            pltpu.SemaphoreType.DMA((4,)),
            pltpu.SemaphoreType.DMA((groups,)),
        ],
        compiler_params=params(slots),
        cost_estimate=SMALL,
        name="dispatch",
    )(hbm(gate_up), hbm(capacity), hbm(hot_row), hbm(ids), hbm(probs), hbm(d_out))


def forward_kernel(
    flight, block, hidden_ref, scale_hbm, quant_hbm, out_hbm,
    scale, hidden, quant, out, scale_sem, in_sems, out_sems
):
    steps, hid, _ = quant.shape
    me = lax.axis_index("expert")
    loads = [
        pltpu.make_async_copy(quant_hbm.at[:, pl.ds(c * block, block)], quant.at[c], in_sems.at[c])
        for c in range(steps)
    ]
    small = pltpu.make_async_copy(scale_hbm, scale, scale_sem)
    for copy in [small] + loads:
        copy.start()
    for r in range(flight):
        place = pl.multiple_of(block_place(me, r, flight) * CAP, CAP)
        hidden[pl.ds(place, CAP), :] = hidden_ref[pl.ds(r * CAP, CAP), :]
    small.wait()
    stores = []
    for c in range(steps):
        cols = pl.ds(c * block, block)
        loads[c].wait()
        for p in range(0, block, PART):
            total = [None] * (PART // QB)
            for i in range(hid // QB):
                part = jnp.dot(
                    hidden[:, i * QB : (i + 1) * QB],
                    quant[c, i * QB : (i + 1) * QB, p : p + PART],
                    preferred_element_type=f32,
                )
                for j in range(PART // QB):
                    factor = scale[i, 0, (c * block + p) // QB + j]
                    scaled = part[:, j * QB : (j + 1) * QB] * factor
                    total[j] = scaled if i == 0 else total[j] + scaled
            for j in range(PART // QB):
                at = pl.ds(c * block + p + j * QB, QB)
                out[:, :, at] = total[j].astype(bf16).reshape(flight, CAP, QB)
        stores.append(
            pltpu.make_async_copy(out.at[:, :, cols], out_hbm.at[:, :, cols], out_sems.at[c])
        )
        stores[c].start()
    for copy in stores:
        copy.wait()


def forward(scale, hidden, quant, flight, block=512):
    hid, width = quant.shape
    steps = width // block
    return pl.pallas_call(
        functools.partial(forward_kernel, flight, block),
        out_shape=pltpu.HBM((flight, CAP, width), bf16),
        in_specs=[VMEM, HBM, HBM],
        out_specs=HBM,
        scratch_shapes=[
            pltpu.SMEM(scale.shape, f32),
            pltpu.VMEM(hidden.shape, bf16),
            pltpu.VMEM((steps, hid, block), bf16),
            pltpu.VMEM((flight, CAP, width), bf16),
            pltpu.SemaphoreType.DMA,
            pltpu.SemaphoreType.DMA((steps,)),
            pltpu.SemaphoreType.DMA((steps,)),
        ],
        compiler_params=params(flight * CAP),
        cost_estimate=SMALL,
        name="expert_forward",
    )(hidden, hbm(scale), hbm(quant))


def sort_kernel(half, keep, picks, *refs):
    chips, messages = refs[:half], refs[half : half + len(picks)]
    sibling, mine, *passed = refs[-2 - len(picks) :]
    for c in range(half):
        sibling[c] = chips[c][1]
        mine[c] = chips[c][0]
    for message, out, pick in zip(messages, passed, picks):
        tall = out.shape[0] - keep
        out[:keep] = message[:keep]
        out[keep:] = message[keep + pick * tall : keep + (pick + 1) * tall]


def sort_rows(chips, messages, picks, ties, hid):
    half = len(chips)
    _, groups, cap, share = chips[0].shape
    keep = 2 * half * (hid // TILE)
    return pl.pallas_call(
        functools.partial(sort_kernel, half, keep, picks),
        out_shape=(pltpu.VMEM((half, groups, cap, share), bf16),) * 2
        + (pltpu.VMEM((keep + share // TILE, cap, TILE), bf16),) * len(messages),
        in_specs=[VMEM] * (half + len(messages)) + [ANY] * len(ties),
        out_specs=(VMEM,) * (2 + len(messages)),
        compiler_params=params(2 * half * CAP),
        cost_estimate=SMALL,
        name="sort_rows",
    )(*chips, *messages, *ties)


def split_kernel(mine, swapped, *pieces):
    half = mine.shape[0]
    for j, piece in enumerate(pieces, 1):
        piece[: half - 1] = mine[1:, j]
        piece[half - 1 :] = swapped[:, j]


def split(mine, swapped):
    half, groups, cap, share = swapped.shape
    return pl.pallas_call(
        split_kernel,
        out_shape=(pltpu.VMEM((2 * half - 1, cap, share), bf16),) * (groups - 1),
        in_specs=[VMEM, VMEM],
        out_specs=(VMEM,) * (groups - 1),
        compiler_params=params(2 * half * CAP),
        cost_estimate=SMALL,
        name="split",
    )(mine, swapped)


def backward_kernel(
    flight, groups, scale_hbm, gate_up_hbm, quant_hbm, tie_ref, mine, swapped, out_hbm,
    scale, gate_up, rows, quant, acc, out, scale_sem, gate_sems, in_sems, out_sems
):
    half = flight // 2
    me, group = lax.axis_index("expert"), lax.axis_index("dp")
    slots, hid = acc.shape
    share = quant.shape[2]

    def place(r):
        return pl.ds(pl.multiple_of(block_place(me, r, flight) * CAP, CAP), CAP)

    loads = [
        pltpu.make_async_copy(
            quant_hbm.at[:, pl.ds(pl.multiple_of((group ^ j) * share, share), share)],
            quant.at[j],
            in_sems.at[j],
        )
        for j in range(groups)
    ]
    gates = [
        pltpu.make_async_copy(
            gate_up_hbm.at[place(r)], gate_up.at[pl.ds(r * CAP, CAP)], gate_sems.at[r]
        )
        for r in range(flight)
    ]
    small = pltpu.make_async_copy(scale_hbm, scale, scale_sem)
    for copy in [small] + loads + gates:
        copy.start()
    for c in range(half):
        rows[:, c * CAP : (c + 1) * CAP, :] = mine[c]
        rows[:, (half + c) * CAP : (half + c + 1) * CAP, :] = swapped[c]
    small.wait()
    for j in range(groups):
        loads[j].wait()
        for b in range(share // QB):
            cols = slice(b * QB, (b + 1) * QB)
            part = lax.dot_general(
                rows[j, :, cols],
                quant[j, :, cols],
                (((1,), (1,)), ((), ())),
                preferred_element_type=f32,
            )
            for i in range(hid // QB):
                at = (slice(None), slice(i * QB, (i + 1) * QB))
                scaled = part[at] * scale[i, 0, (group ^ j) * (share // QB) + b]
                if j == 0 and b == 0:
                    acc[at] = scaled
                else:
                    acc[at] += scaled
    for copy in gates:
        copy.wait()
    gate = gate_up[:, :hid].astype(f32)
    up = gate_up[:, hid:].astype(f32)
    sig = jax.nn.sigmoid(gate)
    d_hidden = acc[...]
    out[:, :hid] = (d_hidden * up * sig * (1.0 + gate * (1.0 - sig))).astype(bf16)
    out[:, hid:] = (d_hidden * (gate * sig)).astype(bf16)
    stores = [
        pltpu.make_async_copy(out.at[pl.ds(r * CAP, CAP)], out_hbm.at[place(r)], out_sems.at[r])
        for r in range(flight)
    ]
    for copy in stores:
        copy.start()
    for copy in stores:
        copy.wait()


def backward(scale, gate_up, quant, tie, mine, swapped):
    slots, double = gate_up.shape
    hid, width = quant.shape
    half, groups, cap, share = swapped.shape
    flight = 2 * half
    return pl.pallas_call(
        functools.partial(backward_kernel, flight, groups),
        out_shape=pltpu.HBM((slots, double), bf16),
        in_specs=[HBM, HBM, HBM, ANY, VMEM, VMEM],
        out_specs=HBM,
        scratch_shapes=[
            pltpu.SMEM(scale.shape, f32),
            pltpu.VMEM((slots, double), bf16),
            pltpu.VMEM((groups, slots, share), bf16),
            pltpu.VMEM((groups, hid, share), bf16),
            pltpu.VMEM((slots, hid), f32),
            pltpu.VMEM((slots, double), bf16),
            pltpu.SemaphoreType.DMA,
            pltpu.SemaphoreType.DMA((flight,)),
            pltpu.SemaphoreType.DMA((groups,)),
            pltpu.SemaphoreType.DMA((flight,)),
        ],
        compiler_params=params(slots),
        cost_estimate=SMALL,
        name="expert_backward",
    )(hbm(scale), hbm(gate_up), hbm(quant), tie, mine, swapped)


def combine_kernel(
    block, ids_hbm, own_hbm, dout_hbm, ret_hbm, out_ref, dprobs_ref, ids_ref, own_ref, dout, ret_ref, sems
):
    copies = [
        pltpu.make_async_copy(ids_hbm, ids_ref, sems.at[0]),
        pltpu.make_async_copy(own_hbm, own_ref, sems.at[1]),
        pltpu.make_async_copy(dout_hbm, dout, sems.at[2]),
        pltpu.make_async_copy(ret_hbm, ret_ref, sems.at[3]),
    ]
    for copy in copies:
        copy.start()
    topk, tokens = ids_ref.shape
    slots = own_ref.shape[0]
    width = dout.shape[1]
    flight = slots // CAP
    me = lax.axis_index("expert")
    copies[1].wait()
    own = own_ref[...]
    turned = own.T
    high = turned.astype(bf16)
    low = (turned - high.astype(f32)).astype(bf16)
    total = jnp.zeros((slots, tokens), f32)
    for copy in (copies[0], copies[2], copies[3]):
        copy.wait()
    for cols in chunks(width, block):
        here = jnp.concatenate(
            [ret_ref[block_place(me, r, flight), :, cols] for r in range(flight)], axis=0
        )
        out = jnp.dot(high, here, preferred_element_type=f32)
        out = out + jnp.dot(low, here, preferred_element_type=f32)
        out_ref[:, cols] = out.astype(bf16)
        total = total + lax.dot_general(
            here, dout[:, cols], (((1,), (1,)), ((), ())), preferred_element_type=f32
        )
    inner = jnp.where(own > 0.0, total, 0.0)
    row_expert = block_place(me, lax.broadcasted_iota(jnp.int32, (slots, 1), 0) // CAP, flight)
    for k in range(topk):
        mine = jnp.where(ids_ref[k : k + 1, :] == row_expert, inner, 0.0)
        dprobs_ref[k : k + 1, :] = jnp.sum(mine, axis=0, keepdims=True)


def combine(ids, own, d_out, returned, block=1024):
    tokens, width = d_out.shape
    return pl.pallas_call(
        functools.partial(combine_kernel, block),
        out_shape=(
            pltpu.HBM((tokens, width), bf16),
            pltpu.HBM(ids.shape, f32),
        ),
        in_specs=[HBM, HBM, HBM, HBM],
        out_specs=(VMEM, VMEM),
        scratch_shapes=[
            pltpu.VMEM(ids.shape, jnp.int32),
            pltpu.VMEM(own.shape, f32),
            pltpu.VMEM((tokens, width), bf16),
            pltpu.VMEM(returned.shape, bf16),
            pltpu.SemaphoreType.DMA((4,)),
        ],
        compiler_params=params(own.shape[0]),
        cost_estimate=SMALL,
        name="combine",
    )(hbm(ids), hbm(own), hbm(d_out), hbm(returned))


def weight_grad_kernel(groups, block, tie_ref, mine, swapped, hidden_ref, *refs):
    parts, messages = refs[: groups - 1], refs[groups - 1 : 2 * groups - 2]
    out_hbm, hidden, own, out, out_sems = refs[2 * groups - 2 :]
    half = mine.shape[0]
    cap, share = parts[0].shape[1:]
    flight = 2 * half
    slots = flight * cap
    wide = hidden_ref.shape[1] // TILE
    hidden[:slots, :] = hidden_ref[...]
    for j in range(1, groups):
        bit = j if j % 2 else max(b for b in bits_of(groups) if b <= j)
        message = messages[j - 1]
        for r in range(flight):
            for q in range(wide):
                hidden[
                    j * slots + r * cap : j * slots + (r + 1) * cap, q * TILE : (q + 1) * TILE
                ] = message[r * wide + q]
        for q in range(share // TILE):
            own[j - 1, :, q * TILE : (q + 1) * TILE] = message[
                flight * wide + (j - bit) * (share // TILE) + q
            ]
    stores = []
    for n, cols in enumerate(chunks(share, block)):
        grads = [mine[c, 0, :, cols] for c in range(half)]
        grads += [swapped[c, 0, :, cols] for c in range(half)]
        for j in range(1, groups):
            grads.append(own[j - 1, :, cols])
            grads.append(parts[j - 1][:, :, cols].reshape(slots - cap, block))
        out[cols, :] = lax.dot_general(
            jnp.concatenate(grads, axis=0),
            hidden[...],
            (((0,), (0,)), ((), ())),
            preferred_element_type=f32,
        ).astype(bf16)
        stores.append(pltpu.make_async_copy(out.at[cols], out_hbm.at[cols], out_sems.at[n]))
        stores[n].start()
    for copy in stores:
        copy.wait()


def weight_grad(tie, mine, swapped, hidden, parts, messages, block=256):
    half, groups, cap, share = swapped.shape
    slots, hid = hidden.shape
    return pl.pallas_call(
        functools.partial(weight_grad_kernel, groups, block),
        out_shape=pltpu.HBM((share, hid), bf16),
        in_specs=[HBM] + [VMEM] * (1 + 2 * groups),
        out_specs=HBM,
        scratch_shapes=[
            pltpu.VMEM((groups * slots, hid), bf16),
            pltpu.VMEM((groups - 1, cap, share), bf16),
            pltpu.VMEM((share, hid), bf16),
            pltpu.SemaphoreType.DMA((share // block,)),
        ],
        compiler_params=params(slots),
        cost_estimate=SMALL,
        name="weight_grad",
    )(hbm(tie), mine, swapped, hidden, *parts, *messages)


def swap(value, axis, j):
    size = lax.axis_size(axis)
    return lax.ppermute(value, axis, [(i, i ^ j) for i in range(size)])


def shards(route_ids, route_probs, capacity, hot_lists, gate_up, w_quant, w_scale, d_out):
    flight = lax.axis_size("expert")
    groups = lax.axis_size("dp")
    gate_up = gate_up[0, 0]
    ids, probs = route_ids.T, route_probs.T
    scale = w_scale.transpose(1, 0, 2)
    own, hidden, *rest = dispatch(
        gate_up, capacity, hot_lists, ids, probs, d_out, flight, groups
    )
    half, bits = flight // 2, bits_of(groups)
    chips = rest[:1] + [swap(rest[c], "expert", 2 * c) for c in range(1, half)]
    messages = {}
    for bit, message in zip(bits, rest[half:]):
        if bit > 1:
            for j in sorted(messages):
                messages[j ^ bit] = swap(messages[j], "dp", bit)
        messages[bit] = swap(message, "dp", bit)
    even = list(range(2, groups, 2))
    picks = [j + 1 - max(bit for bit in bits if bit <= j) for j in even]
    expert_out = forward(scale, hidden, w_quant[0], flight)
    returned = lax.all_to_all(expert_out, "expert", split_axis=0, concat_axis=0, tiled=True)
    sibling, mine, *passed = sort_rows(
        chips, [messages[j] for j in even], picks, [hbm(expert_out), messages[1]], hidden.shape[1]
    )
    for j, message in zip(even, passed):
        messages[j + 1] = swap(message, "dp", 1)
    messages = [messages[j] for j in range(1, groups)]
    swapped = swap(sibling, "expert", 1)
    pieces = split(mine, swapped)
    parts = [swap(pieces[j - 1], "dp", j) for j in range(1, groups)]
    d_gate_up = backward(scale, gate_up, w_quant[0], pieces[0], mine, swapped)
    combined, d_probs = combine(ids, own, d_out, returned)
    d_weight = weight_grad(d_probs, mine, swapped, hidden, parts, messages)
    return (combined, d_probs.T, d_gate_up[None, None], d_weight[None])


def solution(mesh):
    placed = (
        P(("dp", "expert"), None),
        P(("dp", "expert"), None),
        P(),
        P("dp", None),
        P("dp", "expert", None, None),
        P("expert", None, None),
        P("expert", None, None),
        P(("dp", "expert"), None),
    )
    return jax.shard_map(
        shards,
        mesh=mesh,
        in_specs=placed,
        out_specs=(
            P(("dp", "expert"), None),
            P(("dp", "expert"), None),
            P("dp", "expert", None, None),
            P("expert", "dp", None),
        ),
        check_vma=False,
    )
```

```python
import functools

import jax
import jax.numpy as jnp
from jax import lax
from jax.experimental import pallas as pl
from jax.experimental.pallas import tpu as pltpu
from jax.sharding import PartitionSpec as P

QB = 128
CAP = 16
TILE = 256
PART = 256

bf16 = jnp.bfloat16
f32 = jnp.float32

SMALL = pl.CostEstimate(flops=1024, bytes_accessed=1024, transcendentals=0)

VMEM = pl.BlockSpec(memory_space=pltpu.VMEM)
ANY = pl.BlockSpec(memory_space=pl.ANY)
HBM = pl.BlockSpec(memory_space=pltpu.HBM)


def params(slots):
    return pltpu.CompilerParams(vmem_limit_bytes=(12 + slots // 32) * 1024 * 1024)


def hbm(value):
    return pltpu.with_memory_space_constraint(value, pltpu.HBM)


def chunks(total, size):
    return [pl.ds(start, size) for start in range(0, total, size)]


def bits_of(groups):
    bits = []
    while groups > 1:
        groups //= 2
        bits.append(groups)
    return bits


def message_tiles(flight, groups, bit, hid, share):
    far = 1 if 2 * bit == groups else 0
    return flight * (hid // TILE) + bit * (share // TILE) + far


def block_place(me, r, flight):
    half = flight // 2
    return me ^ (2 * (r % half) + r // half)


def dispatch_kernel(flight, groups, gate_up_hbm, cap_hbm, hot_hbm, ids_hbm, probs_hbm, dout_hbm, *refs):
    half = flight // 2
    bits = bits_of(groups)
    outs = 1 + half + len(bits)
    own_hbm, *chips = refs[: 1 + half]
    messages = dict(zip(bits, refs[1 + half : outs]))
    gate_up, cap_ref, hot_ref, ids_ref, probs_ref, dout, own_ref = refs[outs : outs + 7]
    gate_sems, own_sem, small_sems, in_sems = refs[outs + 7 :]
    topk, tokens = ids_ref.shape
    slots = flight * CAP
    me, group = lax.axis_index("expert"), lax.axis_index("dp")
    share = dout_hbm.shape[1] // groups
    hid = gate_up_hbm.shape[1] // 2
    small = [
        pltpu.make_async_copy(src, dst, small_sems.at[i])
        for i, (src, dst) in enumerate(
            [(ids_hbm, ids_ref), (probs_hbm, probs_ref), (cap_hbm, cap_ref), (hot_hbm, hot_ref)]
        )
    ]
    loads = [
        pltpu.make_async_copy(
            dout_hbm.at[:, pl.ds(pl.multiple_of((group ^ j) * share, share), share)],
            dout.at[j],
            in_sems.at[j],
        )
        for j in range(groups)
    ]
    gates = [
        pltpu.make_async_copy(
            gate_up_hbm.at[pl.ds(pl.multiple_of(block_place(me, r, flight) * CAP, CAP), CAP)],
            gate_up.at[pl.ds(r * CAP, CAP)],
            gate_sems.at[r],
        )
        for r in range(flight)
    ]
    for copy in small + loads + gates:
        copy.start()
    for copy in small:
        copy.wait()
    row = lax.broadcasted_iota(jnp.int32, (slots, 1), 0)
    row_expert = block_place(me, row // CAP, flight)
    row_rank = (row % CAP).astype(f32)
    limit = jnp.zeros((slots, 1), jnp.int32)
    for e in range(flight):
        hot = hot_ref[0, 0] == e
        for h in range(1, hot_ref.shape[1]):
            hot = jnp.logical_or(hot, hot_ref[0, h] == e)
        limit = jnp.where(row_expert == e, jnp.where(hot, CAP, cap_ref[e]), limit)
    limit = limit.astype(f32)
    named = jnp.zeros((slots, tokens), f32)
    weight = jnp.zeros((slots, tokens), f32)
    for k in range(topk):
        hit = ids_ref[k : k + 1, :] == row_expert
        named = jnp.where(hit, 1.0, named)
        weight = jnp.where(hit, probs_ref[k : k + 1, :], weight)
    earlier = lax.broadcasted_iota(jnp.int32, (tokens, tokens), 0)
    later = lax.broadcasted_iota(jnp.int32, (tokens, tokens), 1)
    before = (earlier < later).astype(f32).astype(bf16)
    rank = jnp.dot(named.astype(bf16), before, preferred_element_type=f32)
    owns = (named > 0.0) & (rank == row_rank) & (rank < limit)
    own_weight = jnp.where(owns, weight, 0.0)
    own_ref[...] = own_weight
    own_copy = pltpu.make_async_copy(own_ref, own_hbm, own_sem)
    own_copy.start()
    owner = jnp.where(owns, 1.0, 0.0).astype(bf16)
    slot_weight = jnp.sum(own_weight, axis=1, keepdims=True)
    for copy in loads:
        copy.wait()
    for j in range(groups):
        part = jnp.dot(owner, dout[j], preferred_element_type=f32)
        part = (part * slot_weight).astype(bf16)
        for r in range(flight):
            chips[r % half][r // half, j] = part[r * CAP : (r + 1) * CAP, :]
        for bit in bits:
            if bit <= j < 2 * bit:
                first = flight * (hid // TILE) + (j - bit) * (share // TILE)
                for q in range(share // TILE):
                    messages[bit][first + q] = part[:CAP, q * TILE : (q + 1) * TILE]
    messages[bits[0]][messages[bits[0]].shape[0] - 1] = jnp.zeros((CAP, TILE), bf16)
    for copy in gates:
        copy.wait()
    for r in range(flight):
        at = slice(r * CAP, (r + 1) * CAP)
        gate = gate_up[at, :hid].astype(f32)
        up = gate_up[at, hid:].astype(f32)
        block = (gate * jax.nn.sigmoid(gate) * up).astype(bf16)
        for bit in bits:
            for q in range(hid // TILE):
                messages[bit][r * (hid // TILE) + q] = block[:, q * TILE : (q + 1) * TILE]
    own_copy.wait()


def dispatch(gate_up, capacity, hot_row, ids, probs, d_out, flight, groups):
    tokens, width = d_out.shape
    rows, double = gate_up.shape
    slots = flight * CAP
    share = width // groups
    half = flight // 2
    return pl.pallas_call(
        functools.partial(dispatch_kernel, flight, groups),
        out_shape=(pltpu.HBM((slots, tokens), f32),)
        + (pltpu.VMEM((2, groups, CAP, share), bf16),) * half
        + tuple(
            pltpu.VMEM((message_tiles(flight, groups, bit, double // 2, share), CAP, TILE), bf16)
            for bit in bits_of(groups)
        ),
        in_specs=[HBM] * 6,
        out_specs=(HBM,) + (VMEM,) * (half + len(bits_of(groups))),
        scratch_shapes=[
            pltpu.VMEM((rows, double), bf16),
            pltpu.SMEM(capacity.shape, jnp.int32),
            pltpu.SMEM(hot_row.shape, jnp.int32),
            pltpu.VMEM(ids.shape, jnp.int32),
            pltpu.VMEM(probs.shape, f32),
            pltpu.VMEM((groups, tokens, share), bf16),
            pltpu.VMEM((slots, tokens), f32),
            pltpu.SemaphoreType.DMA((flight,)),
            pltpu.SemaphoreType.DMA,
            pltpu.SemaphoreType.DMA((4,)),
            pltpu.SemaphoreType.DMA((groups,)),
        ],
        compiler_params=params(slots),
        cost_estimate=SMALL,
        name="dispatch",
    )(hbm(gate_up), hbm(capacity), hbm(hot_row), hbm(ids), hbm(probs), hbm(d_out))


def forward_kernel(
    flight, block, gate_up_hbm, scale_hbm, quant_hbm, out_hbm,
    gate_up, scale, hidden, quant, out, small_sems, in_sems, out_sems
):
    steps, hid, _ = quant.shape
    tall = hid // in_sems.shape[1]
    loads = [
        [
            pltpu.make_async_copy(
                quant_hbm.at[pl.ds(t * tall, tall), pl.ds(c * block, block)],
                quant.at[c, pl.ds(t * tall, tall)],
                in_sems.at[c, t],
            )
            for t in range(hid // tall)
        ]
        for c in range(steps)
    ]
    small = [
        pltpu.make_async_copy(gate_up_hbm, gate_up, small_sems.at[0]),
        pltpu.make_async_copy(scale_hbm, scale, small_sems.at[1]),
    ]
    for copy in sum(loads, small):
        copy.start()
    for copy in small:
        copy.wait()
    gate = gate_up[:, :hid].astype(f32)
    up = gate_up[:, hid:].astype(f32)
    hidden[...] = (gate * jax.nn.sigmoid(gate) * up).astype(bf16)
    stores = []
    for c in range(steps):
        cols = pl.ds(c * block, block)
        for copy in loads[c]:
            copy.wait()
        for p in range(0, block, PART):
            total = [None] * (PART // QB)
            for i in range(hid // QB):
                part = jnp.dot(
                    hidden[:, i * QB : (i + 1) * QB],
                    quant[c, i * QB : (i + 1) * QB, p : p + PART],
                    preferred_element_type=f32,
                )
                for j in range(PART // QB):
                    factor = scale[i, 0, (c * block + p) // QB + j]
                    scaled = part[:, j * QB : (j + 1) * QB] * factor
                    total[j] = scaled if i == 0 else total[j] + scaled
            for j in range(PART // QB):
                at = pl.ds(c * block + p + j * QB, QB)
                out[:, :, at] = total[j].astype(bf16).reshape(flight, CAP, QB)
        stores.append(
            pltpu.make_async_copy(out.at[:, :, cols], out_hbm.at[:, :, cols], out_sems.at[c])
        )
        stores[c].start()
    for copy in stores:
        copy.wait()


def forward(scale, gate_up, quant, flight, block=1024, parts=3):
    slots, double = gate_up.shape
    hid, width = quant.shape
    steps = width // block
    return pl.pallas_call(
        functools.partial(forward_kernel, flight, block),
        out_shape=pltpu.HBM((flight, CAP, width), bf16),
        in_specs=[HBM, HBM, HBM],
        out_specs=HBM,
        scratch_shapes=[
            pltpu.VMEM((slots, double), bf16),
            pltpu.SMEM(scale.shape, f32),
            pltpu.VMEM((slots, hid), bf16),
            pltpu.VMEM((steps, hid, block), bf16),
            pltpu.VMEM((flight, CAP, width), bf16),
            pltpu.SemaphoreType.DMA((2,)),
            pltpu.SemaphoreType.DMA((steps, parts)),
            pltpu.SemaphoreType.DMA((steps,)),
        ],
        compiler_params=params(flight * CAP),
        cost_estimate=SMALL,
        name="expert_forward",
    )(hbm(gate_up), hbm(scale), hbm(quant))


def sort_kernel(half, keep, picks, *refs):
    chips, messages = refs[:half], refs[half : half + len(picks)]
    sibling, mine, *passed = refs[-2 - len(picks) :]
    for c in range(half):
        sibling[c] = chips[c][1]
        mine[c] = chips[c][0]
    for message, out, pick in zip(messages, passed, picks):
        tall = out.shape[0] - keep
        out[:keep] = message[:keep]
        out[keep:] = message[keep + pick * tall : keep + (pick + 1) * tall]


def sort_rows(chips, messages, picks, ties, hid):
    half = len(chips)
    _, groups, cap, share = chips[0].shape
    keep = 2 * half * (hid // TILE)
    return pl.pallas_call(
        functools.partial(sort_kernel, half, keep, picks),
        out_shape=(pltpu.VMEM((half, groups, cap, share), bf16),) * 2
        + (pltpu.VMEM((keep + share // TILE, cap, TILE), bf16),) * len(messages),
        in_specs=[VMEM] * (half + len(messages)) + [ANY] * len(ties),
        out_specs=(VMEM,) * (2 + len(messages)),
        compiler_params=params(2 * half * CAP),
        cost_estimate=SMALL,
        name="sort_rows",
    )(*chips, *messages, *ties)


def split_kernel(mine, swapped, *pieces):
    half = mine.shape[0]
    for j, piece in enumerate(pieces, 1):
        piece[: half - 1] = mine[1:, j]
        piece[half - 1 :] = swapped[:, j]


def split(mine, swapped):
    half, groups, cap, share = swapped.shape
    return pl.pallas_call(
        split_kernel,
        out_shape=(pltpu.VMEM((2 * half - 1, cap, share), bf16),) * (groups - 1),
        in_specs=[VMEM, VMEM],
        out_specs=(VMEM,) * (groups - 1),
        compiler_params=params(2 * half * CAP),
        cost_estimate=SMALL,
        name="split",
    )(mine, swapped)


def backward_kernel(
    flight, groups, scale_hbm, gate_up_hbm, quant_hbm, tie_ref, mine, swapped, out_hbm, hidden_ref,
    scale, gate_up, rows, quant, acc, out, scale_sem, gate_sems, in_sems, out_sems
):
    half = flight // 2
    me, group = lax.axis_index("expert"), lax.axis_index("dp")
    slots, hid = acc.shape
    share = quant.shape[2]

    def place(r):
        return pl.ds(pl.multiple_of(block_place(me, r, flight) * CAP, CAP), CAP)

    loads = [
        pltpu.make_async_copy(
            quant_hbm.at[:, pl.ds(pl.multiple_of((group ^ j) * share, share), share)],
            quant.at[j],
            in_sems.at[j],
        )
        for j in range(groups)
    ]
    gates = [
        pltpu.make_async_copy(
            gate_up_hbm.at[place(r)], gate_up.at[pl.ds(r * CAP, CAP)], gate_sems.at[r]
        )
        for r in range(flight)
    ]
    small = pltpu.make_async_copy(scale_hbm, scale, scale_sem)
    for copy in [small] + loads + gates:
        copy.start()
    for c in range(half):
        rows[:, c * CAP : (c + 1) * CAP, :] = mine[c]
        rows[:, (half + c) * CAP : (half + c + 1) * CAP, :] = swapped[c]
    small.wait()
    for j in range(groups):
        loads[j].wait()
        for b in range(share // QB):
            cols = slice(b * QB, (b + 1) * QB)
            part = lax.dot_general(
                rows[j, :, cols],
                quant[j, :, cols],
                (((1,), (1,)), ((), ())),
                preferred_element_type=f32,
            )
            for i in range(hid // QB):
                at = (slice(None), slice(i * QB, (i + 1) * QB))
                scaled = part[at] * scale[i, 0, (group ^ j) * (share // QB) + b]
                if j == 0 and b == 0:
                    acc[at] = scaled
                else:
                    acc[at] += scaled
    for copy in gates:
        copy.wait()
    gate = gate_up[:, :hid].astype(f32)
    up = gate_up[:, hid:].astype(f32)
    sig = jax.nn.sigmoid(gate)
    d_hidden = acc[...]
    out[:, :hid] = (d_hidden * up * sig * (1.0 + gate * (1.0 - sig))).astype(bf16)
    silu = gate * sig
    out[:, hid:] = (d_hidden * silu).astype(bf16)
    hidden_ref[...] = (silu * up).astype(bf16)
    stores = [
        pltpu.make_async_copy(out.at[pl.ds(r * CAP, CAP)], out_hbm.at[place(r)], out_sems.at[r])
        for r in range(flight)
    ]
    for copy in stores:
        copy.start()
    for copy in stores:
        copy.wait()


def backward(scale, gate_up, quant, tie, mine, swapped):
    slots, double = gate_up.shape
    hid, width = quant.shape
    half, groups, cap, share = swapped.shape
    flight = 2 * half
    return pl.pallas_call(
        functools.partial(backward_kernel, flight, groups),
        out_shape=(pltpu.HBM((slots, double), bf16), pltpu.VMEM((slots, hid), bf16)),
        in_specs=[HBM, HBM, HBM, ANY, VMEM, VMEM],
        out_specs=(HBM, VMEM),
        scratch_shapes=[
            pltpu.SMEM(scale.shape, f32),
            pltpu.VMEM((slots, double), bf16),
            pltpu.VMEM((groups, slots, share), bf16),
            pltpu.VMEM((groups, hid, share), bf16),
            pltpu.VMEM((slots, hid), f32),
            pltpu.VMEM((slots, double), bf16),
            pltpu.SemaphoreType.DMA,
            pltpu.SemaphoreType.DMA((flight,)),
            pltpu.SemaphoreType.DMA((groups,)),
            pltpu.SemaphoreType.DMA((flight,)),
        ],
        compiler_params=params(slots),
        cost_estimate=SMALL,
        name="expert_backward",
    )(hbm(scale), hbm(gate_up), hbm(quant), tie, mine, swapped)


def combine_kernel(
    block, ids_hbm, own_hbm, dout_hbm, ret_hbm, out_ref, dprobs_ref, ids_ref, own_ref, dout, ret_ref, sems
):
    copies = [
        pltpu.make_async_copy(ids_hbm, ids_ref, sems.at[0]),
        pltpu.make_async_copy(own_hbm, own_ref, sems.at[1]),
        pltpu.make_async_copy(dout_hbm, dout, sems.at[2]),
        pltpu.make_async_copy(ret_hbm, ret_ref, sems.at[3]),
    ]
    for copy in copies:
        copy.start()
    topk, tokens = ids_ref.shape
    slots = own_ref.shape[0]
    width = dout.shape[1]
    flight = slots // CAP
    me = lax.axis_index("expert")
    copies[1].wait()
    own = own_ref[...]
    turned = own.T
    high = turned.astype(bf16)
    low = (turned - high.astype(f32)).astype(bf16)
    total = jnp.zeros((slots, tokens), f32)
    for copy in (copies[0], copies[2], copies[3]):
        copy.wait()
    for cols in chunks(width, block):
        here = jnp.concatenate(
            [ret_ref[block_place(me, r, flight), :, cols] for r in range(flight)], axis=0
        )
        out = jnp.dot(high, here, preferred_element_type=f32)
        out = out + jnp.dot(low, here, preferred_element_type=f32)
        out_ref[:, cols] = out.astype(bf16)
        total = total + lax.dot_general(
            here, dout[:, cols], (((1,), (1,)), ((), ())), preferred_element_type=f32
        )
    inner = jnp.where(own > 0.0, total, 0.0)
    row_expert = block_place(me, lax.broadcasted_iota(jnp.int32, (slots, 1), 0) // CAP, flight)
    for k in range(topk):
        mine = jnp.where(ids_ref[k : k + 1, :] == row_expert, inner, 0.0)
        dprobs_ref[k : k + 1, :] = jnp.sum(mine, axis=0, keepdims=True)


def combine(ids, own, d_out, returned, block=1024):
    tokens, width = d_out.shape
    return pl.pallas_call(
        functools.partial(combine_kernel, block),
        out_shape=(
            pltpu.HBM((tokens, width), bf16),
            pltpu.HBM(ids.shape, f32),
        ),
        in_specs=[HBM, HBM, HBM, HBM],
        out_specs=(VMEM, VMEM),
        scratch_shapes=[
            pltpu.VMEM(ids.shape, jnp.int32),
            pltpu.VMEM(own.shape, f32),
            pltpu.VMEM((tokens, width), bf16),
            pltpu.VMEM(returned.shape, bf16),
            pltpu.SemaphoreType.DMA((4,)),
        ],
        compiler_params=params(own.shape[0]),
        cost_estimate=SMALL,
        name="combine",
    )(hbm(ids), hbm(own), hbm(d_out), hbm(returned))


def weight_grad_kernel(groups, block, tie_ref, mine, swapped, hidden_ref, *refs):
    parts, messages = refs[: groups - 1], refs[groups - 1 : 2 * groups - 2]
    out_hbm, hidden, own, out, out_sems = refs[2 * groups - 2 :]
    half = mine.shape[0]
    cap, share = parts[0].shape[1:]
    flight = 2 * half
    slots = flight * cap
    wide = hidden_ref.shape[1] // TILE
    hidden[:slots, :] = hidden_ref[...]
    for j in range(1, groups):
        bit = j if j % 2 else max(b for b in bits_of(groups) if b <= j)
        message = messages[j - 1]
        for r in range(flight):
            for q in range(wide):
                hidden[
                    j * slots + r * cap : j * slots + (r + 1) * cap, q * TILE : (q + 1) * TILE
                ] = message[r * wide + q]
        for q in range(share // TILE):
            own[j - 1, :, q * TILE : (q + 1) * TILE] = message[
                flight * wide + (j - bit) * (share // TILE) + q
            ]
    stores = []
    for n, cols in enumerate(chunks(share, block)):
        grads = [mine[c, 0, :, cols] for c in range(half)]
        grads += [swapped[c, 0, :, cols] for c in range(half)]
        for j in range(1, groups):
            grads.append(own[j - 1, :, cols])
            grads.append(parts[j - 1][:, :, cols].reshape(slots - cap, block))
        out[cols, :] = lax.dot_general(
            jnp.concatenate(grads, axis=0),
            hidden[...],
            (((0,), (0,)), ((), ())),
            preferred_element_type=f32,
        ).astype(bf16)
        stores.append(pltpu.make_async_copy(out.at[cols], out_hbm.at[cols], out_sems.at[n]))
        stores[n].start()
    for copy in stores:
        copy.wait()


def weight_grad(tie, mine, swapped, hidden, parts, messages, block=256):
    half, groups, cap, share = swapped.shape
    slots, hid = hidden.shape
    return pl.pallas_call(
        functools.partial(weight_grad_kernel, groups, block),
        out_shape=pltpu.HBM((share, hid), bf16),
        in_specs=[HBM] + [VMEM] * (1 + 2 * groups),
        out_specs=HBM,
        scratch_shapes=[
            pltpu.VMEM((groups * slots, hid), bf16),
            pltpu.VMEM((groups - 1, cap, share), bf16),
            pltpu.VMEM((share, hid), bf16),
            pltpu.SemaphoreType.DMA((share // block,)),
        ],
        compiler_params=params(slots),
        cost_estimate=SMALL,
        name="weight_grad",
    )(hbm(tie), mine, swapped, hidden, *parts, *messages)


def swap(value, axis, j):
    size = lax.axis_size(axis)
    return lax.ppermute(value, axis, [(i, i ^ j) for i in range(size)])


def shards(route_ids, route_probs, capacity, hot_lists, gate_up, w_quant, w_scale, d_out):
    flight = lax.axis_size("expert")
    groups = lax.axis_size("dp")
    gate_up = gate_up[0, 0]
    ids, probs = route_ids.T, route_probs.T
    scale = w_scale.transpose(1, 0, 2)
    own, *rest = dispatch(
        gate_up, capacity, hot_lists, ids, probs, d_out, flight, groups
    )
    half, bits = flight // 2, bits_of(groups)
    chips = rest[:1] + [swap(rest[c], "expert", 2 * c) for c in range(1, half)]
    messages = {}
    for bit, message in zip(bits, rest[half:]):
        if bit > 1:
            for j in sorted(messages):
                messages[j ^ bit] = swap(messages[j], "dp", bit)
        messages[bit] = swap(message, "dp", bit)
    even = list(range(2, groups, 2))
    picks = [j + 1 - max(bit for bit in bits if bit <= j) for j in even]
    expert_out = forward(scale, gate_up, w_quant[0], flight)
    returned = lax.all_to_all(expert_out, "expert", split_axis=0, concat_axis=0, tiled=True)
    sibling, mine, *passed = sort_rows(
        chips, [messages[j] for j in even], picks, [hbm(expert_out), messages[1]], gate_up.shape[1] // 2
    )
    for j, message in zip(even, passed):
        messages[j + 1] = swap(message, "dp", 1)
    messages = [messages[j] for j in range(1, groups)]
    swapped = swap(sibling, "expert", 1)
    pieces = split(mine, swapped)
    parts = [swap(pieces[j - 1], "dp", j) for j in range(1, groups)]
    d_gate_up, hidden = backward(scale, gate_up, w_quant[0], pieces[0], mine, swapped)
    combined, d_probs = combine(ids, own, d_out, returned)
    d_weight = weight_grad(d_probs, mine, swapped, hidden, parts, messages)
    return (combined, d_probs.T, d_gate_up[None, None], d_weight[None])


def solution(mesh):
    placed = (
        P(("dp", "expert"), None),
        P(("dp", "expert"), None),
        P(),
        P("dp", None),
        P("dp", "expert", None, None),
        P("expert", None, None),
        P("expert", None, None),
        P(("dp", "expert"), None),
    )
    return jax.shard_map(
        shards,
        mesh=mesh,
        in_specs=placed,
        out_specs=(
            P(("dp", "expert"), None),
            P(("dp", "expert"), None),
            P("dp", "expert", None, None),
            P("expert", "dp", None),
        ),
        check_vma=False,
    )
```

```python
import functools

import jax
import jax.numpy as jnp
from jax import lax
from jax.experimental import pallas as pl
from jax.experimental.pallas import tpu as pltpu
from jax.sharding import PartitionSpec as P

QB = 128
CAP = 16
TILE = 256
PART = 256

bf16 = jnp.bfloat16
f32 = jnp.float32

SMALL = pl.CostEstimate(flops=1024, bytes_accessed=1024, transcendentals=0)

VMEM = pl.BlockSpec(memory_space=pltpu.VMEM)
ANY = pl.BlockSpec(memory_space=pl.ANY)
HBM = pl.BlockSpec(memory_space=pltpu.HBM)


def params(slots):
    return pltpu.CompilerParams(vmem_limit_bytes=(12 + slots // 32) * 1024 * 1024)


def hbm(value):
    return pltpu.with_memory_space_constraint(value, pltpu.HBM)


def chunks(total, size):
    return [pl.ds(start, size) for start in range(0, total, size)]


def bits_of(groups):
    bits = []
    while groups > 1:
        groups //= 2
        bits.append(groups)
    return bits


def message_tiles(flight, groups, bit, hid, share):
    far = 1 if 2 * bit == groups else 0
    return flight * (hid // TILE) + bit * (share // TILE) + far


def block_place(me, r, flight):
    half = flight // 2
    return me ^ (2 * (r % half) + r // half)


def dispatch_kernel(flight, groups, gate_up_hbm, cap_hbm, hot_hbm, ids_hbm, probs_hbm, dout_hbm, *refs):
    half = flight // 2
    bits = bits_of(groups)
    outs = 2 + half + len(bits)
    own_hbm, hidden_ref, *chips = refs[: 2 + half]
    messages = dict(zip(bits, refs[2 + half : outs]))
    gate_up, cap_ref, hot_ref, ids_ref, probs_ref, dout, own_ref = refs[outs : outs + 7]
    gate_sems, own_sem, small_sems, in_sems = refs[outs + 7 :]
    topk, tokens = ids_ref.shape
    slots = flight * CAP
    me, group = lax.axis_index("expert"), lax.axis_index("dp")
    share = dout_hbm.shape[1] // groups
    hid = hidden_ref.shape[1]
    small = [
        pltpu.make_async_copy(src, dst, small_sems.at[i])
        for i, (src, dst) in enumerate(
            [(ids_hbm, ids_ref), (probs_hbm, probs_ref), (cap_hbm, cap_ref), (hot_hbm, hot_ref)]
        )
    ]
    loads = [
        pltpu.make_async_copy(
            dout_hbm.at[:, pl.ds(pl.multiple_of((group ^ j) * share, share), share)],
            dout.at[j],
            in_sems.at[j],
        )
        for j in range(groups)
    ]
    gates = [
        pltpu.make_async_copy(
            gate_up_hbm.at[pl.ds(pl.multiple_of(block_place(me, r, flight) * CAP, CAP), CAP)],
            gate_up.at[pl.ds(r * CAP, CAP)],
            gate_sems.at[r],
        )
        for r in range(flight)
    ]
    for copy in small + loads + gates:
        copy.start()
    for copy in small:
        copy.wait()
    row = lax.broadcasted_iota(jnp.int32, (slots, 1), 0)
    row_expert = block_place(me, row // CAP, flight)
    row_rank = (row % CAP).astype(f32)
    limit = jnp.zeros((slots, 1), jnp.int32)
    for e in range(flight):
        hot = hot_ref[0, 0] == e
        for h in range(1, hot_ref.shape[1]):
            hot = jnp.logical_or(hot, hot_ref[0, h] == e)
        limit = jnp.where(row_expert == e, jnp.where(hot, CAP, cap_ref[e]), limit)
    limit = limit.astype(f32)
    named = jnp.zeros((slots, tokens), f32)
    weight = jnp.zeros((slots, tokens), f32)
    for k in range(topk):
        hit = ids_ref[k : k + 1, :] == row_expert
        named = jnp.where(hit, 1.0, named)
        weight = jnp.where(hit, probs_ref[k : k + 1, :], weight)
    earlier = lax.broadcasted_iota(jnp.int32, (tokens, tokens), 0)
    later = lax.broadcasted_iota(jnp.int32, (tokens, tokens), 1)
    before = (earlier < later).astype(f32).astype(bf16)
    rank = jnp.dot(named.astype(bf16), before, preferred_element_type=f32)
    owns = (named > 0.0) & (rank == row_rank) & (rank < limit)
    own_weight = jnp.where(owns, weight, 0.0)
    own_ref[...] = own_weight
    own_copy = pltpu.make_async_copy(own_ref, own_hbm, own_sem)
    own_copy.start()
    owner = jnp.where(owns, 1.0, 0.0).astype(bf16)
    slot_weight = jnp.sum(own_weight, axis=1, keepdims=True)
    for copy in loads:
        copy.wait()
    for j in range(groups):
        part = jnp.dot(owner, dout[j], preferred_element_type=f32)
        part = (part * slot_weight).astype(bf16)
        for r in range(flight):
            chips[r % half][r // half, j] = part[r * CAP : (r + 1) * CAP, :]
        for bit in bits:
            if bit <= j < 2 * bit:
                first = flight * (hid // TILE) + (j - bit) * (share // TILE)
                for q in range(share // TILE):
                    messages[bit][first + q] = part[:CAP, q * TILE : (q + 1) * TILE]
    messages[bits[0]][messages[bits[0]].shape[0] - 1] = jnp.zeros((CAP, TILE), bf16)
    for copy in gates:
        copy.wait()
    for r in range(flight):
        at = slice(r * CAP, (r + 1) * CAP)
        gate = gate_up[at, :hid].astype(f32)
        up = gate_up[at, hid:].astype(f32)
        block = (gate * jax.nn.sigmoid(gate) * up).astype(bf16)
        hidden_ref[at, :] = block
        for bit in bits:
            for q in range(hid // TILE):
                messages[bit][r * (hid // TILE) + q] = block[:, q * TILE : (q + 1) * TILE]
    own_copy.wait()


def dispatch(gate_up, capacity, hot_row, ids, probs, d_out, flight, groups):
    tokens, width = d_out.shape
    rows, double = gate_up.shape
    slots = flight * CAP
    share = width // groups
    half = flight // 2
    return pl.pallas_call(
        functools.partial(dispatch_kernel, flight, groups),
        out_shape=(pltpu.HBM((slots, tokens), f32), pltpu.VMEM((rows, double // 2), bf16))
        + (pltpu.VMEM((2, groups, CAP, share), bf16),) * half
        + tuple(
            pltpu.VMEM((message_tiles(flight, groups, bit, double // 2, share), CAP, TILE), bf16)
            for bit in bits_of(groups)
        ),
        in_specs=[HBM] * 6,
        out_specs=(HBM, VMEM) + (VMEM,) * (half + len(bits_of(groups))),
        scratch_shapes=[
            pltpu.VMEM((rows, double), bf16),
            pltpu.SMEM(capacity.shape, jnp.int32),
            pltpu.SMEM(hot_row.shape, jnp.int32),
            pltpu.VMEM(ids.shape, jnp.int32),
            pltpu.VMEM(probs.shape, f32),
            pltpu.VMEM((groups, tokens, share), bf16),
            pltpu.VMEM((slots, tokens), f32),
            pltpu.SemaphoreType.DMA((flight,)),
            pltpu.SemaphoreType.DMA,
            pltpu.SemaphoreType.DMA((4,)),
            pltpu.SemaphoreType.DMA((groups,)),
        ],
        compiler_params=params(slots),
        cost_estimate=SMALL,
        name="dispatch",
    )(hbm(gate_up), hbm(capacity), hbm(hot_row), hbm(ids), hbm(probs), hbm(d_out))


def forward_kernel(
    flight, block, hidden_ref, scale_hbm, quant_hbm, out_hbm,
    scale, hidden, quant, out, scale_sem, in_sems, out_sems
):
    steps, hid, _ = quant.shape
    me = lax.axis_index("expert")
    loads = [
        pltpu.make_async_copy(quant_hbm.at[:, pl.ds(c * block, block)], quant.at[c], in_sems.at[c])
        for c in range(steps)
    ]
    small = pltpu.make_async_copy(scale_hbm, scale, scale_sem)
    for copy in [small] + loads:
        copy.start()
    for r in range(flight):
        place = pl.multiple_of(block_place(me, r, flight) * CAP, CAP)
        hidden[pl.ds(place, CAP), :] = hidden_ref[pl.ds(r * CAP, CAP), :]
    small.wait()
    stores = []
    for c in range(steps):
        cols = pl.ds(c * block, block)
        loads[c].wait()
        for p in range(0, block, PART):
            total = [None] * (PART // QB)
            for i in range(hid // QB):
                part = jnp.dot(
                    hidden[:, i * QB : (i + 1) * QB],
                    quant[c, i * QB : (i + 1) * QB, p : p + PART],
                    preferred_element_type=f32,
                )
                for j in range(PART // QB):
                    factor = scale[i, 0, (c * block + p) // QB + j]
                    scaled = part[:, j * QB : (j + 1) * QB] * factor
                    total[j] = scaled if i == 0 else total[j] + scaled
            for j in range(PART // QB):
                at = pl.ds(c * block + p + j * QB, QB)
                out[:, :, at] = total[j].astype(bf16).reshape(flight, CAP, QB)
        stores.append(
            pltpu.make_async_copy(out.at[:, :, cols], out_hbm.at[:, :, cols], out_sems.at[c])
        )
        stores[c].start()
    for copy in stores:
        copy.wait()


def forward(scale, hidden, quant, flight, block=512):
    hid, width = quant.shape
    steps = width // block
    return pl.pallas_call(
        functools.partial(forward_kernel, flight, block),
        out_shape=pltpu.HBM((flight, CAP, width), bf16),
        in_specs=[VMEM, HBM, HBM],
        out_specs=HBM,
        scratch_shapes=[
            pltpu.SMEM(scale.shape, f32),
            pltpu.VMEM(hidden.shape, bf16),
            pltpu.VMEM((steps, hid, block), bf16),
            pltpu.VMEM((flight, CAP, width), bf16),
            pltpu.SemaphoreType.DMA,
            pltpu.SemaphoreType.DMA((steps,)),
            pltpu.SemaphoreType.DMA((steps,)),
        ],
        compiler_params=params(flight * CAP),
        cost_estimate=SMALL,
        name="expert_forward",
    )(hidden, hbm(scale), hbm(quant))


def sort_kernel(half, keep, picks, *refs):
    chips, messages = refs[:half], refs[half : half + len(picks)]
    sibling, mine, *passed = refs[-2 - len(picks) :]
    for c in range(half):
        sibling[c] = chips[c][1]
        mine[c] = chips[c][0]
    for message, out, pick in zip(messages, passed, picks):
        tall = out.shape[0] - keep
        out[:keep] = message[:keep]
        out[keep:] = message[keep + pick * tall : keep + (pick + 1) * tall]


def sort_rows(chips, messages, picks, ties, hid):
    half = len(chips)
    _, groups, cap, share = chips[0].shape
    keep = 2 * half * (hid // TILE)
    return pl.pallas_call(
        functools.partial(sort_kernel, half, keep, picks),
        out_shape=(pltpu.VMEM((half, groups, cap, share), bf16),) * 2
        + (pltpu.VMEM((keep + share // TILE, cap, TILE), bf16),) * len(messages),
        in_specs=[VMEM] * (half + len(messages)) + [ANY] * len(ties),
        out_specs=(VMEM,) * (2 + len(messages)),
        compiler_params=params(2 * half * CAP),
        cost_estimate=SMALL,
        name="sort_rows",
    )(*chips, *messages, *ties)


def split_kernel(mine, swapped, *pieces):
    half = mine.shape[0]
    for j, piece in enumerate(pieces, 1):
        piece[: half - 1] = mine[1:, j]
        piece[half - 1 :] = swapped[:, j]


def split(mine, swapped):
    half, groups, cap, share = swapped.shape
    return pl.pallas_call(
        split_kernel,
        out_shape=(pltpu.VMEM((2 * half - 1, cap, share), bf16),) * (groups - 1),
        in_specs=[VMEM, VMEM],
        out_specs=(VMEM,) * (groups - 1),
        compiler_params=params(2 * half * CAP),
        cost_estimate=SMALL,
        name="split",
    )(mine, swapped)


def backward_kernel(
    flight, groups, scale_hbm, gate_up_hbm, quant_hbm, message_hbm, tie_ref, mine, swapped,
    out_hbm, message_ref,
    scale, gate_up, rows, quant, acc, out, small_sems, gate_sems, in_sems, out_sems
):
    half = flight // 2
    message_copy = pltpu.make_async_copy(message_hbm, message_ref, small_sems.at[1])
    message_copy.start()
    me, group = lax.axis_index("expert"), lax.axis_index("dp")
    slots, hid = acc.shape
    share = quant.shape[2]

    def place(r):
        return pl.ds(pl.multiple_of(block_place(me, r, flight) * CAP, CAP), CAP)

    loads = [
        pltpu.make_async_copy(
            quant_hbm.at[:, pl.ds(pl.multiple_of((group ^ j) * share, share), share)],
            quant.at[j],
            in_sems.at[j],
        )
        for j in range(groups)
    ]
    gates = [
        pltpu.make_async_copy(
            gate_up_hbm.at[place(r)], gate_up.at[pl.ds(r * CAP, CAP)], gate_sems.at[r]
        )
        for r in range(flight)
    ]
    small = pltpu.make_async_copy(scale_hbm, scale, small_sems.at[0])
    for copy in [small] + loads + gates:
        copy.start()
    for c in range(half):
        rows[:, c * CAP : (c + 1) * CAP, :] = mine[c]
        rows[:, (half + c) * CAP : (half + c + 1) * CAP, :] = swapped[c]
    small.wait()
    for j in range(groups):
        loads[j].wait()
        for b in range(share // QB):
            cols = slice(b * QB, (b + 1) * QB)
            part = lax.dot_general(
                rows[j, :, cols],
                quant[j, :, cols],
                (((1,), (1,)), ((), ())),
                preferred_element_type=f32,
            )
            for i in range(hid // QB):
                at = (slice(None), slice(i * QB, (i + 1) * QB))
                scaled = part[at] * scale[i, 0, (group ^ j) * (share // QB) + b]
                if j == 0 and b == 0:
                    acc[at] = scaled
                else:
                    acc[at] += scaled
    for copy in gates:
        copy.wait()
    gate = gate_up[:, :hid].astype(f32)
    up = gate_up[:, hid:].astype(f32)
    sig = jax.nn.sigmoid(gate)
    d_hidden = acc[...]
    out[:, :hid] = (d_hidden * up * sig * (1.0 + gate * (1.0 - sig))).astype(bf16)
    out[:, hid:] = (d_hidden * (gate * sig)).astype(bf16)
    stores = [
        pltpu.make_async_copy(out.at[pl.ds(r * CAP, CAP)], out_hbm.at[place(r)], out_sems.at[r])
        for r in range(flight)
    ]
    for copy in stores:
        copy.start()
    for copy in stores:
        copy.wait()
    message_copy.wait()


def backward(scale, gate_up, quant, message, tie, mine, swapped):
    slots, double = gate_up.shape
    hid, width = quant.shape
    half, groups, cap, share = swapped.shape
    flight = 2 * half
    return pl.pallas_call(
        functools.partial(backward_kernel, flight, groups),
        out_shape=(pltpu.HBM((slots, double), bf16), pltpu.VMEM(message.shape, bf16)),
        in_specs=[HBM, HBM, HBM, HBM, ANY, VMEM, VMEM],
        out_specs=(HBM, VMEM),
        scratch_shapes=[
            pltpu.SMEM(scale.shape, f32),
            pltpu.VMEM((slots, double), bf16),
            pltpu.VMEM((groups, slots, share), bf16),
            pltpu.VMEM((groups, hid, share), bf16),
            pltpu.VMEM((slots, hid), f32),
            pltpu.VMEM((slots, double), bf16),
            pltpu.SemaphoreType.DMA((2,)),
            pltpu.SemaphoreType.DMA((flight,)),
            pltpu.SemaphoreType.DMA((groups,)),
            pltpu.SemaphoreType.DMA((flight,)),
        ],
        compiler_params=params(slots),
        cost_estimate=SMALL,
        name="expert_backward",
    )(hbm(scale), hbm(gate_up), hbm(quant), hbm(message), tie, mine, swapped)


def combine_kernel(
    block, ids_hbm, own_hbm, dout_hbm, ret_hbm, out_ref, dprobs_ref, ids_ref, own_ref, dout, ret_ref, sems
):
    copies = [
        pltpu.make_async_copy(ids_hbm, ids_ref, sems.at[0]),
        pltpu.make_async_copy(own_hbm, own_ref, sems.at[1]),
        pltpu.make_async_copy(dout_hbm, dout, sems.at[2]),
        pltpu.make_async_copy(ret_hbm, ret_ref, sems.at[3]),
    ]
    for copy in copies:
        copy.start()
    topk, tokens = ids_ref.shape
    slots = own_ref.shape[0]
    width = dout.shape[1]
    flight = slots // CAP
    me = lax.axis_index("expert")
    copies[1].wait()
    own = own_ref[...]
    turned = own.T
    high = turned.astype(bf16)
    low = (turned - high.astype(f32)).astype(bf16)
    total = jnp.zeros((slots, tokens), f32)
    for copy in (copies[0], copies[2], copies[3]):
        copy.wait()
    for cols in chunks(width, block):
        here = jnp.concatenate(
            [ret_ref[block_place(me, r, flight), :, cols] for r in range(flight)], axis=0
        )
        out = jnp.dot(high, here, preferred_element_type=f32)
        out = out + jnp.dot(low, here, preferred_element_type=f32)
        out_ref[:, cols] = out.astype(bf16)
        total = total + lax.dot_general(
            here, dout[:, cols], (((1,), (1,)), ((), ())), preferred_element_type=f32
        )
    inner = jnp.where(own > 0.0, total, 0.0)
    row_expert = block_place(me, lax.broadcasted_iota(jnp.int32, (slots, 1), 0) // CAP, flight)
    for k in range(topk):
        mine = jnp.where(ids_ref[k : k + 1, :] == row_expert, inner, 0.0)
        dprobs_ref[k : k + 1, :] = jnp.sum(mine, axis=0, keepdims=True)


def combine(ids, own, d_out, returned, block=1024):
    tokens, width = d_out.shape
    return pl.pallas_call(
        functools.partial(combine_kernel, block),
        out_shape=(
            pltpu.HBM((tokens, width), bf16),
            pltpu.HBM(ids.shape, f32),
        ),
        in_specs=[HBM, HBM, HBM, HBM],
        out_specs=(VMEM, VMEM),
        scratch_shapes=[
            pltpu.VMEM(ids.shape, jnp.int32),
            pltpu.VMEM(own.shape, f32),
            pltpu.VMEM((tokens, width), bf16),
            pltpu.VMEM(returned.shape, bf16),
            pltpu.SemaphoreType.DMA((4,)),
        ],
        compiler_params=params(own.shape[0]),
        cost_estimate=SMALL,
        name="combine",
    )(hbm(ids), hbm(own), hbm(d_out), hbm(returned))


def weight_grad_kernel(groups, block, tie_ref, mine, swapped, hidden_ref, *refs):
    parts, messages = refs[: groups - 1], refs[groups - 1 : 2 * groups - 2]
    out_hbm, hidden, own, out, out_sems = refs[2 * groups - 2 :]
    half = mine.shape[0]
    cap, share = parts[0].shape[1:]
    flight = 2 * half
    slots = flight * cap
    wide = hidden_ref.shape[1] // TILE
    hidden[:slots, :] = hidden_ref[...]
    for j in range(1, groups):
        bit = j if j % 2 else max(b for b in bits_of(groups) if b <= j)
        message = messages[j - 1]
        for r in range(flight):
            for q in range(wide):
                hidden[
                    j * slots + r * cap : j * slots + (r + 1) * cap, q * TILE : (q + 1) * TILE
                ] = message[r * wide + q]
        for q in range(share // TILE):
            own[j - 1, :, q * TILE : (q + 1) * TILE] = message[
                flight * wide + (j - bit) * (share // TILE) + q
            ]
    stores = []
    for n, cols in enumerate(chunks(share, block)):
        grads = [mine[c, 0, :, cols] for c in range(half)]
        grads += [swapped[c, 0, :, cols] for c in range(half)]
        for j in range(1, groups):
            grads.append(own[j - 1, :, cols])
            grads.append(parts[j - 1][:, :, cols].reshape(slots - cap, block))
        out[cols, :] = lax.dot_general(
            jnp.concatenate(grads, axis=0),
            hidden[...],
            (((0,), (0,)), ((), ())),
            preferred_element_type=f32,
        ).astype(bf16)
        stores.append(pltpu.make_async_copy(out.at[cols], out_hbm.at[cols], out_sems.at[n]))
        stores[n].start()
    for copy in stores:
        copy.wait()


def weight_grad(tie, mine, swapped, hidden, parts, messages, block=256):
    half, groups, cap, share = swapped.shape
    slots, hid = hidden.shape
    return pl.pallas_call(
        functools.partial(weight_grad_kernel, groups, block),
        out_shape=pltpu.HBM((share, hid), bf16),
        in_specs=[HBM] + [VMEM] * (1 + 2 * groups),
        out_specs=HBM,
        scratch_shapes=[
            pltpu.VMEM((groups * slots, hid), bf16),
            pltpu.VMEM((groups - 1, cap, share), bf16),
            pltpu.VMEM((share, hid), bf16),
            pltpu.SemaphoreType.DMA((share // block,)),
        ],
        compiler_params=params(slots),
        cost_estimate=SMALL,
        name="weight_grad",
    )(hbm(tie), mine, swapped, hidden, *parts, *messages)


def swap(value, axis, j):
    size = lax.axis_size(axis)
    return lax.ppermute(value, axis, [(i, i ^ j) for i in range(size)])


def shards(route_ids, route_probs, capacity, hot_lists, gate_up, w_quant, w_scale, d_out):
    flight = lax.axis_size("expert")
    groups = lax.axis_size("dp")
    gate_up = gate_up[0, 0]
    ids, probs = route_ids.T, route_probs.T
    scale = w_scale.transpose(1, 0, 2)
    own, hidden, *rest = dispatch(
        gate_up, capacity, hot_lists, ids, probs, d_out, flight, groups
    )
    half, bits = flight // 2, bits_of(groups)
    chips = rest[:1] + [swap(rest[c], "expert", 2 * c) for c in range(1, half)]
    messages = {}
    for bit, message in zip(bits, rest[half:]):
        if bit > 1:
            for j in sorted(messages):
                messages[j ^ bit] = swap(messages[j], "dp", bit)
        messages[bit] = swap(message, "dp", bit)
    even = list(range(2, groups, 2))
    picks = [j + 1 - max(bit for bit in bits if bit <= j) for j in even]
    expert_out = forward(scale, hidden, w_quant[0], flight)
    returned = lax.all_to_all(expert_out, "expert", split_axis=0, concat_axis=0, tiled=True)
    sibling, mine, *passed = sort_rows(
        chips, [messages[j] for j in even], picks, [hbm(expert_out), hbm(messages[1])], hidden.shape[1]
    )
    for j, message in zip(even, passed):
        messages[j + 1] = swap(message, "dp", 1)
    messages = [messages[j] for j in range(1, groups)]
    swapped = swap(sibling, "expert", 1)
    pieces = split(mine, swapped)
    parts = [swap(pieces[j - 1], "dp", j) for j in range(1, groups)]
    d_gate_up, messages[0] = backward(
        scale, gate_up, w_quant[0], messages[0], pieces[0], mine, swapped
    )
    combined, d_probs = combine(ids, own, d_out, returned)
    d_weight = weight_grad(d_probs, mine, swapped, hidden, parts, messages)
    return (combined, d_probs.T, d_gate_up[None, None], d_weight[None])


def solution(mesh):
    placed = (
        P(("dp", "expert"), None),
        P(("dp", "expert"), None),
        P(),
        P("dp", None),
        P("dp", "expert", None, None),
        P("expert", None, None),
        P("expert", None, None),
        P(("dp", "expert"), None),
    )
    return jax.shard_map(
        shards,
        mesh=mesh,
        in_specs=placed,
        out_specs=(
            P(("dp", "expert"), None),
            P(("dp", "expert"), None),
            P("dp", "expert", None, None),
            P("expert", "dp", None),
        ),
        check_vma=False,
    )
```

```python
import functools

import jax
import jax.numpy as jnp
from jax import lax
from jax.experimental import pallas as pl
from jax.experimental.pallas import tpu as pltpu
from jax.sharding import PartitionSpec as P

QB = 128
CAP = 16
TILE = 256
PART = 256

bf16 = jnp.bfloat16
f32 = jnp.float32

SMALL = pl.CostEstimate(flops=1024, bytes_accessed=1024, transcendentals=0)

VMEM = pl.BlockSpec(memory_space=pltpu.VMEM)
ANY = pl.BlockSpec(memory_space=pl.ANY)
HBM = pl.BlockSpec(memory_space=pltpu.HBM)


def params(slots):
    return pltpu.CompilerParams(vmem_limit_bytes=3 * (slots // 32) * 1024 * 1024)


def hbm(value):
    return pltpu.with_memory_space_constraint(value, pltpu.HBM)


def chunks(total, size):
    return [pl.ds(start, size) for start in range(0, total, size)]


def bits_of(groups):
    bits = []
    while groups > 1:
        groups //= 2
        bits.append(groups)
    return bits


def message_tiles(flight, groups, bit, hid, share):
    far = 1 if 2 * bit == groups else 0
    return flight * (hid // TILE) + bit * (share // TILE) + far


def block_place(me, r, flight):
    half = flight // 2
    return me ^ (2 * (r % half) + r // half)


def dispatch_kernel(flight, groups, gate_up_hbm, cap_hbm, hot_hbm, ids_hbm, probs_hbm, dout_hbm, *refs):
    half = flight // 2
    bits = bits_of(groups)
    outs = 2 + half + len(bits)
    own_hbm, hidden_ref, *chips = refs[: 2 + half]
    messages = dict(zip(bits, refs[2 + half : outs]))
    gate_up, cap_ref, hot_ref, ids_ref, probs_ref, dout, own_ref = refs[outs : outs + 7]
    gate_sems, own_sem, small_sems, in_sems = refs[outs + 7 :]
    topk, tokens = ids_ref.shape
    slots = flight * CAP
    me, group = lax.axis_index("expert"), lax.axis_index("dp")
    share = dout_hbm.shape[1] // groups
    hid = hidden_ref.shape[1]
    small = [
        pltpu.make_async_copy(src, dst, small_sems.at[i])
        for i, (src, dst) in enumerate(
            [(ids_hbm, ids_ref), (probs_hbm, probs_ref), (cap_hbm, cap_ref), (hot_hbm, hot_ref)]
        )
    ]
    loads = [
        pltpu.make_async_copy(
            dout_hbm.at[:, pl.ds(pl.multiple_of((group ^ j) * share, share), share)],
            dout.at[j],
            in_sems.at[j],
        )
        for j in range(groups)
    ]
    gates = [
        pltpu.make_async_copy(
            gate_up_hbm.at[pl.ds(pl.multiple_of(block_place(me, r, flight) * CAP, CAP), CAP)],
            gate_up.at[pl.ds(r * CAP, CAP)],
            gate_sems.at[r],
        )
        for r in range(flight)
    ]
    for copy in small + loads + gates:
        copy.start()
    for copy in small:
        copy.wait()
    row = lax.broadcasted_iota(jnp.int32, (slots, 1), 0)
    row_expert = block_place(me, row // CAP, flight)
    row_rank = (row % CAP).astype(f32)
    limit = jnp.zeros((slots, 1), jnp.int32)
    for e in range(flight):
        hot = hot_ref[0, 0] == e
        for h in range(1, hot_ref.shape[1]):
            hot = jnp.logical_or(hot, hot_ref[0, h] == e)
        limit = jnp.where(row_expert == e, jnp.where(hot, CAP, cap_ref[e]), limit)
    limit = limit.astype(f32)
    named = jnp.zeros((slots, tokens), f32)
    weight = jnp.zeros((slots, tokens), f32)
    for k in range(topk):
        hit = ids_ref[k : k + 1, :] == row_expert
        named = jnp.where(hit, 1.0, named)
        weight = jnp.where(hit, probs_ref[k : k + 1, :], weight)
    earlier = lax.broadcasted_iota(jnp.int32, (tokens, tokens), 0)
    later = lax.broadcasted_iota(jnp.int32, (tokens, tokens), 1)
    before = (earlier < later).astype(f32).astype(bf16)
    rank = jnp.dot(named.astype(bf16), before, preferred_element_type=f32)
    owns = (named > 0.0) & (rank == row_rank) & (rank < limit)
    own_weight = jnp.where(owns, weight, 0.0)
    own_ref[...] = own_weight
    own_copy = pltpu.make_async_copy(own_ref, own_hbm, own_sem)
    own_copy.start()
    owner = jnp.where(owns, 1.0, 0.0).astype(bf16)
    slot_weight = jnp.sum(own_weight, axis=1, keepdims=True)
    for copy in loads:
        copy.wait()
    for j in range(groups):
        part = jnp.dot(owner, dout[j], preferred_element_type=f32)
        part = (part * slot_weight).astype(bf16)
        for r in range(flight):
            chips[r % half][r // half, j] = part[r * CAP : (r + 1) * CAP, :]
        for bit in bits:
            if bit <= j < 2 * bit:
                first = flight * (hid // TILE) + (j - bit) * (share // TILE)
                for q in range(share // TILE):
                    messages[bit][first + q] = part[:CAP, q * TILE : (q + 1) * TILE]
    messages[bits[0]][messages[bits[0]].shape[0] - 1] = jnp.zeros((CAP, TILE), bf16)
    for copy in gates:
        copy.wait()
    for r in range(flight):
        at = slice(r * CAP, (r + 1) * CAP)
        gate = gate_up[at, :hid].astype(f32)
        up = gate_up[at, hid:].astype(f32)
        block = (gate * jax.nn.sigmoid(gate) * up).astype(bf16)
        hidden_ref[at, :] = block
        for bit in bits:
            for q in range(hid // TILE):
                messages[bit][r * (hid // TILE) + q] = block[:, q * TILE : (q + 1) * TILE]
    own_copy.wait()


def dispatch(gate_up, capacity, hot_row, ids, probs, d_out, flight, groups):
    tokens, width = d_out.shape
    rows, double = gate_up.shape
    slots = flight * CAP
    share = width // groups
    half = flight // 2
    return pl.pallas_call(
        functools.partial(dispatch_kernel, flight, groups),
        out_shape=(pltpu.HBM((slots, tokens), f32), pltpu.VMEM((rows, double // 2), bf16))
        + (pltpu.VMEM((2, groups, CAP, share), bf16),) * half
        + tuple(
            pltpu.VMEM((message_tiles(flight, groups, bit, double // 2, share), CAP, TILE), bf16)
            for bit in bits_of(groups)
        ),
        in_specs=[HBM] * 6,
        out_specs=(HBM, VMEM) + (VMEM,) * (half + len(bits_of(groups))),
        scratch_shapes=[
            pltpu.VMEM((rows, double), bf16),
            pltpu.SMEM(capacity.shape, jnp.int32),
            pltpu.SMEM(hot_row.shape, jnp.int32),
            pltpu.VMEM(ids.shape, jnp.int32),
            pltpu.VMEM(probs.shape, f32),
            pltpu.VMEM((groups, tokens, share), bf16),
            pltpu.VMEM((slots, tokens), f32),
            pltpu.SemaphoreType.DMA((flight,)),
            pltpu.SemaphoreType.DMA,
            pltpu.SemaphoreType.DMA((4,)),
            pltpu.SemaphoreType.DMA((groups,)),
        ],
        compiler_params=params(slots),
        cost_estimate=SMALL,
        name="dispatch",
    )(hbm(gate_up), hbm(capacity), hbm(hot_row), hbm(ids), hbm(probs), hbm(d_out))


def forward_kernel(
    flight, block, hidden_ref, scale_hbm, quant_hbm, out_hbm,
    scale, hidden, quant, out, scale_sem, in_sems, out_sems
):
    steps, hid, _ = quant.shape
    me = lax.axis_index("expert")
    loads = [
        pltpu.make_async_copy(quant_hbm.at[:, pl.ds(c * block, block)], quant.at[c], in_sems.at[c])
        for c in range(steps)
    ]
    small = pltpu.make_async_copy(scale_hbm, scale, scale_sem)
    for copy in [small] + loads:
        copy.start()
    for r in range(flight):
        place = pl.multiple_of(block_place(me, r, flight) * CAP, CAP)
        hidden[pl.ds(place, CAP), :] = hidden_ref[pl.ds(r * CAP, CAP), :]
    small.wait()
    stores = []
    for c in range(steps):
        cols = pl.ds(c * block, block)
        loads[c].wait()
        for p in range(0, block, PART):
            total = [None] * (PART // QB)
            for i in range(hid // QB):
                part = jnp.dot(
                    hidden[:, i * QB : (i + 1) * QB],
                    quant[c, i * QB : (i + 1) * QB, p : p + PART],
                    preferred_element_type=f32,
                )
                for j in range(PART // QB):
                    factor = scale[i, 0, (c * block + p) // QB + j]
                    scaled = part[:, j * QB : (j + 1) * QB] * factor
                    total[j] = scaled if i == 0 else total[j] + scaled
            for j in range(PART // QB):
                at = pl.ds(c * block + p + j * QB, QB)
                out[:, :, at] = total[j].astype(bf16).reshape(flight, CAP, QB)
        stores.append(
            pltpu.make_async_copy(out.at[:, :, cols], out_hbm.at[:, :, cols], out_sems.at[c])
        )
        stores[c].start()
    for copy in stores:
        copy.wait()


def forward(scale, hidden, quant, flight, block=512):
    hid, width = quant.shape
    steps = width // block
    return pl.pallas_call(
        functools.partial(forward_kernel, flight, block),
        out_shape=pltpu.HBM((flight, CAP, width), bf16),
        in_specs=[VMEM, HBM, HBM],
        out_specs=HBM,
        scratch_shapes=[
            pltpu.SMEM(scale.shape, f32),
            pltpu.VMEM(hidden.shape, bf16),
            pltpu.VMEM((steps, hid, block), bf16),
            pltpu.VMEM((flight, CAP, width), bf16),
            pltpu.SemaphoreType.DMA,
            pltpu.SemaphoreType.DMA((steps,)),
            pltpu.SemaphoreType.DMA((steps,)),
        ],
        compiler_params=params(flight * CAP),
        cost_estimate=SMALL,
        name="expert_forward",
    )(hidden, hbm(scale), hbm(quant))


def sort_kernel(half, keep, picks, *refs):
    chips, messages = refs[:half], refs[half : half + len(picks)]
    sibling, mine, *passed = refs[-2 - len(picks) :]
    for c in range(half):
        sibling[c] = chips[c][1]
        mine[c] = chips[c][0]
    for message, out, pick in zip(messages, passed, picks):
        tall = out.shape[0] - keep
        out[:keep] = message[:keep]
        out[keep:] = message[keep + pick * tall : keep + (pick + 1) * tall]


def sort_rows(chips, messages, picks, ties, hid):
    half = len(chips)
    _, groups, cap, share = chips[0].shape
    keep = 2 * half * (hid // TILE)
    return pl.pallas_call(
        functools.partial(sort_kernel, half, keep, picks),
        out_shape=(pltpu.VMEM((half, groups, cap, share), bf16),) * 2
        + (pltpu.VMEM((keep + share // TILE, cap, TILE), bf16),) * len(messages),
        in_specs=[VMEM] * (half + len(messages)) + [ANY] * len(ties),
        out_specs=(VMEM,) * (2 + len(messages)),
        compiler_params=params(2 * half * CAP),
        cost_estimate=SMALL,
        name="sort_rows",
    )(*chips, *messages, *ties)


def split_kernel(mine, swapped, *pieces):
    half = mine.shape[0]
    for j, piece in enumerate(pieces, 1):
        piece[: half - 1] = mine[1:, j]
        piece[half - 1 :] = swapped[:, j]


def split(mine, swapped):
    half, groups, cap, share = swapped.shape
    return pl.pallas_call(
        split_kernel,
        out_shape=(pltpu.VMEM((2 * half - 1, cap, share), bf16),) * (groups - 1),
        in_specs=[VMEM, VMEM],
        out_specs=(VMEM,) * (groups - 1),
        compiler_params=params(2 * half * CAP),
        cost_estimate=SMALL,
        name="split",
    )(mine, swapped)


def backward_kernel(
    flight, groups, scale_hbm, gate_up_hbm, quant_hbm, tie_ref, mine, swapped, out_hbm,
    scale, gate_up, rows, quant, acc, out, scale_sem, gate_sems, in_sems, out_sems
):
    half = flight // 2
    me, group = lax.axis_index("expert"), lax.axis_index("dp")
    slots, hid = acc.shape
    share = quant.shape[2]

    def place(r):
        return pl.ds(pl.multiple_of(block_place(me, r, flight) * CAP, CAP), CAP)

    loads = [
        pltpu.make_async_copy(
            quant_hbm.at[:, pl.ds(pl.multiple_of((group ^ j) * share, share), share)],
            quant.at[j],
            in_sems.at[j],
        )
        for j in range(groups)
    ]
    gates = [
        pltpu.make_async_copy(
            gate_up_hbm.at[place(r)], gate_up.at[pl.ds(r * CAP, CAP)], gate_sems.at[r]
        )
        for r in range(flight)
    ]
    small = pltpu.make_async_copy(scale_hbm, scale, scale_sem)
    for copy in [small] + loads + gates:
        copy.start()
    for c in range(half):
        rows[:, c * CAP : (c + 1) * CAP, :] = mine[c]
        rows[:, (half + c) * CAP : (half + c + 1) * CAP, :] = swapped[c]
    small.wait()
    for j in range(groups):
        loads[j].wait()
        for b in range(share // QB):
            cols = slice(b * QB, (b + 1) * QB)
            part = lax.dot_general(
                rows[j, :, cols],
                quant[j, :, cols],
                (((1,), (1,)), ((), ())),
                preferred_element_type=f32,
            )
            for i in range(hid // QB):
                at = (slice(None), slice(i * QB, (i + 1) * QB))
                scaled = part[at] * scale[i, 0, (group ^ j) * (share // QB) + b]
                if j == 0 and b == 0:
                    acc[at] = scaled
                else:
                    acc[at] += scaled
    for copy in gates:
        copy.wait()
    gate = gate_up[:, :hid].astype(f32)
    up = gate_up[:, hid:].astype(f32)
    sig = jax.nn.sigmoid(gate)
    d_hidden = acc[...]
    out[:, :hid] = (d_hidden * up * sig * (1.0 + gate * (1.0 - sig))).astype(bf16)
    out[:, hid:] = (d_hidden * (gate * sig)).astype(bf16)
    stores = [
        pltpu.make_async_copy(out.at[pl.ds(r * CAP, CAP)], out_hbm.at[place(r)], out_sems.at[r])
        for r in range(flight)
    ]
    for copy in stores:
        copy.start()
    for copy in stores:
        copy.wait()


def backward(scale, gate_up, quant, tie, mine, swapped):
    slots, double = gate_up.shape
    hid, width = quant.shape
    half, groups, cap, share = swapped.shape
    flight = 2 * half
    return pl.pallas_call(
        functools.partial(backward_kernel, flight, groups),
        out_shape=pltpu.HBM((slots, double), bf16),
        in_specs=[HBM, HBM, HBM, ANY, VMEM, VMEM],
        out_specs=HBM,
        scratch_shapes=[
            pltpu.SMEM(scale.shape, f32),
            pltpu.VMEM((slots, double), bf16),
            pltpu.VMEM((groups, slots, share), bf16),
            pltpu.VMEM((groups, hid, share), bf16),
            pltpu.VMEM((slots, hid), f32),
            pltpu.VMEM((slots, double), bf16),
            pltpu.SemaphoreType.DMA,
            pltpu.SemaphoreType.DMA((flight,)),
            pltpu.SemaphoreType.DMA((groups,)),
            pltpu.SemaphoreType.DMA((flight,)),
        ],
        compiler_params=params(slots),
        cost_estimate=SMALL,
        name="expert_backward",
    )(hbm(scale), hbm(gate_up), hbm(quant), tie, mine, swapped)


def combine_kernel(
    block, ids_hbm, own_hbm, dout_hbm, ret_hbm, out_ref, dprobs_ref, ids_ref, own_ref, dout, ret_ref, sems
):
    copies = [
        pltpu.make_async_copy(ids_hbm, ids_ref, sems.at[0]),
        pltpu.make_async_copy(own_hbm, own_ref, sems.at[1]),
        pltpu.make_async_copy(dout_hbm, dout, sems.at[2]),
        pltpu.make_async_copy(ret_hbm, ret_ref, sems.at[3]),
    ]
    for copy in copies:
        copy.start()
    topk, tokens = ids_ref.shape
    slots = own_ref.shape[0]
    width = dout.shape[1]
    flight = slots // CAP
    me = lax.axis_index("expert")
    copies[1].wait()
    own = own_ref[...]
    turned = own.T
    high = turned.astype(bf16)
    low = (turned - high.astype(f32)).astype(bf16)
    total = jnp.zeros((slots, tokens), f32)
    for copy in (copies[0], copies[2], copies[3]):
        copy.wait()
    for cols in chunks(width, block):
        here = jnp.concatenate(
            [ret_ref[block_place(me, r, flight), :, cols] for r in range(flight)], axis=0
        )
        out = jnp.dot(high, here, preferred_element_type=f32)
        out = out + jnp.dot(low, here, preferred_element_type=f32)
        out_ref[:, cols] = out.astype(bf16)
        total = total + lax.dot_general(
            here, dout[:, cols], (((1,), (1,)), ((), ())), preferred_element_type=f32
        )
    inner = jnp.where(own > 0.0, total, 0.0)
    row_expert = block_place(me, lax.broadcasted_iota(jnp.int32, (slots, 1), 0) // CAP, flight)
    for k in range(topk):
        mine = jnp.where(ids_ref[k : k + 1, :] == row_expert, inner, 0.0)
        dprobs_ref[k : k + 1, :] = jnp.sum(mine, axis=0, keepdims=True)


def combine(ids, own, d_out, returned, block=1024):
    tokens, width = d_out.shape
    return pl.pallas_call(
        functools.partial(combine_kernel, block),
        out_shape=(
            pltpu.HBM((tokens, width), bf16),
            pltpu.HBM(ids.shape, f32),
        ),
        in_specs=[HBM, HBM, HBM, HBM],
        out_specs=(VMEM, VMEM),
        scratch_shapes=[
            pltpu.VMEM(ids.shape, jnp.int32),
            pltpu.VMEM(own.shape, f32),
            pltpu.VMEM((tokens, width), bf16),
            pltpu.VMEM(returned.shape, bf16),
            pltpu.SemaphoreType.DMA((4,)),
        ],
        compiler_params=params(own.shape[0]),
        cost_estimate=SMALL,
        name="combine",
    )(hbm(ids), hbm(own), hbm(d_out), hbm(returned))


def weight_grad_kernel(groups, block, tie_ref, mine, swapped, hidden_ref, *refs):
    parts, messages = refs[: groups - 1], refs[groups - 1 : 2 * groups - 2]
    out_hbm, hidden, own, out, out_sems = refs[2 * groups - 2 :]
    half = mine.shape[0]
    cap, share = parts[0].shape[1:]
    flight = 2 * half
    slots = flight * cap
    wide = hidden_ref.shape[1] // TILE
    hidden[:slots, :] = hidden_ref[...]
    for j in range(1, groups):
        bit = j if j % 2 else max(b for b in bits_of(groups) if b <= j)
        message = messages[j - 1]
        for r in range(flight):
            for q in range(wide):
                hidden[
                    j * slots + r * cap : j * slots + (r + 1) * cap, q * TILE : (q + 1) * TILE
                ] = message[r * wide + q]
        for q in range(share // TILE):
            own[j - 1, :, q * TILE : (q + 1) * TILE] = message[
                flight * wide + (j - bit) * (share // TILE) + q
            ]
    stores = []
    for n, cols in enumerate(chunks(share, block)):
        grads = [mine[c, 0, :, cols] for c in range(half)]
        grads += [swapped[c, 0, :, cols] for c in range(half)]
        for j in range(1, groups):
            grads.append(own[j - 1, :, cols])
            grads.append(parts[j - 1][:, :, cols].reshape(slots - cap, block))
        out[cols, :] = lax.dot_general(
            jnp.concatenate(grads, axis=0),
            hidden[...],
            (((0,), (0,)), ((), ())),
            preferred_element_type=f32,
        ).astype(bf16)
        stores.append(pltpu.make_async_copy(out.at[cols], out_hbm.at[cols], out_sems.at[n]))
        stores[n].start()
    for copy in stores:
        copy.wait()


def weight_grad(tie, mine, swapped, hidden, parts, messages, block=256):
    half, groups, cap, share = swapped.shape
    slots, hid = hidden.shape
    return pl.pallas_call(
        functools.partial(weight_grad_kernel, groups, block),
        out_shape=pltpu.HBM((share, hid), bf16),
        in_specs=[HBM] + [VMEM] * (1 + 2 * groups),
        out_specs=HBM,
        scratch_shapes=[
            pltpu.VMEM((groups * slots, hid), bf16),
            pltpu.VMEM((groups - 1, cap, share), bf16),
            pltpu.VMEM((share, hid), bf16),
            pltpu.SemaphoreType.DMA((share // block,)),
        ],
        compiler_params=params(slots),
        cost_estimate=SMALL,
        name="weight_grad",
    )(hbm(tie), mine, swapped, hidden, *parts, *messages)


def swap(value, axis, j):
    size = lax.axis_size(axis)
    return lax.ppermute(value, axis, [(i, i ^ j) for i in range(size)])


def shards(route_ids, route_probs, capacity, hot_lists, gate_up, w_quant, w_scale, d_out):
    flight = lax.axis_size("expert")
    groups = lax.axis_size("dp")
    gate_up = gate_up[0, 0]
    ids, probs = route_ids.T, route_probs.T
    scale = w_scale.transpose(1, 0, 2)
    own, hidden, *rest = dispatch(
        gate_up, capacity, hot_lists, ids, probs, d_out, flight, groups
    )
    half, bits = flight // 2, bits_of(groups)
    chips = rest[:1] + [swap(rest[c], "expert", 2 * c) for c in range(1, half)]
    messages = {}
    for bit, message in zip(bits, rest[half:]):
        if bit > 1:
            for j in sorted(messages):
                messages[j ^ bit] = swap(messages[j], "dp", bit)
        messages[bit] = swap(message, "dp", bit)
    even = list(range(2, groups, 2))
    picks = [j + 1 - max(bit for bit in bits if bit <= j) for j in even]
    expert_out = forward(scale, hidden, w_quant[0], flight)
    returned = lax.all_to_all(expert_out, "expert", split_axis=0, concat_axis=0, tiled=True)
    sibling, mine, *passed = sort_rows(
        chips, [messages[j] for j in even], picks, [hbm(expert_out), messages[1]], hidden.shape[1]
    )
    for j, message in zip(even, passed):
        messages[j + 1] = swap(message, "dp", 1)
    messages = [messages[j] for j in range(1, groups)]
    swapped = swap(sibling, "expert", 1)
    pieces = split(mine, swapped)
    parts = [swap(pieces[j - 1], "dp", j) for j in range(1, groups)]
    d_gate_up = backward(scale, gate_up, w_quant[0], pieces[0], mine, swapped)
    combined, d_probs = combine(ids, own, d_out, returned)
    d_weight = weight_grad(d_probs, mine, swapped, hidden, parts, messages)
    return (combined, d_probs.T, d_gate_up[None, None], d_weight[None])


def solution(mesh):
    placed = (
        P(("dp", "expert"), None),
        P(("dp", "expert"), None),
        P(),
        P("dp", None),
        P("dp", "expert", None, None),
        P("expert", None, None),
        P("expert", None, None),
        P(("dp", "expert"), None),
    )
    return jax.shard_map(
        shards,
        mesh=mesh,
        in_specs=placed,
        out_specs=(
            P(("dp", "expert"), None),
            P(("dp", "expert"), None),
            P("dp", "expert", None, None),
            P("expert", "dp", None),
        ),
        check_vma=False,
    )
```

```python
import functools

import jax
import jax.numpy as jnp
from jax import lax
from jax.experimental import pallas as pl
from jax.experimental.pallas import tpu as pltpu
from jax.sharding import PartitionSpec as P

QB = 128
CAP = 16
TILE = 256

bf16 = jnp.bfloat16
f32 = jnp.float32

SMALL = pl.CostEstimate(flops=1024, bytes_accessed=1024, transcendentals=0)

VMEM = pl.BlockSpec(memory_space=pltpu.VMEM)
ANY = pl.BlockSpec(memory_space=pl.ANY)
HBM = pl.BlockSpec(memory_space=pltpu.HBM)


def params(slots):
    return pltpu.CompilerParams(vmem_limit_bytes=(12 + slots // 32) * 1024 * 1024)


def hbm(value):
    return pltpu.with_memory_space_constraint(value, pltpu.HBM)


def chunks(total, size):
    return [pl.ds(start, size) for start in range(0, total, size)]


def bits_of(groups):
    bits = []
    while groups > 1:
        groups //= 2
        bits.append(groups)
    return bits


def message_tiles(flight, groups, bit, hid, share):
    far = 1 if 2 * bit == groups else 0
    return flight * (hid // TILE) + bit * (share // TILE) + far


def block_place(me, r, flight):
    half = flight // 2
    return me ^ (2 * (r % half) + r // half)


def dispatch_kernel(flight, groups, gate_up_hbm, cap_hbm, hot_hbm, ids_hbm, probs_hbm, dout_hbm, *refs):
    half = flight // 2
    bits = bits_of(groups)
    outs = 2 + half + len(bits)
    own_hbm, hidden_ref, *chips = refs[: 2 + half]
    messages = dict(zip(bits, refs[2 + half : outs]))
    gate_up, cap_ref, hot_ref, ids_ref, probs_ref, dout, own_ref = refs[outs : outs + 7]
    gate_sems, own_sem, small_sems, in_sems = refs[outs + 7 :]
    topk, tokens = ids_ref.shape
    slots = flight * CAP
    me, group = lax.axis_index("expert"), lax.axis_index("dp")
    share = dout_hbm.shape[1] // groups
    hid = hidden_ref.shape[1]
    small = [
        pltpu.make_async_copy(src, dst, small_sems.at[i])
        for i, (src, dst) in enumerate(
            [(ids_hbm, ids_ref), (probs_hbm, probs_ref), (cap_hbm, cap_ref), (hot_hbm, hot_ref)]
        )
    ]
    loads = [
        pltpu.make_async_copy(
            dout_hbm.at[:, pl.ds(pl.multiple_of((group ^ j) * share, share), share)],
            dout.at[j],
            in_sems.at[j],
        )
        for j in range(groups)
    ]
    gates = [
        pltpu.make_async_copy(
            gate_up_hbm.at[pl.ds(pl.multiple_of(block_place(me, r, flight) * CAP, CAP), CAP)],
            gate_up.at[pl.ds(r * CAP, CAP)],
            gate_sems.at[r],
        )
        for r in range(flight)
    ]
    for copy in small + loads + gates:
        copy.start()
    for copy in small:
        copy.wait()
    row = lax.broadcasted_iota(jnp.int32, (slots, 1), 0)
    row_expert = block_place(me, row // CAP, flight)
    row_rank = (row % CAP).astype(f32)
    limit = jnp.zeros((slots, 1), jnp.int32)
    for e in range(flight):
        hot = hot_ref[0, 0] == e
        for h in range(1, hot_ref.shape[1]):
            hot = jnp.logical_or(hot, hot_ref[0, h] == e)
        limit = jnp.where(row_expert == e, jnp.where(hot, CAP, cap_ref[e]), limit)
    limit = limit.astype(f32)
    named = jnp.zeros((slots, tokens), f32)
    weight = jnp.zeros((slots, tokens), f32)
    for k in range(topk):
        hit = ids_ref[k : k + 1, :] == row_expert
        named = jnp.where(hit, 1.0, named)
        weight = jnp.where(hit, probs_ref[k : k + 1, :], weight)
    earlier = lax.broadcasted_iota(jnp.int32, (tokens, tokens), 0)
    later = lax.broadcasted_iota(jnp.int32, (tokens, tokens), 1)
    before = (earlier < later).astype(f32).astype(bf16)
    rank = jnp.dot(named.astype(bf16), before, preferred_element_type=f32)
    owns = (named > 0.0) & (rank == row_rank) & (rank < limit)
    own_weight = jnp.where(owns, weight, 0.0)
    own_ref[...] = own_weight
    own_copy = pltpu.make_async_copy(own_ref, own_hbm, own_sem)
    own_copy.start()
    owner = jnp.where(owns, 1.0, 0.0).astype(bf16)
    slot_weight = jnp.sum(own_weight, axis=1, keepdims=True)
    for copy in loads:
        copy.wait()
    for j in range(groups):
        part = jnp.dot(owner, dout[j], preferred_element_type=f32)
        part = (part * slot_weight).astype(bf16)
        for r in range(flight):
            chips[r % half][r // half, j] = part[r * CAP : (r + 1) * CAP, :]
        for bit in bits:
            if bit <= j < 2 * bit:
                first = flight * (hid // TILE) + (j - bit) * (share // TILE)
                for q in range(share // TILE):
                    messages[bit][first + q] = part[:CAP, q * TILE : (q + 1) * TILE]
    messages[bits[0]][messages[bits[0]].shape[0] - 1] = jnp.zeros((CAP, TILE), bf16)
    for copy in gates:
        copy.wait()
    for r in range(flight):
        at = slice(r * CAP, (r + 1) * CAP)
        gate = gate_up[at, :hid].astype(f32)
        up = gate_up[at, hid:].astype(f32)
        block = (gate * jax.nn.sigmoid(gate) * up).astype(bf16)
        hidden_ref[at, :] = block
        for bit in bits:
            for q in range(hid // TILE):
                messages[bit][r * (hid // TILE) + q] = block[:, q * TILE : (q + 1) * TILE]
    own_copy.wait()


def dispatch(gate_up, capacity, hot_row, ids, probs, d_out, flight, groups):
    tokens, width = d_out.shape
    rows, double = gate_up.shape
    slots = flight * CAP
    share = width // groups
    half = flight // 2
    return pl.pallas_call(
        functools.partial(dispatch_kernel, flight, groups),
        out_shape=(pltpu.HBM((slots, tokens), f32), pltpu.VMEM((rows, double // 2), bf16))
        + (pltpu.VMEM((2, groups, CAP, share), bf16),) * half
        + tuple(
            pltpu.VMEM((message_tiles(flight, groups, bit, double // 2, share), CAP, TILE), bf16)
            for bit in bits_of(groups)
        ),
        in_specs=[HBM] * 6,
        out_specs=(HBM, VMEM) + (VMEM,) * (half + len(bits_of(groups))),
        scratch_shapes=[
            pltpu.VMEM((rows, double), bf16),
            pltpu.SMEM(capacity.shape, jnp.int32),
            pltpu.SMEM(hot_row.shape, jnp.int32),
            pltpu.VMEM(ids.shape, jnp.int32),
            pltpu.VMEM(probs.shape, f32),
            pltpu.VMEM((groups, tokens, share), bf16),
            pltpu.VMEM((slots, tokens), f32),
            pltpu.SemaphoreType.DMA((flight,)),
            pltpu.SemaphoreType.DMA,
            pltpu.SemaphoreType.DMA((4,)),
            pltpu.SemaphoreType.DMA((groups,)),
        ],
        compiler_params=params(slots),
        cost_estimate=SMALL,
        name="dispatch",
    )(hbm(gate_up), hbm(capacity), hbm(hot_row), hbm(ids), hbm(probs), hbm(d_out))


def forward_kernel(
    flight, block, hidden_ref, scale_hbm, quant_hbm, out_hbm,
    scale, hidden, quant, out, scale_sem, in_sems, out_sems
):
    steps, hid, _ = quant.shape
    me = lax.axis_index("expert")
    loads = [
        pltpu.make_async_copy(quant_hbm.at[:, pl.ds(c * block, block)], quant.at[c], in_sems.at[c])
        for c in range(steps)
    ]
    small = pltpu.make_async_copy(scale_hbm, scale, scale_sem)
    for copy in [small] + loads:
        copy.start()
    for r in range(flight):
        place = pl.multiple_of(block_place(me, r, flight) * CAP, CAP)
        hidden[pl.ds(place, CAP), :] = hidden_ref[pl.ds(r * CAP, CAP), :]
    small.wait()
    stores = []
    for c in range(steps):
        cols = pl.ds(c * block, block)
        loads[c].wait()
        total = [None] * (block // QB)
        for i in range(hid // QB):
            part = jnp.dot(
                hidden[:, i * QB : (i + 1) * QB],
                quant[c, i * QB : (i + 1) * QB, :],
                preferred_element_type=f32,
            )
            for j in range(block // QB):
                scaled = part[:, j * QB : (j + 1) * QB] * scale[i, 0, c * (block // QB) + j]
                total[j] = scaled if i == 0 else total[j] + scaled
        for j in range(block // QB):
            at = pl.ds(c * block + j * QB, QB)
            out[:, :, at] = total[j].astype(bf16).reshape(flight, CAP, QB)
        stores.append(
            pltpu.make_async_copy(out.at[:, :, cols], out_hbm.at[:, :, cols], out_sems.at[c])
        )
        stores[c].start()
    for copy in stores:
        copy.wait()


def forward(scale, hidden, quant, flight, block=512):
    hid, width = quant.shape
    steps = width // block
    return pl.pallas_call(
        functools.partial(forward_kernel, flight, block),
        out_shape=pltpu.HBM((flight, CAP, width), bf16),
        in_specs=[VMEM, HBM, HBM],
        out_specs=HBM,
        scratch_shapes=[
            pltpu.SMEM(scale.shape, f32),
            pltpu.VMEM(hidden.shape, bf16),
            pltpu.VMEM((steps, hid, block), bf16),
            pltpu.VMEM((flight, CAP, width), bf16),
            pltpu.SemaphoreType.DMA,
            pltpu.SemaphoreType.DMA((steps,)),
            pltpu.SemaphoreType.DMA((steps,)),
        ],
        compiler_params=params(flight * CAP),
        cost_estimate=SMALL,
        name="expert_forward",
    )(hidden, hbm(scale), hbm(quant))


def sort_kernel(half, *refs):
    chips, (sibling, mine) = refs[:half], refs[-2:]
    for c in range(half):
        sibling[c] = chips[c][1]
        mine[c] = chips[c][0]


def sort_rows(chips, ties):
    half = len(chips)
    return pl.pallas_call(
        functools.partial(sort_kernel, half),
        out_shape=(pltpu.VMEM((half,) + chips[0].shape[1:], bf16),) * 2,
        in_specs=[VMEM] * half + [ANY] * len(ties),
        out_specs=(VMEM, VMEM),
        compiler_params=params(2 * half * CAP),
        cost_estimate=SMALL,
        name="sort_rows",
    )(*chips, *ties)


def split_kernel(mine, swapped, *pieces):
    half = mine.shape[0]
    for j, piece in enumerate(pieces, 1):
        piece[: half - 1] = mine[1:, j]
        piece[half - 1 :] = swapped[:, j]


def split(mine, swapped):
    half, groups, cap, share = swapped.shape
    return pl.pallas_call(
        split_kernel,
        out_shape=(pltpu.VMEM((2 * half - 1, cap, share), bf16),) * (groups - 1),
        in_specs=[VMEM, VMEM],
        out_specs=(VMEM,) * (groups - 1),
        compiler_params=params(2 * half * CAP),
        cost_estimate=SMALL,
        name="split",
    )(mine, swapped)


def backward_kernel(
    flight, groups, scale_hbm, gate_up_hbm, quant_hbm, tie_ref, mine, swapped, out_hbm,
    scale, gate_up, rows, quant, acc, out, scale_sem, gate_sems, in_sems, out_sems
):
    half = flight // 2
    me, group = lax.axis_index("expert"), lax.axis_index("dp")
    slots, hid = acc.shape
    share = quant.shape[2]

    def place(r):
        return pl.ds(pl.multiple_of(block_place(me, r, flight) * CAP, CAP), CAP)

    loads = [
        pltpu.make_async_copy(
            quant_hbm.at[:, pl.ds(pl.multiple_of((group ^ j) * share, share), share)],
            quant.at[j],
            in_sems.at[j],
        )
        for j in range(groups)
    ]
    gates = [
        pltpu.make_async_copy(
            gate_up_hbm.at[place(r)], gate_up.at[pl.ds(r * CAP, CAP)], gate_sems.at[r]
        )
        for r in range(flight)
    ]
    small = pltpu.make_async_copy(scale_hbm, scale, scale_sem)
    for copy in [small] + loads + gates:
        copy.start()
    for c in range(half):
        rows[:, c * CAP : (c + 1) * CAP, :] = mine[c]
        rows[:, (half + c) * CAP : (half + c + 1) * CAP, :] = swapped[c]
    small.wait()
    for j in range(groups):
        loads[j].wait()
        for b in range(share // QB):
            cols = slice(b * QB, (b + 1) * QB)
            part = lax.dot_general(
                rows[j, :, cols],
                quant[j, :, cols],
                (((1,), (1,)), ((), ())),
                preferred_element_type=f32,
            )
            for i in range(hid // QB):
                at = (slice(None), slice(i * QB, (i + 1) * QB))
                scaled = part[at] * scale[i, 0, (group ^ j) * (share // QB) + b]
                if j == 0 and b == 0:
                    acc[at] = scaled
                else:
                    acc[at] += scaled
    for copy in gates:
        copy.wait()
    gate = gate_up[:, :hid].astype(f32)
    up = gate_up[:, hid:].astype(f32)
    sig = jax.nn.sigmoid(gate)
    d_hidden = acc[...]
    out[:, :hid] = (d_hidden * up * sig * (1.0 + gate * (1.0 - sig))).astype(bf16)
    out[:, hid:] = (d_hidden * (gate * sig)).astype(bf16)
    stores = [
        pltpu.make_async_copy(out.at[pl.ds(r * CAP, CAP)], out_hbm.at[place(r)], out_sems.at[r])
        for r in range(flight)
    ]
    for copy in stores:
        copy.start()
    for copy in stores:
        copy.wait()


def backward(scale, gate_up, quant, tie, mine, swapped):
    slots, double = gate_up.shape
    hid, width = quant.shape
    half, groups, cap, share = swapped.shape
    flight = 2 * half
    return pl.pallas_call(
        functools.partial(backward_kernel, flight, groups),
        out_shape=pltpu.HBM((slots, double), bf16),
        in_specs=[HBM, HBM, HBM, ANY, VMEM, VMEM],
        out_specs=HBM,
        scratch_shapes=[
            pltpu.SMEM(scale.shape, f32),
            pltpu.VMEM((slots, double), bf16),
            pltpu.VMEM((groups, slots, share), bf16),
            pltpu.VMEM((groups, hid, share), bf16),
            pltpu.VMEM((slots, hid), f32),
            pltpu.VMEM((slots, double), bf16),
            pltpu.SemaphoreType.DMA,
            pltpu.SemaphoreType.DMA((flight,)),
            pltpu.SemaphoreType.DMA((groups,)),
            pltpu.SemaphoreType.DMA((flight,)),
        ],
        compiler_params=params(slots),
        cost_estimate=SMALL,
        name="expert_backward",
    )(hbm(scale), hbm(gate_up), hbm(quant), tie, mine, swapped)


def combine_kernel(
    block, ids_hbm, own_hbm, dout_hbm, ret_hbm, out_ref, dprobs_ref, ids_ref, own_ref, dout, ret_ref, sems
):
    copies = [
        pltpu.make_async_copy(ids_hbm, ids_ref, sems.at[0]),
        pltpu.make_async_copy(own_hbm, own_ref, sems.at[1]),
        pltpu.make_async_copy(dout_hbm, dout, sems.at[2]),
        pltpu.make_async_copy(ret_hbm, ret_ref, sems.at[3]),
    ]
    for copy in copies:
        copy.start()
    topk, tokens = ids_ref.shape
    slots = own_ref.shape[0]
    width = dout.shape[1]
    flight = slots // CAP
    me = lax.axis_index("expert")
    copies[1].wait()
    own = own_ref[...]
    turned = own.T
    high = turned.astype(bf16)
    low = (turned - high.astype(f32)).astype(bf16)
    total = jnp.zeros((slots, tokens), f32)
    for copy in (copies[0], copies[2], copies[3]):
        copy.wait()
    for cols in chunks(width, block):
        here = jnp.concatenate(
            [ret_ref[block_place(me, r, flight), :, cols] for r in range(flight)], axis=0
        )
        out = jnp.dot(high, here, preferred_element_type=f32)
        out = out + jnp.dot(low, here, preferred_element_type=f32)
        out_ref[:, cols] = out.astype(bf16)
        total = total + lax.dot_general(
            here, dout[:, cols], (((1,), (1,)), ((), ())), preferred_element_type=f32
        )
    inner = jnp.where(own > 0.0, total, 0.0)
    row_expert = block_place(me, lax.broadcasted_iota(jnp.int32, (slots, 1), 0) // CAP, flight)
    for k in range(topk):
        mine = jnp.where(ids_ref[k : k + 1, :] == row_expert, inner, 0.0)
        dprobs_ref[k : k + 1, :] = jnp.sum(mine, axis=0, keepdims=True)


def combine(ids, own, d_out, returned, block=1024):
    tokens, width = d_out.shape
    return pl.pallas_call(
        functools.partial(combine_kernel, block),
        out_shape=(
            pltpu.HBM((tokens, width), bf16),
            pltpu.HBM(ids.shape, f32),
        ),
        in_specs=[HBM, HBM, HBM, HBM],
        out_specs=(VMEM, VMEM),
        scratch_shapes=[
            pltpu.VMEM(ids.shape, jnp.int32),
            pltpu.VMEM(own.shape, f32),
            pltpu.VMEM((tokens, width), bf16),
            pltpu.VMEM(returned.shape, bf16),
            pltpu.SemaphoreType.DMA((4,)),
        ],
        compiler_params=params(own.shape[0]),
        cost_estimate=SMALL,
        name="combine",
    )(hbm(ids), hbm(own), hbm(d_out), hbm(returned))


def weight_grad_kernel(groups, block, tie_ref, mine, swapped, hidden_ref, *refs):
    parts, messages = refs[: groups - 1], refs[groups - 1 : 2 * groups - 2]
    out_hbm, hidden, own, out, out_sems = refs[2 * groups - 2 :]
    half = mine.shape[0]
    cap, share = parts[0].shape[1:]
    flight = 2 * half
    slots = flight * cap
    wide = hidden_ref.shape[1] // TILE
    hidden[:slots, :] = hidden_ref[...]
    for j in range(1, groups):
        bit = max(b for b in bits_of(groups) if b <= j)
        message = messages[j - 1]
        for r in range(flight):
            for q in range(wide):
                hidden[
                    j * slots + r * cap : j * slots + (r + 1) * cap, q * TILE : (q + 1) * TILE
                ] = message[r * wide + q]
        for q in range(share // TILE):
            own[j - 1, :, q * TILE : (q + 1) * TILE] = message[
                flight * wide + (j - bit) * (share // TILE) + q
            ]
    stores = []
    for n, cols in enumerate(chunks(share, block)):
        grads = [mine[c, 0, :, cols] for c in range(half)]
        grads += [swapped[c, 0, :, cols] for c in range(half)]
        for j in range(1, groups):
            grads.append(own[j - 1, :, cols])
            grads.append(parts[j - 1][:, :, cols].reshape(slots - cap, block))
        out[cols, :] = lax.dot_general(
            jnp.concatenate(grads, axis=0),
            hidden[...],
            (((0,), (0,)), ((), ())),
            preferred_element_type=f32,
        ).astype(bf16)
        stores.append(pltpu.make_async_copy(out.at[cols], out_hbm.at[cols], out_sems.at[n]))
        stores[n].start()
    for copy in stores:
        copy.wait()


def weight_grad(tie, mine, swapped, hidden, parts, messages, block=256):
    half, groups, cap, share = swapped.shape
    slots, hid = hidden.shape
    return pl.pallas_call(
        functools.partial(weight_grad_kernel, groups, block),
        out_shape=pltpu.HBM((share, hid), bf16),
        in_specs=[HBM] + [VMEM] * (1 + 2 * groups),
        out_specs=HBM,
        scratch_shapes=[
            pltpu.VMEM((groups * slots, hid), bf16),
            pltpu.VMEM((groups - 1, cap, share), bf16),
            pltpu.VMEM((share, hid), bf16),
            pltpu.SemaphoreType.DMA((share // block,)),
        ],
        compiler_params=params(slots),
        cost_estimate=SMALL,
        name="weight_grad",
    )(hbm(tie), mine, swapped, hidden, *parts, *messages)


def swap(value, axis, j):
    size = lax.axis_size(axis)
    return lax.ppermute(value, axis, [(i, i ^ j) for i in range(size)])


def shards(route_ids, route_probs, capacity, hot_lists, gate_up, w_quant, w_scale, d_out):
    flight = lax.axis_size("expert")
    groups = lax.axis_size("dp")
    gate_up = gate_up[0, 0]
    ids, probs = route_ids.T, route_probs.T
    scale = w_scale.transpose(1, 0, 2)
    own, hidden, *rest = dispatch(
        gate_up, capacity, hot_lists, ids, probs, d_out, flight, groups
    )
    half, bits = flight // 2, bits_of(groups)
    chips = rest[:1] + [swap(rest[c], "expert", 2 * c) for c in range(1, half)]
    messages, early = {}, []
    for bit, message in zip(bits, rest[half:]):
        for j in sorted(messages):
            messages[j ^ bit] = swap(messages[j], "dp", bit)
        messages[bit] = swap(message, "dp", bit)
        early.append(messages[bit])
    messages = [messages[j] for j in range(1, groups)]
    expert_out = forward(scale, hidden, w_quant[0], flight)
    returned = lax.all_to_all(expert_out, "expert", split_axis=0, concat_axis=0, tiled=True)
    sibling, mine = sort_rows(chips, [hbm(expert_out)] + early)
    swapped = swap(sibling, "expert", 1)
    pieces = split(mine, swapped)
    parts = [swap(pieces[j - 1], "dp", j) for j in range(1, groups)]
    d_gate_up = backward(scale, gate_up, w_quant[0], pieces[0], mine, swapped)
    combined, d_probs = combine(ids, own, d_out, returned)
    d_weight = weight_grad(d_probs, mine, swapped, hidden, parts, messages)
    return (combined, d_probs.T, d_gate_up[None, None], d_weight[None])


def solution(mesh):
    placed = (
        P(("dp", "expert"), None),
        P(("dp", "expert"), None),
        P(),
        P("dp", None),
        P("dp", "expert", None, None),
        P("expert", None, None),
        P("expert", None, None),
        P(("dp", "expert"), None),
    )
    return jax.shard_map(
        shards,
        mesh=mesh,
        in_specs=placed,
        out_specs=(
            P(("dp", "expert"), None),
            P(("dp", "expert"), None),
            P("dp", "expert", None, None),
            P("expert", "dp", None),
        ),
        check_vma=False,
    )
```

```python
import functools

import jax
import jax.numpy as jnp
from jax import lax
from jax.experimental import pallas as pl
from jax.experimental.pallas import tpu as pltpu
from jax.sharding import PartitionSpec as P

QB = 128
CAP = 16
TILE = 256

bf16 = jnp.bfloat16
f32 = jnp.float32

SMALL = pl.CostEstimate(flops=1024, bytes_accessed=1024, transcendentals=0)

VMEM = pl.BlockSpec(memory_space=pltpu.VMEM)
ANY = pl.BlockSpec(memory_space=pl.ANY)
HBM = pl.BlockSpec(memory_space=pltpu.HBM)


def params(slots):
    return pltpu.CompilerParams(vmem_limit_bytes=(12 + slots // 32) * 1024 * 1024)


def hbm(value):
    return pltpu.with_memory_space_constraint(value, pltpu.HBM)


def chunks(total, size):
    return [pl.ds(start, size) for start in range(0, total, size)]


def bits_of(groups):
    bits = []
    while groups > 1:
        groups //= 2
        bits.append(groups)
    return bits


def message_tiles(flight, groups, bit, hid, share):
    far = 1 if 2 * bit == groups else 0
    return flight * (hid // TILE) + bit * (share // TILE) + far


def block_place(me, r, flight):
    half = flight // 2
    return me ^ (2 * (r % half) + r // half)


def dispatch_kernel(flight, groups, gate_up_hbm, cap_hbm, hot_hbm, ids_hbm, probs_hbm, dout_hbm, *refs):
    half = flight // 2
    bits = bits_of(groups)
    outs = 2 + half + len(bits)
    own_hbm, hidden_ref, *chips = refs[: 2 + half]
    messages = dict(zip(bits, refs[2 + half : outs]))
    gate_up, cap_ref, hot_ref, ids_ref, probs_ref, dout, own_ref = refs[outs : outs + 7]
    gate_sems, own_sem, small_sems, in_sems = refs[outs + 7 :]
    topk, tokens = ids_ref.shape
    slots = flight * CAP
    me, group = lax.axis_index("expert"), lax.axis_index("dp")
    share = dout_hbm.shape[1] // groups
    hid = hidden_ref.shape[1]
    small = [
        pltpu.make_async_copy(src, dst, small_sems.at[i])
        for i, (src, dst) in enumerate(
            [(ids_hbm, ids_ref), (probs_hbm, probs_ref), (cap_hbm, cap_ref), (hot_hbm, hot_ref)]
        )
    ]
    loads = [
        pltpu.make_async_copy(
            dout_hbm.at[:, pl.ds(pl.multiple_of((group ^ j) * share, share), share)],
            dout.at[j],
            in_sems.at[j],
        )
        for j in range(groups)
    ]
    gates = [
        pltpu.make_async_copy(
            gate_up_hbm.at[pl.ds(pl.multiple_of(block_place(me, r, flight) * CAP, CAP), CAP)],
            gate_up.at[pl.ds(r * CAP, CAP)],
            gate_sems.at[r],
        )
        for r in range(flight)
    ]
    for copy in small + loads + gates:
        copy.start()
    for copy in small:
        copy.wait()
    row = lax.broadcasted_iota(jnp.int32, (slots, 1), 0)
    row_expert = block_place(me, row // CAP, flight)
    row_rank = (row % CAP).astype(f32)
    limit = jnp.zeros((slots, 1), jnp.int32)
    for e in range(flight):
        hot = hot_ref[0, 0] == e
        for h in range(1, hot_ref.shape[1]):
            hot = jnp.logical_or(hot, hot_ref[0, h] == e)
        limit = jnp.where(row_expert == e, jnp.where(hot, CAP, cap_ref[e]), limit)
    limit = limit.astype(f32)
    named = jnp.zeros((slots, tokens), f32)
    weight = jnp.zeros((slots, tokens), f32)
    for k in range(topk):
        hit = ids_ref[k : k + 1, :] == row_expert
        named = jnp.where(hit, 1.0, named)
        weight = jnp.where(hit, probs_ref[k : k + 1, :], weight)
    earlier = lax.broadcasted_iota(jnp.int32, (tokens, tokens), 0)
    later = lax.broadcasted_iota(jnp.int32, (tokens, tokens), 1)
    before = (earlier < later).astype(f32).astype(bf16)
    rank = jnp.dot(named.astype(bf16), before, preferred_element_type=f32)
    owns = (named > 0.0) & (rank == row_rank) & (rank < limit)
    own_weight = jnp.where(owns, weight, 0.0)
    own_ref[...] = own_weight
    own_copy = pltpu.make_async_copy(own_ref, own_hbm, own_sem)
    own_copy.start()
    owner = jnp.where(owns, 1.0, 0.0).astype(bf16)
    slot_weight = jnp.sum(own_weight, axis=1, keepdims=True)
    for copy in loads:
        copy.wait()
    for j in range(groups):
        part = jnp.dot(owner, dout[j], preferred_element_type=f32)
        part = (part * slot_weight).astype(bf16)
        for r in range(flight):
            chips[r % half][r // half, j] = part[r * CAP : (r + 1) * CAP, :]
        for bit in bits:
            if bit <= j < 2 * bit:
                first = flight * (hid // TILE) + (j - bit) * (share // TILE)
                for q in range(share // TILE):
                    messages[bit][first + q] = part[:CAP, q * TILE : (q + 1) * TILE]
    messages[bits[0]][messages[bits[0]].shape[0] - 1] = jnp.zeros((CAP, TILE), bf16)
    for copy in gates:
        copy.wait()
    for r in range(flight):
        at = slice(r * CAP, (r + 1) * CAP)
        gate = gate_up[at, :hid].astype(f32)
        up = gate_up[at, hid:].astype(f32)
        block = (gate * jax.nn.sigmoid(gate) * up).astype(bf16)
        hidden_ref[at, :] = block
        for bit in bits:
            for q in range(hid // TILE):
                messages[bit][r * (hid // TILE) + q] = block[:, q * TILE : (q + 1) * TILE]
    own_copy.wait()


def dispatch(gate_up, capacity, hot_row, ids, probs, d_out, flight, groups):
    tokens, width = d_out.shape
    rows, double = gate_up.shape
    slots = flight * CAP
    share = width // groups
    half = flight // 2
    return pl.pallas_call(
        functools.partial(dispatch_kernel, flight, groups),
        out_shape=(pltpu.HBM((slots, tokens), f32), pltpu.VMEM((rows, double // 2), bf16))
        + (pltpu.VMEM((2, groups, CAP, share), bf16),) * half
        + tuple(
            pltpu.VMEM((message_tiles(flight, groups, bit, double // 2, share), CAP, TILE), bf16)
            for bit in bits_of(groups)
        ),
        in_specs=[HBM] * 6,
        out_specs=(HBM, VMEM) + (VMEM,) * (half + len(bits_of(groups))),
        scratch_shapes=[
            pltpu.VMEM((rows, double), bf16),
            pltpu.SMEM(capacity.shape, jnp.int32),
            pltpu.SMEM(hot_row.shape, jnp.int32),
            pltpu.VMEM(ids.shape, jnp.int32),
            pltpu.VMEM(probs.shape, f32),
            pltpu.VMEM((groups, tokens, share), bf16),
            pltpu.VMEM((slots, tokens), f32),
            pltpu.SemaphoreType.DMA((flight,)),
            pltpu.SemaphoreType.DMA,
            pltpu.SemaphoreType.DMA((4,)),
            pltpu.SemaphoreType.DMA((groups,)),
        ],
        compiler_params=params(slots),
        cost_estimate=SMALL,
        name="dispatch",
    )(hbm(gate_up), hbm(capacity), hbm(hot_row), hbm(ids), hbm(probs), hbm(d_out))


def forward_kernel(
    flight, block, hidden_ref, scale_hbm, quant_hbm, out_hbm,
    scale, hidden, quant, out, scale_sem, in_sems, out_sems
):
    steps, hid, _ = quant.shape
    me = lax.axis_index("expert")
    loads = [
        pltpu.make_async_copy(quant_hbm.at[:, pl.ds(c * block, block)], quant.at[c], in_sems.at[c])
        for c in range(steps)
    ]
    small = pltpu.make_async_copy(scale_hbm, scale, scale_sem)
    for copy in [small] + loads:
        copy.start()
    for r in range(flight):
        place = pl.multiple_of(block_place(me, r, flight) * CAP, CAP)
        hidden[pl.ds(place, CAP), :] = hidden_ref[pl.ds(r * CAP, CAP), :]
    small.wait()
    stores = []
    for c in range(steps):
        cols = pl.ds(c * block, block)
        loads[c].wait()
        total = [None] * (block // QB)
        for i in range(hid // QB):
            part = jnp.dot(
                hidden[:, i * QB : (i + 1) * QB],
                quant[c, i * QB : (i + 1) * QB, :],
                preferred_element_type=f32,
            )
            for j in range(block // QB):
                scaled = part[:, j * QB : (j + 1) * QB] * scale[i, 0, c * (block // QB) + j]
                total[j] = scaled if i == 0 else total[j] + scaled
        for j in range(block // QB):
            at = pl.ds(c * block + j * QB, QB)
            out[:, :, at] = total[j].astype(bf16).reshape(flight, CAP, QB)
        stores.append(
            pltpu.make_async_copy(out.at[:, :, cols], out_hbm.at[:, :, cols], out_sems.at[c])
        )
        stores[c].start()
    for copy in stores:
        copy.wait()


def forward(scale, hidden, quant, flight, block=512):
    hid, width = quant.shape
    steps = width // block
    return pl.pallas_call(
        functools.partial(forward_kernel, flight, block),
        out_shape=pltpu.HBM((flight, CAP, width), bf16),
        in_specs=[VMEM, HBM, HBM],
        out_specs=HBM,
        scratch_shapes=[
            pltpu.SMEM(scale.shape, f32),
            pltpu.VMEM(hidden.shape, bf16),
            pltpu.VMEM((steps, hid, block), bf16),
            pltpu.VMEM((flight, CAP, width), bf16),
            pltpu.SemaphoreType.DMA,
            pltpu.SemaphoreType.DMA((steps,)),
            pltpu.SemaphoreType.DMA((steps,)),
        ],
        compiler_params=params(flight * CAP),
        cost_estimate=SMALL,
        name="expert_forward",
    )(hidden, hbm(scale), hbm(quant))


def sort_kernel(half, *refs):
    chips, (sibling, mine) = refs[:half], refs[-2:]
    for c in range(half):
        sibling[c] = chips[c][1]
        mine[c] = chips[c][0]


def sort_rows(chips, ties):
    half = len(chips)
    return pl.pallas_call(
        functools.partial(sort_kernel, half),
        out_shape=(pltpu.VMEM((half,) + chips[0].shape[1:], bf16),) * 2,
        in_specs=[VMEM] * half + [ANY] * len(ties),
        out_specs=(VMEM, VMEM),
        compiler_params=params(2 * half * CAP),
        cost_estimate=SMALL,
        name="sort_rows",
    )(*chips, *ties)


def cut_kernel(keep, picks, *refs):
    count = len(picks)
    messages, outs, sems = refs[:count], refs[count + 1 : 2 * count + 1], refs[-1]
    copies = []
    for n, (message, out, pick) in enumerate(zip(messages, outs, picks)):
        tall = out.shape[0] - keep
        first = keep + pick * tall
        for k, (src, dst) in enumerate(
            [(pl.ds(0, keep), pl.ds(0, keep)), (pl.ds(first, tall), pl.ds(keep, tall))]
        ):
            copies.append(pltpu.make_async_copy(message.at[src], out.at[dst], sems.at[n, k]))
    for copy in copies:
        copy.start()
    for copy in copies:
        copy.wait()


def cut(messages, picks, tie, keep, tall):
    count = len(messages)
    return pl.pallas_call(
        functools.partial(cut_kernel, keep, picks),
        out_shape=(pltpu.HBM((keep + tall, CAP, TILE), bf16),) * count,
        in_specs=[ANY] * (count + 1),
        out_specs=(HBM,) * count,
        scratch_shapes=[pltpu.SemaphoreType.DMA((count, 2))],
        compiler_params=params(4 * QB),
        cost_estimate=SMALL,
        name="cut",
    )(*messages, tie)


def split_kernel(mine, swapped, *pieces):
    half = mine.shape[0]
    for j, piece in enumerate(pieces, 1):
        piece[: half - 1] = mine[1:, j]
        piece[half - 1 :] = swapped[:, j]


def split(mine, swapped):
    half, groups, cap, share = swapped.shape
    return pl.pallas_call(
        split_kernel,
        out_shape=(pltpu.VMEM((2 * half - 1, cap, share), bf16),) * (groups - 1),
        in_specs=[VMEM, VMEM],
        out_specs=(VMEM,) * (groups - 1),
        compiler_params=params(2 * half * CAP),
        cost_estimate=SMALL,
        name="split",
    )(mine, swapped)


def backward_kernel(
    flight, groups, scale_hbm, gate_up_hbm, quant_hbm, tie_ref, mine, swapped, out_hbm,
    scale, gate_up, rows, quant, acc, out, scale_sem, gate_sems, in_sems, out_sems
):
    half = flight // 2
    me, group = lax.axis_index("expert"), lax.axis_index("dp")
    slots, hid = acc.shape
    share = quant.shape[2]

    def place(r):
        return pl.ds(pl.multiple_of(block_place(me, r, flight) * CAP, CAP), CAP)

    loads = [
        pltpu.make_async_copy(
            quant_hbm.at[:, pl.ds(pl.multiple_of((group ^ j) * share, share), share)],
            quant.at[j],
            in_sems.at[j],
        )
        for j in range(groups)
    ]
    gates = [
        pltpu.make_async_copy(
            gate_up_hbm.at[place(r)], gate_up.at[pl.ds(r * CAP, CAP)], gate_sems.at[r]
        )
        for r in range(flight)
    ]
    small = pltpu.make_async_copy(scale_hbm, scale, scale_sem)
    for copy in [small] + loads + gates:
        copy.start()
    for c in range(half):
        rows[:, c * CAP : (c + 1) * CAP, :] = mine[c]
        rows[:, (half + c) * CAP : (half + c + 1) * CAP, :] = swapped[c]
    small.wait()
    for j in range(groups):
        loads[j].wait()
        for b in range(share // QB):
            cols = slice(b * QB, (b + 1) * QB)
            part = lax.dot_general(
                rows[j, :, cols],
                quant[j, :, cols],
                (((1,), (1,)), ((), ())),
                preferred_element_type=f32,
            )
            for i in range(hid // QB):
                at = (slice(None), slice(i * QB, (i + 1) * QB))
                scaled = part[at] * scale[i, 0, (group ^ j) * (share // QB) + b]
                if j == 0 and b == 0:
                    acc[at] = scaled
                else:
                    acc[at] += scaled
    for copy in gates:
        copy.wait()
    gate = gate_up[:, :hid].astype(f32)
    up = gate_up[:, hid:].astype(f32)
    sig = jax.nn.sigmoid(gate)
    d_hidden = acc[...]
    out[:, :hid] = (d_hidden * up * sig * (1.0 + gate * (1.0 - sig))).astype(bf16)
    out[:, hid:] = (d_hidden * (gate * sig)).astype(bf16)
    stores = [
        pltpu.make_async_copy(out.at[pl.ds(r * CAP, CAP)], out_hbm.at[place(r)], out_sems.at[r])
        for r in range(flight)
    ]
    for copy in stores:
        copy.start()
    for copy in stores:
        copy.wait()


def backward(scale, gate_up, quant, tie, mine, swapped):
    slots, double = gate_up.shape
    hid, width = quant.shape
    half, groups, cap, share = swapped.shape
    flight = 2 * half
    return pl.pallas_call(
        functools.partial(backward_kernel, flight, groups),
        out_shape=pltpu.HBM((slots, double), bf16),
        in_specs=[HBM, HBM, HBM, ANY, VMEM, VMEM],
        out_specs=HBM,
        scratch_shapes=[
            pltpu.SMEM(scale.shape, f32),
            pltpu.VMEM((slots, double), bf16),
            pltpu.VMEM((groups, slots, share), bf16),
            pltpu.VMEM((groups, hid, share), bf16),
            pltpu.VMEM((slots, hid), f32),
            pltpu.VMEM((slots, double), bf16),
            pltpu.SemaphoreType.DMA,
            pltpu.SemaphoreType.DMA((flight,)),
            pltpu.SemaphoreType.DMA((groups,)),
            pltpu.SemaphoreType.DMA((flight,)),
        ],
        compiler_params=params(slots),
        cost_estimate=SMALL,
        name="expert_backward",
    )(hbm(scale), hbm(gate_up), hbm(quant), tie, mine, swapped)


def combine_kernel(
    block, ids_hbm, own_hbm, dout_hbm, ret_hbm, out_ref, dprobs_ref, ids_ref, own_ref, dout, ret_ref, sems
):
    copies = [
        pltpu.make_async_copy(ids_hbm, ids_ref, sems.at[0]),
        pltpu.make_async_copy(own_hbm, own_ref, sems.at[1]),
        pltpu.make_async_copy(dout_hbm, dout, sems.at[2]),
        pltpu.make_async_copy(ret_hbm, ret_ref, sems.at[3]),
    ]
    for copy in copies:
        copy.start()
    topk, tokens = ids_ref.shape
    slots = own_ref.shape[0]
    width = dout.shape[1]
    flight = slots // CAP
    me = lax.axis_index("expert")
    copies[1].wait()
    own = own_ref[...]
    turned = own.T
    high = turned.astype(bf16)
    low = (turned - high.astype(f32)).astype(bf16)
    total = jnp.zeros((slots, tokens), f32)
    for copy in (copies[0], copies[2], copies[3]):
        copy.wait()
    for cols in chunks(width, block):
        here = jnp.concatenate(
            [ret_ref[block_place(me, r, flight), :, cols] for r in range(flight)], axis=0
        )
        out = jnp.dot(high, here, preferred_element_type=f32)
        out = out + jnp.dot(low, here, preferred_element_type=f32)
        out_ref[:, cols] = out.astype(bf16)
        total = total + lax.dot_general(
            here, dout[:, cols], (((1,), (1,)), ((), ())), preferred_element_type=f32
        )
    inner = jnp.where(own > 0.0, total, 0.0)
    row_expert = block_place(me, lax.broadcasted_iota(jnp.int32, (slots, 1), 0) // CAP, flight)
    for k in range(topk):
        mine = jnp.where(ids_ref[k : k + 1, :] == row_expert, inner, 0.0)
        dprobs_ref[k : k + 1, :] = jnp.sum(mine, axis=0, keepdims=True)


def combine(ids, own, d_out, returned, block=1024):
    tokens, width = d_out.shape
    return pl.pallas_call(
        functools.partial(combine_kernel, block),
        out_shape=(
            pltpu.HBM((tokens, width), bf16),
            pltpu.HBM(ids.shape, f32),
        ),
        in_specs=[HBM, HBM, HBM, HBM],
        out_specs=(VMEM, VMEM),
        scratch_shapes=[
            pltpu.VMEM(ids.shape, jnp.int32),
            pltpu.VMEM(own.shape, f32),
            pltpu.VMEM((tokens, width), bf16),
            pltpu.VMEM(returned.shape, bf16),
            pltpu.SemaphoreType.DMA((4,)),
        ],
        compiler_params=params(own.shape[0]),
        cost_estimate=SMALL,
        name="combine",
    )(hbm(ids), hbm(own), hbm(d_out), hbm(returned))


def weight_grad_kernel(groups, block, tie_ref, mine, swapped, hidden_ref, *refs):
    parts, messages = refs[: groups - 1], refs[groups - 1 : 2 * groups - 2]
    out_hbm, hidden, own, out, out_sems = refs[2 * groups - 2 :]
    half = mine.shape[0]
    cap, share = parts[0].shape[1:]
    flight = 2 * half
    slots = flight * cap
    wide = hidden_ref.shape[1] // TILE
    hidden[:slots, :] = hidden_ref[...]
    for j in range(1, groups):
        bit = j if j % 2 else max(b for b in bits_of(groups) if b <= j)
        message = messages[j - 1]
        for r in range(flight):
            for q in range(wide):
                hidden[
                    j * slots + r * cap : j * slots + (r + 1) * cap, q * TILE : (q + 1) * TILE
                ] = message[r * wide + q]
        for q in range(share // TILE):
            own[j - 1, :, q * TILE : (q + 1) * TILE] = message[
                flight * wide + (j - bit) * (share // TILE) + q
            ]
    stores = []
    for n, cols in enumerate(chunks(share, block)):
        grads = [mine[c, 0, :, cols] for c in range(half)]
        grads += [swapped[c, 0, :, cols] for c in range(half)]
        for j in range(1, groups):
            grads.append(own[j - 1, :, cols])
            grads.append(parts[j - 1][:, :, cols].reshape(slots - cap, block))
        out[cols, :] = lax.dot_general(
            jnp.concatenate(grads, axis=0),
            hidden[...],
            (((0,), (0,)), ((), ())),
            preferred_element_type=f32,
        ).astype(bf16)
        stores.append(pltpu.make_async_copy(out.at[cols], out_hbm.at[cols], out_sems.at[n]))
        stores[n].start()
    for copy in stores:
        copy.wait()


def weight_grad(tie, mine, swapped, hidden, parts, messages, block=256):
    half, groups, cap, share = swapped.shape
    slots, hid = hidden.shape
    return pl.pallas_call(
        functools.partial(weight_grad_kernel, groups, block),
        out_shape=pltpu.HBM((share, hid), bf16),
        in_specs=[HBM] + [VMEM] * (1 + 2 * groups),
        out_specs=HBM,
        scratch_shapes=[
            pltpu.VMEM((groups * slots, hid), bf16),
            pltpu.VMEM((groups - 1, cap, share), bf16),
            pltpu.VMEM((share, hid), bf16),
            pltpu.SemaphoreType.DMA((share // block,)),
        ],
        compiler_params=params(slots),
        cost_estimate=SMALL,
        name="weight_grad",
    )(hbm(tie), mine, swapped, hidden, *parts, *messages)


def swap(value, axis, j):
    size = lax.axis_size(axis)
    return lax.ppermute(value, axis, [(i, i ^ j) for i in range(size)])


def shards(route_ids, route_probs, capacity, hot_lists, gate_up, w_quant, w_scale, d_out):
    flight = lax.axis_size("expert")
    groups = lax.axis_size("dp")
    gate_up = gate_up[0, 0]
    ids, probs = route_ids.T, route_probs.T
    scale = w_scale.transpose(1, 0, 2)
    own, hidden, *rest = dispatch(
        gate_up, capacity, hot_lists, ids, probs, d_out, flight, groups
    )
    half, bits = flight // 2, bits_of(groups)
    chips = rest[:1] + [swap(rest[c], "expert", 2 * c) for c in range(1, half)]
    messages, early = {}, []
    for bit, message in zip(bits, rest[half:]):
        if bit > 1:
            for j in sorted(messages):
                messages[j ^ bit] = swap(messages[j], "dp", bit)
        messages[bit] = swap(message, "dp", bit)
        early.append(messages[bit])
    even = list(range(2, groups, 2))
    picks = [j + 1 - max(bit for bit in bits if bit <= j) for j in even]
    expert_out = forward(scale, hidden, w_quant[0], flight)
    returned = lax.all_to_all(expert_out, "expert", split_axis=0, concat_axis=0, tiled=True)
    sibling, mine = sort_rows(chips, [hbm(expert_out)] + early)
    swapped = swap(sibling, "expert", 1)
    keep, tall = flight * (hidden.shape[1] // TILE), d_out.shape[1] // groups // TILE
    for j, message in zip(even, cut([messages[j] for j in even], picks, mine, keep, tall)):
        messages[j + 1] = swap(message, "dp", 1)
    messages = [messages[j] for j in range(1, groups)]
    pieces = split(mine, swapped)
    parts = [swap(pieces[j - 1], "dp", j) for j in range(1, groups)]
    d_gate_up = backward(scale, gate_up, w_quant[0], pieces[0], mine, swapped)
    combined, d_probs = combine(ids, own, d_out, returned)
    d_weight = weight_grad(d_probs, mine, swapped, hidden, parts, messages)
    return (combined, d_probs.T, d_gate_up[None, None], d_weight[None])


def solution(mesh):
    placed = (
        P(("dp", "expert"), None),
        P(("dp", "expert"), None),
        P(),
        P("dp", None),
        P("dp", "expert", None, None),
        P("expert", None, None),
        P("expert", None, None),
        P(("dp", "expert"), None),
    )
    return jax.shard_map(
        shards,
        mesh=mesh,
        in_specs=placed,
        out_specs=(
            P(("dp", "expert"), None),
            P(("dp", "expert"), None),
            P("dp", "expert", None, None),
            P("expert", "dp", None),
        ),
        check_vma=False,
    )
```

```python
import functools

import jax
import jax.numpy as jnp
from jax import lax
from jax.experimental import pallas as pl
from jax.experimental.pallas import tpu as pltpu
from jax.sharding import PartitionSpec as P

QB = 128
CAP = 16
TILE = 256

bf16 = jnp.bfloat16
f32 = jnp.float32

SMALL = pl.CostEstimate(flops=1024, bytes_accessed=1024, transcendentals=0)

VMEM = pl.BlockSpec(memory_space=pltpu.VMEM)
ANY = pl.BlockSpec(memory_space=pl.ANY)
HBM = pl.BlockSpec(memory_space=pltpu.HBM)


def params(slots):
    return pltpu.CompilerParams(vmem_limit_bytes=(12 + slots // 32) * 1024 * 1024)


def hbm(value):
    return pltpu.with_memory_space_constraint(value, pltpu.HBM)


def chunks(total, size):
    return [pl.ds(start, size) for start in range(0, total, size)]


def bits_of(groups):
    bits = []
    while groups > 1:
        groups //= 2
        bits.append(groups)
    return bits


def message_tiles(flight, groups, bit, hid, share):
    far = 1 if 2 * bit == groups else 0
    return flight * (hid // TILE) + bit * (share // TILE) + far


def block_place(me, r, flight):
    half = flight // 2
    return me ^ (2 * (r % half) + r // half)


def dispatch_kernel(flight, groups, gate_up_hbm, cap_hbm, hot_hbm, ids_hbm, probs_hbm, dout_hbm, *refs):
    half = flight // 2
    bits = bits_of(groups)
    outs = 2 + half + len(bits)
    own_hbm, hidden_ref, *chips = refs[: 2 + half]
    messages = dict(zip(bits, refs[2 + half : outs]))
    gate_up, cap_ref, hot_ref, ids_ref, probs_ref, dout, own_ref = refs[outs : outs + 7]
    gate_sems, own_sem, small_sems, in_sems = refs[outs + 7 :]
    topk, tokens = ids_ref.shape
    slots = flight * CAP
    me, group = lax.axis_index("expert"), lax.axis_index("dp")
    share = dout_hbm.shape[1] // groups
    hid = hidden_ref.shape[1]
    small = [
        pltpu.make_async_copy(src, dst, small_sems.at[i])
        for i, (src, dst) in enumerate(
            [(ids_hbm, ids_ref), (probs_hbm, probs_ref), (cap_hbm, cap_ref), (hot_hbm, hot_ref)]
        )
    ]
    loads = [
        pltpu.make_async_copy(
            dout_hbm.at[:, pl.ds(pl.multiple_of((group ^ j) * share, share), share)],
            dout.at[j],
            in_sems.at[j],
        )
        for j in range(groups)
    ]
    gates = [
        pltpu.make_async_copy(
            gate_up_hbm.at[pl.ds(pl.multiple_of(block_place(me, r, flight) * CAP, CAP), CAP)],
            gate_up.at[pl.ds(r * CAP, CAP)],
            gate_sems.at[r],
        )
        for r in range(flight)
    ]
    for copy in small + loads + gates:
        copy.start()
    for copy in small:
        copy.wait()
    row = lax.broadcasted_iota(jnp.int32, (slots, 1), 0)
    row_expert = block_place(me, row // CAP, flight)
    row_rank = (row % CAP).astype(f32)
    limit = jnp.zeros((slots, 1), jnp.int32)
    for e in range(flight):
        hot = hot_ref[0, 0] == e
        for h in range(1, hot_ref.shape[1]):
            hot = jnp.logical_or(hot, hot_ref[0, h] == e)
        limit = jnp.where(row_expert == e, jnp.where(hot, CAP, cap_ref[e]), limit)
    limit = limit.astype(f32)
    named = jnp.zeros((slots, tokens), f32)
    weight = jnp.zeros((slots, tokens), f32)
    for k in range(topk):
        hit = ids_ref[k : k + 1, :] == row_expert
        named = jnp.where(hit, 1.0, named)
        weight = jnp.where(hit, probs_ref[k : k + 1, :], weight)
    earlier = lax.broadcasted_iota(jnp.int32, (tokens, tokens), 0)
    later = lax.broadcasted_iota(jnp.int32, (tokens, tokens), 1)
    before = (earlier < later).astype(f32).astype(bf16)
    rank = jnp.dot(named.astype(bf16), before, preferred_element_type=f32)
    owns = (named > 0.0) & (rank == row_rank) & (rank < limit)
    own_weight = jnp.where(owns, weight, 0.0)
    own_ref[...] = own_weight
    own_copy = pltpu.make_async_copy(own_ref, own_hbm, own_sem)
    own_copy.start()
    owner = jnp.where(owns, 1.0, 0.0).astype(bf16)
    slot_weight = jnp.sum(own_weight, axis=1, keepdims=True)
    for copy in loads:
        copy.wait()
    for j in range(groups):
        part = jnp.dot(owner, dout[j], preferred_element_type=f32)
        part = (part * slot_weight).astype(bf16)
        for r in range(flight):
            chips[r % half][r // half, j] = part[r * CAP : (r + 1) * CAP, :]
        for bit in bits:
            if bit <= j < 2 * bit:
                first = flight * (hid // TILE) + (j - bit) * (share // TILE)
                for q in range(share // TILE):
                    messages[bit][first + q] = part[:CAP, q * TILE : (q + 1) * TILE]
    messages[bits[0]][messages[bits[0]].shape[0] - 1] = jnp.zeros((CAP, TILE), bf16)
    for copy in gates:
        copy.wait()
    for r in range(flight):
        at = slice(r * CAP, (r + 1) * CAP)
        gate = gate_up[at, :hid].astype(f32)
        up = gate_up[at, hid:].astype(f32)
        block = (gate * jax.nn.sigmoid(gate) * up).astype(bf16)
        hidden_ref[at, :] = block
        for bit in bits:
            for q in range(hid // TILE):
                messages[bit][r * (hid // TILE) + q] = block[:, q * TILE : (q + 1) * TILE]
    own_copy.wait()


def dispatch(gate_up, capacity, hot_row, ids, probs, d_out, flight, groups):
    tokens, width = d_out.shape
    rows, double = gate_up.shape
    slots = flight * CAP
    share = width // groups
    half = flight // 2
    return pl.pallas_call(
        functools.partial(dispatch_kernel, flight, groups),
        out_shape=(pltpu.HBM((slots, tokens), f32), pltpu.VMEM((rows, double // 2), bf16))
        + (pltpu.VMEM((2, groups, CAP, share), bf16),) * half
        + tuple(
            pltpu.VMEM((message_tiles(flight, groups, bit, double // 2, share), CAP, TILE), bf16)
            for bit in bits_of(groups)
        ),
        in_specs=[HBM] * 6,
        out_specs=(HBM, VMEM) + (VMEM,) * (half + len(bits_of(groups))),
        scratch_shapes=[
            pltpu.VMEM((rows, double), bf16),
            pltpu.SMEM(capacity.shape, jnp.int32),
            pltpu.SMEM(hot_row.shape, jnp.int32),
            pltpu.VMEM(ids.shape, jnp.int32),
            pltpu.VMEM(probs.shape, f32),
            pltpu.VMEM((groups, tokens, share), bf16),
            pltpu.VMEM((slots, tokens), f32),
            pltpu.SemaphoreType.DMA((flight,)),
            pltpu.SemaphoreType.DMA,
            pltpu.SemaphoreType.DMA((4,)),
            pltpu.SemaphoreType.DMA((groups,)),
        ],
        compiler_params=params(slots),
        cost_estimate=SMALL,
        name="dispatch",
    )(hbm(gate_up), hbm(capacity), hbm(hot_row), hbm(ids), hbm(probs), hbm(d_out))


def forward_kernel(
    flight, block, hidden_ref, scale_hbm, quant_hbm, out_hbm,
    scale, hidden, quant, out, scale_sem, in_sems, out_sems
):
    steps, hid, _ = quant.shape
    me = lax.axis_index("expert")
    loads = [
        pltpu.make_async_copy(quant_hbm.at[:, pl.ds(c * block, block)], quant.at[c], in_sems.at[c])
        for c in range(steps)
    ]
    small = pltpu.make_async_copy(scale_hbm, scale, scale_sem)
    for copy in [small] + loads:
        copy.start()
    for r in range(flight):
        place = pl.multiple_of(block_place(me, r, flight) * CAP, CAP)
        hidden[pl.ds(place, CAP), :] = hidden_ref[pl.ds(r * CAP, CAP), :]
    small.wait()
    stores = []
    for c in range(steps):
        cols = pl.ds(c * block, block)
        loads[c].wait()
        total = [None] * (block // QB)
        for i in range(hid // QB):
            part = jnp.dot(
                hidden[:, i * QB : (i + 1) * QB],
                quant[c, i * QB : (i + 1) * QB, :],
                preferred_element_type=f32,
            )
            for j in range(block // QB):
                scaled = part[:, j * QB : (j + 1) * QB] * scale[i, 0, c * (block // QB) + j]
                total[j] = scaled if i == 0 else total[j] + scaled
        for j in range(block // QB):
            at = pl.ds(c * block + j * QB, QB)
            out[:, :, at] = total[j].astype(bf16).reshape(flight, CAP, QB)
        stores.append(
            pltpu.make_async_copy(out.at[:, :, cols], out_hbm.at[:, :, cols], out_sems.at[c])
        )
        stores[c].start()
    for copy in stores:
        copy.wait()


def forward(scale, hidden, quant, flight, block=512):
    hid, width = quant.shape
    steps = width // block
    return pl.pallas_call(
        functools.partial(forward_kernel, flight, block),
        out_shape=pltpu.HBM((flight, CAP, width), bf16),
        in_specs=[VMEM, HBM, HBM],
        out_specs=HBM,
        scratch_shapes=[
            pltpu.SMEM(scale.shape, f32),
            pltpu.VMEM(hidden.shape, bf16),
            pltpu.VMEM((steps, hid, block), bf16),
            pltpu.VMEM((flight, CAP, width), bf16),
            pltpu.SemaphoreType.DMA,
            pltpu.SemaphoreType.DMA((steps,)),
            pltpu.SemaphoreType.DMA((steps,)),
        ],
        compiler_params=params(flight * CAP),
        cost_estimate=SMALL,
        name="expert_forward",
    )(hidden, hbm(scale), hbm(quant))


def sort_kernel(half, *refs):
    chips, (sibling, mine) = refs[:half], refs[-2:]
    for c in range(half):
        sibling[c] = chips[c][1]
        mine[c] = chips[c][0]


def sort_rows(chips, ties):
    half = len(chips)
    return pl.pallas_call(
        functools.partial(sort_kernel, half),
        out_shape=(pltpu.VMEM((half,) + chips[0].shape[1:], bf16),) * 2,
        in_specs=[VMEM] * half + [ANY] * len(ties),
        out_specs=(VMEM, VMEM),
        compiler_params=params(2 * half * CAP),
        cost_estimate=SMALL,
        name="sort_rows",
    )(*chips, *ties)


def split_kernel(mine, swapped, *pieces):
    half = mine.shape[0]
    for j, piece in enumerate(pieces, 1):
        piece[: half - 1] = mine[1:, j]
        piece[half - 1 :] = swapped[:, j]


def split(mine, swapped):
    half, groups, cap, share = swapped.shape
    return pl.pallas_call(
        split_kernel,
        out_shape=(pltpu.VMEM((2 * half - 1, cap, share), bf16),) * (groups - 1),
        in_specs=[VMEM, VMEM],
        out_specs=(VMEM,) * (groups - 1),
        compiler_params=params(2 * half * CAP),
        cost_estimate=SMALL,
        name="split",
    )(mine, swapped)


def backward_kernel(
    flight, groups, scale_hbm, gate_up_hbm, quant_hbm, tie_ref, mine, swapped, out_hbm,
    scale, gate_up, rows, quant, acc, out, scale_sem, gate_sems, in_sems, out_sems
):
    half = flight // 2
    me, group = lax.axis_index("expert"), lax.axis_index("dp")
    slots, hid = acc.shape
    share = quant.shape[2]

    def place(r):
        return pl.ds(pl.multiple_of(block_place(me, r, flight) * CAP, CAP), CAP)

    loads = [
        pltpu.make_async_copy(
            quant_hbm.at[:, pl.ds(pl.multiple_of((group ^ j) * share, share), share)],
            quant.at[j],
            in_sems.at[j],
        )
        for j in range(groups)
    ]
    gates = [
        pltpu.make_async_copy(
            gate_up_hbm.at[place(r)], gate_up.at[pl.ds(r * CAP, CAP)], gate_sems.at[r]
        )
        for r in range(flight)
    ]
    small = pltpu.make_async_copy(scale_hbm, scale, scale_sem)
    for copy in [small] + loads + gates:
        copy.start()
    for c in range(half):
        rows[:, c * CAP : (c + 1) * CAP, :] = mine[c]
        rows[:, (half + c) * CAP : (half + c + 1) * CAP, :] = swapped[c]
    small.wait()
    for j in range(groups):
        loads[j].wait()
        for b in range(share // QB):
            cols = slice(b * QB, (b + 1) * QB)
            part = lax.dot_general(
                rows[j, :, cols],
                quant[j, :, cols],
                (((1,), (1,)), ((), ())),
                preferred_element_type=f32,
            )
            for i in range(hid // QB):
                at = (slice(None), slice(i * QB, (i + 1) * QB))
                scaled = part[at] * scale[i, 0, (group ^ j) * (share // QB) + b]
                if j == 0 and b == 0:
                    acc[at] = scaled
                else:
                    acc[at] += scaled
    for copy in gates:
        copy.wait()
    gate = gate_up[:, :hid].astype(f32)
    up = gate_up[:, hid:].astype(f32)
    sig = jax.nn.sigmoid(gate)
    d_hidden = acc[...]
    out[:, :hid] = (d_hidden * up * sig * (1.0 + gate * (1.0 - sig))).astype(bf16)
    out[:, hid:] = (d_hidden * (gate * sig)).astype(bf16)
    stores = [
        pltpu.make_async_copy(out.at[pl.ds(r * CAP, CAP)], out_hbm.at[place(r)], out_sems.at[r])
        for r in range(flight)
    ]
    for copy in stores:
        copy.start()
    for copy in stores:
        copy.wait()


def backward(scale, gate_up, quant, tie, mine, swapped):
    slots, double = gate_up.shape
    hid, width = quant.shape
    half, groups, cap, share = swapped.shape
    flight = 2 * half
    return pl.pallas_call(
        functools.partial(backward_kernel, flight, groups),
        out_shape=pltpu.HBM((slots, double), bf16),
        in_specs=[HBM, HBM, HBM, ANY, VMEM, VMEM],
        out_specs=HBM,
        scratch_shapes=[
            pltpu.SMEM(scale.shape, f32),
            pltpu.VMEM((slots, double), bf16),
            pltpu.VMEM((groups, slots, share), bf16),
            pltpu.VMEM((groups, hid, share), bf16),
            pltpu.VMEM((slots, hid), f32),
            pltpu.VMEM((slots, double), bf16),
            pltpu.SemaphoreType.DMA,
            pltpu.SemaphoreType.DMA((flight,)),
            pltpu.SemaphoreType.DMA((groups,)),
            pltpu.SemaphoreType.DMA((flight,)),
        ],
        compiler_params=params(slots),
        cost_estimate=SMALL,
        name="expert_backward",
    )(hbm(scale), hbm(gate_up), hbm(quant), tie, mine, swapped)


def combine_kernel(
    block, ids_hbm, own_hbm, dout_hbm, ret_hbm, out_ref, dprobs_ref, ids_ref, own_ref, dout, ret_ref, sems
):
    copies = [
        pltpu.make_async_copy(ids_hbm, ids_ref, sems.at[0]),
        pltpu.make_async_copy(own_hbm, own_ref, sems.at[1]),
        pltpu.make_async_copy(dout_hbm, dout, sems.at[2]),
        pltpu.make_async_copy(ret_hbm, ret_ref, sems.at[3]),
    ]
    for copy in copies:
        copy.start()
    topk, tokens = ids_ref.shape
    slots = own_ref.shape[0]
    width = dout.shape[1]
    flight = slots // CAP
    me = lax.axis_index("expert")
    copies[1].wait()
    own = own_ref[...]
    turned = own.T
    high = turned.astype(bf16)
    low = (turned - high.astype(f32)).astype(bf16)
    total = jnp.zeros((slots, tokens), f32)
    for copy in (copies[0], copies[2], copies[3]):
        copy.wait()
    for cols in chunks(width, block):
        here = jnp.concatenate(
            [ret_ref[block_place(me, r, flight), :, cols] for r in range(flight)], axis=0
        )
        out = jnp.dot(high, here, preferred_element_type=f32)
        out = out + jnp.dot(low, here, preferred_element_type=f32)
        out_ref[:, cols] = out.astype(bf16)
        total = total + lax.dot_general(
            here, dout[:, cols], (((1,), (1,)), ((), ())), preferred_element_type=f32
        )
    inner = jnp.where(own > 0.0, total, 0.0)
    row_expert = block_place(me, lax.broadcasted_iota(jnp.int32, (slots, 1), 0) // CAP, flight)
    for k in range(topk):
        mine = jnp.where(ids_ref[k : k + 1, :] == row_expert, inner, 0.0)
        dprobs_ref[k : k + 1, :] = jnp.sum(mine, axis=0, keepdims=True)


def combine(ids, own, d_out, returned, block=1024):
    tokens, width = d_out.shape
    return pl.pallas_call(
        functools.partial(combine_kernel, block),
        out_shape=(
            pltpu.HBM((tokens, width), bf16),
            pltpu.HBM(ids.shape, f32),
        ),
        in_specs=[HBM, HBM, HBM, HBM],
        out_specs=(VMEM, VMEM),
        scratch_shapes=[
            pltpu.VMEM(ids.shape, jnp.int32),
            pltpu.VMEM(own.shape, f32),
            pltpu.VMEM((tokens, width), bf16),
            pltpu.VMEM(returned.shape, bf16),
            pltpu.SemaphoreType.DMA((4,)),
        ],
        compiler_params=params(own.shape[0]),
        cost_estimate=SMALL,
        name="combine",
    )(hbm(ids), hbm(own), hbm(d_out), hbm(returned))


def weight_grad_kernel(groups, block, tie_ref, mine, swapped, hidden_ref, *refs):
    parts, messages = refs[: groups - 1], refs[groups - 1 : 2 * groups - 2]
    out_hbm, hidden, own, out, out_sems = refs[2 * groups - 2 :]
    half = mine.shape[0]
    cap, share = parts[0].shape[1:]
    flight = 2 * half
    slots = flight * cap
    wide = hidden_ref.shape[1] // TILE
    hidden[:slots, :] = hidden_ref[...]
    for j in range(1, groups):
        bit = max(b for b in bits_of(groups) if b <= j)
        message = messages[j - 1]
        for r in range(flight):
            for q in range(wide):
                hidden[
                    j * slots + r * cap : j * slots + (r + 1) * cap, q * TILE : (q + 1) * TILE
                ] = message[r * wide + q]
        for q in range(share // TILE):
            own[j - 1, :, q * TILE : (q + 1) * TILE] = message[
                flight * wide + (j - bit) * (share // TILE) + q
            ]
    stores = []
    for n, cols in enumerate(chunks(share, block)):
        grads = [mine[c, 0, :, cols] for c in range(half)]
        grads += [swapped[c, 0, :, cols] for c in range(half)]
        for j in range(1, groups):
            grads.append(own[j - 1, :, cols])
            grads.append(parts[j - 1][:, :, cols].reshape(slots - cap, block))
        out[cols, :] = lax.dot_general(
            jnp.concatenate(grads, axis=0),
            hidden[...],
            (((0,), (0,)), ((), ())),
            preferred_element_type=f32,
        ).astype(bf16)
        stores.append(pltpu.make_async_copy(out.at[cols], out_hbm.at[cols], out_sems.at[n]))
        stores[n].start()
    for copy in stores:
        copy.wait()


def weight_grad(tie, mine, swapped, hidden, parts, messages, block=512):
    half, groups, cap, share = swapped.shape
    slots, hid = hidden.shape
    return pl.pallas_call(
        functools.partial(weight_grad_kernel, groups, block),
        out_shape=pltpu.HBM((share, hid), bf16),
        in_specs=[HBM] + [VMEM] * (1 + 2 * groups),
        out_specs=HBM,
        scratch_shapes=[
            pltpu.VMEM((groups * slots, hid), bf16),
            pltpu.VMEM((groups - 1, cap, share), bf16),
            pltpu.VMEM((share, hid), bf16),
            pltpu.SemaphoreType.DMA((share // block,)),
        ],
        compiler_params=params(slots),
        cost_estimate=SMALL,
        name="weight_grad",
    )(hbm(tie), mine, swapped, hidden, *parts, *messages)


def swap(value, axis, j):
    size = lax.axis_size(axis)
    return lax.ppermute(value, axis, [(i, i ^ j) for i in range(size)])


def shards(route_ids, route_probs, capacity, hot_lists, gate_up, w_quant, w_scale, d_out):
    flight = lax.axis_size("expert")
    groups = lax.axis_size("dp")
    gate_up = gate_up[0, 0]
    ids, probs = route_ids.T, route_probs.T
    scale = w_scale.transpose(1, 0, 2)
    own, hidden, *rest = dispatch(
        gate_up, capacity, hot_lists, ids, probs, d_out, flight, groups
    )
    half, bits = flight // 2, bits_of(groups)
    chips = rest[:1] + [swap(rest[c], "expert", 2 * c) for c in range(1, half)]
    messages, early = {}, []
    for bit, message in zip(bits, rest[half:]):
        for j in sorted(messages):
            messages[j ^ bit] = swap(messages[j], "dp", bit)
        messages[bit] = swap(message, "dp", bit)
        early.append(messages[bit])
    messages = [messages[j] for j in range(1, groups)]
    expert_out = forward(scale, hidden, w_quant[0], flight)
    returned = lax.all_to_all(expert_out, "expert", split_axis=0, concat_axis=0, tiled=True)
    sibling, mine = sort_rows(chips, [hbm(expert_out)] + early)
    swapped = swap(sibling, "expert", 1)
    pieces = split(mine, swapped)
    parts = [swap(pieces[j - 1], "dp", j) for j in range(1, groups)]
    d_gate_up = backward(scale, gate_up, w_quant[0], pieces[0], mine, swapped)
    combined, d_probs = combine(ids, own, d_out, returned)
    d_weight = weight_grad(d_probs, mine, swapped, hidden, parts, messages)
    return (combined, d_probs.T, d_gate_up[None, None], d_weight[None])


def solution(mesh):
    placed = (
        P(("dp", "expert"), None),
        P(("dp", "expert"), None),
        P(),
        P("dp", None),
        P("dp", "expert", None, None),
        P("expert", None, None),
        P("expert", None, None),
        P(("dp", "expert"), None),
    )
    return jax.shard_map(
        shards,
        mesh=mesh,
        in_specs=placed,
        out_specs=(
            P(("dp", "expert"), None),
            P(("dp", "expert"), None),
            P("dp", "expert", None, None),
            P("expert", "dp", None),
        ),
        check_vma=False,
    )
```
